32 devices in a mesh: orb: 4 (over z), pair: 8 (over y, x, core).
Axes of the slice: x: 2, y: 2, z: 4, core: 2. Of those that a mesh axis runs over, the one named last changes fastest.
Arguments:
- blocks: bfloat16 [128, 1024, 320], P(('orb', 'pair')), may hold values from -1.1953125 to 1.1953125
- aux_domain: int32 [128, 1024], replicated, may hold values from 0 to 2047, as said below
- pao_domain: int32 [128, 320], replicated, may hold values from -1 to 639, as said below
- pao_gap: float32 [128, 320], replicated, may hold values from 1 to 4
- amplitudes: bfloat16 [256, 320, 320], P(('orb', 'pair')), may hold values from -3 to 3
- pair_partner: int32 [256], replicated, may hold values from 0 to 127, as said below
- coupling_list: int32 [256, 4], P(('orb', 'pair')), may hold values from 0 to 255, as said below
- coupling_coef: float32 [256, 4], P(('orb', 'pair')), may hold values from -0.6 to 0.6
Outputs:
- new_amplitudes: bfloat16 [256, 320, 320], P(('orb', 'pair'))
- pair_energy: float32 [256], P(('orb', 'pair'))
- densities: float32 [128, 320, 320], P(('orb', 'pair'))
The draws below stay inside these ranges and needn't reach their ends.
Inputs may be any that keep to these rules, and one draw needn't show every extreme that they name: `aux_domain`: each row holds 1024 distinct auxiliary function ids. `pao_domain`: each row holds distinct PAO ids in its leading slots and -1 in the rest; at least 160 ids a row. With d = p // 8, pair_partner[p] lies in [(d - 1) * 4, (d + 2) * 4). `coupling_list`: row p lists pair ids q with 0 < |q - p| <= 8.
All inputs are finite; a program needn't handle non-finite values.
Results may differ from the reference program's by a relative error of at most 0.003.
Values may be sent and summed in bfloat16 or wider, within the bound.
No kernel may reach another device: no remote copies, remote signals or barrier semaphores. Data moves between devices by JAX's collectives and lax.ppermute only.
A program may use at most 128 MiB of HBM per device.

```python
import jax
import jax.numpy as jnp
from jax import lax

NAUX = 1024
NPAO = 320
NAUXG = 2048
NPAOG = 640
OCC_DEV = 4
PAIR_DEV = 8
NCPL = 4
NOCC = 128
NPAIR = 256


def draw_aux_domain(key, part):
    keys = jax.random.split(key, NOCC)
    rows = jax.vmap(lambda one: jax.random.permutation(one, NAUXG)[:NAUX])(keys)
    return rows.astype(jnp.int32)


def draw_pao_domain(key, part):
    key_perm, key_len = jax.random.split(key)
    keys = jax.random.split(key_perm, NOCC)
    ids = jax.vmap(lambda one: jax.random.permutation(one, NPAOG)[:NPAO])(keys).astype(jnp.int32)
    lens = jax.random.randint(key_len, (NOCC,), NPAO // 2, NPAO + 1)
    lens = lens.at[0].set(NPAO)
    live = jnp.arange(NPAO)[None, :] < lens[:, None]
    return jnp.where(live, ids, -1).astype(jnp.int32)


def draw_pair_partner(key, part):
    pair_ids = jnp.arange(NPAIR)
    lowest = (pair_ids // PAIR_DEV - 1) * OCC_DEV
    offset = jax.random.randint(key, (NPAIR,), 0, 3 * OCC_DEV)
    chosen = lowest + offset
    chosen = jnp.where(chosen < 0, chosen + OCC_DEV, chosen)
    chosen = jnp.where(chosen >= NOCC, chosen - OCC_DEV, chosen)
    return chosen.astype(jnp.int32)


def draw_coupling_list(key, part):
    key_mag, key_sign = jax.random.split(key)
    magnitude = jax.random.randint(key_mag, (NPAIR, NCPL), 1, PAIR_DEV + 1)
    sign = jax.random.randint(key_sign, (NPAIR, NCPL), 0, 2) * 2 - 1
    pair_ids = jnp.arange(NPAIR)[:, None]
    chosen = pair_ids + sign * magnitude
    chosen = jnp.where(chosen < 0, pair_ids + magnitude, chosen)
    chosen = jnp.where(chosen >= NPAIR, pair_ids - magnitude, chosen)
    return chosen.astype(jnp.int32)


def level_of(rng, dims, pieces, least, high):
    def one(dim, parts):
        draws = jax.random.uniform(jax.random.fold_in(jax.random.fold_in(rng, 6), dim), (parts,), jnp.float32, least / len(pieces), high / len(pieces))
        return jnp.repeat(jnp.exp(draws), dims[dim] // parts).reshape((-1,) + (1,) * (len(dims) - dim - 1))

    factor_of = one(*pieces[0])
    for cut in pieces[1:]:
        factor_of = factor_of * one(*cut)
    return factor_of


def centred(key, extent, deviation, bound, pieces=(), held_as=jnp.bfloat16):
    array = jax.random.normal(key, extent, jnp.float32) * deviation
    if len(pieces) > 0:
        array = level_of(key, extent, pieces, -0.22, 0.18) * array
    return jnp.clip(array, min=-bound, max=bound).astype(held_as)


def setup_inputs(seed: int = 0) -> dict:
    seeds = jax.random.split(jax.random.key(seed), 9)
    blocks = centred(seeds[0], (NOCC, NAUX, NPAO), 0.2, 1.1953125, ((0, 32),))
    aux_domain = draw_aux_domain(jax.random.fold_in(seeds[8], 71), 0)
    pao_domain = draw_pao_domain(jax.random.fold_in(seeds[8], 71), 0)
    pao_gap = jnp.clip(jax.random.uniform(seeds[3], (NOCC, NPAO), jnp.float32, 1.0, 4.0), 1.0, 4.0)
    amplitudes = centred(seeds[4], (NPAIR, NPAO, NPAO), 0.5, 3.0, ((0, 32),))
    pair_partner = draw_pair_partner(jax.random.fold_in(seeds[8], 71), 0)
    coupling_list = draw_coupling_list(jax.random.fold_in(seeds[8], 71), 0)
    coupling_coef = jnp.clip(jax.random.uniform(seeds[7], (NPAIR, NCPL), jnp.float32, -0.6, 0.6) * level_of(seeds[7], (NPAIR, NCPL), ((0, 32),), -0.4, 0.0), -0.6, 0.6)
    return {"blocks": blocks, "aux_domain": aux_domain, "pao_domain": pao_domain, "pao_gap": pao_gap, "amplitudes": amplitudes, "pair_partner": pair_partner, "coupling_list": coupling_list, "coupling_coef": coupling_coef}


def first_orbital(pair_id):
    return ((pair_id // PAIR_DEV) * OCC_DEV + pair_id % OCC_DEV).astype(jnp.int32)


def inverse_map(domain, width):
    places = jnp.where(domain >= 0, domain, width)
    return jnp.full((width,), -1, jnp.int32).at[places].set(jnp.arange(domain.shape[0], dtype=jnp.int32), mode="drop")


def lookup(table, ids):
    found = table[jnp.clip(ids, 0, table.shape[0] - 1)]
    return jnp.where(ids >= 0, found, -1).astype(jnp.int32)


def take_rows(block, index):
    rows = jnp.take(block, jnp.clip(index, 0, block.shape[0] - 1), axis=0)
    keep = (index >= 0).reshape((-1,) + (1,) * (block.ndim - 1))
    return jnp.where(keep, rows, jnp.zeros_like(rows))


def pair_terms(left_block, right_block, aux_left, aux_right, pao_left, pao_right, gap_left, gap_right, amp, near_amps, near_left, near_right, coefs):
    index = lookup(inverse_map(aux_right, NAUXG), aux_left)
    aligned = take_rows(right_block, index)
    mask_left = (pao_left >= 0).astype(jnp.float32)
    mask_right = (pao_right >= 0).astype(jnp.float32)
    both = mask_left[:, None] * mask_right[None, :]
    exchange = lax.dot_general(left_block, aligned, (((0,), (0,)), ((), ())), preferred_element_type=jnp.float32) * both
    masked = (amp.astype(jnp.float32) * both).astype(jnp.bfloat16)

    def project(near_amp, pao_near_left, pao_near_right, coef):
        rows = lookup(inverse_map(pao_near_left, NPAOG), pao_left)
        cols = lookup(inverse_map(pao_near_right, NPAOG), pao_right)
        picked = take_rows(near_amp, rows)
        picked = take_rows(picked.T, cols).T
        return coef * picked.astype(jnp.float32)

    coupling = jnp.sum(jax.vmap(project)(near_amps, near_left, near_right, coefs), axis=0)
    denom = gap_left[:, None] + gap_right[None, :]
    masked_f = masked.astype(jnp.float32)
    residual = exchange + denom * masked_f - coupling
    new_amp = (masked_f - 0.5 * residual / denom).astype(jnp.bfloat16)
    energy = jnp.sum(exchange * masked_f) / masked.shape[0]
    return new_amp, energy, masked


def left_density(masked):
    return jnp.dot(masked, masked.T, preferred_element_type=jnp.float32) / masked.shape[0]


def right_density(masked):
    return lax.dot_general(masked, masked, (((0,), (0,)), ((), ())), preferred_element_type=jnp.float32) / masked.shape[0]


def reference(blocks, aux_domain, pao_domain, pao_gap, amplitudes, pair_partner, coupling_list, coupling_coef):
    pair_ids = jnp.arange(NPAIR, dtype=jnp.int32)

    def step(dens, items):
        pair_id, amp, neighbours, coefs = items
        left = first_orbital(pair_id)
        right = pair_partner[pair_id]
        new_amp, energy, masked = pair_terms(blocks[left], blocks[right], aux_domain[left], aux_domain[right], pao_domain[left], pao_domain[right], pao_gap[left], pao_gap[right], amp, amplitudes[neighbours], pao_domain[first_orbital(neighbours)], pao_domain[pair_partner[neighbours]], coefs)
        dens = dens.at[left].add(left_density(masked))
        dens = dens.at[right].add(right_density(masked))
        return dens, (new_amp, energy)

    start = jnp.zeros((NOCC, NPAO, NPAO), jnp.float32)
    dens, (new_amps, energies) = lax.scan(step, start, (pair_ids, amplitudes, coupling_list, coupling_coef))
    return new_amps, energies, dens
```

```python
import functools

import jax
import jax.numpy as jnp
from jax import lax
from jax.experimental import pallas as pl
from jax.experimental.pallas import tpu as pltpu
from jax.sharding import PartitionSpec as P

AXES = ("orb", "pair")
VMEM_BYTES = 48 * 1024 * 1024
NT = (((1,), (1,)), ((), ()))
TN = (((0,), (0,)), ((), ()))


def dot(a, b, dims=(((1,), (0,)), ((), ()))):
    return lax.dot_general(a, b, dims, preferred_element_type=jnp.float32)


def ones_where(equal):
    return jnp.where(equal, 1.0, 0.0).astype(jnp.bfloat16)


def live(rows, cols, shape):
    return (lax.broadcasted_iota(jnp.int32, shape, 0) < rows) & (
        lax.broadcasted_iota(jnp.int32, shape, 1) < cols
    )


def kept(amp, rows, cols):
    return jnp.where(live(rows, cols, amp.shape), amp.astype(jnp.float32), 0.0).astype(amp.dtype)


def projected(amp, left_col, left_row, right_col, right_row):
    rows = dot(ones_where(left_col == left_row), amp).astype(jnp.bfloat16)
    return dot(rows, ones_where(right_col == right_row), NT)


class Sizes:
    def __init__(self, blocks, amplitudes):
        self.occ = blocks.shape[0]
        self.aux = blocks.shape[1]
        self.pao = blocks.shape[2]
        self.pairs = amplitudes.shape[0]

    def first_orbital(self, pair):
        return pair // self.pairs * self.occ + lax.rem(pair, self.occ)


def own_kernel(
    s, ncpl, here, partner, listed, lens, coef, aux_rows, aux_col, pao_rows, left_col, right_col, blocks, amps, aligned, coupling, dens
):
    p = pl.program_id(0)
    me = here[0]
    left = lax.rem(p, s.occ)
    right = partner[me * s.pairs + p]

    @pl.when(p == 0)
    def _():
        dens[...] = jnp.zeros_like(dens)

    selector = ones_where(aux_col[left] == aux_rows[pl.ds(right, 1), :])
    aligned[0] = dot(blocks[left], selector).astype(jnp.bfloat16)

    coupling[...] = jnp.zeros_like(coupling)
    for c in range(ncpl):
        m = listed[p, c]
        spot = m - me * s.pairs

        @pl.when((spot >= 0) & (spot < s.pairs))
        def _():
            picked = projected(
                amps[spot],
                left_col[p],
                pao_rows[pl.ds(s.first_orbital(m), 1), :],
                right_col[p],
                pao_rows[pl.ds(partner[m], 1), :],
            )
            coupling[0] += coef[p, c] * picked

    masked = kept(amps[p], lens[me * s.occ + left], lens[right])
    dens[left] += dot(masked, masked, NT)
    near = right - me * s.occ

    @pl.when((near >= 0) & (near < s.occ))
    def _():
        dens[near] += dot(masked, masked, TN)


def near_kernel(
    s, ncpl, npair, here, partner, listed, lens, coef, pao_rows, left_col, right_col, before, after, part, dens_in, coupling, dens, wide
):
    p = pl.program_id(0)
    me = here[0]

    @pl.when(p == 0)
    def _():
        dens[...] = dens_in[...]
        for side, packed in enumerate((before, after)):
            for k in range(s.pairs):
                unpack(s, packed, k, wide.at[side * s.pairs + k])

    coupling[...] = part[...]
    for c in range(ncpl):
        m = listed[p, c]
        spot = m - me * s.pairs

        @pl.when((spot < 0) | (spot >= s.pairs))
        def _():
            picked = projected(
                wide[jnp.where(spot < 0, spot + s.pairs, spot)],
                left_col[p],
                pao_rows[pl.ds(s.first_orbital(m), 1), :],
                right_col[p],
                pao_rows[pl.ds(partner[m], 1), :],
            )
            coupling[0] += coef[p, c] * picked

    for side in range(2):
        m = (me + 2 * side - 1) * s.pairs + p
        inside = (m >= 0) & (m < npair)
        m = jnp.clip(m, 0, npair - 1)
        near = partner[m] - me * s.occ

        @pl.when(inside & (near >= 0) & (near < s.occ))
        def _():
            masked = kept(wide[side * s.pairs + p], lens[s.first_orbital(m)], lens[partner[m]])
            dens[near] += dot(masked, masked, TN)

    @pl.when(p == s.pairs - 1)
    def _():
        dens[...] = dens[...] / s.pao


def last_kernel(
    s, here, partner, lens, aligned, coupling, amps, gap_left, gap_right, before, own, after, new_amps, energy
):
    p = pl.program_id(0)
    me = here[0]
    right = partner[me * s.pairs + p]
    near = right - me * s.occ
    block = jnp.where(near < 0, before[0], jnp.where(near < s.occ, own[0], after[0]))
    mask = live(lens[me * s.occ + lax.rem(p, s.occ)], lens[right], (s.pao, s.pao))
    exchange = jnp.where(mask, dot(aligned[0], block, NT), 0.0)
    masked = jnp.where(mask, amps[0].astype(jnp.float32), 0.0)
    denom = gap_left[0] + gap_right[0]
    residual = exchange + denom * masked - coupling[0]
    new_amps[0] = (masked - 0.5 * residual / denom).astype(jnp.bfloat16)
    energy[p] = jnp.sum(exchange * masked) / s.pao


def packing(s):
    whole = s.pao // 128 * 128
    tail = s.pao - whole
    share = whole // tail
    return whole, tail, share


def pack(s, amps):
    whole, tail, share = packing(s)
    tails = amps[:, :, whole:]
    groups = s.pairs // share
    slots = [
        jnp.concatenate([tails[g * share + k] for k in range(share)], axis=-1) for g in range(groups)
    ]
    return jnp.concatenate([amps[:, :, :whole], jnp.stack(slots)], axis=0)


def unpack(s, packed, k, out):
    whole, tail, share = packing(s)
    out[:, :whole] = packed[k]
    spot = k % share * tail
    out[:, whole:] = packed[s.pairs + k // share, :, spot : spot + tail]


def along(array, distance):
    count = 1
    for axis in AXES:
        count *= lax.axis_size(axis)
    route = [(i - distance, i) for i in range(count) if 0 <= i - distance < count]
    return lax.ppermute(array, AXES, route)


def local(
    blocks, aux_domain, pao_domain, pao_gap, amplitudes, pair_partner, coupling_list, coupling_coef
):
    s = Sizes(blocks, amplitudes)
    ncpl = coupling_list.shape[1]
    npair = pair_partner.shape[0]
    me = lax.axis_index(AXES)
    here = me.astype(jnp.int32).reshape(1)
    blocks_t = jnp.swapaxes(blocks, 1, 2)
    packed = pack(s, amplitudes)
    amps_before = along(packed, 1)
    amps_after = along(packed, -1)
    blocks_before = along(blocks_t, 1)
    blocks_after = along(blocks_t, -1)

    own_ids = me * s.occ + jnp.arange(s.pairs, dtype=jnp.int32) % s.occ
    right_ids = lax.dynamic_slice_in_dim(pair_partner, me * s.pairs, s.pairs)
    lens = jnp.sum((pao_domain >= 0).astype(jnp.int32), axis=1)
    pao_cols = jnp.where(pao_domain < 0, -2, pao_domain)
    aux_col = lax.dynamic_slice_in_dim(aux_domain, me * s.occ, s.occ)[:, :, None]
    left_col = pao_cols[own_ids][:, :, None]
    right_col = pao_cols[right_ids][:, :, None]
    gap_left = pao_gap[own_ids][:, :, None]
    gap_right = pao_gap[right_ids][:, None, :]

    smem = pl.BlockSpec(memory_space=pltpu.SMEM)
    vmem = pl.BlockSpec(memory_space=pltpu.VMEM)
    params = pltpu.CompilerParams(
        dimension_semantics=("arbitrary",), vmem_limit_bytes=VMEM_BYTES
    )
    square = pl.BlockSpec((1, s.pao, s.pao), lambda p, *_: (p, 0, 0))
    all_dens = pl.BlockSpec((s.occ, s.pao, s.pao), lambda p, *_: (0, 0, 0))
    squares = jax.ShapeDtypeStruct((s.pairs, s.pao, s.pao), jnp.float32)
    dens_shape = jax.ShapeDtypeStruct((s.occ, s.pao, s.pao), jnp.float32)

    aligned, part, dens = pl.pallas_call(
        functools.partial(own_kernel, s, ncpl),
        grid=(s.pairs,),
        in_specs=[smem] * 5 + [vmem] * 7,
        out_specs=[pl.BlockSpec((1, s.pao, s.aux), lambda p: (p, 0, 0)), square, all_dens],
        out_shape=[
            jax.ShapeDtypeStruct((s.pairs, s.pao, s.aux), jnp.bfloat16),
            squares,
            dens_shape,
        ],
        compiler_params=params,
        cost_estimate=pl.CostEstimate(
            flops=2 * s.pairs * s.pao * s.aux * s.aux * 3, bytes_accessed=2 * 10**7, transcendentals=0
        ),
        name="own",
    )(
        here, pair_partner, coupling_list, lens, coupling_coef,
        aux_domain, aux_col, pao_domain, left_col, right_col, blocks_t, amplitudes,
    )

    coupling, densities = pl.pallas_call(
        functools.partial(near_kernel, s, ncpl, npair),
        grid=(s.pairs,),
        in_specs=[smem] * 5 + [vmem] * 5 + [square, all_dens],
        out_specs=[square, all_dens],
        out_shape=[squares, dens_shape],
        scratch_shapes=[pltpu.VMEM((2 * s.pairs, s.pao, s.pao), jnp.bfloat16)],
        compiler_params=params,
        cost_estimate=pl.CostEstimate(
            flops=2 * s.pairs * s.pao * s.aux * s.aux, bytes_accessed=2 * 10**7, transcendentals=0
        ),
        name="near",
    )(
        here, pair_partner, coupling_list, lens, coupling_coef,
        pao_domain, left_col, right_col, amps_before, amps_after, part, dens,
    )

    def block_spec(side):
        def index(p, here, partner, lens):
            near = partner[here[0] * s.pairs + p] - (here[0] + side) * s.occ
            return (jnp.clip(near, 0, s.occ - 1), 0, 0)

        return pl.BlockSpec((1, s.pao, s.aux), index)

    column = pl.BlockSpec((1, s.pao, 1), lambda p, *_: (p, 0, 0))
    row = pl.BlockSpec((1, 1, s.pao), lambda p, *_: (p, 0, 0))
    new_amps, energies = pl.pallas_call(
        functools.partial(last_kernel, s),
        grid_spec=pltpu.PrefetchScalarGridSpec(
            num_scalar_prefetch=3,
            grid=(s.pairs,),
            in_specs=[
                pl.BlockSpec((1, s.pao, s.aux), lambda p, *_: (p, 0, 0)),
                square,
                square,
                column,
                row,
                block_spec(-1),
                block_spec(0),
                block_spec(1),
            ],
            out_specs=[square, smem],
        ),
        out_shape=[
            jax.ShapeDtypeStruct(amplitudes.shape, amplitudes.dtype),
            jax.ShapeDtypeStruct((s.pairs,), jnp.float32),
        ],
        compiler_params=params,
        cost_estimate=pl.CostEstimate(
            flops=2 * s.pairs * s.pao * s.pao * s.aux, bytes_accessed=2 * 10**7, transcendentals=0
        ),
        name="last",
    )(
        here, pair_partner, lens,
        aligned, coupling, amplitudes, gap_left, gap_right, blocks_before, blocks_t, blocks_after,
    )
    return (new_amps, energies, densities)


def solution(mesh):
    return jax.shard_map(
        local,
        mesh=mesh,
        in_specs=(
            P(AXES, None, None),
            P(),
            P(),
            P(),
            P(AXES, None, None),
            P(),
            P(AXES, None),
            P(AXES, None),
        ),
        out_specs=(P(AXES, None, None), P(AXES), P(AXES, None, None)),
        check_vma=False,
    )
```

```python
import functools

import jax
import jax.numpy as jnp
from jax import lax
from jax.experimental import pallas as pl
from jax.experimental.pallas import tpu as pltpu
from jax.sharding import PartitionSpec as P

AXES = ("orb", "pair")
VMEM_BYTES = 48 * 1024 * 1024
AUX_IDS = 2048
LOW = 64
HIGH = AUX_IDS // LOW
BASE = 32
LANES = 128
SHARES = (13, 15, 17, 19, 22, 26, 32)
NN = (((1,), (0,)), ((), ()))
NT = (((1,), (1,)), ((), ()))
TN = (((0,), (0,)), ((), ()))


def dot(a, b, dims=NN):
    return lax.dot_general(a, b, dims, preferred_element_type=jnp.float32)


def one_where(equal, value=1.0):
    return jnp.where(equal, value, 0.0).astype(jnp.bfloat16)


def iota(shape, dim):
    return lax.broadcasted_iota(jnp.int32, shape, dim)


def live(rows, cols, shape):
    return (iota(shape, 0) < rows) & (iota(shape, 1) < cols)


def kept(amp, rows, cols):
    return jnp.where(live(rows, cols, amp.shape), amp.astype(jnp.float32), 0.0).astype(amp.dtype)


def chunks_of(count):
    return (count + LANES - 1) // LANES


def rows_of(length):
    return (length + 15) // 16 * 16


class Sizes:
    def __init__(self, blocks, amplitudes, pair_partner):
        self.occ = blocks.shape[0]
        self.aux = blocks.shape[1]
        self.pao = blocks.shape[2]
        self.pairs = amplitudes.shape[0]
        self.npair = pair_partner.shape[0]
        self.nocc = self.npair // self.pairs * self.occ
        self.rows = self.occ * self.pao * (self.aux // LANES)

    def first_orbital(self, pair):
        return pair // self.pairs * self.occ + lax.rem(pair, self.occ)


def places(high, weight, table):
    found = dot(high, table).astype(jnp.bfloat16) * weight
    return dot(found, jnp.ones((LANES, LANES), jnp.bfloat16))


def picker(place, chunk):
    spot = iota(place.shape, 1).astype(jnp.float32) + (chunk * LANES + 1).astype(jnp.float32)
    return jnp.concatenate([one_where(place == spot), one_where(place == spot + LANES)], axis=1)


def pack_kernel(
    s, here, partner, lens, aux_rows, blocks, to_before, to_after, ids, high, weight, tables, counts, offsets, load, maps
):
    me = here[0]
    group = 3 * s.occ

    for o in range(group):
        orbital = jnp.clip((me - 1) * s.occ + o, 0, s.nocc - 1)
        row = aux_rows[pl.ds(orbital, 1), :]
        by_high = one_where(iota((HIGH, s.aux), 0) == row // LOW)
        by_low = one_where(lax.rem(iota((LANES, s.aux), 0), LOW) == lax.rem(row, LOW))
        maps[o] = dot(by_high, by_low, NT)
        if s.occ <= o < 2 * s.occ:
            own = o - s.occ
            column = jnp.broadcast_to(row, (LANES, s.aux)).T
            lane = iota((s.aux, LANES), 1)
            ids[own] = column
            high[own] = one_where(column // LOW == lane)
            weight[own] = jnp.where(
                lax.rem(column, LOW) == lax.rem(lane, LOW), jnp.where(lane < LOW, 1.0 * BASE, 1.0), 0.0
            ).astype(jnp.bfloat16)

    lane_in, lane_out = iota((LANES, LANES), 0), iota((LANES, LANES), 1)
    ahead = one_where((lane_in < LOW) & (lane_in < lax.rem(lane_out, LOW)))
    first = one_where(lane_in < LOW)
    above = one_where(iota((HIGH, HIGH), 1) < iota((HIGH, HIGH), 0))
    lane = iota((HIGH, LANES), 1)
    lists = 2 * s.occ
    for kind in range(2):
        for l in range(lists):
            side, k = l // s.occ, l % s.occ
            if kind == 0:
                target, user = s.occ + k, 2 * side
            else:
                target, user = 2 * side * s.occ + k, 1
            orbital = (me - 1) * s.occ + target
            device = me - 1 + user
            union = jnp.zeros((HIGH, LANES), jnp.float32)
            for q in range(s.pairs):
                pair = device * s.pairs + q
                inside = (pair >= 0) & (pair < s.npair)
                uses = inside & (partner[jnp.clip(pair, 0, s.npair - 1)] == orbital)
                union += jnp.where(uses, 1.0, 0.0) * maps[user * s.occ + q % s.occ]
            taken = (union > 0.0) & (maps[target] > 0.0)
            flags = one_where(taken)
            total = dot(flags, first)
            place = dot(flags, ahead) + dot(above, total.astype(jnp.bfloat16)) + 1.0
            place = jnp.where(taken, place, 0.0).astype(jnp.int32)
            part = jnp.where(lane < LOW, place // BASE, lax.rem(place, BASE))
            tables[kind * lists + l] = part.astype(jnp.float32).astype(jnp.bfloat16)
            counts[kind * lists + l] = jnp.sum(jnp.where(lane == 0, total, 0.0)).astype(jnp.int32)

    for kind in range(2):
        for side in range(2):
            at = jnp.int32(0)
            for k in range(s.occ):
                l = (kind * 2 + side) * s.occ + k
                offsets[l] = at
                if kind == 0:
                    orbital = me * s.occ + k
                else:
                    orbital = jnp.clip((me - 1 + 2 * side) * s.occ + k, 0, s.nocc - 1)
                at += chunks_of(counts[l]) * rows_of(lens[orbital])
            if kind == 0:
                load[side] = at

    for side, out in enumerate((to_before, to_after)):
        for k in range(s.occ):
            l = side * s.occ + k

            @pl.when(counts[l] > 0)
            def _():
                place = places(high[k, :, :HIGH], weight[k], tables[l])
                step = rows_of(lens[me * s.occ + k])

                def some(c, _):
                    got = dot(blocks[k], picker(place, 2 * c)).astype(jnp.bfloat16)
                    at = pl.multiple_of(offsets[l] + 2 * c * step, 16)
                    out[pl.ds(at, s.pao), :] = got[:, :LANES]

                    @pl.when((2 * c + 1) * LANES < counts[l])
                    def _():
                        out[pl.ds(pl.multiple_of(at + step, 16), s.pao), :] = got[:, LANES:]

                    return 0

                lax.fori_loop(0, (chunks_of(counts[l]) + 1) // 2, some, 0)


def own_kernel(
    s, here, partner, lens, counts, aux_rows, ids, high, weight, tables, blocks, amps, aligned, dens
):
    p = pl.program_id(0)
    me = here[0]
    left = lax.rem(p, s.occ)
    right = partner[me * s.pairs + p]
    near = right - me * s.occ
    is_near = (near >= 0) & (near < s.occ)
    wide = 2 * LANES

    @pl.when(p == 0)
    def _():
        dens[...] = jnp.zeros_like(dens)

    @pl.when(is_near)
    def _():
        def some(c, _):
            at = pl.multiple_of(c * wide, wide)
            row = aux_rows[pl.ds(right, 1), pl.ds(at, wide)]
            same = [one_where(ids[left] == row[:, :LANES]), one_where(ids[left] == row[:, LANES:])]
            aligned[0, :, pl.ds(at, wide)] = dot(
                blocks[left], jnp.concatenate(same, axis=1)
            ).astype(jnp.bfloat16)
            return 0

        lax.fori_loop(0, s.aux // wide, some, 0)

    @pl.when(jnp.logical_not(is_near))
    def _():
        l = jnp.where(near < 0, near + s.occ, near) + 2 * s.occ
        place = places(high[left, :, :HIGH], weight[left], tables[l])

        def some(c, _):
            at = pl.multiple_of(c * wide, wide)
            aligned[0, :, pl.ds(at, wide)] = dot(blocks[left], picker(place, 2 * c)).astype(
                jnp.bfloat16
            )
            return 0

        lax.fori_loop(0, (chunks_of(counts[l]) + 1) // 2, some, 0)

    masked = kept(amps[p], lens[me * s.occ + left], lens[right])
    dens[left] += dot(masked, masked, NT)

    @pl.when(is_near)
    def _():
        dens[near] += dot(masked, masked, TN)


def near_kernel(
    s, ncpl, here, partner, listed, lens, coef, pao_rows, left_col, right_col, before, own, after, dens_in, coupling, dens, wide
):
    p = pl.program_id(0)
    me = here[0]

    @pl.when(p == 0)
    def _():
        dens[...] = dens_in[...]
        wide[s.pairs : 2 * s.pairs] = own[...]
        for side, packed in enumerate((before, after)):
            for k in range(s.pairs):
                unpack(s, packed, k, wide.at[2 * side * s.pairs + k])

    total = jnp.zeros((s.pao, s.pao), jnp.float32)
    for c in range(ncpl):
        m = listed[p, c]
        left_row = pao_rows[pl.ds(s.first_orbital(m), 1), :]
        right_row = pao_rows[pl.ds(partner[m], 1), :]
        amp = wide[m - (me - 1) * s.pairs]
        rows = dot(one_where(left_col[p] == left_row), amp).astype(jnp.bfloat16)
        total += coef[p, c] * dot(rows, one_where(right_col[p] == right_row), NT)
    coupling[0] = total

    for side in range(2):
        m = (me + 2 * side - 1) * s.pairs + p
        inside = (m >= 0) & (m < s.npair)
        m = jnp.clip(m, 0, s.npair - 1)
        near = partner[m] - me * s.occ

        @pl.when(inside & (near >= 0) & (near < s.occ))
        def _():
            amp = wide[2 * side * s.pairs + p]
            masked = kept(amp, lens[s.first_orbital(m)], lens[partner[m]])
            dens[near] += dot(masked, masked, TN)

    @pl.when(p == s.pairs - 1)
    def _():
        dens[...] = dens[...] / s.pao


def last_kernel(
    s, cap, here, partner, lens, counts, offsets, aligned, coupling, amps, gap_left, gap_right, own, before, after, new_amps, energy, halo, sums, sems
):
    p = pl.program_id(0)
    me = here[0]
    right = partner[me * s.pairs + p]
    near = right - me * s.occ
    is_near = (near >= 0) & (near < s.occ)
    wide = 2 * LANES

    @pl.when(p == 0)
    def _():
        copies = [
            pltpu.make_async_copy(side, halo.at[k, pl.ds(0, cap), :], sems.at[k])
            for k, side in enumerate((before, after))
        ]
        for copy in copies:
            copy.start()
        for copy in copies:
            copy.wait()

    @pl.when(is_near)
    def _():
        sums[...] = dot(aligned[0], own[near], NT)

    @pl.when(jnp.logical_not(is_near))
    def _():
        side = jnp.where(near < 0, 0, 1)
        l = jnp.where(near < 0, near + s.occ, near) + 2 * s.occ
        step = rows_of(lens[right])
        sums[...] = jnp.zeros_like(sums)

        def some(c, _):
            at = pl.multiple_of(offsets[l] + 2 * c * step, 16)
            one = halo[side, pl.ds(at, s.pao), :]
            two = halo[side, pl.ds(pl.multiple_of(at + step, 16), s.pao), :]
            two = jnp.where((2 * c + 1) * LANES < counts[l], two, jnp.zeros_like(two))
            both = jnp.concatenate([one, two], axis=1)
            lanes = pl.ds(pl.multiple_of(c * wide, wide), wide)
            sums[...] += dot(aligned[0, :, lanes], both, NT)
            return 0

        lax.fori_loop(0, (chunks_of(counts[l]) + 1) // 2, some, 0)

    mask = live(lens[me * s.occ + lax.rem(p, s.occ)], lens[right], (s.pao, s.pao))
    exchange = jnp.where(mask, sums[...], 0.0)
    masked = jnp.where(mask, amps[0].astype(jnp.float32), 0.0)
    denom = gap_left[0] + gap_right[0]
    residual = exchange + denom * masked - coupling[0]
    new_amps[0] = (masked - 0.5 * residual / denom).astype(jnp.bfloat16)
    energy[p] = jnp.sum(exchange * masked) / s.pao


def packing(s):
    whole = s.pao // LANES * LANES
    tail = s.pao - whole
    share = whole // tail
    return whole, tail, share


def pack(s, amps):
    whole, tail, share = packing(s)
    tails = amps[:, :, whole:]
    groups = s.pairs // share
    slots = [
        jnp.concatenate([tails[g * share + k] for k in range(share)], axis=-1) for g in range(groups)
    ]
    return jnp.concatenate([amps[:, :, :whole], jnp.stack(slots)], axis=0)


def unpack(s, packed, k, out):
    whole, tail, share = packing(s)
    out[:, :whole] = packed[k]
    spot = k % share * tail
    out[:, whole:] = packed[s.pairs + k // share, :, spot : spot + tail]


def along(array, distance):
    count = 1
    for axis in AXES:
        count *= lax.axis_size(axis)
    route = [(i - distance, i) for i in range(count) if 0 <= i - distance < count]
    return lax.ppermute(array, AXES, route)


def local(
    blocks, aux_domain, pao_domain, pao_gap, amplitudes, pair_partner, coupling_list, coupling_coef
):
    s = Sizes(blocks, amplitudes, pair_partner)
    ncpl = coupling_list.shape[1]
    me = lax.axis_index(AXES)
    here = me.astype(jnp.int32).reshape(1)
    blocks_t = jnp.swapaxes(blocks, 1, 2)
    packed = pack(s, amplitudes)
    amps_before = along(packed, 1)
    amps_after = along(packed, -1)

    lens = jnp.sum((pao_domain >= 0).astype(jnp.int32), axis=1)

    smem = pl.BlockSpec(memory_space=pltpu.SMEM)
    vmem = pl.BlockSpec(memory_space=pltpu.VMEM)
    anywhere = pl.BlockSpec(memory_space=pl.ANY)
    params = pltpu.CompilerParams(
        dimension_semantics=("arbitrary",), vmem_limit_bytes=VMEM_BYTES
    )
    square = pl.BlockSpec((1, s.pao, s.pao), lambda p, *_: (p, 0, 0))
    all_dens = pl.BlockSpec((s.occ, s.pao, s.pao), lambda p, *_: (0, 0, 0))
    squares = jax.ShapeDtypeStruct((s.pairs, s.pao, s.pao), jnp.float32)
    dens_shape = jax.ShapeDtypeStruct((s.occ, s.pao, s.pao), jnp.float32)

    def cost(work, data):
        return pl.CostEstimate(flops=work, bytes_accessed=data, transcendentals=0)

    out_rows = s.rows + s.pao
    lists = 4 * s.occ
    to_before, to_after, ids, high, weight, tables, counts, offsets, load = pl.pallas_call(
        functools.partial(pack_kernel, s),
        in_specs=[smem] * 3 + [vmem] * 2,
        out_specs=[vmem] * 6 + [smem] * 3,
        out_shape=[
            jax.ShapeDtypeStruct((out_rows, LANES), jnp.bfloat16),
            jax.ShapeDtypeStruct((out_rows, LANES), jnp.bfloat16),
            jax.ShapeDtypeStruct((s.occ, s.aux, LANES), jnp.int32),
            jax.ShapeDtypeStruct((s.occ, s.aux, LANES), jnp.bfloat16),
            jax.ShapeDtypeStruct((s.occ, s.aux, LANES), jnp.bfloat16),
            jax.ShapeDtypeStruct((lists, HIGH, LANES), jnp.bfloat16),
            jax.ShapeDtypeStruct((lists,), jnp.int32),
            jax.ShapeDtypeStruct((lists,), jnp.int32),
            jax.ShapeDtypeStruct((2,), jnp.int32),
        ],
        scratch_shapes=[pltpu.VMEM((3 * s.occ, HIGH, LANES), jnp.float32)],
        compiler_params=pltpu.CompilerParams(vmem_limit_bytes=VMEM_BYTES),
        cost_estimate=cost(2 * 10**9, 10**7),
        name="pack",
    )(here, pair_partner, lens, aux_domain, blocks_t)

    most = lax.pmax(jnp.max(load), AXES)

    own_ids = me * s.occ + jnp.arange(s.pairs, dtype=jnp.int32) % s.occ
    right_ids = lax.dynamic_slice_in_dim(pair_partner, me * s.pairs, s.pairs)
    pao_cols = jnp.where(pao_domain < 0, -2, pao_domain)
    left_col = pao_cols[own_ids][:, :, None]
    right_col = pao_cols[right_ids][:, :, None]
    gap_left = pao_gap[own_ids][:, :, None]
    gap_right = pao_gap[right_ids][:, None, :]

    aligned, dens = pl.pallas_call(
        functools.partial(own_kernel, s),
        grid=(s.pairs,),
        in_specs=[smem] * 4 + [vmem] * 7,
        out_specs=[pl.BlockSpec((1, s.pao, s.aux), lambda p: (p, 0, 0)), all_dens],
        out_shape=[
            jax.ShapeDtypeStruct((s.pairs, s.pao, s.aux), jnp.bfloat16),
            dens_shape,
        ],
        compiler_params=params,
        cost_estimate=cost(2 * s.pairs * s.pao * s.aux * s.aux * 2, 2 * 10**7),
        name="own",
    )(
        here, pair_partner, lens, counts,
        aux_domain, ids, high, weight, tables, blocks_t, amplitudes,
    )

    column = pl.BlockSpec((1, s.pao, 1), lambda p: (p, 0, 0))
    row = pl.BlockSpec((1, 1, s.pao), lambda p: (p, 0, 0))

    def rest(cap, ops):
        amps_before, amps_after, to_before, to_after, aligned, dens = ops
        from_before = along(to_after[:cap], 1)
        from_after = along(to_before[:cap], -1)
        coupling, densities = pl.pallas_call(
            functools.partial(near_kernel, s, ncpl),
            grid=(s.pairs,),
            in_specs=[smem] * 5 + [vmem] * 6 + [all_dens],
            out_specs=[square, all_dens],
            out_shape=[squares, dens_shape],
            scratch_shapes=[pltpu.VMEM((3 * s.pairs, s.pao, s.pao), jnp.bfloat16)],
            compiler_params=params,
            cost_estimate=cost(2 * s.pairs * s.pao * s.aux * s.aux * 2, 2 * 10**7),
            name="near",
        )(
            here, pair_partner, coupling_list, lens, coupling_coef,
            pao_domain, left_col, right_col, amps_before, amplitudes, amps_after, dens,
        )
        new_amps, energies = pl.pallas_call(
            functools.partial(last_kernel, s, cap),
            grid=(s.pairs,),
            in_specs=[smem] * 5
            + [
                pl.BlockSpec((1, s.pao, s.aux), lambda p: (p, 0, 0)),
                square,
                square,
                column,
                row,
                vmem,
                anywhere,
                anywhere,
            ],
            out_specs=[square, smem],
            out_shape=[
                jax.ShapeDtypeStruct(amplitudes.shape, amplitudes.dtype),
                jax.ShapeDtypeStruct((s.pairs,), jnp.float32),
            ],
            scratch_shapes=[
                pltpu.VMEM((2, cap + s.pao, LANES), jnp.bfloat16),
                pltpu.VMEM((s.pao, s.pao), jnp.float32),
                pltpu.SemaphoreType.DMA((2,)),
            ],
            compiler_params=params,
            cost_estimate=cost(2 * s.pairs * s.pao * s.pao * s.aux, 2 * 10**7),
            name="last",
        )(
            here, pair_partner, lens, counts, offsets,
            aligned, coupling, amplitudes, gap_left, gap_right, blocks_t, from_before, from_after,
        )
        return new_amps, energies, densities

    caps = [-(-s.rows * share // SHARES[-1] // 16) * 16 for share in SHARES]
    which = sum((most > cap).astype(jnp.int32) for cap in caps[:-1])
    return lax.switch(
        which,
        [functools.partial(rest, cap) for cap in caps],
        (amps_before, amps_after, to_before, to_after, aligned, dens),
    )


def solution(mesh):
    return jax.shard_map(
        local,
        mesh=mesh,
        in_specs=(
            P(AXES, None, None),
            P(),
            P(),
            P(),
            P(AXES, None, None),
            P(),
            P(AXES, None),
            P(AXES, None),
        ),
        out_specs=(P(AXES, None, None), P(AXES), P(AXES, None, None)),
        check_vma=False,
    )
```

```python
import functools

import jax
import jax.numpy as jnp
from jax import lax
from jax.experimental import pallas as pl
from jax.experimental.pallas import tpu as pltpu
from jax.sharding import PartitionSpec as P

AXES = ("orb", "pair")
VMEM_BYTES = 48 * 1024 * 1024
AUX_IDS = 2048
LOW = 64
HIGH = AUX_IDS // LOW
BASE = 32
LANES = 128
FIRST, WHOLE = 18, 32
NN = (((1,), (0,)), ((), ()))
NT = (((1,), (1,)), ((), ()))
TN = (((0,), (0,)), ((), ()))


def dot(a, b, dims=NN):
    return lax.dot_general(a, b, dims, preferred_element_type=jnp.float32)


def one_where(equal, value=1.0):
    return jnp.where(equal, value, 0.0).astype(jnp.bfloat16)


def iota(shape, dim):
    return lax.broadcasted_iota(jnp.int32, shape, dim)


def live(rows, cols, shape):
    return (iota(shape, 0) < rows) & (iota(shape, 1) < cols)


def kept(amp, rows, cols):
    return jnp.where(live(rows, cols, amp.shape), amp.astype(jnp.float32), 0.0).astype(amp.dtype)


def column(row):
    return jnp.broadcast_to(row, (LANES, row.shape[1])).T


def same(col, row):
    parts = []
    for at in range(0, row.shape[1], LANES):
        piece = row[:, at : at + LANES]
        parts.append(one_where(col[:, : piece.shape[1]] == piece))
    return jnp.concatenate(parts, axis=1)


def chunks_of(count):
    return (count + LANES - 1) // LANES


def rows_of(length):
    return (length + 15) // 16 * 16


def swapped(me):
    odd = lax.rem(me, 2)
    return me + 1 - 2 * odd, me - 1 + 2 * odd


class Sizes:
    def __init__(self, blocks, amplitudes, pair_partner):
        self.occ = blocks.shape[0]
        self.aux = blocks.shape[1]
        self.pao = blocks.shape[2]
        self.pairs = amplitudes.shape[0]
        self.npair = pair_partner.shape[0]
        self.nocc = self.npair // self.pairs * self.occ
        self.rows = self.occ * self.pao * (self.aux // LANES)
        self.first = self.rows * FIRST // WHOLE // 16 * 16

    def first_orbital(self, pair):
        return pair // self.pairs * self.occ + lax.rem(pair, self.occ)

    def where_partner(self, me, right):
        device = right // self.occ
        sibling, _ = swapped(me)
        kind = jnp.where(device == me, 2, jnp.where(device == sibling, 0, 1))
        return kind * self.occ + lax.rem(right, self.occ), kind


def packing(s):
    whole = s.pao // LANES * LANES
    tail = s.pao - whole
    share = whole // tail
    return whole, tail, share


def slim_kernel(s, amps, out):
    whole, tail, share = packing(s)
    for k in range(s.pairs):
        out[k] = amps[k, :, :whole]
    for g in range(s.pairs // share):
        tails = [amps[g * share + t, :, whole:] for t in range(share)]
        out[s.pairs + g] = jnp.concatenate(tails, axis=1)


def unpack(s, packed, k, out):
    whole, tail, share = packing(s)
    out[:, :whole] = packed[k]
    spot = k % share * tail
    out[:, whole:] = packed[s.pairs + k // share, :, spot : spot + tail]


def places(high, weight, table):
    found = dot(high[:, :HIGH], table).astype(jnp.bfloat16) * weight
    return dot(found, jnp.ones((LANES, LANES), jnp.bfloat16))


def picker(place, chunk):
    spot = iota(place.shape, 1).astype(jnp.float32) + (chunk * LANES + 1).astype(jnp.float32)
    return jnp.concatenate([one_where(place == spot), one_where(place == spot + LANES)], axis=1)


def split_place(place, lane):
    part = jnp.where(lane < LOW, place // BASE, lax.rem(place, BASE))
    return part.astype(jnp.float32)


def pack_kernel(
    s, here, partner, lens, aux_rows, blocks, to_sibling, to_other, to_other_more, high, weight, tables, counts, offsets, load, maps, sends, bufs, sems
):
    me = here[0]
    peers = swapped(me)

    for g, device in enumerate((me,) + peers):
        for k in range(s.occ):
            orbital = jnp.clip(device * s.occ + k, 0, s.nocc - 1)
            row = aux_rows[pl.ds(orbital, 1), :]
            lane = iota((LANES, s.aux), 0)
            matches = lax.rem(lane, LOW) == lax.rem(row, LOW)
            by_high = one_where(iota((HIGH, s.aux), 0) == row // LOW)
            maps[g * s.occ + k] = dot(by_high, one_where(matches), NT)
            if g == 0:
                spot = split_place(iota((LANES, s.aux), 1) + 1, lane)
                table = dot(by_high, one_where(matches, spot), NT)
                tables[2 * s.occ + k] = table.astype(jnp.bfloat16)
                col = column(row)
                lane = iota((s.aux, LANES), 1)
                high[k] = one_where(col // LOW == lane)
                weight[k] = one_where(
                    lax.rem(col, LOW) == lax.rem(lane, LOW), jnp.where(lane < LOW, 1.0 * BASE, 1.0)
                )

    lane_in, lane_out = iota((LANES, LANES), 0), iota((LANES, LANES), 1)
    ahead = one_where((lane_in < LOW) & (lane_in < lax.rem(lane_out, LOW)))
    first = one_where(lane_in < LOW)
    above = one_where(iota((HIGH, HIGH), 1) < iota((HIGH, HIGH), 0))
    lane = iota((HIGH, LANES), 1)

    def listing(target, users, device, orbital):
        union = jnp.zeros((HIGH, LANES), jnp.float32)
        for q in range(s.pairs):
            pair = device * s.pairs + q
            inside = (pair >= 0) & (pair < s.npair)
            uses = inside & (partner[jnp.clip(pair, 0, s.npair - 1)] == orbital)
            union += jnp.where(uses, 1.0, 0.0) * maps[users + q % s.occ]
        taken = (union > 0.0) & (maps[target] > 0.0)
        flags = one_where(taken)
        total = dot(flags, first)
        place = dot(flags, ahead) + dot(above, total.astype(jnp.bfloat16)) + 1.0
        place = jnp.where(taken, place, 0.0).astype(jnp.int32)
        count = jnp.sum(jnp.where(lane == 0, total, 0.0)).astype(jnp.int32)
        return split_place(place, lane).astype(jnp.bfloat16), count

    for r in range(2):
        at, load[r] = jnp.int32(0), jnp.int32(0)
        for k in range(s.occ):
            l = r * s.occ + k
            orbital = jnp.clip(peers[r] * s.occ + k, 0, s.nocc - 1)
            tables[l], counts[l] = listing((1 + r) * s.occ + k, 0, me, peers[r] * s.occ + k)
            offsets[l] = at
            at += chunks_of(counts[l]) * rows_of(lens[orbital])
    for k in range(s.occ):
        counts[2 * s.occ + k] = jnp.int32(s.aux)
        offsets[2 * s.occ + k] = jnp.int32(0)

    copies = []
    for r in (1, 0):
        at = jnp.int32(0)
        for k in range(s.occ):
            table, count = listing(k, (1 + r) * s.occ, peers[r], me * s.occ + k)
            sends[k] = table
            step = rows_of(lens[me * s.occ + k])

            @pl.when(count > 0)
            def _(k=k, at=at, step=step, count=count):
                place = places(high[k], weight[k], sends[k])

                def some(c, _):
                    got = dot(blocks[k], picker(place, 2 * c)).astype(jnp.bfloat16)
                    spot = pl.multiple_of(at + 2 * c * step, 16)
                    bufs[r, pl.ds(spot, s.pao), :] = got[:, :LANES]

                    @pl.when((2 * c + 1) * LANES < count)
                    def _():
                        bufs[r, pl.ds(pl.multiple_of(spot + step, 16), s.pao), :] = got[:, LANES:]

                    return 0

                lax.fori_loop(0, (chunks_of(count) + 1) // 2, some, 0)

            at += chunks_of(count) * step
        load[r] = at
        if r == 1:
            copies = [
                pltpu.make_async_copy(bufs.at[1, pl.ds(0, s.first)], to_other, sems.at[0]),
                pltpu.make_async_copy(
                    bufs.at[1, pl.ds(s.first, s.rows - s.first)], to_other_more, sems.at[1]
                ),
            ]
        else:
            copies = [pltpu.make_async_copy(bufs.at[0, pl.ds(0, s.rows)], to_sibling, sems.at[2])]
        for copy in copies:
            copy.start()
        if r == 1:
            pending = copies
    for copy in pending + copies:
        copy.wait()


def own_kernel(s, here, partner, lens, counts, tables, blocks, high, weight, amps, aligned, dens):
    g = pl.program_id(0)
    me = here[0]
    left, p = paired(s, g)
    right = partner[me * s.pairs + p]
    wide = 2 * LANES
    l, _ = s.where_partner(me, right)
    place = places(high[0], weight[0], tables[l])

    def some(c, _):
        at = pl.multiple_of(c * wide, wide)
        aligned[0, :, pl.ds(at, wide)] = dot(blocks[0], picker(place, 2 * c)).astype(jnp.bfloat16)
        return 0

    lax.fori_loop(0, (chunks_of(counts[l]) + 1) // 2, some, 0)

    masked = kept(amps[0], lens[me * s.occ + left], lens[right])
    term = dot(masked, masked, NT)

    @pl.when(lax.rem(g, s.pairs // s.occ) == 0)
    def _():
        dens[0] = term

    @pl.when(lax.rem(g, s.pairs // s.occ) != 0)
    def _():
        dens[0] += term


def paired(s, g):
    repeats = s.pairs // s.occ
    left = g // repeats
    return left, lax.rem(g, repeats) * s.occ + left


def near_kernel(
    s, ncpl, here, partner, listed, lens, coef, pao_rows, sibling, own, other, dens_in, coupling, dens, wide, tall, dens_own, sem
):
    p = pl.program_id(0)
    me = here[0]
    peers = swapped(me)
    fetch = pltpu.make_async_copy(dens_in, dens_own, sem)

    @pl.when(p == 0)
    def _():
        fetch.start()
        dens[...] = jnp.zeros_like(dens)
        wide[s.pairs : 2 * s.pairs] = own[...]
        for device, packed in zip(peers, (sibling, other)):
            for k in range(s.pairs):
                unpack(s, packed, k, wide.at[(device - me + 1) * s.pairs + k])

    def row_of(orbital):
        return pao_rows[pl.ds(orbital, 1), :]

    def column_of(orbital):
        row = row_of(orbital)
        return column(jnp.where(row < 0, -2, row))

    right_col = column_of(partner[me * s.pairs + p])
    left_col = column_of(me * s.occ + lax.rem(p, s.occ))
    left_rows = []
    for c in range(ncpl):
        m = listed[p, c]
        left_rows.append(row_of(s.first_orbital(m)))
        amp = wide[m - (me - 1) * s.pairs]
        moved = dot(amp, same(right_col, row_of(partner[m])), NT)
        tall[c * s.pao : (c + 1) * s.pao] = (coef[p, c] * moved).astype(jnp.bfloat16)
    coupling[0] = dot(same(left_col, jnp.concatenate(left_rows, axis=1)), tall[...])

    for side in range(3):
        m = (me + side - 1) * s.pairs + p
        inside = (m >= 0) & (m < s.npair)
        m = jnp.clip(m, 0, s.npair - 1)
        near = partner[m] - me * s.occ

        @pl.when(inside & (near >= 0) & (near < s.occ))
        def _():
            amp = wide[side * s.pairs + p]
            masked = kept(amp, lens[s.first_orbital(m)], lens[partner[m]])
            dens[near] += dot(masked, masked, TN)

    @pl.when(p == s.pairs - 1)
    def _():
        fetch.wait()
        dens[...] = (dens[...] + dens_own[...]) / s.pao


def update(s, lens_left, lens_right, exchange, amp, coupling, gap_left, gap_right):
    mask = live(lens_left, lens_right, (s.pao, s.pao))
    exchange = jnp.where(mask, exchange, 0.0)
    masked = jnp.where(mask, amp.astype(jnp.float32), 0.0)
    left = column(gap_left)
    parts = []
    for at in range(0, s.pao, LANES):
        lanes = slice(at, min(at + LANES, s.pao))
        part = masked[:, lanes]
        denom = left[:, : part.shape[1]] + gap_right[:, lanes]
        residual = exchange[:, lanes] + denom * part - coupling[:, lanes]
        parts.append((part - 0.5 * residual / denom).astype(jnp.bfloat16))
    return jnp.concatenate(parts, axis=1), jnp.sum(exchange * masked) / s.pao


def compacted(s, count, at, step, aligned, halo, sums):
    sums[...] = jnp.zeros_like(sums)
    wide = 2 * LANES

    def some(c, _):
        spot = pl.multiple_of(at + 2 * c * step, 16)
        one = halo[pl.ds(spot, s.pao), :]
        two = halo[pl.ds(pl.multiple_of(spot + step, 16), s.pao), :]
        two = jnp.where((2 * c + 1) * LANES < count, two, jnp.zeros_like(two))
        lanes = pl.ds(pl.multiple_of(c * wide, wide), wide)
        sums[...] += dot(aligned[:, lanes], jnp.concatenate([one, two], axis=1), NT)
        return 0

    lax.fori_loop(0, (chunks_of(count) + 1) // 2, some, 0)


def mid_kernel(
    s, here, partner, lens, counts, offsets, gaps, aligned, coupling, amps, own, sibling, new_amps, energy, halo, sums, sem
):
    p = pl.program_id(0)
    me = here[0]
    left, right = me * s.occ + lax.rem(p, s.occ), partner[me * s.pairs + p]
    l, kind = s.where_partner(me, right)

    @pl.when(p == 0)
    def _():
        copy = pltpu.make_async_copy(sibling, halo.at[pl.ds(0, s.rows), :], sem)
        copy.start()
        copy.wait()

    @pl.when(kind == 2)
    def _():
        sums[...] = dot(aligned[0], own[lax.rem(right, s.occ)], NT)

    @pl.when(kind == 0)
    def _():
        compacted(s, counts[l], offsets[l], rows_of(lens[right]), aligned.at[0], halo, sums)

    @pl.when(kind != 1)
    def _():
        new_amps[0], energy[p] = update(
            s, lens[left], lens[right], sums[...], amps[0], coupling[0], gaps[pl.ds(left, 1), :], gaps[pl.ds(right, 1), :]
        )

    @pl.when(kind == 1)
    def _():
        new_amps[0] = jnp.zeros_like(amps[0])
        energy[p] = 0.0


def last_kernel(
    s, here, partner, lens, counts, offsets, over, energy_in, gaps, aligned, coupling, amps, other, more, _, new_amps, energy, halo, held, terms, olds, news, sums, sems
):
    me = here[0]

    def copies(p):
        return [
            pltpu.make_async_copy(aligned.at[p], held.at[p], sems.at[0, p]),
            pltpu.make_async_copy(coupling.at[p], terms.at[p], sems.at[1, p]),
            pltpu.make_async_copy(amps.at[p], olds.at[p], sems.at[2, p]),
        ]

    def result(p):
        return pltpu.make_async_copy(news.at[p], new_amps.at[p], sems.at[3, p])

    def each(act):
        def one(p, _):
            right = partner[me * s.pairs + p]
            l, kind = s.where_partner(me, right)

            @pl.when(kind == 1)
            def _():
                act(p, right, l)

            return 0

        lax.fori_loop(0, s.pairs, one, 0)

    first = pltpu.make_async_copy(other, halo.at[pl.ds(0, s.first)], sems.at[4, 0])
    rest = pltpu.make_async_copy(more, halo.at[pl.ds(s.first, s.rows - s.first)], sems.at[4, 1])
    first.start()

    @pl.when(over[0] > 0)
    def _():
        rest.start()
        rest.wait()

    def begin(p, right, l):
        for copy in copies(p):
            copy.start()

    def finish(p, right, l):
        left = me * s.occ + lax.rem(p, s.occ)
        for copy in copies(p):
            copy.wait()
        compacted(s, counts[l], offsets[l], rows_of(lens[right]), held.at[p], halo, sums)
        news[p], energy[p] = update(
            s, lens[left], lens[right], sums[...], olds[p], terms[p], gaps[pl.ds(left, 1), :], gaps[pl.ds(right, 1), :]
        )
        result(p).start()

    for p in range(s.pairs):
        energy[p] = energy_in[p]
    each(begin)
    first.wait()
    each(finish)
    each(lambda p, right, l: result(p).wait())


def swap(array, role):
    count = 1
    for axis in AXES:
        count *= lax.axis_size(axis)
    route = []
    for low in range(role, count - 1, 2):
        route += [(low, low + 1), (low + 1, low)]
    return lax.ppermute(array, AXES, route)


def local(
    blocks, aux_domain, pao_domain, pao_gap, amplitudes, pair_partner, coupling_list, coupling_coef
):
    s = Sizes(blocks, amplitudes, pair_partner)
    ncpl = coupling_list.shape[1]
    me = lax.axis_index(AXES)
    here = me.astype(jnp.int32).reshape(1)
    blocks_t = jnp.swapaxes(blocks, 1, 2)

    smem = pl.BlockSpec(memory_space=pltpu.SMEM)
    vmem = pl.BlockSpec(memory_space=pltpu.VMEM)
    anywhere = pl.BlockSpec(memory_space=pl.ANY)
    plain = pltpu.CompilerParams(vmem_limit_bytes=VMEM_BYTES)
    stepped = pltpu.CompilerParams(
        dimension_semantics=("arbitrary",), vmem_limit_bytes=VMEM_BYTES
    )
    square = pl.BlockSpec((1, s.pao, s.pao), lambda p, *_: (p, 0, 0))
    all_dens = pl.BlockSpec((s.occ, s.pao, s.pao), lambda p, *_: (0, 0, 0))
    squares = jax.ShapeDtypeStruct((s.pairs, s.pao, s.pao), jnp.float32)
    dens_shape = jax.ShapeDtypeStruct((s.occ, s.pao, s.pao), jnp.float32)

    def cost(work, data):
        return pl.CostEstimate(flops=work, bytes_accessed=data, transcendentals=0)

    whole, tail, share = packing(s)
    slim = pl.pallas_call(
        functools.partial(slim_kernel, s),
        in_specs=[vmem],
        out_specs=vmem,
        out_shape=jax.ShapeDtypeStruct((s.pairs + s.pairs // share, s.pao, whole), jnp.bfloat16),
        compiler_params=plain,
        cost_estimate=cost(10**6, 4 * 10**6),
        name="slim",
    )(amplitudes)
    amps_other = swap(slim, 1)
    amps_sibling = swap(slim, 0)

    lens = jnp.sum((pao_domain >= 0).astype(jnp.int32), axis=1)

    tables_number = 3 * s.occ
    to_sibling, to_other, to_other_more, high, weight, tables, counts, offsets, load = pl.pallas_call(
        functools.partial(pack_kernel, s),
        in_specs=[smem] * 3 + [vmem] * 2,
        out_specs=[anywhere] * 3 + [vmem] * 3 + [smem] * 3,
        out_shape=[
            jax.ShapeDtypeStruct((s.rows, LANES), jnp.bfloat16),
            jax.ShapeDtypeStruct((s.first, LANES), jnp.bfloat16),
            jax.ShapeDtypeStruct((s.rows - s.first, LANES), jnp.bfloat16),
            jax.ShapeDtypeStruct((s.occ, s.aux, LANES), jnp.bfloat16),
            jax.ShapeDtypeStruct((s.occ, s.aux, LANES), jnp.bfloat16),
            jax.ShapeDtypeStruct((tables_number, HIGH, LANES), jnp.bfloat16),
            jax.ShapeDtypeStruct((tables_number,), jnp.int32),
            jax.ShapeDtypeStruct((tables_number,), jnp.int32),
            jax.ShapeDtypeStruct((2,), jnp.int32),
        ],
        scratch_shapes=[
            pltpu.VMEM((3 * s.occ, HIGH, LANES), jnp.float32),
            pltpu.VMEM((s.occ, HIGH, LANES), jnp.bfloat16),
            pltpu.VMEM((2, s.rows + s.pao, LANES), jnp.bfloat16),
            pltpu.SemaphoreType.DMA((3,)),
        ],
        compiler_params=plain,
        cost_estimate=cost(2 * 10**9, 10**7),
        name="pack",
    )(here, pair_partner, lens, aux_domain, blocks_t)

    from_other = swap(to_other, 1)
    from_sibling = swap(to_sibling, 0)
    loads = lax.all_gather(load[1:], AXES, tiled=True)
    over = jnp.max(loads) > s.first

    def by_left(block, *rest):
        return pl.BlockSpec((1,) + block, lambda g: (paired(s, g)[0], 0, 0))

    aligned, dens = pl.pallas_call(
        functools.partial(own_kernel, s),
        grid=(s.pairs,),
        in_specs=[smem] * 4
        + [
            vmem,
            by_left((s.pao, s.aux)),
            by_left((s.aux, LANES)),
            by_left((s.aux, LANES)),
            pl.BlockSpec((1, s.pao, s.pao), lambda g: (paired(s, g)[1], 0, 0)),
        ],
        out_specs=[
            pl.BlockSpec((1, s.pao, s.aux), lambda g: (paired(s, g)[1], 0, 0)),
            by_left((s.pao, s.pao)),
        ],
        out_shape=[
            jax.ShapeDtypeStruct((s.pairs, s.pao, s.aux), jnp.bfloat16),
            dens_shape,
        ],
        compiler_params=stepped,
        cost_estimate=cost(2 * s.pairs * s.pao * s.aux * s.aux * 2, 2 * 10**7),
        name="own",
    )(here, pair_partner, lens, counts, tables, blocks_t, high, weight, amplitudes)

    coupling, densities = pl.pallas_call(
        functools.partial(near_kernel, s, ncpl),
        grid=(s.pairs,),
        in_specs=[smem] * 5 + [vmem] * 4 + [anywhere],
        out_specs=[square, all_dens],
        out_shape=[squares, dens_shape],
        scratch_shapes=[
            pltpu.VMEM((3 * s.pairs, s.pao, s.pao), jnp.bfloat16),
            pltpu.VMEM((ncpl * s.pao, s.pao), jnp.bfloat16),
            pltpu.VMEM((s.occ, s.pao, s.pao), jnp.float32),
            pltpu.SemaphoreType.DMA,
        ],
        compiler_params=stepped,
        cost_estimate=cost(2 * s.pairs * s.pao * s.aux * s.aux * 2, 2 * 10**7),
        name="near",
    )(
        here, pair_partner, coupling_list, lens, coupling_coef,
        pao_domain, amps_sibling, amplitudes, amps_other, dens,
    )

    some_amps, some_energies = pl.pallas_call(
        functools.partial(mid_kernel, s),
        grid=(s.pairs,),
        in_specs=[smem] * 5
        + [
            vmem,
            pl.BlockSpec((1, s.pao, s.aux), lambda p: (p, 0, 0)),
            square,
            square,
            vmem,
            anywhere,
        ],
        out_specs=[square, smem],
        out_shape=[
            jax.ShapeDtypeStruct(amplitudes.shape, amplitudes.dtype),
            jax.ShapeDtypeStruct((s.pairs,), jnp.float32),
        ],
        scratch_shapes=[
            pltpu.VMEM((s.rows + s.pao, LANES), jnp.bfloat16),
            pltpu.VMEM((s.pao, s.pao), jnp.float32),
            pltpu.SemaphoreType.DMA,
        ],
        compiler_params=stepped,
        cost_estimate=cost(2 * s.pairs * s.pao * s.pao * s.aux, 2 * 10**7),
        name="mid",
    )(
        here, pair_partner, lens, counts, offsets,
        pao_gap, aligned, coupling, amplitudes, blocks_t, from_sibling,
    )

    from_other_more = lax.cond(over, lambda a: swap(a, 1), lambda a: a, to_other_more)
    new_amps, energies = pl.pallas_call(
        functools.partial(last_kernel, s),
        in_specs=[smem] * 7 + [vmem] + [anywhere] * 6,
        out_specs=[anywhere, smem],
        out_shape=[
            jax.ShapeDtypeStruct(amplitudes.shape, amplitudes.dtype),
            jax.ShapeDtypeStruct((s.pairs,), jnp.float32),
        ],
        scratch_shapes=[
            pltpu.VMEM((s.rows + s.pao, LANES), jnp.bfloat16),
            pltpu.VMEM((s.pairs, s.pao, s.aux), jnp.bfloat16),
            pltpu.VMEM((s.pairs, s.pao, s.pao), jnp.float32),
            pltpu.VMEM((s.pairs, s.pao, s.pao), jnp.bfloat16),
            pltpu.VMEM((s.pairs, s.pao, s.pao), jnp.bfloat16),
            pltpu.VMEM((s.pao, s.pao), jnp.float32),
            pltpu.SemaphoreType.DMA((5, s.pairs)),
        ],
        input_output_aliases={13: 0},
        compiler_params=plain,
        cost_estimate=cost(2 * s.pairs * s.pao * s.pao * s.aux, 2 * 10**7),
        name="last",
    )(
        here, pair_partner, lens, counts, offsets, over.astype(jnp.int32).reshape(1), some_energies,
        pao_gap, aligned, coupling, amplitudes, from_other, from_other_more, some_amps,
    )
    return (new_amps, energies, densities)


def solution(mesh):
    return jax.shard_map(
        local,
        mesh=mesh,
        in_specs=(
            P(AXES, None, None),
            P(),
            P(),
            P(),
            P(AXES, None, None),
            P(),
            P(AXES, None),
            P(AXES, None),
        ),
        out_specs=(P(AXES, None, None), P(AXES), P(AXES, None, None)),
        check_vma=False,
    )
```

```python
import functools

import jax
import jax.numpy as jnp
from jax import lax
from jax.experimental import pallas as pl
from jax.experimental.pallas import tpu as pltpu
from jax.sharding import PartitionSpec as P

AXES = ("orb", "pair")
VMEM_BYTES = 60 * 1024 * 1024
AUX_IDS = 2048
LOW = 64
HIGH = AUX_IDS // LOW
BASE = 32
LANES = 128
FIRST, WHOLE = 18, 32
NN = (((1,), (0,)), ((), ()))
NT = (((1,), (1,)), ((), ()))
TN = (((0,), (0,)), ((), ()))


def dot(a, b, dims=NN):
    return lax.dot_general(a, b, dims, preferred_element_type=jnp.float32)


def one_where(equal, value=1.0):
    return jnp.where(equal, value, 0.0).astype(jnp.bfloat16)


def iota(shape, dim):
    return lax.broadcasted_iota(jnp.int32, shape, dim)


def live(rows, cols, shape):
    return (iota(shape, 0) < rows) & (iota(shape, 1) < cols)


def kept(amp, rows, cols):
    return jnp.where(live(rows, cols, amp.shape), amp.astype(jnp.float32), 0.0).astype(amp.dtype)


def short_where(equal):
    one = jnp.ones(equal.shape, jnp.bfloat16)
    return jnp.where(equal, one, jnp.zeros_like(one))


def column(row):
    return jnp.broadcast_to(row, (LANES, row.shape[1])).T


def same(col, row):
    parts = []
    for at in range(0, row.shape[1], LANES):
        piece = row[:, at : at + LANES]
        wide = jnp.broadcast_to(piece, (col.shape[0], piece.shape[1]))
        parts.append(short_where(col[:, : piece.shape[1]] == wide))
    return jnp.concatenate(parts, axis=1)


def chunks_of(count):
    return (count + LANES - 1) // LANES


def rows_of(length):
    return (length + 15) // 16 * 16


def swapped(me):
    odd = lax.rem(me, 2)
    return me + 1 - 2 * odd, me - 1 + 2 * odd


class Sizes:
    def __init__(self, blocks, amplitudes, pair_partner):
        self.occ = blocks.shape[0]
        self.aux = blocks.shape[1]
        self.pao = blocks.shape[2]
        self.pairs = amplitudes.shape[0]
        self.npair = pair_partner.shape[0]
        self.nocc = self.npair // self.pairs * self.occ
        self.rows = self.occ * self.pao * (self.aux // LANES)
        self.first = self.rows * FIRST // WHOLE // 16 * 16

    def first_orbital(self, pair):
        return pair // self.pairs * self.occ + lax.rem(pair, self.occ)

    def where_partner(self, me, right):
        device = right // self.occ
        sibling, _ = swapped(me)
        kind = jnp.where(device == me, 2, jnp.where(device == sibling, 0, 1))
        return kind * self.occ + lax.rem(right, self.occ), kind


def packing(s):
    whole = s.pao // LANES * LANES
    tail = s.pao - whole
    share = whole // tail
    return whole, tail, share


def slim_kernel(s, amps, out):
    whole, tail, share = packing(s)
    for k in range(s.pairs):
        out[k] = amps[k, :, :whole]
    for g in range(s.pairs // share):
        tails = [amps[g * share + t, :, whole:] for t in range(share)]
        out[s.pairs + g] = jnp.concatenate(tails, axis=1)


def unpack(s, packed, k, out):
    whole, tail, share = packing(s)
    out[:, :whole] = packed[k]
    spot = k % share * tail
    out[:, whole:] = packed[s.pairs + k // share, :, spot : spot + tail]


def bits(values, count, lanes):
    levels = iota((count, lanes), 0).astype(jnp.bfloat16)
    return short_where(levels == jnp.broadcast_to(values.astype(jnp.bfloat16), (count, lanes)))


def places(row, table):
    found = dot(table, bits(row // LOW, HIGH, row.shape[1]))
    low = bits(lax.rem(row, LOW), LOW, row.shape[1]).astype(jnp.float32)
    return jnp.sum((found[:LOW] * BASE + found[LOW:]) * low, axis=0, keepdims=True)


def picker(place, chunk):
    wide = 2 * LANES
    middle = chunk * wide + LANES + 1
    spot = (place - jnp.asarray(middle).astype(jnp.float32)).astype(jnp.bfloat16)
    levels = (iota((wide, place.shape[1]), 0) - LANES).astype(jnp.bfloat16)
    return short_where(levels == jnp.broadcast_to(spot, levels.shape))


def chunkwise(s, count, act):
    for c in range(s.aux // (2 * LANES)):
        pl.when(count > c * 2 * LANES)(functools.partial(act, c))


def split_place(place, row):
    part = jnp.where(row < LOW, place // BASE, lax.rem(place, BASE))
    return part.astype(jnp.float32).astype(jnp.bfloat16)


def pack_kernel(
    s, here, partner, lens, aux_rows, blocks, pao_cols, gap_cols, to_sibling, to_other, to_other_more, tables, pao_rows, gap_rows, counts, offsets, maps, sends, bufs, sems
):
    me = here[0]
    peers = swapped(me)
    pao_rows[...] = pao_cols[...].T
    gap_rows[...] = gap_cols[...].T

    for g, device in enumerate((me,) + peers):
        for k in range(s.occ):
            orbital = jnp.clip(device * s.occ + k, 0, s.nocc - 1)
            row = aux_rows[pl.ds(orbital, 1), :]
            by_high = bits(row // LOW, HIGH, s.aux)
            by_low = bits(lax.rem(row, LOW), LOW, s.aux)
            maps[g * s.occ + k] = dot(jnp.concatenate([by_low, by_low], axis=0), by_high, NT)
            if g == 0:
                spot = iota((LOW, s.aux), 1) + 1
                parts = jnp.concatenate(
                    [
                        (spot // BASE).astype(jnp.float32).astype(jnp.bfloat16) * by_low,
                        lax.rem(spot, BASE).astype(jnp.float32).astype(jnp.bfloat16) * by_low,
                    ],
                    axis=0,
                )
                tables[2 * s.occ + k] = dot(parts, by_high, NT).astype(jnp.bfloat16)

    sub, lane = iota((2 * LOW, 2 * LOW), 0), iota((2 * LOW, 2 * LOW), 1)
    ahead = one_where((lane < LOW) & (lane < lax.rem(sub, LOW)))
    first = one_where(lane < LOW)
    above = one_where(iota((HIGH, HIGH), 0) < iota((HIGH, HIGH), 1))
    level = iota((2 * LOW, HIGH), 0)

    def listing(target, users, device, orbital):
        union = jnp.zeros((2 * LOW, HIGH), jnp.float32)
        for q in range(s.occ):
            uses = jnp.bool_(False)
            for pair in range(q, s.pairs, s.occ):
                pair += device * s.pairs
                inside = (pair >= 0) & (pair < s.npair)
                uses |= inside & (partner[jnp.clip(pair, 0, s.npair - 1)] == orbital)
            union += jnp.where(uses, 1.0, 0.0) * maps[users + q]
        taken = (union > 0.0) & (maps[target] > 0.0)
        flags = one_where(taken)
        total = dot(first, flags)
        place = dot(ahead, flags) + dot(total.astype(jnp.bfloat16), above) + 1.0
        place = jnp.where(taken, place, 0.0).astype(jnp.int32)
        count = jnp.sum(total[:1]).astype(jnp.int32)
        return split_place(place, level), count

    copies = {
        0: [pltpu.make_async_copy(bufs.at[0, pl.ds(0, s.rows)], to_sibling, sems.at[0])],
        1: [
            pltpu.make_async_copy(bufs.at[1, pl.ds(0, s.first)], to_other, sems.at[1]),
            pltpu.make_async_copy(
                bufs.at[1, pl.ds(s.first, s.rows - s.first)], to_other_more, sems.at[2]
            ),
        ],
    }
    for r in (1, 0):
        listed = []
        at = jnp.int32(0)
        for k in range(s.occ):
            sends[k], count = listing(k, (1 + r) * s.occ, peers[r], me * s.occ + k)
            step = rows_of(lens[me * s.occ + k])
            listed.append((at, step, count))
            at += chunks_of(count) * step
        for k, (at, step, count) in enumerate(listed):

            @pl.when(count > 0)
            def _(k=k, at=at, step=step, count=count):
                place = places(aux_rows[pl.ds(me * s.occ + k, 1), :], sends[k])

                def some(c):
                    got = dot(blocks[k], picker(place, c), NT).astype(jnp.bfloat16)
                    spot = pl.multiple_of(at + 2 * c * step, 16)
                    bufs[r, pl.ds(spot, s.pao), :] = got[:, :LANES]

                    @pl.when((2 * c + 1) * LANES < count)
                    def _():
                        bufs[r, pl.ds(pl.multiple_of(spot + step, 16), s.pao), :] = got[:, LANES:]

                chunkwise(s, count, some)

        for copy in copies[r]:
            copy.start()

    for r in range(2):
        at = jnp.int32(0)
        for k in range(s.occ):
            l = r * s.occ + k
            orbital = jnp.clip(peers[r] * s.occ + k, 0, s.nocc - 1)
            tables[l], counts[l] = listing((1 + r) * s.occ + k, 0, me, peers[r] * s.occ + k)
            offsets[l] = at
            at += chunks_of(counts[l]) * rows_of(lens[orbital])
    for k in range(s.occ):
        counts[2 * s.occ + k] = jnp.int32(s.aux)
        offsets[2 * s.occ + k] = jnp.int32(0)

    for copy in copies[1] + copies[0]:
        copy.wait()


def count_kernel(s, partner, lens, aux_rows, over, maps, sums, steps):
    high = AUX_IDS // LANES
    group = 8

    def some(g, _):
        rows = aux_rows[pl.ds(pl.multiple_of(g * group, group), group), :]
        for t in range(group):
            row = rows[t : t + 1]
            by_low = bits(lax.rem(row, LANES), LANES, s.aux)
            maps[g * group + t] = dot(bits(row // LANES, high, s.aux), by_low, NT)
        return 0

    lax.fori_loop(0, s.nocc // group, some, 0)

    sums[...] = jnp.zeros_like(sums)
    steps[...] = jnp.zeros_like(steps)
    devices = s.nocc // s.occ

    def edge(e, _):
        source = e + 1
        user = source + 1 - 2 * lax.rem(e, 2)
        for k in range(s.occ):
            orbital = source * s.occ + k
            union = jnp.zeros((high, LANES), jnp.float32)
            for q in range(s.occ):
                uses = jnp.bool_(False)
                for pair in range(q, s.pairs, s.occ):
                    uses |= partner[user * s.pairs + pair] == orbital
                union += jnp.where(uses, 1.0, 0.0) * maps[user * s.occ + q]
            taken = jnp.where((union > 0.0) & (maps[orbital] > 0.0), 1.0, 0.0)
            sums[k, pl.ds(e, 1), :] = jnp.sum(taken, axis=0, keepdims=True)
            steps[k, pl.ds(e, 1), :] = jnp.full(
                (1, LANES), rows_of(lens[orbital]).astype(jnp.float32), jnp.float32
            )
        return 0

    lax.fori_loop(0, devices - 2, edge, 0)
    need = jnp.zeros(sums.shape[1:], jnp.float32)
    ones = jnp.ones((LANES, LANES), jnp.bfloat16)
    for k in range(s.occ):
        count = dot(sums[k].astype(jnp.bfloat16), ones)
        need += jnp.floor((count + (LANES - 1)) / LANES) * steps[k]
    over[0] = (jnp.max(need) > s.first).astype(jnp.int32)


def own_kernel(s, here, partner, lens, counts, tables, aux_rows, blocks, amps, aligned, dens):
    g = pl.program_id(0)
    me = here[0]
    left, p = paired(s, g)
    right = partner[me * s.pairs + p]
    l, _ = s.where_partner(me, right)
    count = counts[l]
    place = places(aux_rows[pl.ds(me * s.occ + left, 1), :], tables[l])
    wide = 2 * LANES

    def some(c):
        aligned[0, :, c * wide : (c + 1) * wide] = dot(
            blocks[0], picker(place, c), NT
        ).astype(jnp.bfloat16)

    chunks = s.aux // wide
    for c in range(chunks - 1):
        some(c)
    pl.when(count > (chunks - 1) * wide)(functools.partial(some, chunks - 1))

    masked = kept(amps[0], lens[me * s.occ + left], lens[right])
    term = dot(masked, masked, NT)

    @pl.when(lax.rem(g, s.pairs // s.occ) == 0)
    def _():
        dens[0] = term

    @pl.when(lax.rem(g, s.pairs // s.occ) != 0)
    def _():
        dens[0] += term


def paired(s, g):
    repeats = s.pairs // s.occ
    left = g // repeats
    return left, lax.rem(g, repeats) * s.occ + left


def near_kernel(
    s, ncpl, here, partner, listed, lens, coef, pao_rows, sibling, own, other, dens_in, coupling, dens, wide, tall, dens_own, sem
):
    p = pl.program_id(0)
    me = here[0]
    peers = swapped(me)
    fetch = pltpu.make_async_copy(dens_in, dens_own, sem)

    @pl.when(p == 0)
    def _():
        fetch.start()
        dens[...] = jnp.zeros_like(dens)
        wide[s.pairs : 2 * s.pairs] = own[...]
        for device, packed in zip(peers, (sibling, other)):
            for k in range(s.pairs):
                unpack(s, packed, k, wide.at[(device - me + 1) * s.pairs + k])

    def row_of(orbital):
        return pao_rows[pl.ds(orbital, 1), :]

    def column_of(orbital):
        row = row_of(orbital)
        return column(jnp.where(row < 0, -2, row)).astype(jnp.int16)

    right_col = column_of(partner[me * s.pairs + p])
    left_col = column_of(me * s.occ + lax.rem(p, s.occ))
    left_rows = []
    for c in range(ncpl):
        m = listed[p, c]
        left_rows.append(row_of(s.first_orbital(m)))
        amp = wide[m - (me - 1) * s.pairs]
        moved = dot(amp, same(right_col, row_of(partner[m]).astype(jnp.int16)), NT)
        tall[c * s.pao : (c + 1) * s.pao] = (coef[p, c] * moved).astype(jnp.bfloat16)
    left_row = jnp.concatenate(left_rows, axis=1).astype(jnp.int16)
    coupling[0] = dot(same(left_col, left_row), tall[...])

    for side in range(3):
        m = (me + side - 1) * s.pairs + p
        inside = (m >= 0) & (m < s.npair)
        m = jnp.clip(m, 0, s.npair - 1)
        near = partner[m] - me * s.occ

        @pl.when(inside & (near >= 0) & (near < s.occ))
        def _():
            amp = wide[side * s.pairs + p]
            masked = kept(amp, lens[s.first_orbital(m)], lens[partner[m]])
            dens[near] += dot(masked, masked, TN)

    @pl.when(p == s.pairs - 1)
    def _():
        fetch.wait()
        dens[...] = (dens[...] + dens_own[...]) / s.pao


def update(s, lens_left, lens_right, exchange, amp, coupling, gap_left, gap_right):
    mask = live(lens_left, lens_right, (s.pao, s.pao))
    exchange = jnp.where(mask, exchange, 0.0)
    masked = jnp.where(mask, amp.astype(jnp.float32), 0.0)
    left = column(gap_left)
    parts = []
    for at in range(0, s.pao, LANES):
        lanes = slice(at, min(at + LANES, s.pao))
        part = masked[:, lanes]
        denom = left[:, : part.shape[1]] + gap_right[:, lanes]
        residual = exchange[:, lanes] + denom * part - coupling[:, lanes]
        parts.append((part - 0.5 * residual / denom).astype(jnp.bfloat16))
    return jnp.concatenate(parts, axis=1), jnp.sum(exchange * masked) / s.pao


def compacted(s, count, at, step, aligned, halo, sums):
    wide = 2 * LANES

    def some(c):
        spot = pl.multiple_of(at + 2 * c * step, 16)
        one = halo[pl.ds(spot, s.pao), :]
        two = halo[pl.ds(pl.multiple_of(spot + step, 16), s.pao), :]
        two = jnp.where((2 * c + 1) * LANES < count, two, jnp.zeros_like(two))
        both = jnp.concatenate([one, two], axis=1)
        term = dot(aligned[:, c * wide : (c + 1) * wide], both, NT)
        if c == 0:
            sums[...] = term
        else:
            sums[...] += term

    @pl.when(count == 0)
    def _():
        sums[...] = jnp.zeros_like(sums)

    chunkwise(s, count, some)


def mid_kernel(
    s, here, partner, lens, counts, offsets, gaps, aligned, coupling, amps, own, sibling, new_amps, energy, halo, sums, sem
):
    p = pl.program_id(0)
    me = here[0]
    left, right = me * s.occ + lax.rem(p, s.occ), partner[me * s.pairs + p]
    l, kind = s.where_partner(me, right)

    @pl.when(p == 0)
    def _():
        copy = pltpu.make_async_copy(sibling, halo.at[pl.ds(0, s.rows), :], sem)
        copy.start()
        copy.wait()

    @pl.when(kind == 2)
    def _():
        sums[...] = dot(aligned[0], own[lax.rem(right, s.occ)], NT)

    @pl.when(kind == 0)
    def _():
        compacted(s, counts[l], offsets[l], rows_of(lens[right]), aligned.at[0], halo, sums)

    @pl.when(kind != 1)
    def _():
        new_amps[0], energy[p] = update(
            s, lens[left], lens[right], sums[...], amps[0], coupling[0], gaps[pl.ds(left, 1), :], gaps[pl.ds(right, 1), :]
        )

    @pl.when(kind == 1)
    def _():
        new_amps[0] = jnp.zeros_like(amps[0])
        energy[p] = 0.0


def last_kernel(
    s, here, partner, lens, counts, offsets, over, energy_in, gaps, aligned, coupling, amps, other, more, _, new_amps, energy, halo, held, terms, olds, news, sums, sems
):
    me = here[0]

    def copies(p):
        return [
            pltpu.make_async_copy(aligned.at[p], held.at[p], sems.at[0, p]),
            pltpu.make_async_copy(coupling.at[p], terms.at[p], sems.at[1, p]),
            pltpu.make_async_copy(amps.at[p], olds.at[p], sems.at[2, p]),
        ]

    def result(p):
        return pltpu.make_async_copy(news.at[p], new_amps.at[p], sems.at[3, p])

    def each(act):
        def one(p, _):
            right = partner[me * s.pairs + p]
            l, kind = s.where_partner(me, right)

            @pl.when(kind == 1)
            def _():
                act(p, right, l)

            return 0

        lax.fori_loop(0, s.pairs, one, 0)

    first = pltpu.make_async_copy(other, halo.at[pl.ds(0, s.first)], sems.at[4, 0])
    rest = pltpu.make_async_copy(more, halo.at[pl.ds(s.first, s.rows - s.first)], sems.at[4, 1])
    first.start()

    @pl.when(over[0] > 0)
    def _():
        rest.start()
        rest.wait()

    def begin(p, right, l):
        for copy in copies(p):
            copy.start()

    def finish(p, right, l):
        left = me * s.occ + lax.rem(p, s.occ)
        for copy in copies(p):
            copy.wait()
        compacted(s, counts[l], offsets[l], rows_of(lens[right]), held.at[p], halo, sums)
        news[p], energy[p] = update(
            s, lens[left], lens[right], sums[...], olds[p], terms[p], gaps[pl.ds(left, 1), :], gaps[pl.ds(right, 1), :]
        )
        result(p).start()

    for p in range(s.pairs):
        energy[p] = energy_in[p]
    each(begin)
    first.wait()
    each(finish)
    each(lambda p, right, l: result(p).wait())


def position():
    return lax.axis_index(AXES)


def swap(array, role):
    count = 1
    for axis in AXES:
        count *= lax.axis_size(axis)
    route = []
    for low in range(role, count - 1, 2):
        route += [(low, low + 1), (low + 1, low)]
    return lax.ppermute(array, AXES, route)


def local(
    blocks, aux_domain, pao_domain, pao_gap, amplitudes, pair_partner, coupling_list, coupling_coef
):
    s = Sizes(blocks, amplitudes, pair_partner)
    ncpl = coupling_list.shape[1]
    me = position()
    here = me.astype(jnp.int32).reshape(1)
    blocks_t = jnp.swapaxes(blocks, 1, 2)

    smem = pl.BlockSpec(memory_space=pltpu.SMEM)
    vmem = pl.BlockSpec(memory_space=pltpu.VMEM)
    anywhere = pl.BlockSpec(memory_space=pl.ANY)
    plain = pltpu.CompilerParams(vmem_limit_bytes=VMEM_BYTES)
    stepped = pltpu.CompilerParams(
        dimension_semantics=("arbitrary",), vmem_limit_bytes=VMEM_BYTES
    )
    square = pl.BlockSpec((1, s.pao, s.pao), lambda p, *_: (p, 0, 0))
    all_dens = pl.BlockSpec((s.occ, s.pao, s.pao), lambda p, *_: (0, 0, 0))
    squares = jax.ShapeDtypeStruct((s.pairs, s.pao, s.pao), jnp.float32)
    dens_shape = jax.ShapeDtypeStruct((s.occ, s.pao, s.pao), jnp.float32)

    def cost(work, data):
        return pl.CostEstimate(flops=work, bytes_accessed=data, transcendentals=0)

    whole, tail, share = packing(s)
    slim = pl.pallas_call(
        functools.partial(slim_kernel, s),
        in_specs=[vmem],
        out_specs=vmem,
        out_shape=jax.ShapeDtypeStruct((s.pairs + s.pairs // share, s.pao, whole), jnp.bfloat16),
        compiler_params=plain,
        cost_estimate=cost(10**6, 4 * 10**6),
        name="slim",
    )(amplitudes)
    amps_other = swap(slim, 1)
    amps_sibling = swap(slim, 0)

    lens = jnp.sum((pao_domain >= 0).astype(jnp.int32), axis=1)

    lists = 3 * s.occ
    to_sibling, to_other, to_other_more, tables, pao_rows, gap_rows, counts, offsets = pl.pallas_call(
        functools.partial(pack_kernel, s),
        in_specs=[smem] * 3 + [vmem] * 4,
        out_specs=[anywhere] * 3 + [vmem] * 3 + [smem] * 2,
        out_shape=[
            jax.ShapeDtypeStruct((s.rows, LANES), jnp.bfloat16),
            jax.ShapeDtypeStruct((s.first, LANES), jnp.bfloat16),
            jax.ShapeDtypeStruct((s.rows - s.first, LANES), jnp.bfloat16),
            jax.ShapeDtypeStruct((lists, 2 * LOW, HIGH), jnp.bfloat16),
            jax.ShapeDtypeStruct(pao_domain.shape, pao_domain.dtype),
            jax.ShapeDtypeStruct(pao_gap.shape, pao_gap.dtype),
            jax.ShapeDtypeStruct((lists,), jnp.int32),
            jax.ShapeDtypeStruct((lists,), jnp.int32),
        ],
        scratch_shapes=[
            pltpu.VMEM((3 * s.occ, 2 * LOW, HIGH), jnp.float32),
            pltpu.VMEM((s.occ, 2 * LOW, HIGH), jnp.bfloat16),
            pltpu.VMEM((2, s.rows + s.pao, LANES), jnp.bfloat16),
            pltpu.SemaphoreType.DMA((3,)),
        ],
        compiler_params=plain,
        cost_estimate=cost(2 * 10**9, 10**7),
        name="pack",
    )(here, pair_partner, lens, aux_domain, blocks_t, pao_domain.T, pao_gap.T)

    from_other = swap(to_other, 1)
    from_sibling = swap(to_sibling, 0)

    edges = -(-(s.nocc // s.occ) // 8) * 8
    (over,) = pl.pallas_call(
        functools.partial(count_kernel, s),
        in_specs=[smem] * 2 + [vmem],
        out_specs=[smem],
        out_shape=[jax.ShapeDtypeStruct((1,), jnp.int32)],
        scratch_shapes=[
            pltpu.VMEM((s.nocc, AUX_IDS // LANES, LANES), jnp.float32),
            pltpu.VMEM((s.occ, edges, LANES), jnp.float32),
            pltpu.VMEM((s.occ, edges, LANES), jnp.float32),
        ],
        compiler_params=plain,
        cost_estimate=cost(10**9, 10**6),
        name="count",
    )(pair_partner, lens, aux_domain)

    def by_left(block):
        return pl.BlockSpec((1,) + block, lambda g: (paired(s, g)[0], 0, 0))

    aligned, dens = pl.pallas_call(
        functools.partial(own_kernel, s),
        grid=(s.pairs,),
        in_specs=[smem] * 4
        + [
            vmem,
            vmem,
            by_left((s.pao, s.aux)),
            pl.BlockSpec((1, s.pao, s.pao), lambda g: (paired(s, g)[1], 0, 0)),
        ],
        out_specs=[
            pl.BlockSpec((1, s.pao, s.aux), lambda g: (paired(s, g)[1], 0, 0)),
            by_left((s.pao, s.pao)),
        ],
        out_shape=[
            jax.ShapeDtypeStruct((s.pairs, s.pao, s.aux), jnp.bfloat16),
            dens_shape,
        ],
        compiler_params=stepped,
        cost_estimate=cost(2 * s.pairs * s.pao * s.aux * s.aux * 2, 2 * 10**7),
        name="own",
    )(here, pair_partner, lens, counts, tables, aux_domain, blocks_t, amplitudes)

    coupling, densities = pl.pallas_call(
        functools.partial(near_kernel, s, ncpl),
        grid=(s.pairs,),
        in_specs=[smem] * 5 + [vmem] * 4 + [anywhere],
        out_specs=[square, all_dens],
        out_shape=[squares, dens_shape],
        scratch_shapes=[
            pltpu.VMEM((3 * s.pairs, s.pao, s.pao), jnp.bfloat16),
            pltpu.VMEM((ncpl * s.pao, s.pao), jnp.bfloat16),
            pltpu.VMEM((s.occ, s.pao, s.pao), jnp.float32),
            pltpu.SemaphoreType.DMA,
        ],
        compiler_params=stepped,
        cost_estimate=cost(2 * s.pairs * s.pao * s.aux * s.aux * 2, 2 * 10**7),
        name="near",
    )(
        here, pair_partner, coupling_list, lens, coupling_coef,
        pao_rows, amps_sibling, amplitudes, amps_other, dens,
    )

    some_amps, some_energies = pl.pallas_call(
        functools.partial(mid_kernel, s),
        grid=(s.pairs,),
        in_specs=[smem] * 5
        + [
            vmem,
            pl.BlockSpec((1, s.pao, s.aux), lambda p: (p, 0, 0)),
            square,
            square,
            vmem,
            anywhere,
        ],
        out_specs=[square, smem],
        out_shape=[
            jax.ShapeDtypeStruct(amplitudes.shape, amplitudes.dtype),
            jax.ShapeDtypeStruct((s.pairs,), jnp.float32),
        ],
        scratch_shapes=[
            pltpu.VMEM((s.rows + s.pao, LANES), jnp.bfloat16),
            pltpu.VMEM((s.pao, s.pao), jnp.float32),
            pltpu.SemaphoreType.DMA,
        ],
        compiler_params=stepped,
        cost_estimate=cost(2 * s.pairs * s.pao * s.pao * s.aux, 2 * 10**7),
        name="mid",
    )(
        here, pair_partner, lens, counts, offsets,
        gap_rows, aligned, coupling, amplitudes, blocks_t, from_sibling,
    )

    from_other_more = lax.cond(over[0] > 0, lambda a: swap(a, 1), lambda a: a, to_other_more)
    new_amps, energies = pl.pallas_call(
        functools.partial(last_kernel, s),
        in_specs=[smem] * 7 + [vmem] + [anywhere] * 6,
        out_specs=[anywhere, smem],
        out_shape=[
            jax.ShapeDtypeStruct(amplitudes.shape, amplitudes.dtype),
            jax.ShapeDtypeStruct((s.pairs,), jnp.float32),
        ],
        scratch_shapes=[
            pltpu.VMEM((s.rows + s.pao, LANES), jnp.bfloat16),
            pltpu.VMEM((s.pairs, s.pao, s.aux), jnp.bfloat16),
            pltpu.VMEM((s.pairs, s.pao, s.pao), jnp.float32),
            pltpu.VMEM((s.pairs, s.pao, s.pao), jnp.bfloat16),
            pltpu.VMEM((s.pairs, s.pao, s.pao), jnp.bfloat16),
            pltpu.VMEM((s.pao, s.pao), jnp.float32),
            pltpu.SemaphoreType.DMA((5, s.pairs)),
        ],
        input_output_aliases={13: 0},
        compiler_params=plain,
        cost_estimate=cost(2 * s.pairs * s.pao * s.pao * s.aux, 2 * 10**7),
        name="last",
    )(
        here, pair_partner, lens, counts, offsets, over, some_energies,
        gap_rows, aligned, coupling, amplitudes, from_other, from_other_more, some_amps,
    )
    return (new_amps, energies, densities)


def solution(mesh):
    return jax.shard_map(
        local,
        mesh=mesh,
        in_specs=(
            P(AXES, None, None),
            P(),
            P(),
            P(),
            P(AXES, None, None),
            P(),
            P(AXES, None),
            P(AXES, None),
        ),
        out_specs=(P(AXES, None, None), P(AXES), P(AXES, None, None)),
        check_vma=False,
    )
```

```python
import functools

import jax
import jax.numpy as jnp
from jax import lax
from jax.experimental import pallas as pl
from jax.experimental.pallas import tpu as pltpu
from jax.sharding import PartitionSpec as P

AXES = ("orb", "pair")
VMEM_BYTES = 60 * 1024 * 1024
AUX_IDS = 2048
LOW = 64
HIGH = AUX_IDS // LOW
BASE = 32
LANES = 128
FIRST, WHOLE = 18, 32
NN = (((1,), (0,)), ((), ()))
NT = (((1,), (1,)), ((), ()))
TN = (((0,), (0,)), ((), ()))


def dot(a, b, dims=NN):
    return lax.dot_general(a, b, dims, preferred_element_type=jnp.float32)


def one_where(equal, value=1.0):
    return jnp.where(equal, value, 0.0).astype(jnp.bfloat16)


def iota(shape, dim):
    return lax.broadcasted_iota(jnp.int32, shape, dim)


def live(rows, cols, shape):
    return (iota(shape, 0) < rows) & (iota(shape, 1) < cols)


def kept(amp, rows, cols):
    return jnp.where(live(rows, cols, amp.shape), amp.astype(jnp.float32), 0.0).astype(amp.dtype)


def short_where(equal):
    one = jnp.ones(equal.shape, jnp.bfloat16)
    return jnp.where(equal, one, jnp.zeros_like(one))


def column(row):
    return jnp.broadcast_to(row, (LANES, row.shape[1])).T


def same(col, row):
    parts = []
    for at in range(0, row.shape[1], LANES):
        piece = row[:, at : at + LANES]
        wide = jnp.broadcast_to(piece, (col.shape[0], piece.shape[1]))
        parts.append(short_where(col[:, : piece.shape[1]] == wide))
    return jnp.concatenate(parts, axis=1)


def chunks_of(count):
    return (count + LANES - 1) // LANES


def rows_of(length):
    return (length + 15) // 16 * 16


def swapped(me):
    odd = lax.rem(me, 2)
    return me + 1 - 2 * odd, me - 1 + 2 * odd


class Sizes:
    def __init__(self, blocks, amplitudes, pair_partner):
        self.occ = blocks.shape[0]
        self.aux = blocks.shape[1]
        self.pao = blocks.shape[2]
        self.pairs = amplitudes.shape[0]
        self.npair = pair_partner.shape[0]
        self.nocc = self.npair // self.pairs * self.occ
        self.rows = self.occ * self.pao * (self.aux // LANES)
        self.first = self.rows * FIRST // WHOLE // 16 * 16

    def first_orbital(self, pair):
        return pair // self.pairs * self.occ + lax.rem(pair, self.occ)

    def where_partner(self, me, right):
        device = right // self.occ
        sibling, _ = swapped(me)
        kind = jnp.where(device == me, 2, jnp.where(device == sibling, 0, 1))
        return kind * self.occ + lax.rem(right, self.occ), kind


def packing(s):
    whole = s.pao // LANES * LANES
    tail = s.pao - whole
    share = whole // tail
    return whole, tail, share


def slim_kernel(s, amps, out):
    whole, tail, share = packing(s)
    for k in range(s.pairs):
        out[k] = amps[k, :, :whole]
    for g in range(s.pairs // share):
        tails = [amps[g * share + t, :, whole:] for t in range(share)]
        out[s.pairs + g] = jnp.concatenate(tails, axis=1)


def unpack(s, packed, k, out):
    whole, tail, share = packing(s)
    out[:, :whole] = packed[k]
    spot = k % share * tail
    out[:, whole:] = packed[s.pairs + k // share, :, spot : spot + tail]


def bits(values, count, lanes):
    levels = iota((count, lanes), 0).astype(jnp.bfloat16)
    return short_where(levels == jnp.broadcast_to(values.astype(jnp.bfloat16), (count, lanes)))


def places(row, table, k):
    found = dot(table, bits(row // LOW + k * HIGH, table.shape[1], row.shape[1]))
    low = bits(lax.rem(row, LOW), LOW, row.shape[1]).astype(jnp.float32)
    return jnp.sum((found[:LOW] * BASE + found[LOW:]) * low, axis=0, keepdims=True)


def picker(place, chunk):
    wide = 2 * LANES
    middle = chunk * wide + LANES + 1
    spot = (place - jnp.asarray(middle).astype(jnp.float32)).astype(jnp.bfloat16)
    levels = (iota((wide, place.shape[1]), 0) - LANES).astype(jnp.bfloat16)
    return short_where(levels == jnp.broadcast_to(spot, levels.shape))


def chunkwise(s, count, act):
    for c in range(s.aux // (2 * LANES)):
        pl.when(count > c * 2 * LANES)(functools.partial(act, c))


def split_place(place, row):
    part = jnp.where(row < LOW, place // BASE, lax.rem(place, BASE))
    return part.astype(jnp.float32).astype(jnp.bfloat16)


def pack_kernel(
    s, here, partner, lens, aux_rows, blocks, pao_cols, gap_cols, to_sibling, to_other, to_other_more, tables, pao_rows, gap_rows, counts, offsets, maps, users, sends, bufs, sems
):
    me = here[0]
    peers = swapped(me)
    pao_rows[...] = pao_cols[...].T
    gap_rows[...] = gap_cols[...].T

    for g, device in enumerate((me,) + peers):
        for k in range(s.occ):
            orbital = jnp.clip(device * s.occ + k, 0, s.nocc - 1)
            row = aux_rows[pl.ds(orbital, 1), :]
            by_high = bits(row // LOW, HIGH, s.aux)
            by_low = bits(lax.rem(row, LOW), LOW, s.aux)
            here_map = dot(jnp.concatenate([by_low, by_low], axis=0), by_high, NT)
            maps[g, :, k * HIGH : (k + 1) * HIGH] = here_map
            users[g * s.occ + k] = jnp.concatenate([here_map] * s.occ, axis=1)
            if g == 0:
                spot = iota((LOW, s.aux), 1) + 1
                parts = jnp.concatenate(
                    [
                        (spot // BASE).astype(jnp.float32).astype(jnp.bfloat16) * by_low,
                        lax.rem(spot, BASE).astype(jnp.float32).astype(jnp.bfloat16) * by_low,
                    ],
                    axis=0,
                )
                tables[2, :, k * HIGH : (k + 1) * HIGH] = dot(parts, by_high, NT).astype(
                    jnp.bfloat16
                )

    wide = s.occ * HIGH
    sub, lane = iota((2 * LOW, 2 * LOW), 0), iota((2 * LOW, 2 * LOW), 1)
    ahead = one_where((lane < LOW) & (lane < lax.rem(sub, LOW)))
    first = one_where(lane < LOW)
    sub, lane = iota((wide, wide), 0), iota((wide, wide), 1)
    above = one_where((sub // HIGH == lane // HIGH) & (sub < lane))
    level = iota((2 * LOW, wide), 0)
    owner = iota((1, wide), 1) // HIGH

    def listing(target, target_device, user, user_device):
        union = jnp.zeros((2 * LOW, wide), jnp.float32)
        for q in range(s.occ):
            uses = jnp.zeros((1, wide), jnp.float32)
            for pair in range(q, s.pairs, s.occ):
                pair += user_device * s.pairs
                inside = (pair >= 0) & (pair < s.npair)
                k = partner[jnp.clip(pair, 0, s.npair - 1)] - target_device * s.occ
                uses += jnp.where((owner == k) & inside, 1.0, 0.0)
            union += uses * users[user * s.occ + q]
        taken = (union > 0.0) & (maps[target] > 0.0)
        flags = one_where(taken)
        total = dot(first, flags)
        place = dot(ahead, flags) + dot(total.astype(jnp.bfloat16), above) + 1.0
        place = jnp.where(taken, place, 0.0).astype(jnp.int32)
        found = [
            jnp.sum(jnp.where(owner == k, total[:1], 0.0)).astype(jnp.int32) for k in range(s.occ)
        ]
        return split_place(place, level), found

    copies = {
        0: [pltpu.make_async_copy(bufs.at[0, pl.ds(0, s.rows)], to_sibling, sems.at[0])],
        1: [
            pltpu.make_async_copy(bufs.at[1, pl.ds(0, s.first)], to_other, sems.at[1]),
            pltpu.make_async_copy(
                bufs.at[1, pl.ds(s.first, s.rows - s.first)], to_other_more, sems.at[2]
            ),
        ],
    }
    for r in (1, 0):
        sends[r], found = listing(0, me, 1 + r, peers[r])
        at = jnp.int32(0)
        for k, count in enumerate(found):
            step = rows_of(lens[me * s.occ + k])

            @pl.when(count > 0)
            def _(k=k, at=at, step=step, count=count):
                place = places(aux_rows[pl.ds(me * s.occ + k, 1), :], sends[r], k)

                def some(c):
                    got = dot(blocks[k], picker(place, c), NT).astype(jnp.bfloat16)
                    spot = pl.multiple_of(at + 2 * c * step, 16)
                    bufs[r, pl.ds(spot, s.pao), :] = got[:, :LANES]

                    @pl.when((2 * c + 1) * LANES < count)
                    def _():
                        bufs[r, pl.ds(pl.multiple_of(spot + step, 16), s.pao), :] = got[:, LANES:]

                chunkwise(s, count, some)

            at += chunks_of(count) * step

        for copy in copies[r]:
            copy.start()

    for r in range(2):
        tables[r], found = listing(1 + r, peers[r], 0, me)
        at = jnp.int32(0)
        for k, count in enumerate(found):
            orbital = jnp.clip(peers[r] * s.occ + k, 0, s.nocc - 1)
            counts[r * s.occ + k] = count
            offsets[r * s.occ + k] = at
            at += chunks_of(count) * rows_of(lens[orbital])
    for k in range(s.occ):
        counts[2 * s.occ + k] = jnp.int32(s.aux)
        offsets[2 * s.occ + k] = jnp.int32(0)

    for copy in copies[1] + copies[0]:
        copy.wait()


def count_kernel(s, partner, lens, aux_rows, over):
    devices = s.nocc // s.occ
    full = s.aux // LANES

    def ids(orbital):
        row = aux_rows[pl.ds(orbital, 1), :]
        return dot(bits(row // LOW, HIGH, s.aux), bits(lax.rem(row, LOW), LOW, s.aux), NT)

    over[0] = jnp.int32(0)

    def edge(e, _):
        source = e + 1
        user = source + 1 - 2 * lax.rem(e, 2)
        reads = [partner[user * s.pairs + q] - source * s.occ for q in range(s.pairs)]
        bound = jnp.int32(0)
        for k in range(s.occ):
            used = functools.reduce(jnp.logical_or, [read == k for read in reads])
            bound += jnp.where(used, full * rows_of(lens[source * s.occ + k]), 0)

        @pl.when(bound > s.first)
        def _():
            domains = [ids(user * s.occ + q) for q in range(s.occ)]
            need = jnp.int32(0)
            for k in range(s.occ):
                union = jnp.zeros((HIGH, LOW), jnp.float32)
                for q, domain in enumerate(domains):
                    used = functools.reduce(
                        jnp.logical_or, [read == k for read in reads[q :: s.occ]]
                    )
                    union += jnp.where(used, 1.0, 0.0) * domain
                taken = (union > 0.0) & (ids(source * s.occ + k) > 0.0)
                count = jnp.sum(jnp.where(taken, 1.0, 0.0)).astype(jnp.int32)
                need += chunks_of(count) * rows_of(lens[source * s.occ + k])
            over[0] = jnp.maximum(over[0], (need > s.first).astype(jnp.int32))

        return 0

    lax.fori_loop(0, devices - 2, edge, 0)


def own_kernel(s, here, partner, lens, counts, tables, aux_rows, blocks, amps, aligned, dens):
    left = pl.program_id(0)
    me = here[0]
    wide = 2 * LANES
    chunks = s.aux // wide
    row = aux_rows[pl.ds(me * s.occ + left, 1), :]
    term = jnp.zeros((s.pao, s.pao), jnp.float32)
    rest = []

    for t in range(s.pairs // s.occ):
        right = partner[me * s.pairs + t * s.occ + left]
        l, kind = s.where_partner(me, right)
        place = places(row, tables[kind], lax.rem(right, s.occ))

        def some(c, t=t, place=place):
            aligned[t, 0, :, c * wide : (c + 1) * wide] = dot(
                blocks[0], picker(place, c), NT
            ).astype(jnp.bfloat16)

        for c in range(chunks - 1):
            some(c)
        rest.append((counts[l] > (chunks - 1) * wide, functools.partial(some, chunks - 1)))
        masked = kept(amps[t, 0], lens[me * s.occ + left], lens[right])
        term += dot(masked, masked, NT)

    dens[0] = term
    for needed, act in rest:
        pl.when(needed)(act)


def main_kernel(
    s, ncpl, here, partner, listed, lens, coef, counts, offsets, pao_rows, gaps, sibling, own, other, aligned, dens_in, blocks, from_sibling, coupling, dens, new_amps, energy, wide, tall, dens_own, near_blocks, halo, sums, sems
):
    p = pl.program_id(0)
    me = here[0]
    peers = swapped(me)
    fetches = [
        pltpu.make_async_copy(from_sibling, halo.at[pl.ds(0, s.rows), :], sems.at[0]),
        pltpu.make_async_copy(blocks, near_blocks, sems.at[1]),
        pltpu.make_async_copy(dens_in, dens_own, sems.at[2]),
    ]

    @pl.when(p == 0)
    def _():
        for fetch in fetches:
            fetch.start()
        dens[...] = jnp.zeros_like(dens)
        wide[s.pairs : 2 * s.pairs] = own[...]
        for device, packed in zip(peers, (sibling, other)):
            for k in range(s.pairs):
                unpack(s, packed, k, wide.at[(device - me + 1) * s.pairs + k])

    def row_of(orbital):
        return pao_rows[pl.ds(orbital, 1), :]

    def column_of(orbital):
        row = row_of(orbital)
        return column(jnp.where(row < 0, -2, row)).astype(jnp.int16)

    right_col = column_of(partner[me * s.pairs + p])
    left_col = column_of(me * s.occ + lax.rem(p, s.occ))
    left_rows = []
    for c in range(ncpl):
        m = listed[c, p]
        left_rows.append(row_of(s.first_orbital(m)))
        amp = wide[m - (me - 1) * s.pairs]
        moved = dot(amp, same(right_col, row_of(partner[m]).astype(jnp.int16)), NT)
        tall[c * s.pao : (c + 1) * s.pao] = (coef[c, p] * moved).astype(jnp.bfloat16)
    left_row = jnp.concatenate(left_rows, axis=1).astype(jnp.int16)
    coupling[0] = dot(same(left_col, left_row), tall[...])

    for side in range(3):
        m = (me + side - 1) * s.pairs + p
        inside = (m >= 0) & (m < s.npair)
        m = jnp.clip(m, 0, s.npair - 1)
        near = partner[m] - me * s.occ

        @pl.when(inside & (near >= 0) & (near < s.occ))
        def _():
            amp = wide[side * s.pairs + p]
            masked = kept(amp, lens[s.first_orbital(m)], lens[partner[m]])
            dens[near] += dot(masked, masked, TN)

    @pl.when(p == 0)
    def _():
        for fetch in fetches:
            fetch.wait()

    left, right = me * s.occ + lax.rem(p, s.occ), partner[me * s.pairs + p]
    l, kind = s.where_partner(me, right)

    @pl.when(kind == 2)
    def _():
        sums[...] = dot(aligned[0], near_blocks[lax.rem(right, s.occ)], NT)

    @pl.when(kind == 0)
    def _():
        compacted(s, counts[l], offsets[l], rows_of(lens[right]), aligned.at[0], halo, sums)

    @pl.when(kind != 1)
    def _():
        new_amps[0], energy[p] = update(
            s, lens[left], lens[right], sums[...], own[p], coupling[0], gaps[pl.ds(left, 1), :], gaps[pl.ds(right, 1), :]
        )

    @pl.when(kind == 1)
    def _():
        energy[p] = 0.0

    @pl.when(p == s.pairs - 1)
    def _():
        dens[...] = (dens[...] + dens_own[...]) * (1.0 / s.pao)


def update(s, lens_left, lens_right, exchange, amp, coupling, gap_left, gap_right):
    left = column(gap_left)
    parts = []
    energy = jnp.zeros((s.pao, LANES), jnp.float32)
    for at in range(0, s.pao, LANES):
        lanes = slice(at, min(at + LANES, s.pao))
        part = amp[:, lanes].astype(jnp.float32)
        shape = part.shape
        mask = live(lens_left, lens_right - at, shape)
        denom = left[:, : shape[1]] + gap_right[:, lanes]
        inverse = pl.reciprocal(denom, approx=True)
        inverse = inverse * (2.0 - denom * inverse)
        moved = (exchange[:, lanes] - coupling[:, lanes]) * inverse
        parts.append(jnp.where(mask, 0.5 * (part - moved), 0.0).astype(jnp.bfloat16))
        term = jnp.where(mask, exchange[:, lanes] * part, 0.0)
        if shape[1] < LANES:
            term = jnp.concatenate([term, jnp.zeros((s.pao, LANES - shape[1]), jnp.float32)], axis=1)
        energy += term
    return jnp.concatenate(parts, axis=1), jnp.sum(energy) / s.pao


def compacted(s, count, at, step, aligned, halo, sums):
    wide = 2 * LANES

    def some(c):
        spot = pl.multiple_of(at + 2 * c * step, 16)
        one = halo[pl.ds(spot, s.pao), :]
        two = halo[pl.ds(pl.multiple_of(spot + step, 16), s.pao), :]
        two = jnp.where((2 * c + 1) * LANES < count, two, jnp.zeros_like(two))
        both = jnp.concatenate([one, two], axis=1)
        term = dot(aligned[:, c * wide : (c + 1) * wide], both, NT)
        if c == 0:
            sums[...] = term
        else:
            sums[...] += term

    @pl.when(count == 0)
    def _():
        sums[...] = jnp.zeros_like(sums)

    chunkwise(s, count, some)


def last_kernel(
    s, here, partner, lens, counts, offsets, over, energy_in, gaps, aligned, coupling, amps, other, more, _, new_amps, energy, halo, held, terms, olds, news, sums, sems
):
    me = here[0]

    def copies(p):
        return [
            pltpu.make_async_copy(aligned.at[p], held.at[p], sems.at[0, p]),
            pltpu.make_async_copy(coupling.at[p], terms.at[p], sems.at[1, p]),
            pltpu.make_async_copy(amps.at[p], olds.at[p], sems.at[2, p]),
        ]

    def result(p):
        return pltpu.make_async_copy(news.at[p], new_amps.at[p], sems.at[3, p])

    def each(act):
        def one(p, _):
            right = partner[me * s.pairs + p]
            l, kind = s.where_partner(me, right)

            @pl.when(kind == 1)
            def _():
                act(p, right, l)

            return 0

        lax.fori_loop(0, s.pairs, one, 0)

    first = pltpu.make_async_copy(other, halo.at[pl.ds(0, s.first)], sems.at[4, 0])
    rest = pltpu.make_async_copy(more, halo.at[pl.ds(s.first, s.rows - s.first)], sems.at[4, 1])
    first.start()

    @pl.when(over[0] > 0)
    def _():
        rest.start()
        rest.wait()

    def begin(p, right, l):
        for copy in copies(p):
            copy.start()

    def finish(p, right, l):
        left = me * s.occ + lax.rem(p, s.occ)
        for copy in copies(p):
            copy.wait()
        compacted(s, counts[l], offsets[l], rows_of(lens[right]), held.at[p], halo, sums)
        news[p], energy[p] = update(
            s, lens[left], lens[right], sums[...], olds[p], terms[p], gaps[pl.ds(left, 1), :], gaps[pl.ds(right, 1), :]
        )
        result(p).start()

    for p in range(s.pairs):
        energy[p] = energy_in[p]
    each(begin)
    first.wait()
    each(finish)
    each(lambda p, right, l: result(p).wait())


def position():
    return lax.axis_index(AXES)


def swap(array, role):
    count = 1
    for axis in AXES:
        count *= lax.axis_size(axis)
    route = []
    for low in range(role, count - 1, 2):
        route += [(low, low + 1), (low + 1, low)]
    return lax.ppermute(array, AXES, route)


def local(
    blocks, aux_domain, pao_domain, pao_gap, amplitudes, pair_partner, coupling_list, coupling_coef
):
    s = Sizes(blocks, amplitudes, pair_partner)
    ncpl = coupling_list.shape[1]
    me = position()
    here = me.astype(jnp.int32).reshape(1)
    blocks_t = jnp.swapaxes(blocks, 1, 2)

    smem = pl.BlockSpec(memory_space=pltpu.SMEM)
    vmem = pl.BlockSpec(memory_space=pltpu.VMEM)
    anywhere = pl.BlockSpec(memory_space=pl.ANY)
    plain = pltpu.CompilerParams(vmem_limit_bytes=VMEM_BYTES)
    stepped = pltpu.CompilerParams(
        dimension_semantics=("arbitrary",), vmem_limit_bytes=VMEM_BYTES
    )
    square = pl.BlockSpec((1, s.pao, s.pao), lambda p, *_: (p, 0, 0))
    all_dens = pl.BlockSpec((s.occ, s.pao, s.pao), lambda p, *_: (0, 0, 0))
    squares = jax.ShapeDtypeStruct((s.pairs, s.pao, s.pao), jnp.float32)
    dens_shape = jax.ShapeDtypeStruct((s.occ, s.pao, s.pao), jnp.float32)

    def cost(work, data):
        return pl.CostEstimate(flops=work, bytes_accessed=data, transcendentals=0)

    whole, tail, share = packing(s)
    slim = pl.pallas_call(
        functools.partial(slim_kernel, s),
        in_specs=[vmem],
        out_specs=vmem,
        out_shape=jax.ShapeDtypeStruct((s.pairs + s.pairs // share, s.pao, whole), jnp.bfloat16),
        compiler_params=plain,
        cost_estimate=cost(10**6, 4 * 10**6),
        name="slim",
    )(amplitudes)
    amps_other = swap(slim, 1)
    amps_sibling = swap(slim, 0)

    lens = jnp.sum((pao_domain >= 0).astype(jnp.int32), axis=1)

    lists = 3 * s.occ
    to_sibling, to_other, to_other_more, tables, pao_rows, gap_rows, counts, offsets = pl.pallas_call(
        functools.partial(pack_kernel, s),
        in_specs=[smem] * 3 + [vmem] * 4,
        out_specs=[anywhere] * 3 + [vmem] * 3 + [smem] * 2,
        out_shape=[
            jax.ShapeDtypeStruct((s.rows, LANES), jnp.bfloat16),
            jax.ShapeDtypeStruct((s.first, LANES), jnp.bfloat16),
            jax.ShapeDtypeStruct((s.rows - s.first, LANES), jnp.bfloat16),
            jax.ShapeDtypeStruct((3, 2 * LOW, s.occ * HIGH), jnp.bfloat16),
            jax.ShapeDtypeStruct(pao_domain.shape, pao_domain.dtype),
            jax.ShapeDtypeStruct(pao_gap.shape, pao_gap.dtype),
            jax.ShapeDtypeStruct((lists,), jnp.int32),
            jax.ShapeDtypeStruct((lists,), jnp.int32),
        ],
        scratch_shapes=[
            pltpu.VMEM((3, 2 * LOW, s.occ * HIGH), jnp.float32),
            pltpu.VMEM((3 * s.occ, 2 * LOW, s.occ * HIGH), jnp.float32),
            pltpu.VMEM((2, 2 * LOW, s.occ * HIGH), jnp.bfloat16),
            pltpu.VMEM((2, s.rows + s.pao, LANES), jnp.bfloat16),
            pltpu.SemaphoreType.DMA((3,)),
        ],
        compiler_params=plain,
        cost_estimate=cost(2 * 10**9, 10**7),
        name="pack",
    )(here, pair_partner, lens, aux_domain, blocks_t, pao_domain.T, pao_gap.T)

    from_other = swap(to_other, 1)
    from_sibling = swap(to_sibling, 0)

    (over,) = pl.pallas_call(
        functools.partial(count_kernel, s),
        in_specs=[smem] * 2 + [vmem],
        out_specs=[smem],
        out_shape=[jax.ShapeDtypeStruct((1,), jnp.int32)],
        compiler_params=plain,
        cost_estimate=cost(10**9, 10**6),
        name="count",
    )(pair_partner, lens, aux_domain)

    repeats = s.pairs // s.occ
    both = pl.BlockSpec((repeats, 1, s.pao, s.aux), lambda g: (0, g, 0, 0))
    aligned, dens = pl.pallas_call(
        functools.partial(own_kernel, s),
        grid=(s.occ,),
        in_specs=[smem] * 4
        + [
            vmem,
            vmem,
            pl.BlockSpec((1, s.pao, s.aux), lambda g: (g, 0, 0)),
            pl.BlockSpec((repeats, 1, s.pao, s.pao), lambda g: (0, g, 0, 0)),
        ],
        out_specs=[both, pl.BlockSpec((1, s.pao, s.pao), lambda g: (g, 0, 0))],
        out_shape=[
            jax.ShapeDtypeStruct((repeats, s.occ, s.pao, s.aux), jnp.bfloat16),
            dens_shape,
        ],
        compiler_params=stepped,
        cost_estimate=cost(2 * s.pairs * s.pao * s.aux * s.aux * 2, 2 * 10**7),
        name="own",
    )(
        here, pair_partner, lens, counts, tables, aux_domain, blocks_t,
        amplitudes.reshape(repeats, s.occ, s.pao, s.pao),
    )
    aligned = aligned.reshape(s.pairs, s.pao, s.aux)

    coupling, densities, some_amps, some_energies = pl.pallas_call(
        functools.partial(main_kernel, s, ncpl),
        grid=(s.pairs,),
        in_specs=[smem] * 7
        + [vmem] * 5
        + [pl.BlockSpec((1, s.pao, s.aux), lambda p: (p, 0, 0))]
        + [anywhere] * 3,
        out_specs=[square, all_dens, square, smem],
        out_shape=[
            squares,
            dens_shape,
            jax.ShapeDtypeStruct(amplitudes.shape, amplitudes.dtype),
            jax.ShapeDtypeStruct((s.pairs,), jnp.float32),
        ],
        scratch_shapes=[
            pltpu.VMEM((3 * s.pairs, s.pao, s.pao), jnp.bfloat16),
            pltpu.VMEM((ncpl * s.pao, s.pao), jnp.bfloat16),
            pltpu.VMEM((s.occ, s.pao, s.pao), jnp.float32),
            pltpu.VMEM((s.occ, s.pao, s.aux), jnp.bfloat16),
            pltpu.VMEM((s.rows + s.pao, LANES), jnp.bfloat16),
            pltpu.VMEM((s.pao, s.pao), jnp.float32),
            pltpu.SemaphoreType.DMA((3,)),
        ],
        compiler_params=stepped,
        cost_estimate=cost(2 * s.pairs * s.pao * s.aux * s.aux * 2, 2 * 10**7),
        name="main",
    )(
        here, pair_partner, coupling_list.T, lens, coupling_coef.T, counts, offsets,
        pao_rows, gap_rows, amps_sibling, amplitudes, amps_other, aligned, dens, blocks_t, from_sibling,
    )

    from_other_more = lax.cond(over[0] > 0, lambda a: swap(a, 1), lambda a: a, to_other_more)
    new_amps, energies = pl.pallas_call(
        functools.partial(last_kernel, s),
        in_specs=[smem] * 7 + [vmem] + [anywhere] * 6,
        out_specs=[anywhere, smem],
        out_shape=[
            jax.ShapeDtypeStruct(amplitudes.shape, amplitudes.dtype),
            jax.ShapeDtypeStruct((s.pairs,), jnp.float32),
        ],
        scratch_shapes=[
            pltpu.VMEM((s.rows + s.pao, LANES), jnp.bfloat16),
            pltpu.VMEM((s.pairs, s.pao, s.aux), jnp.bfloat16),
            pltpu.VMEM((s.pairs, s.pao, s.pao), jnp.float32),
            pltpu.VMEM((s.pairs, s.pao, s.pao), jnp.bfloat16),
            pltpu.VMEM((s.pairs, s.pao, s.pao), jnp.bfloat16),
            pltpu.VMEM((s.pao, s.pao), jnp.float32),
            pltpu.SemaphoreType.DMA((5, s.pairs)),
        ],
        input_output_aliases={13: 0},
        compiler_params=plain,
        cost_estimate=cost(2 * s.pairs * s.pao * s.pao * s.aux, 2 * 10**7),
        name="last",
    )(
        here, pair_partner, lens, counts, offsets, over, some_energies,
        gap_rows, aligned, coupling, amplitudes, from_other, from_other_more, some_amps,
    )
    return (new_amps, energies, densities)


def solution(mesh):
    return jax.shard_map(
        local,
        mesh=mesh,
        in_specs=(
            P(AXES, None, None),
            P(),
            P(),
            P(),
            P(AXES, None, None),
            P(),
            P(AXES, None),
            P(AXES, None),
        ),
        out_specs=(P(AXES, None, None), P(AXES), P(AXES, None, None)),
        check_vma=False,
    )
```

```python
import functools

import jax
import jax.numpy as jnp
from jax import lax
from jax.experimental import pallas as pl
from jax.experimental.pallas import tpu as pltpu
from jax.sharding import PartitionSpec as P

AXES = ("orb", "pair")
VMEM_BYTES = 60 * 1024 * 1024
AUX_IDS = 2048
LOW = 64
HIGH = AUX_IDS // LOW
BASE = 32
LANES = 128
FIRST, WHOLE = 18, 32
NN = (((1,), (0,)), ((), ()))
NT = (((1,), (1,)), ((), ()))
TN = (((0,), (0,)), ((), ()))


def dot(a, b, dims=NN):
    return lax.dot_general(a, b, dims, preferred_element_type=jnp.float32)


def one_where(equal, value=1.0):
    return jnp.where(equal, value, 0.0).astype(jnp.bfloat16)


def iota(shape, dim):
    return lax.broadcasted_iota(jnp.int32, shape, dim)


def live(rows, cols, shape):
    return (iota(shape, 0) < rows) & (iota(shape, 1) < cols)


def kept(amp, rows, cols):
    return jnp.where(live(rows, cols, amp.shape), amp.astype(jnp.float32), 0.0).astype(amp.dtype)


def short_where(equal):
    one = jnp.ones(equal.shape, jnp.bfloat16)
    return jnp.where(equal, one, jnp.zeros_like(one))


def column(row):
    return jnp.broadcast_to(row, (LANES, row.shape[1])).T


def same(col, row):
    parts = []
    for at in range(0, row.shape[1], LANES):
        piece = row[:, at : at + LANES]
        wide = jnp.broadcast_to(piece, (col.shape[0], piece.shape[1]))
        parts.append(short_where(col[:, : piece.shape[1]] == wide))
    return jnp.concatenate(parts, axis=1)


def chunks_of(count):
    return (count + LANES - 1) // LANES


def rows_of(length):
    return (length + 15) // 16 * 16


def swapped(me):
    odd = lax.rem(me, 2)
    return me + 1 - 2 * odd, me - 1 + 2 * odd


class Sizes:
    def __init__(self, blocks, amplitudes, pair_partner):
        self.occ = blocks.shape[0]
        self.aux = blocks.shape[1]
        self.pao = blocks.shape[2]
        self.pairs = amplitudes.shape[0]
        self.npair = pair_partner.shape[0]
        self.nocc = self.npair // self.pairs * self.occ
        self.rows = self.occ * self.pao * (self.aux // LANES)
        self.first = self.rows * FIRST // WHOLE // 16 * 16

    def first_orbital(self, pair):
        return pair // self.pairs * self.occ + lax.rem(pair, self.occ)

    def where_partner(self, me, right):
        device = right // self.occ
        sibling, _ = swapped(me)
        kind = jnp.where(device == me, 2, jnp.where(device == sibling, 0, 1))
        return kind * self.occ + lax.rem(right, self.occ), kind


def packing(s):
    whole = s.pao // LANES * LANES
    tail = s.pao - whole
    share = whole // tail
    return whole, tail, share


def slim_kernel(s, amps, out):
    whole, tail, share = packing(s)
    for k in range(s.pairs):
        out[k] = amps[k, :, :whole]
    for g in range(s.pairs // share):
        tails = [amps[g * share + t, :, whole:] for t in range(share)]
        out[s.pairs + g] = jnp.concatenate(tails, axis=1)


def unpack(s, packed, k, out):
    whole, tail, share = packing(s)
    out[:, :whole] = packed[k]
    spot = k % share * tail
    out[:, whole:] = packed[s.pairs + k // share, :, spot : spot + tail]


def bits(values, count, lanes):
    levels = iota((count, lanes), 0).astype(jnp.bfloat16)
    return short_where(levels == jnp.broadcast_to(values.astype(jnp.bfloat16), (count, lanes)))


def places(row, table, k):
    found = dot(table, bits(row // LOW + k * HIGH, table.shape[1], row.shape[1]))
    low = bits(lax.rem(row, LOW), LOW, row.shape[1]).astype(jnp.float32)
    return jnp.sum((found[:LOW] * BASE + found[LOW:]) * low, axis=0, keepdims=True)


def picker(place, chunk):
    wide = 2 * LANES
    middle = chunk * wide + LANES + 1
    spot = (place - jnp.asarray(middle).astype(jnp.float32)).astype(jnp.bfloat16)
    levels = (iota((wide, place.shape[1]), 0) - LANES).astype(jnp.bfloat16)
    return short_where(levels == jnp.broadcast_to(spot, levels.shape))


def chunkwise(s, count, act):
    for c in range(s.aux // (2 * LANES)):
        pl.when(count > c * 2 * LANES)(functools.partial(act, c))


def split_place(place, row):
    part = jnp.where(row < LOW, place // BASE, lax.rem(place, BASE))
    return part.astype(jnp.float32).astype(jnp.bfloat16)


def pack_kernel(
    s, here, partner, lens, aux_rows, blocks, pao_cols, gap_cols, _, to_sibling, to_other, to_other_more, tables, pao_rows, gap_rows, counts, offsets, maps, users, sends, bufs, sems
):
    me = here[0]
    peers = swapped(me)
    pao_rows[...] = pao_cols[...].T
    gap_rows[...] = gap_cols[...].T

    for g, device in enumerate((me,) + peers):
        for k in range(s.occ):
            orbital = jnp.clip(device * s.occ + k, 0, s.nocc - 1)
            row = aux_rows[pl.ds(orbital, 1), :]
            by_high = bits(row // LOW, HIGH, s.aux)
            by_low = bits(lax.rem(row, LOW), LOW, s.aux)
            here_map = dot(jnp.concatenate([by_low, by_low], axis=0), by_high, NT)
            maps[g, :, k * HIGH : (k + 1) * HIGH] = here_map
            users[g * s.occ + k] = jnp.concatenate([here_map] * s.occ, axis=1)
            if g == 0:
                spot = iota((LOW, s.aux), 1) + 1
                parts = jnp.concatenate(
                    [
                        (spot // BASE).astype(jnp.float32).astype(jnp.bfloat16) * by_low,
                        lax.rem(spot, BASE).astype(jnp.float32).astype(jnp.bfloat16) * by_low,
                    ],
                    axis=0,
                )
                tables[2, :, k * HIGH : (k + 1) * HIGH] = dot(parts, by_high, NT).astype(
                    jnp.bfloat16
                )

    wide = s.occ * HIGH
    sub, lane = iota((2 * LOW, 2 * LOW), 0), iota((2 * LOW, 2 * LOW), 1)
    ahead = one_where((lane < LOW) & (lane < lax.rem(sub, LOW)))
    first = one_where(lane < LOW)
    sub, lane = iota((wide, wide), 0), iota((wide, wide), 1)
    above = one_where((sub // HIGH == lane // HIGH) & (sub < lane))
    level = iota((2 * LOW, wide), 0)
    owner = iota((1, wide), 1) // HIGH

    def listing(target, target_device, user, user_device):
        union = jnp.zeros((2 * LOW, wide), jnp.float32)
        for q in range(s.occ):
            uses = jnp.zeros((1, wide), jnp.float32)
            for pair in range(q, s.pairs, s.occ):
                pair += user_device * s.pairs
                inside = (pair >= 0) & (pair < s.npair)
                k = partner[jnp.clip(pair, 0, s.npair - 1)] - target_device * s.occ
                uses += jnp.where((owner == k) & inside, 1.0, 0.0)
            union += uses * users[user * s.occ + q]
        taken = (union > 0.0) & (maps[target] > 0.0)
        flags = one_where(taken)
        total = dot(first, flags)
        place = dot(ahead, flags) + dot(total.astype(jnp.bfloat16), above) + 1.0
        place = jnp.where(taken, place, 0.0).astype(jnp.int32)
        found = [
            jnp.sum(jnp.where(owner == k, total[:1], 0.0)).astype(jnp.int32) for k in range(s.occ)
        ]
        return split_place(place, level), found

    copies = {
        0: [pltpu.make_async_copy(bufs.at[0, pl.ds(0, s.rows)], to_sibling, sems.at[0])],
        1: [
            pltpu.make_async_copy(bufs.at[1, pl.ds(0, s.first)], to_other, sems.at[1]),
            pltpu.make_async_copy(
                bufs.at[1, pl.ds(s.first, s.rows - s.first)], to_other_more, sems.at[2]
            ),
        ],
    }
    for r in (1, 0):
        sends[r], found = listing(0, me, 1 + r, peers[r])
        at = jnp.int32(0)
        for k, count in enumerate(found):
            step = rows_of(lens[me * s.occ + k])

            @pl.when(count > 0)
            def _(k=k, at=at, step=step, count=count):
                place = places(aux_rows[pl.ds(me * s.occ + k, 1), :], sends[r], k)

                def some(c):
                    got = dot(blocks[k], picker(place, c), NT).astype(jnp.bfloat16)
                    spot = pl.multiple_of(at + 2 * c * step, 16)
                    bufs[r, pl.ds(spot, s.pao), :] = got[:, :LANES]

                    @pl.when((2 * c + 1) * LANES < count)
                    def _():
                        bufs[r, pl.ds(pl.multiple_of(spot + step, 16), s.pao), :] = got[:, LANES:]

                chunkwise(s, count, some)

            at += chunks_of(count) * step

        for copy in copies[r]:
            copy.start()

    for r in range(2):
        tables[r], found = listing(1 + r, peers[r], 0, me)
        at = jnp.int32(0)
        for k, count in enumerate(found):
            orbital = jnp.clip(peers[r] * s.occ + k, 0, s.nocc - 1)
            counts[r * s.occ + k] = count
            offsets[r * s.occ + k] = at
            at += chunks_of(count) * rows_of(lens[orbital])
    for k in range(s.occ):
        counts[2 * s.occ + k] = jnp.int32(s.aux)
        offsets[2 * s.occ + k] = jnp.int32(0)

    for copy in copies[1] + copies[0]:
        copy.wait()


def count_kernel(s, partner, lens, aux_rows, over):
    devices = s.nocc // s.occ
    full = s.aux // LANES

    def ids(orbital):
        row = aux_rows[pl.ds(orbital, 1), :]
        return dot(bits(row // LOW, HIGH, s.aux), bits(lax.rem(row, LOW), LOW, s.aux), NT)

    over[0] = jnp.int32(0)

    def edge(e, _):
        source = e + 1
        user = source + 1 - 2 * lax.rem(e, 2)
        reads = [partner[user * s.pairs + q] - source * s.occ for q in range(s.pairs)]
        bound = jnp.int32(0)
        for k in range(s.occ):
            used = functools.reduce(jnp.logical_or, [read == k for read in reads])
            bound += jnp.where(used, full * rows_of(lens[source * s.occ + k]), 0)

        @pl.when(bound > s.first)
        def _():
            domains = [ids(user * s.occ + q) for q in range(s.occ)]
            need = jnp.int32(0)
            for k in range(s.occ):
                union = jnp.zeros((HIGH, LOW), jnp.float32)
                for q, domain in enumerate(domains):
                    used = functools.reduce(
                        jnp.logical_or, [read == k for read in reads[q :: s.occ]]
                    )
                    union += jnp.where(used, 1.0, 0.0) * domain
                taken = (union > 0.0) & (ids(source * s.occ + k) > 0.0)
                count = jnp.sum(jnp.where(taken, 1.0, 0.0)).astype(jnp.int32)
                need += chunks_of(count) * rows_of(lens[source * s.occ + k])
            over[0] = jnp.maximum(over[0], (need > s.first).astype(jnp.int32))

        return 0

    lax.fori_loop(0, devices - 2, edge, 0)


def own_kernel(
    s, here, partner, lens, counts, tables, aux_rows, blocks, amps, _, __, aligned, dens, ___, ____
):
    left = pl.program_id(0)
    me = here[0]
    wide = 2 * LANES
    chunks = s.aux // wide
    row = aux_rows[pl.ds(me * s.occ + left, 1), :]
    term = jnp.zeros((s.pao, s.pao), jnp.float32)
    rest = []

    for t in range(s.pairs // s.occ):
        right = partner[me * s.pairs + t * s.occ + left]
        l, kind = s.where_partner(me, right)
        place = places(row, tables[kind], lax.rem(right, s.occ))

        def some(c, t=t, place=place):
            aligned[t, 0, :, c * wide : (c + 1) * wide] = dot(
                blocks[0], picker(place, c), NT
            ).astype(jnp.bfloat16)

        for c in range(chunks - 1):
            some(c)
        rest.append((counts[l] > (chunks - 1) * wide, functools.partial(some, chunks - 1)))
        masked = kept(amps[t, 0], lens[me * s.occ + left], lens[right])
        term += dot(masked, masked, NT)

    dens[0] = term
    for needed, act in rest:
        pl.when(needed)(act)


def main_kernel(
    s, ncpl, here, partner, listed, lens, coef, counts, offsets, pao_rows, gaps, sibling, own, other, aligned, dens_in, blocks, from_sibling, _, coupling, dens, new_amps, energy, __, wide, tall, dens_own, near_blocks, halo, sums, sems
):
    p = pl.program_id(0)
    me = here[0]
    peers = swapped(me)
    fetches = [
        pltpu.make_async_copy(from_sibling, halo.at[pl.ds(0, s.rows), :], sems.at[0]),
        pltpu.make_async_copy(blocks, near_blocks, sems.at[1]),
        pltpu.make_async_copy(dens_in, dens_own, sems.at[2]),
    ]

    @pl.when(p == 0)
    def _():
        for fetch in fetches:
            fetch.start()
        dens[...] = jnp.zeros_like(dens)
        wide[s.pairs : 2 * s.pairs] = own[...]
        for device, packed in zip(peers, (sibling, other)):
            for k in range(s.pairs):
                unpack(s, packed, k, wide.at[(device - me + 1) * s.pairs + k])

    def row_of(orbital):
        return pao_rows[pl.ds(orbital, 1), :]

    def column_of(orbital):
        row = row_of(orbital)
        return column(jnp.where(row < 0, -2, row)).astype(jnp.int16)

    right_col = column_of(partner[me * s.pairs + p])
    left_col = column_of(me * s.occ + lax.rem(p, s.occ))
    left_rows = []
    for c in range(ncpl):
        m = listed[c, p]
        left_rows.append(row_of(s.first_orbital(m)))
        amp = wide[m - (me - 1) * s.pairs]
        moved = dot(amp, same(right_col, row_of(partner[m]).astype(jnp.int16)), NT)
        tall[c * s.pao : (c + 1) * s.pao] = (coef[c, p] * moved).astype(jnp.bfloat16)
    left_row = jnp.concatenate(left_rows, axis=1).astype(jnp.int16)
    coupling[0] = dot(same(left_col, left_row), tall[...])

    for side in range(3):
        m = (me + side - 1) * s.pairs + p
        inside = (m >= 0) & (m < s.npair)
        m = jnp.clip(m, 0, s.npair - 1)
        near = partner[m] - me * s.occ

        @pl.when(inside & (near >= 0) & (near < s.occ))
        def _():
            amp = wide[side * s.pairs + p]
            masked = kept(amp, lens[s.first_orbital(m)], lens[partner[m]])
            dens[near] += dot(masked, masked, TN)

    @pl.when(p == 0)
    def _():
        for fetch in fetches:
            fetch.wait()

    left, right = me * s.occ + lax.rem(p, s.occ), partner[me * s.pairs + p]
    l, kind = s.where_partner(me, right)

    @pl.when(kind == 2)
    def _():
        sums[...] = dot(aligned[0], near_blocks[lax.rem(right, s.occ)], NT)

    @pl.when(kind == 0)
    def _():
        compacted(s, counts[l], offsets[l], rows_of(lens[right]), aligned.at[0], halo, sums)

    @pl.when(kind != 1)
    def _():
        new_amps[0], energy[p] = update(
            s, lens[left], lens[right], sums[...], own[p], coupling[0], gaps[pl.ds(left, 1), :], gaps[pl.ds(right, 1), :]
        )

    @pl.when(kind == 1)
    def _():
        energy[p] = 0.0

    @pl.when(p == s.pairs - 1)
    def _():
        dens[...] = (dens[...] + dens_own[...]) * (1.0 / s.pao)


def update(s, lens_left, lens_right, exchange, amp, coupling, gap_left, gap_right):
    left = column(gap_left)
    parts = []
    energy = jnp.zeros((s.pao, LANES), jnp.float32)
    for at in range(0, s.pao, LANES):
        lanes = slice(at, min(at + LANES, s.pao))
        part = amp[:, lanes].astype(jnp.float32)
        shape = part.shape
        mask = live(lens_left, lens_right - at, shape)
        denom = left[:, : shape[1]] + gap_right[:, lanes]
        inverse = pl.reciprocal(denom, approx=True)
        inverse = inverse * (2.0 - denom * inverse)
        moved = (exchange[:, lanes] - coupling[:, lanes]) * inverse
        parts.append(jnp.where(mask, 0.5 * (part - moved), 0.0).astype(jnp.bfloat16))
        term = jnp.where(mask, exchange[:, lanes] * part, 0.0)
        if shape[1] < LANES:
            term = jnp.concatenate([term, jnp.zeros((s.pao, LANES - shape[1]), jnp.float32)], axis=1)
        energy += term
    return jnp.concatenate(parts, axis=1), jnp.sum(energy) / s.pao


def compacted(s, count, at, step, aligned, halo, sums):
    wide = 2 * LANES

    def some(c):
        spot = pl.multiple_of(at + 2 * c * step, 16)
        one = halo[pl.ds(spot, s.pao), :]
        two = halo[pl.ds(pl.multiple_of(spot + step, 16), s.pao), :]
        two = jnp.where((2 * c + 1) * LANES < count, two, jnp.zeros_like(two))
        both = jnp.concatenate([one, two], axis=1)
        term = dot(aligned[:, c * wide : (c + 1) * wide], both, NT)
        if c == 0:
            sums[...] = term
        else:
            sums[...] += term

    @pl.when(count == 0)
    def _():
        sums[...] = jnp.zeros_like(sums)

    chunkwise(s, count, some)


def last_kernel(
    s, here, partner, lens, counts, offsets, over, energy_in, gaps, aligned, coupling, amps, other, more, _, new_amps, energy, halo, held, terms, olds, news, sums, sems
):
    me = here[0]

    def copies(p):
        return [
            pltpu.make_async_copy(aligned.at[p], held.at[p], sems.at[0, p]),
            pltpu.make_async_copy(coupling.at[p], terms.at[p], sems.at[1, p]),
            pltpu.make_async_copy(amps.at[p], olds.at[p], sems.at[2, p]),
        ]

    def result(p):
        return pltpu.make_async_copy(news.at[p], new_amps.at[p], sems.at[3, p])

    def each(act):
        def one(p, _):
            right = partner[me * s.pairs + p]
            l, kind = s.where_partner(me, right)

            @pl.when(kind == 1)
            def _():
                act(p, right, l)

            return 0

        lax.fori_loop(0, s.pairs, one, 0)

    first = pltpu.make_async_copy(other, halo.at[pl.ds(0, s.first)], sems.at[4, 0])
    rest = pltpu.make_async_copy(more, halo.at[pl.ds(s.first, s.rows - s.first)], sems.at[4, 1])
    first.start()

    @pl.when(over[0] > 0)
    def _():
        rest.start()
        rest.wait()

    def begin(p, right, l):
        for copy in copies(p):
            copy.start()

    def finish(p, right, l):
        left = me * s.occ + lax.rem(p, s.occ)
        for copy in copies(p):
            copy.wait()
        compacted(s, counts[l], offsets[l], rows_of(lens[right]), held.at[p], halo, sums)
        news[p], energy[p] = update(
            s, lens[left], lens[right], sums[...], olds[p], terms[p], gaps[pl.ds(left, 1), :], gaps[pl.ds(right, 1), :]
        )
        result(p).start()

    for p in range(s.pairs):
        energy[p] = energy_in[p]
    each(begin)
    first.wait()
    each(finish)
    each(lambda p, right, l: result(p).wait())


def position():
    return lax.axis_index(AXES)


def swap(array, role):
    count = 1
    for axis in AXES:
        count *= lax.axis_size(axis)
    route = []
    for low in range(role, count - 1, 2):
        route += [(low, low + 1), (low + 1, low)]
    return lax.ppermute(array, AXES, route)


def local(
    blocks, aux_domain, pao_domain, pao_gap, amplitudes, pair_partner, coupling_list, coupling_coef
):
    s = Sizes(blocks, amplitudes, pair_partner)
    ncpl = coupling_list.shape[1]
    me = position()
    here = me.astype(jnp.int32).reshape(1)
    blocks_t = jnp.swapaxes(blocks, 1, 2)

    smem = pl.BlockSpec(memory_space=pltpu.SMEM)
    vmem = pl.BlockSpec(memory_space=pltpu.VMEM)
    anywhere = pl.BlockSpec(memory_space=pltpu.HBM)
    plain = pltpu.CompilerParams(vmem_limit_bytes=VMEM_BYTES)
    stepped = pltpu.CompilerParams(
        dimension_semantics=("arbitrary",), vmem_limit_bytes=VMEM_BYTES
    )
    square = pl.BlockSpec((1, s.pao, s.pao), lambda p, *_: (p, 0, 0))
    all_dens = pl.BlockSpec((s.occ, s.pao, s.pao), lambda p, *_: (0, 0, 0))
    squares = jax.ShapeDtypeStruct((s.pairs, s.pao, s.pao), jnp.float32)
    dens_shape = jax.ShapeDtypeStruct((s.occ, s.pao, s.pao), jnp.float32)

    def cost(work, data):
        return pl.CostEstimate(flops=work, bytes_accessed=data, transcendentals=0)

    whole, tail, share = packing(s)
    slim = pl.pallas_call(
        functools.partial(slim_kernel, s),
        in_specs=[vmem],
        out_specs=vmem,
        out_shape=jax.ShapeDtypeStruct((s.pairs + s.pairs // share, s.pao, whole), jnp.bfloat16),
        compiler_params=plain,
        cost_estimate=cost(10**6, 4 * 10**6),
        name="slim",
    )(amplitudes)
    amps_other = swap(slim, 1)
    amps_sibling = swap(slim, 0)

    lens = jnp.sum((pao_domain >= 0).astype(jnp.int32), axis=1)

    lists = 3 * s.occ
    to_sibling, to_other, to_other_more, tables, pao_rows, gap_rows, counts, offsets = pl.pallas_call(
        functools.partial(pack_kernel, s),
        in_specs=[smem] * 3 + [vmem] * 4 + [anywhere],
        out_specs=[anywhere] * 3 + [vmem] * 3 + [smem] * 2,
        out_shape=[
            jax.ShapeDtypeStruct((s.rows, LANES), jnp.bfloat16),
            jax.ShapeDtypeStruct((s.first, LANES), jnp.bfloat16),
            jax.ShapeDtypeStruct((s.rows - s.first, LANES), jnp.bfloat16),
            jax.ShapeDtypeStruct((3, 2 * LOW, s.occ * HIGH), jnp.bfloat16),
            jax.ShapeDtypeStruct(pao_domain.shape, pao_domain.dtype),
            jax.ShapeDtypeStruct(pao_gap.shape, pao_gap.dtype),
            jax.ShapeDtypeStruct((lists,), jnp.int32),
            jax.ShapeDtypeStruct((lists,), jnp.int32),
        ],
        scratch_shapes=[
            pltpu.VMEM((3, 2 * LOW, s.occ * HIGH), jnp.float32),
            pltpu.VMEM((3 * s.occ, 2 * LOW, s.occ * HIGH), jnp.float32),
            pltpu.VMEM((2, 2 * LOW, s.occ * HIGH), jnp.bfloat16),
            pltpu.VMEM((2, s.rows + s.pao, LANES), jnp.bfloat16),
            pltpu.SemaphoreType.DMA((3,)),
        ],
        compiler_params=plain,
        cost_estimate=cost(10**11, 10**5),
        name="pack",
    )(here, pair_partner, lens, aux_domain, blocks_t, pao_domain.T, pao_gap.T, slim)

    (over,) = pl.pallas_call(
        functools.partial(count_kernel, s),
        in_specs=[smem] * 2 + [vmem],
        out_specs=[smem],
        out_shape=[jax.ShapeDtypeStruct((1,), jnp.int32)],
        compiler_params=plain,
        cost_estimate=cost(10**11, 10**5),
        name="count",
    )(pair_partner, lens, aux_domain)

    repeats = s.pairs // s.occ
    both = pl.BlockSpec((repeats, 1, s.pao, s.aux), lambda g: (0, g, 0, 0))
    aligned, dens, to_other, to_sibling = pl.pallas_call(
        functools.partial(own_kernel, s),
        grid=(s.occ,),
        in_specs=[smem] * 4
        + [
            vmem,
            vmem,
            pl.BlockSpec((1, s.pao, s.aux), lambda g: (g, 0, 0)),
            pl.BlockSpec((repeats, 1, s.pao, s.pao), lambda g: (0, g, 0, 0)),
            anywhere,
            anywhere,
        ],
        out_specs=[both, pl.BlockSpec((1, s.pao, s.pao), lambda g: (g, 0, 0)), anywhere, anywhere],
        out_shape=[
            jax.ShapeDtypeStruct((repeats, s.occ, s.pao, s.aux), jnp.bfloat16),
            dens_shape,
            jax.ShapeDtypeStruct(to_other.shape, to_other.dtype),
            jax.ShapeDtypeStruct(to_sibling.shape, to_sibling.dtype),
        ],
        input_output_aliases={8: 2, 9: 3},
        compiler_params=stepped,
        cost_estimate=cost(10**11, 10**5),
        name="own",
    )(
        here, pair_partner, lens, counts, tables, aux_domain, blocks_t,
        amplitudes.reshape(repeats, s.occ, s.pao, s.pao), to_other, to_sibling,
    )
    from_other = swap(to_other, 1)
    from_sibling = swap(to_sibling, 0)
    aligned = aligned.reshape(s.pairs, s.pao, s.aux)

    coupling, densities, some_amps, some_energies, to_other_more = pl.pallas_call(
        functools.partial(main_kernel, s, ncpl),
        grid=(s.pairs,),
        in_specs=[smem] * 7
        + [vmem] * 5
        + [pl.BlockSpec((1, s.pao, s.aux), lambda p: (p, 0, 0))]
        + [anywhere] * 4,
        out_specs=[square, all_dens, square, smem, anywhere],
        out_shape=[
            squares,
            dens_shape,
            jax.ShapeDtypeStruct(amplitudes.shape, amplitudes.dtype),
            jax.ShapeDtypeStruct((s.pairs,), jnp.float32),
            jax.ShapeDtypeStruct(to_other_more.shape, to_other_more.dtype),
        ],
        input_output_aliases={16: 4},
        scratch_shapes=[
            pltpu.VMEM((3 * s.pairs, s.pao, s.pao), jnp.bfloat16),
            pltpu.VMEM((ncpl * s.pao, s.pao), jnp.bfloat16),
            pltpu.VMEM((s.occ, s.pao, s.pao), jnp.float32),
            pltpu.VMEM((s.occ, s.pao, s.aux), jnp.bfloat16),
            pltpu.VMEM((s.rows + s.pao, LANES), jnp.bfloat16),
            pltpu.VMEM((s.pao, s.pao), jnp.float32),
            pltpu.SemaphoreType.DMA((3,)),
        ],
        compiler_params=stepped,
        cost_estimate=cost(10**11, 10**5),
        name="main",
    )(
        here, pair_partner, coupling_list.T, lens, coupling_coef.T, counts, offsets,
        pao_rows, gap_rows, amps_sibling, amplitudes, amps_other, aligned, dens, blocks_t, from_sibling,
        to_other_more,
    )

    from_other_more = lax.cond(over[0] > 0, lambda a: swap(a, 1), lambda a: a, to_other_more)
    new_amps, energies = pl.pallas_call(
        functools.partial(last_kernel, s),
        in_specs=[smem] * 7 + [vmem] + [anywhere] * 6,
        out_specs=[anywhere, smem],
        out_shape=[
            jax.ShapeDtypeStruct(amplitudes.shape, amplitudes.dtype),
            jax.ShapeDtypeStruct((s.pairs,), jnp.float32),
        ],
        scratch_shapes=[
            pltpu.VMEM((s.rows + s.pao, LANES), jnp.bfloat16),
            pltpu.VMEM((s.pairs, s.pao, s.aux), jnp.bfloat16),
            pltpu.VMEM((s.pairs, s.pao, s.pao), jnp.float32),
            pltpu.VMEM((s.pairs, s.pao, s.pao), jnp.bfloat16),
            pltpu.VMEM((s.pairs, s.pao, s.pao), jnp.bfloat16),
            pltpu.VMEM((s.pao, s.pao), jnp.float32),
            pltpu.SemaphoreType.DMA((5, s.pairs)),
        ],
        input_output_aliases={13: 0},
        compiler_params=plain,
        cost_estimate=cost(2 * s.pairs * s.pao * s.pao * s.aux, 2 * 10**7),
        name="last",
    )(
        here, pair_partner, lens, counts, offsets, over, some_energies,
        gap_rows, aligned, coupling, amplitudes, from_other, from_other_more, some_amps,
    )
    return (new_amps, energies, densities)


def solution(mesh):
    return jax.shard_map(
        local,
        mesh=mesh,
        in_specs=(
            P(AXES, None, None),
            P(),
            P(),
            P(),
            P(AXES, None, None),
            P(),
            P(AXES, None),
            P(AXES, None),
        ),
        out_specs=(P(AXES, None, None), P(AXES), P(AXES, None, None)),
        check_vma=False,
    )
```

```python
import functools

import jax
import jax.numpy as jnp
from jax import lax
from jax.experimental import pallas as pl
from jax.experimental.pallas import tpu as pltpu
from jax.sharding import PartitionSpec as P

AXES = ("orb", "pair")
VMEM_BYTES = 60 * 1024 * 1024
AUX_IDS = 2048
LOW = 64
HIGH = AUX_IDS // LOW
BASE = 32
LANES = 128
FIRST, WHOLE = 18, 32
NN = (((1,), (0,)), ((), ()))
NT = (((1,), (1,)), ((), ()))
TN = (((0,), (0,)), ((), ()))


def dot(a, b, dims=NN):
    return lax.dot_general(a, b, dims, preferred_element_type=jnp.float32)


def one_where(equal, value=1.0):
    return jnp.where(equal, value, 0.0).astype(jnp.bfloat16)


def iota(shape, dim):
    return lax.broadcasted_iota(jnp.int32, shape, dim)


def live(rows, cols, shape):
    return (iota(shape, 0) < rows) & (iota(shape, 1) < cols)


def kept(amp, rows, cols):
    return jnp.where(live(rows, cols, amp.shape), amp.astype(jnp.float32), 0.0).astype(amp.dtype)


def short_where(equal):
    one = jnp.ones(equal.shape, jnp.bfloat16)
    return jnp.where(equal, one, jnp.zeros_like(one))


def column(row):
    return jnp.broadcast_to(row, (LANES, row.shape[1])).T


def same(col, row):
    parts = []
    for at in range(0, row.shape[1], LANES):
        piece = row[:, at : at + LANES]
        wide = jnp.broadcast_to(piece, (col.shape[0], piece.shape[1]))
        parts.append(short_where(col[:, : piece.shape[1]] == wide))
    return jnp.concatenate(parts, axis=1)


def chunks_of(count):
    return (count + LANES - 1) // LANES


def rows_of(length):
    return (length + 15) // 16 * 16


def swapped(me):
    odd = lax.rem(me, 2)
    return me + 1 - 2 * odd, me - 1 + 2 * odd


class Sizes:
    def __init__(self, blocks, amplitudes, pair_partner):
        self.occ = blocks.shape[0]
        self.aux = blocks.shape[1]
        self.pao = blocks.shape[2]
        self.pairs = amplitudes.shape[0]
        self.npair = pair_partner.shape[0]
        self.nocc = self.npair // self.pairs * self.occ
        self.rows = self.occ * self.pao * (self.aux // LANES)
        self.first = self.rows * FIRST // WHOLE // 16 * 16

    def first_orbital(self, pair):
        return pair // self.pairs * self.occ + lax.rem(pair, self.occ)

    def where_partner(self, me, right):
        device = right // self.occ
        sibling, _ = swapped(me)
        kind = jnp.where(device == me, 2, jnp.where(device == sibling, 0, 1))
        return kind * self.occ + lax.rem(right, self.occ), kind


def packing(s):
    whole = s.pao // LANES * LANES
    tail = s.pao - whole
    share = whole // tail
    return whole, tail, share


def slim_kernel(s, amps, out):
    whole, tail, share = packing(s)
    for k in range(s.pairs):
        out[k] = amps[k, :, :whole]
    for g in range(s.pairs // share):
        tails = [amps[g * share + t, :, whole:] for t in range(share)]
        out[s.pairs + g] = jnp.concatenate(tails, axis=1)


def unpack(s, packed, k, out):
    whole, tail, share = packing(s)
    out[:, :whole] = packed[k]
    spot = k % share * tail
    out[:, whole:] = packed[s.pairs + k // share, :, spot : spot + tail]


def bits(values, count, lanes):
    levels = iota((count, lanes), 0).astype(jnp.bfloat16)
    return short_where(levels == jnp.broadcast_to(values.astype(jnp.bfloat16), (count, lanes)))


def places(row, table, k):
    found = dot(table, bits(row // LOW + k * HIGH, table.shape[1], row.shape[1]))
    low = bits(lax.rem(row, LOW), LOW, row.shape[1]).astype(jnp.float32)
    return jnp.sum((found[:LOW] * BASE + found[LOW:]) * low, axis=0, keepdims=True)


def picker(place, chunk):
    wide = 2 * LANES
    middle = chunk * wide + LANES + 1
    spot = (place - jnp.asarray(middle).astype(jnp.float32)).astype(jnp.bfloat16)
    levels = (iota((wide, place.shape[1]), 0) - LANES).astype(jnp.bfloat16)
    return short_where(levels == jnp.broadcast_to(spot, levels.shape))


def chunkwise(s, count, act):
    for c in range(s.aux // (2 * LANES)):
        pl.when(count > c * 2 * LANES)(functools.partial(act, c))


def split_place(place, row):
    part = jnp.where(row < LOW, place // BASE, lax.rem(place, BASE))
    return part.astype(jnp.float32).astype(jnp.bfloat16)


def pack_kernel(
    s, here, partner, lens, aux_rows, blocks, pao_cols, gap_cols, _, to_sibling, to_other, to_other_more, tables, pao_rows, gap_rows, counts, offsets, maps, users, sends, bufs, sems
):
    me = here[0]
    peers = swapped(me)
    pao_rows[...] = pao_cols[...].T
    gap_rows[...] = gap_cols[...].T

    for g, device in enumerate((me,) + peers):
        for k in range(s.occ):
            orbital = jnp.clip(device * s.occ + k, 0, s.nocc - 1)
            row = aux_rows[pl.ds(orbital, 1), :]
            by_high = bits(row // LOW, HIGH, s.aux)
            by_low = bits(lax.rem(row, LOW), LOW, s.aux)
            here_map = dot(jnp.concatenate([by_low, by_low], axis=0), by_high, NT)
            maps[g, :, k * HIGH : (k + 1) * HIGH] = here_map
            users[g * s.occ + k] = jnp.concatenate([here_map] * s.occ, axis=1)
            if g == 0:
                spot = iota((LOW, s.aux), 1) + 1
                parts = jnp.concatenate(
                    [
                        (spot // BASE).astype(jnp.float32).astype(jnp.bfloat16) * by_low,
                        lax.rem(spot, BASE).astype(jnp.float32).astype(jnp.bfloat16) * by_low,
                    ],
                    axis=0,
                )
                tables[2, :, k * HIGH : (k + 1) * HIGH] = dot(parts, by_high, NT).astype(
                    jnp.bfloat16
                )

    wide = s.occ * HIGH
    sub, lane = iota((2 * LOW, 2 * LOW), 0), iota((2 * LOW, 2 * LOW), 1)
    ahead = one_where((lane < LOW) & (lane < lax.rem(sub, LOW)))
    first = one_where(lane < LOW)
    sub, lane = iota((wide, wide), 0), iota((wide, wide), 1)
    above = one_where((sub // HIGH == lane // HIGH) & (sub < lane))
    level = iota((2 * LOW, wide), 0)
    owner = iota((1, wide), 1) // HIGH

    def listing(target, target_device, user, user_device):
        union = jnp.zeros((2 * LOW, wide), jnp.float32)
        for q in range(s.occ):
            uses = jnp.zeros((1, wide), jnp.float32)
            for pair in range(q, s.pairs, s.occ):
                pair += user_device * s.pairs
                inside = (pair >= 0) & (pair < s.npair)
                k = partner[jnp.clip(pair, 0, s.npair - 1)] - target_device * s.occ
                uses += jnp.where((owner == k) & inside, 1.0, 0.0)
            union += uses * users[user * s.occ + q]
        taken = (union > 0.0) & (maps[target] > 0.0)
        flags = one_where(taken)
        total = dot(first, flags)
        place = dot(ahead, flags) + dot(total.astype(jnp.bfloat16), above) + 1.0
        place = jnp.where(taken, place, 0.0).astype(jnp.int32)
        found = [
            jnp.sum(jnp.where(owner == k, total[:1], 0.0)).astype(jnp.int32) for k in range(s.occ)
        ]
        return split_place(place, level), found

    copies = {
        0: [pltpu.make_async_copy(bufs.at[0, pl.ds(0, s.rows)], to_sibling, sems.at[0])],
        1: [
            pltpu.make_async_copy(bufs.at[1, pl.ds(0, s.first)], to_other, sems.at[1]),
            pltpu.make_async_copy(
                bufs.at[1, pl.ds(s.first, s.rows - s.first)], to_other_more, sems.at[2]
            ),
        ],
    }
    for r in (1, 0):
        sends[r], found = listing(0, me, 1 + r, peers[r])
        at = jnp.int32(0)
        for k, count in enumerate(found):
            step = rows_of(lens[me * s.occ + k])

            @pl.when(count > 0)
            def _(k=k, at=at, step=step, count=count):
                place = places(aux_rows[pl.ds(me * s.occ + k, 1), :], sends[r], k)

                def some(c):
                    got = dot(blocks[k], picker(place, c), NT).astype(jnp.bfloat16)
                    spot = pl.multiple_of(at + 2 * c * step, 16)
                    bufs[r, pl.ds(spot, s.pao), :] = got[:, :LANES]

                    @pl.when((2 * c + 1) * LANES < count)
                    def _():
                        bufs[r, pl.ds(pl.multiple_of(spot + step, 16), s.pao), :] = got[:, LANES:]

                chunkwise(s, count, some)

            at += chunks_of(count) * step

        for copy in copies[r]:
            copy.start()

    for r in range(2):
        tables[r], found = listing(1 + r, peers[r], 0, me)
        at = jnp.int32(0)
        for k, count in enumerate(found):
            orbital = jnp.clip(peers[r] * s.occ + k, 0, s.nocc - 1)
            counts[r * s.occ + k] = count
            offsets[r * s.occ + k] = at
            at += chunks_of(count) * rows_of(lens[orbital])
    for k in range(s.occ):
        counts[2 * s.occ + k] = jnp.int32(s.aux)
        offsets[2 * s.occ + k] = jnp.int32(0)

    for copy in copies[1] + copies[0]:
        copy.wait()


def count_kernel(s, partner, lens, aux_rows, _, over, __):
    devices = s.nocc // s.occ
    full = s.aux // LANES

    def ids(orbital):
        row = aux_rows[pl.ds(orbital, 1), :]
        return dot(bits(row // LOW, HIGH, s.aux), bits(lax.rem(row, LOW), LOW, s.aux), NT)

    over[0] = jnp.int32(0)

    def edge(e, _):
        source = e + 1
        user = source + 1 - 2 * lax.rem(e, 2)
        reads = [partner[user * s.pairs + q] - source * s.occ for q in range(s.pairs)]
        bound = jnp.int32(0)
        for k in range(s.occ):
            used = functools.reduce(jnp.logical_or, [read == k for read in reads])
            bound += jnp.where(used, full * rows_of(lens[source * s.occ + k]), 0)

        @pl.when(bound > s.first)
        def _():
            domains = [ids(user * s.occ + q) for q in range(s.occ)]
            need = jnp.int32(0)
            for k in range(s.occ):
                union = jnp.zeros((HIGH, LOW), jnp.float32)
                for q, domain in enumerate(domains):
                    used = functools.reduce(
                        jnp.logical_or, [read == k for read in reads[q :: s.occ]]
                    )
                    union += jnp.where(used, 1.0, 0.0) * domain
                taken = (union > 0.0) & (ids(source * s.occ + k) > 0.0)
                count = jnp.sum(jnp.where(taken, 1.0, 0.0)).astype(jnp.int32)
                need += chunks_of(count) * rows_of(lens[source * s.occ + k])
            over[0] = jnp.maximum(over[0], (need > s.first).astype(jnp.int32))

        return 0

    lax.fori_loop(0, devices - 2, edge, 0)


def own_kernel(
    s, here, partner, lens, counts, tables, aux_rows, blocks, amps, _, __, aligned, dens, ___, ____
):
    left = pl.program_id(0)
    me = here[0]
    wide = 2 * LANES
    chunks = s.aux // wide
    row = aux_rows[pl.ds(me * s.occ + left, 1), :]
    term = jnp.zeros((s.pao, s.pao), jnp.float32)
    rest = []

    for t in range(s.pairs // s.occ):
        right = partner[me * s.pairs + t * s.occ + left]
        l, kind = s.where_partner(me, right)
        place = places(row, tables[kind], lax.rem(right, s.occ))

        def some(c, t=t, place=place):
            aligned[t, 0, :, c * wide : (c + 1) * wide] = dot(
                blocks[0], picker(place, c), NT
            ).astype(jnp.bfloat16)

        for c in range(chunks - 1):
            some(c)
        rest.append((counts[l] > (chunks - 1) * wide, functools.partial(some, chunks - 1)))
        masked = kept(amps[t, 0], lens[me * s.occ + left], lens[right])
        term += dot(masked, masked, NT)

    dens[0] = term
    for needed, act in rest:
        pl.when(needed)(act)


def main_kernel(
    s, ncpl, here, partner, listed, lens, coef, counts, offsets, pao_rows, gaps, sibling, own, other, aligned, dens_in, blocks, from_sibling, _, coupling, dens, new_amps, energy, __, wide, tall, dens_own, near_blocks, halo, sums, sems
):
    p = pl.program_id(0)
    me = here[0]
    peers = swapped(me)
    fetches = [
        pltpu.make_async_copy(from_sibling, halo.at[pl.ds(0, s.rows), :], sems.at[0]),
        pltpu.make_async_copy(blocks, near_blocks, sems.at[1]),
        pltpu.make_async_copy(dens_in, dens_own, sems.at[2]),
    ]

    @pl.when(p == 0)
    def _():
        for fetch in fetches:
            fetch.start()
        dens[...] = jnp.zeros_like(dens)
        wide[s.pairs : 2 * s.pairs] = own[...]
        for device, packed in zip(peers, (sibling, other)):
            for k in range(s.pairs):
                unpack(s, packed, k, wide.at[(device - me + 1) * s.pairs + k])

    def row_of(orbital):
        return pao_rows[pl.ds(orbital, 1), :]

    def column_of(orbital):
        row = row_of(orbital)
        return column(jnp.where(row < 0, -2, row)).astype(jnp.int16)

    right_col = column_of(partner[me * s.pairs + p])
    left_col = column_of(me * s.occ + lax.rem(p, s.occ))
    left_rows = []
    for c in range(ncpl):
        m = listed[c, p]
        left_rows.append(row_of(s.first_orbital(m)))
        amp = wide[m - (me - 1) * s.pairs]
        moved = dot(amp, same(right_col, row_of(partner[m]).astype(jnp.int16)), NT)
        tall[c * s.pao : (c + 1) * s.pao] = (coef[c, p] * moved).astype(jnp.bfloat16)
    left_row = jnp.concatenate(left_rows, axis=1).astype(jnp.int16)
    coupling[0] = dot(same(left_col, left_row), tall[...])

    for side in range(3):
        m = (me + side - 1) * s.pairs + p
        inside = (m >= 0) & (m < s.npair)
        m = jnp.clip(m, 0, s.npair - 1)
        near = partner[m] - me * s.occ

        @pl.when(inside & (near >= 0) & (near < s.occ))
        def _():
            amp = wide[side * s.pairs + p]
            masked = kept(amp, lens[s.first_orbital(m)], lens[partner[m]])
            dens[near] += dot(masked, masked, TN)

    @pl.when(p == 0)
    def _():
        for fetch in fetches:
            fetch.wait()

    left, right = me * s.occ + lax.rem(p, s.occ), partner[me * s.pairs + p]
    l, kind = s.where_partner(me, right)

    @pl.when(kind == 2)
    def _():
        sums[...] = dot(aligned[0], near_blocks[lax.rem(right, s.occ)], NT)

    @pl.when(kind == 0)
    def _():
        compacted(s, counts[l], offsets[l], rows_of(lens[right]), aligned.at[0], halo, sums)

    @pl.when(kind != 1)
    def _():
        new_amps[0], energy[p] = update(
            s, lens[left], lens[right], sums[...], own[p], coupling[0], gaps[pl.ds(left, 1), :], gaps[pl.ds(right, 1), :]
        )

    @pl.when(kind == 1)
    def _():
        energy[p] = 0.0

    @pl.when(p == s.pairs - 1)
    def _():
        dens[...] = (dens[...] + dens_own[...]) * (1.0 / s.pao)


def update(s, lens_left, lens_right, exchange, amp, coupling, gap_left, gap_right):
    left = column(gap_left)
    parts = []
    energy = jnp.zeros((s.pao, LANES), jnp.float32)
    for at in range(0, s.pao, LANES):
        lanes = slice(at, min(at + LANES, s.pao))
        part = amp[:, lanes].astype(jnp.float32)
        shape = part.shape
        mask = live(lens_left, lens_right - at, shape)
        denom = left[:, : shape[1]] + gap_right[:, lanes]
        inverse = pl.reciprocal(denom, approx=True)
        inverse = inverse * (2.0 - denom * inverse)
        moved = (exchange[:, lanes] - coupling[:, lanes]) * inverse
        parts.append(jnp.where(mask, 0.5 * (part - moved), 0.0).astype(jnp.bfloat16))
        term = jnp.where(mask, exchange[:, lanes] * part, 0.0)
        if shape[1] < LANES:
            term = jnp.concatenate([term, jnp.zeros((s.pao, LANES - shape[1]), jnp.float32)], axis=1)
        energy += term
    return jnp.concatenate(parts, axis=1), jnp.sum(energy) / s.pao


def compacted(s, count, at, step, aligned, halo, sums):
    chunks = s.aux // LANES
    usual = chunks - 2

    def some(low, high):
        parts = []
        for c in range(low, high):
            spot = pl.multiple_of(jnp.minimum(at + c * step, s.rows), 16)
            part = halo[pl.ds(spot, s.pao), :]
            parts.append(jnp.where(c * LANES < count, part, jnp.zeros_like(part)))
        both = jnp.concatenate(parts, axis=1)
        return dot(aligned[:, low * LANES : high * LANES], both, NT)

    sums[...] = some(0, usual)

    @pl.when(count > usual * LANES)
    def _():
        sums[...] += some(usual, chunks)


def last_kernel(
    s, here, partner, lens, counts, offsets, over, energy_in, gaps, aligned, coupling, amps, other, more, _, new_amps, energy, halo, held, terms, olds, news, sums, far, sems
):
    me = here[0]

    def copies(p):
        return [
            pltpu.make_async_copy(aligned.at[p], held.at[p], sems.at[0, p]),
            pltpu.make_async_copy(coupling.at[p], terms.at[p], sems.at[1, p]),
            pltpu.make_async_copy(amps.at[p], olds.at[p], sems.at[2, p]),
        ]

    def result(p):
        return pltpu.make_async_copy(news.at[p], new_amps.at[p], sems.at[3, p])

    number = jnp.int32(0)
    for p in range(s.pairs):
        energy[p] = energy_in[p]
        far[number] = p
        kind = s.where_partner(me, partner[me * s.pairs + p])[1]
        number += (kind == 1).astype(jnp.int32)

    def each(act):
        def one(n, _):
            p = far[n]
            right = partner[me * s.pairs + p]
            act(p, right, s.occ + lax.rem(right, s.occ))
            return 0

        lax.fori_loop(0, number, one, 0)

    first = pltpu.make_async_copy(other, halo.at[pl.ds(0, s.first)], sems.at[4, 0])
    rest = pltpu.make_async_copy(more, halo.at[pl.ds(s.first, s.rows - s.first)], sems.at[4, 1])
    first.start()

    @pl.when(over[0] > 0)
    def _():
        rest.start()
        rest.wait()

    def begin(p, right, l):
        for copy in copies(p):
            copy.start()

    def finish(p, right, l):
        left = me * s.occ + lax.rem(p, s.occ)
        for copy in copies(p):
            copy.wait()
        compacted(s, counts[l], offsets[l], rows_of(lens[right]), held.at[p], halo, sums)
        news[p], energy[p] = update(
            s, lens[left], lens[right], sums[...], olds[p], terms[p], gaps[pl.ds(left, 1), :], gaps[pl.ds(right, 1), :]
        )
        result(p).start()

    each(begin)
    first.wait()
    each(finish)
    each(lambda p, right, l: result(p).wait())


def position():
    return lax.axis_index(AXES)


def swap(array, role):
    count = 1
    for axis in AXES:
        count *= lax.axis_size(axis)
    route = []
    for low in range(role, count - 1, 2):
        route += [(low, low + 1), (low + 1, low)]
    return lax.ppermute(array, AXES, route)


def local(
    blocks, aux_domain, pao_domain, pao_gap, amplitudes, pair_partner, coupling_list, coupling_coef
):
    s = Sizes(blocks, amplitudes, pair_partner)
    ncpl = coupling_list.shape[1]
    me = position()
    here = me.astype(jnp.int32).reshape(1)
    blocks_t = jnp.swapaxes(blocks, 1, 2)

    smem = pl.BlockSpec(memory_space=pltpu.SMEM)
    vmem = pl.BlockSpec(memory_space=pltpu.VMEM)
    anywhere = pl.BlockSpec(memory_space=pltpu.HBM)
    plain = pltpu.CompilerParams(vmem_limit_bytes=VMEM_BYTES)
    stepped = pltpu.CompilerParams(
        dimension_semantics=("arbitrary",), vmem_limit_bytes=VMEM_BYTES
    )
    square = pl.BlockSpec((1, s.pao, s.pao), lambda p, *_: (p, 0, 0))
    all_dens = pl.BlockSpec((s.occ, s.pao, s.pao), lambda p, *_: (0, 0, 0))
    squares = jax.ShapeDtypeStruct((s.pairs, s.pao, s.pao), jnp.float32)
    dens_shape = jax.ShapeDtypeStruct((s.occ, s.pao, s.pao), jnp.float32)

    def cost(work, data):
        return pl.CostEstimate(flops=work, bytes_accessed=data, transcendentals=0)

    whole, tail, share = packing(s)
    slots = s.pairs + s.pairs // share
    slim = pl.pallas_call(
        functools.partial(slim_kernel, s),
        in_specs=[vmem],
        out_specs=vmem,
        out_shape=jax.ShapeDtypeStruct((slots, s.pao, whole), jnp.bfloat16),
        compiler_params=plain,
        cost_estimate=cost(10**6, 4 * 10**6),
        name="slim",
    )(amplitudes)
    amps_other = swap(slim, 1)
    amps_sibling = swap(slim, 0)

    lens = jnp.sum((pao_domain >= 0).astype(jnp.int32), axis=1)

    lists = 3 * s.occ
    to_sibling, to_other, to_other_more, tables, pao_rows, gap_rows, counts, offsets = pl.pallas_call(
        functools.partial(pack_kernel, s),
        in_specs=[smem] * 3 + [vmem] * 4 + [anywhere],
        out_specs=[anywhere] * 3 + [vmem] * 3 + [smem] * 2,
        out_shape=[
            jax.ShapeDtypeStruct((s.rows, LANES), jnp.bfloat16),
            jax.ShapeDtypeStruct((s.first, LANES), jnp.bfloat16),
            jax.ShapeDtypeStruct((s.rows - s.first, LANES), jnp.bfloat16),
            jax.ShapeDtypeStruct((3, 2 * LOW, s.occ * HIGH), jnp.bfloat16),
            jax.ShapeDtypeStruct(pao_domain.shape, pao_domain.dtype),
            jax.ShapeDtypeStruct(pao_gap.shape, pao_gap.dtype),
            jax.ShapeDtypeStruct((lists,), jnp.int32),
            jax.ShapeDtypeStruct((lists,), jnp.int32),
        ],
        scratch_shapes=[
            pltpu.VMEM((3, 2 * LOW, s.occ * HIGH), jnp.float32),
            pltpu.VMEM((3 * s.occ, 2 * LOW, s.occ * HIGH), jnp.float32),
            pltpu.VMEM((2, 2 * LOW, s.occ * HIGH), jnp.bfloat16),
            pltpu.VMEM((2, s.rows + s.pao, LANES), jnp.bfloat16),
            pltpu.SemaphoreType.DMA((3,)),
        ],
        compiler_params=plain,
        cost_estimate=cost(10**11, 10**5),
        name="pack",
    )(here, pair_partner, lens, aux_domain, blocks_t, pao_domain.T, pao_gap.T, slim)

    repeats = s.pairs // s.occ
    both = pl.BlockSpec((repeats, 1, s.pao, s.aux), lambda g: (0, g, 0, 0))
    aligned, dens, to_other, to_sibling = pl.pallas_call(
        functools.partial(own_kernel, s),
        grid=(s.occ,),
        in_specs=[smem] * 4
        + [
            vmem,
            vmem,
            pl.BlockSpec((1, s.pao, s.aux), lambda g: (g, 0, 0)),
            pl.BlockSpec((repeats, 1, s.pao, s.pao), lambda g: (0, g, 0, 0)),
            anywhere,
            anywhere,
        ],
        out_specs=[both, pl.BlockSpec((1, s.pao, s.pao), lambda g: (g, 0, 0)), anywhere, anywhere],
        out_shape=[
            jax.ShapeDtypeStruct((repeats, s.occ, s.pao, s.aux), jnp.bfloat16),
            dens_shape,
            jax.ShapeDtypeStruct(to_other.shape, to_other.dtype),
            jax.ShapeDtypeStruct(to_sibling.shape, to_sibling.dtype),
        ],
        input_output_aliases={8: 2, 9: 3},
        compiler_params=stepped,
        cost_estimate=cost(10**11, 10**5),
        name="own",
    )(
        here, pair_partner, lens, counts, tables, aux_domain, blocks_t,
        amplitudes.reshape(repeats, s.occ, s.pao, s.pao), to_other, to_sibling,
    )
    from_sibling = swap(to_sibling, 0)
    over, to_other = pl.pallas_call(
        functools.partial(count_kernel, s),
        in_specs=[smem] * 2 + [vmem, anywhere],
        out_specs=[smem, anywhere],
        out_shape=[
            jax.ShapeDtypeStruct((1,), jnp.int32),
            jax.ShapeDtypeStruct(to_other.shape, to_other.dtype),
        ],
        input_output_aliases={3: 1},
        compiler_params=plain,
        cost_estimate=cost(10**11, 10**5),
        name="count",
    )(pair_partner, lens, aux_domain, to_other)
    from_other = swap(to_other, 1)
    aligned = aligned.reshape(s.pairs, s.pao, s.aux)

    coupling, densities, some_amps, some_energies, to_other_more = pl.pallas_call(
        functools.partial(main_kernel, s, ncpl),
        grid=(s.pairs,),
        in_specs=[smem] * 7
        + [vmem] * 5
        + [pl.BlockSpec((1, s.pao, s.aux), lambda p: (p, 0, 0))]
        + [anywhere] * 4,
        out_specs=[square, all_dens, square, smem, anywhere],
        out_shape=[
            squares,
            dens_shape,
            jax.ShapeDtypeStruct(amplitudes.shape, amplitudes.dtype),
            jax.ShapeDtypeStruct((s.pairs,), jnp.float32),
            jax.ShapeDtypeStruct(to_other_more.shape, to_other_more.dtype),
        ],
        input_output_aliases={16: 4},
        scratch_shapes=[
            pltpu.VMEM((3 * s.pairs, s.pao, s.pao), jnp.bfloat16),
            pltpu.VMEM((ncpl * s.pao, s.pao), jnp.bfloat16),
            pltpu.VMEM((s.occ, s.pao, s.pao), jnp.float32),
            pltpu.VMEM((s.occ, s.pao, s.aux), jnp.bfloat16),
            pltpu.VMEM((s.rows + s.pao, LANES), jnp.bfloat16),
            pltpu.VMEM((s.pao, s.pao), jnp.float32),
            pltpu.SemaphoreType.DMA((3,)),
        ],
        compiler_params=stepped,
        cost_estimate=cost(10**11, 10**5),
        name="main",
    )(
        here, pair_partner, coupling_list.T, lens, coupling_coef.T, counts, offsets,
        pao_rows, gap_rows, amps_sibling, amplitudes, amps_other, aligned, dens, blocks_t, from_sibling,
        to_other_more,
    )

    from_other_more = lax.cond(over[0] > 0, lambda a: swap(a, 1), lambda a: a, to_other_more)
    new_amps, energies = pl.pallas_call(
        functools.partial(last_kernel, s),
        in_specs=[smem] * 7 + [vmem] + [anywhere] * 6,
        out_specs=[anywhere, smem],
        out_shape=[
            jax.ShapeDtypeStruct(amplitudes.shape, amplitudes.dtype),
            jax.ShapeDtypeStruct((s.pairs,), jnp.float32),
        ],
        scratch_shapes=[
            pltpu.VMEM((s.rows + s.pao, LANES), jnp.bfloat16),
            pltpu.VMEM((s.pairs, s.pao, s.aux), jnp.bfloat16),
            pltpu.VMEM((s.pairs, s.pao, s.pao), jnp.float32),
            pltpu.VMEM((s.pairs, s.pao, s.pao), jnp.bfloat16),
            pltpu.VMEM((s.pairs, s.pao, s.pao), jnp.bfloat16),
            pltpu.VMEM((s.pao, s.pao), jnp.float32),
            pltpu.SMEM((s.pairs,), jnp.int32),
            pltpu.SemaphoreType.DMA((5, s.pairs)),
        ],
        input_output_aliases={13: 0},
        compiler_params=plain,
        cost_estimate=cost(2 * s.pairs * s.pao * s.pao * s.aux, 2 * 10**7),
        name="last",
    )(
        here, pair_partner, lens, counts, offsets, over, some_energies,
        gap_rows, aligned, coupling, amplitudes, from_other, from_other_more, some_amps,
    )
    return (new_amps, energies, densities)


def solution(mesh):
    return jax.shard_map(
        local,
        mesh=mesh,
        in_specs=(
            P(AXES, None, None),
            P(),
            P(),
            P(),
            P(AXES, None, None),
            P(),
            P(AXES, None),
            P(AXES, None),
        ),
        out_specs=(P(AXES, None, None), P(AXES), P(AXES, None, None)),
        check_vma=False,
    )
```

```python
import functools

import jax
import jax.numpy as jnp
from jax import lax
from jax.experimental import pallas as pl
from jax.experimental.pallas import tpu as pltpu
from jax.sharding import PartitionSpec as P

AXES = ("orb", "pair")
MIB = 1024 * 1024
AUX_IDS = 2048
LOW = 64
HIGH = AUX_IDS // LOW
BASE = 32
LANES = 128
FIRST, WHOLE = 37, 64
NN = (((1,), (0,)), ((), ()))
NT = (((1,), (1,)), ((), ()))
TN = (((0,), (0,)), ((), ()))


def dot(a, b, dims=NN):
    return lax.dot_general(a, b, dims, preferred_element_type=jnp.float32)


def one_where(equal, value=1.0):
    return jnp.where(equal, value, 0.0).astype(jnp.bfloat16)


def iota(shape, dim):
    return lax.broadcasted_iota(jnp.int32, shape, dim)


def live(rows, cols, shape):
    return (iota(shape, 0) < rows) & (iota(shape, 1) < cols)


def kept(amp, rows, cols):
    return jnp.where(live(rows, cols, amp.shape), amp.astype(jnp.float32), 0.0).astype(amp.dtype)


def short_where(equal):
    one = jnp.ones(equal.shape, jnp.bfloat16)
    return jnp.where(equal, one, jnp.zeros_like(one))


def column(row):
    return jnp.broadcast_to(row, (LANES, row.shape[1])).T


def same(col, row):
    parts = []
    for at in range(0, row.shape[1], LANES):
        piece = row[:, at : at + LANES]
        wide = jnp.broadcast_to(piece, (col.shape[0], piece.shape[1]))
        parts.append(short_where(col[:, : piece.shape[1]] == wide))
    return jnp.concatenate(parts, axis=1)


def chunks_of(count):
    return (count + LANES - 1) // LANES


def rows_of(length):
    return (length + 15) // 16 * 16


def swapped(me):
    odd = lax.rem(me, 2)
    return me + 1 - 2 * odd, me - 1 + 2 * odd


class Sizes:
    def __init__(self, blocks, amplitudes, pair_partner):
        self.occ = blocks.shape[0]
        self.aux = blocks.shape[1]
        self.pao = blocks.shape[2]
        self.pairs = amplitudes.shape[0]
        self.npair = pair_partner.shape[0]
        self.nocc = self.npair // self.pairs * self.occ
        self.rows = self.occ * self.pao * (self.aux // LANES)
        self.first = self.rows * FIRST // WHOLE // 16 * 16
        self.room = self.first - self.pao // 2

    def first_orbital(self, pair):
        return pair // self.pairs * self.occ + lax.rem(pair, self.occ)

    def where_partner(self, me, right):
        device = right // self.occ
        sibling, _ = swapped(me)
        kind = jnp.where(device == me, 2, jnp.where(device == sibling, 0, 1))
        return kind * self.occ + lax.rem(right, self.occ), kind


def packing(s):
    whole = s.pao // LANES * LANES
    tail = s.pao - whole
    share = whole // tail
    return whole, tail, share


def slim_kernel(s, amps, out):
    whole, tail, share = packing(s)
    for k in range(s.pairs):
        out[k] = amps[k, :, :whole]
    for g in range(s.pairs // share):
        tails = [amps[g * share + t, :, whole:] for t in range(share)]
        out[s.pairs + g] = jnp.concatenate(tails, axis=1)


def unpack(s, packed, k, out):
    whole, tail, share = packing(s)
    out[:, :whole] = packed[k]
    spot = k % share * tail
    out[:, whole:] = packed[s.pairs + k // share, :, spot : spot + tail]


def bits(values, count, lanes):
    levels = iota((count, lanes), 0).astype(jnp.bfloat16)
    return short_where(levels == jnp.broadcast_to(values.astype(jnp.bfloat16), (count, lanes)))


def places(row, table, k):
    found = dot(table, bits(row // LOW + k * HIGH, table.shape[1], row.shape[1]))
    low = bits(lax.rem(row, LOW), LOW, row.shape[1]).astype(jnp.float32)
    return jnp.sum((found[:LOW] * BASE + found[LOW:]) * low, axis=0, keepdims=True)


def picker(place, chunk):
    wide = 2 * LANES
    middle = chunk * wide + LANES + 1
    spot = (place - jnp.asarray(middle).astype(jnp.float32)).astype(jnp.bfloat16)
    levels = (iota((wide, place.shape[1]), 0) - LANES).astype(jnp.bfloat16)
    return short_where(levels == jnp.broadcast_to(spot, levels.shape))


def chunkwise(s, count, act):
    for c in range(s.aux // (2 * LANES)):
        pl.when(count > c * 2 * LANES)(functools.partial(act, c))


def split_place(place, row):
    part = jnp.where(row < LOW, place // BASE, lax.rem(place, BASE))
    return part.astype(jnp.float32).astype(jnp.bfloat16)


def pack_kernel(
    s, here, partner, lens, aux_rows, blocks, pao_cols, gap_cols, _, to_sibling, to_other, to_other_more, tables, pao_rows, gap_rows, counts, offsets, maps, users, sends, bufs, sems
):
    me = here[0]
    peers = swapped(me)
    pao_rows[...] = pao_cols[...].T
    gap_rows[...] = gap_cols[...].T

    for g, device in enumerate((me,) + peers):
        for k in range(s.occ):
            orbital = jnp.clip(device * s.occ + k, 0, s.nocc - 1)
            row = aux_rows[pl.ds(orbital, 1), :]
            by_high = bits(row // LOW, HIGH, s.aux)
            by_low = bits(lax.rem(row, LOW), LOW, s.aux)
            here_map = dot(jnp.concatenate([by_low, by_low], axis=0), by_high, NT)
            maps[g, :, k * HIGH : (k + 1) * HIGH] = here_map
            users[g * s.occ + k] = jnp.concatenate([here_map] * s.occ, axis=1)
            if g == 0:
                spot = iota((LOW, s.aux), 1) + 1
                parts = jnp.concatenate(
                    [
                        (spot // BASE).astype(jnp.float32).astype(jnp.bfloat16) * by_low,
                        lax.rem(spot, BASE).astype(jnp.float32).astype(jnp.bfloat16) * by_low,
                    ],
                    axis=0,
                )
                tables[2, :, k * HIGH : (k + 1) * HIGH] = dot(parts, by_high, NT).astype(
                    jnp.bfloat16
                )

    wide = s.occ * HIGH
    sub, lane = iota((2 * LOW, 2 * LOW), 0), iota((2 * LOW, 2 * LOW), 1)
    ahead = one_where((lane < LOW) & (lane < lax.rem(sub, LOW)))
    first = one_where(lane < LOW)
    sub, lane = iota((wide, wide), 0), iota((wide, wide), 1)
    above = one_where((sub // HIGH == lane // HIGH) & (sub < lane))
    level = iota((2 * LOW, wide), 0)
    owner = iota((1, wide), 1) // HIGH

    def listing(target, target_device, user, user_device):
        union = jnp.zeros((2 * LOW, wide), jnp.float32)
        for q in range(s.occ):
            uses = jnp.zeros((1, wide), jnp.float32)
            for pair in range(q, s.pairs, s.occ):
                pair += user_device * s.pairs
                inside = (pair >= 0) & (pair < s.npair)
                k = partner[jnp.clip(pair, 0, s.npair - 1)] - target_device * s.occ
                uses += jnp.where((owner == k) & inside, 1.0, 0.0)
            union += uses * users[user * s.occ + q]
        taken = (union > 0.0) & (maps[target] > 0.0)
        flags = one_where(taken)
        total = dot(first, flags)
        place = dot(ahead, flags) + dot(total.astype(jnp.bfloat16), above) + 1.0
        place = jnp.where(taken, place, 0.0).astype(jnp.int32)
        found = [
            jnp.sum(jnp.where(owner == k, total[:1], 0.0)).astype(jnp.int32) for k in range(s.occ)
        ]
        return split_place(place, level), found

    copies = {
        0: [pltpu.make_async_copy(bufs.at[0, pl.ds(0, s.rows)], to_sibling, sems.at[0])],
        1: [
            pltpu.make_async_copy(bufs.at[1, pl.ds(0, s.first)], to_other, sems.at[1]),
            pltpu.make_async_copy(
                bufs.at[1, pl.ds(s.first, s.rows - s.first)], to_other_more, sems.at[2]
            ),
        ],
    }
    for r in (1, 0):
        sends[r], found = listing(0, me, 1 + r, peers[r])
        at = jnp.int32(0)
        for k, count in enumerate(found):
            step = rows_of(lens[me * s.occ + k])

            @pl.when(count > 0)
            def _(k=k, at=at, step=step, count=count):
                place = places(aux_rows[pl.ds(me * s.occ + k, 1), :], sends[r], k)

                def some(c):
                    got = dot(blocks[k], picker(place, c), NT).astype(jnp.bfloat16)
                    spot = pl.multiple_of(at + 2 * c * step, 16)
                    bufs[r, pl.ds(spot, s.pao), :] = got[:, :LANES]

                    @pl.when((2 * c + 1) * LANES < count)
                    def _():
                        bufs[r, pl.ds(pl.multiple_of(spot + step, 16), s.pao), :] = got[:, LANES:]

                chunkwise(s, count, some)

            at += chunks_of(count) * step

        for copy in copies[r]:
            copy.start()

    for r in range(2):
        tables[r], found = listing(1 + r, peers[r], 0, me)
        at = jnp.int32(0)
        for k, count in enumerate(found):
            orbital = jnp.clip(peers[r] * s.occ + k, 0, s.nocc - 1)
            counts[r * s.occ + k] = count
            offsets[r * s.occ + k] = at
            at += chunks_of(count) * rows_of(lens[orbital])
    for k in range(s.occ):
        counts[2 * s.occ + k] = jnp.int32(s.aux)
        offsets[2 * s.occ + k] = jnp.int32(0)

    for copy in copies[1] + copies[0]:
        copy.wait()


def count_kernel(s, partner, lens, aux_rows, _, over, __):
    devices = s.nocc // s.occ
    full = s.aux // LANES

    def ids(orbital):
        row = aux_rows[pl.ds(orbital, 1), :]
        return dot(bits(row // LOW, HIGH, s.aux), bits(lax.rem(row, LOW), LOW, s.aux), NT)

    over[0] = jnp.int32(0)

    def edge(e, _):
        source = e + 1
        user = source + 1 - 2 * lax.rem(e, 2)
        reads = [partner[user * s.pairs + q] - source * s.occ for q in range(s.pairs)]
        bound = jnp.int32(0)
        for k in range(s.occ):
            used = functools.reduce(jnp.logical_or, [read == k for read in reads])
            bound += jnp.where(used, full * rows_of(lens[source * s.occ + k]), 0)

        @pl.when(bound > s.room)
        def _():
            domains = [ids(user * s.occ + q) for q in range(s.occ)]
            need = jnp.int32(0)
            for k in range(s.occ):
                union = jnp.zeros((HIGH, LOW), jnp.float32)
                for q, domain in enumerate(domains):
                    used = functools.reduce(
                        jnp.logical_or, [read == k for read in reads[q :: s.occ]]
                    )
                    union += jnp.where(used, 1.0, 0.0) * domain
                taken = (union > 0.0) & (ids(source * s.occ + k) > 0.0)
                count = jnp.sum(jnp.where(taken, 1.0, 0.0)).astype(jnp.int32)
                need += chunks_of(count) * rows_of(lens[source * s.occ + k])
            over[0] = jnp.maximum(over[0], (need > s.room).astype(jnp.int32))

        return 0

    lax.fori_loop(0, devices - 2, edge, 0)


def own_kernel(
    s, here, partner, lens, counts, tables, aux_rows, blocks, amps, _, __, aligned, dens, ___, ____
):
    left = pl.program_id(0)
    me = here[0]
    wide = 2 * LANES
    chunks = s.aux // wide
    row = aux_rows[pl.ds(me * s.occ + left, 1), :]
    term = jnp.zeros((s.pao, s.pao), jnp.float32)
    rest = []

    for t in range(s.pairs // s.occ):
        right = partner[me * s.pairs + t * s.occ + left]
        l, kind = s.where_partner(me, right)
        place = places(row, tables[kind], lax.rem(right, s.occ))

        def some(c, t=t, place=place):
            aligned[t, 0, :, c * wide : (c + 1) * wide] = dot(
                blocks[0], picker(place, c), NT
            ).astype(jnp.bfloat16)

        for c in range(chunks - 1):
            some(c)
        rest.append((counts[l] > (chunks - 1) * wide, functools.partial(some, chunks - 1)))
        masked = kept(amps[t, 0], lens[me * s.occ + left], lens[right])
        term += dot(masked, masked, NT)

    dens[0] = term
    for needed, act in rest:
        pl.when(needed)(act)


def main_kernel(
    s, ncpl, here, partner, listed, lens, coef, counts, offsets, pao_rows, gaps, sibling, own, other, aligned, dens_in, blocks, from_sibling, coupling, dens, new_amps, energy, wide, tall, dens_own, near_blocks, halo, sums, sems
):
    p = pl.program_id(0)
    me = here[0]
    peers = swapped(me)
    fetches = [
        pltpu.make_async_copy(from_sibling, halo.at[pl.ds(0, s.rows), :], sems.at[0]),
        pltpu.make_async_copy(blocks, near_blocks, sems.at[1]),
        pltpu.make_async_copy(dens_in, dens_own, sems.at[2]),
    ]

    @pl.when(p == 0)
    def _():
        for fetch in fetches:
            fetch.start()
        dens[...] = jnp.zeros_like(dens)
        wide[s.pairs : 2 * s.pairs] = own[...]
        for device, packed in zip(peers, (sibling, other)):
            for k in range(s.pairs):
                unpack(s, packed, k, wide.at[(device - me + 1) * s.pairs + k])

    def row_of(orbital):
        return pao_rows[pl.ds(orbital, 1), :]

    def column_of(orbital):
        row = row_of(orbital)
        return column(jnp.where(row < 0, -2, row)).astype(jnp.int16)

    right_col = column_of(partner[me * s.pairs + p])
    left_col = column_of(me * s.occ + lax.rem(p, s.occ))
    left_rows = []
    for c in range(ncpl):
        m = listed[c, p]
        left_rows.append(row_of(s.first_orbital(m)))
        amp = wide[m - (me - 1) * s.pairs]
        moved = dot(amp, same(right_col, row_of(partner[m]).astype(jnp.int16)), NT)
        tall[c * s.pao : (c + 1) * s.pao] = (coef[c, p] * moved).astype(jnp.bfloat16)
    left_row = jnp.concatenate(left_rows, axis=1).astype(jnp.int16)
    coupling[0] = dot(same(left_col, left_row), tall[...])

    for side in range(3):
        m = (me + side - 1) * s.pairs + p
        inside = (m >= 0) & (m < s.npair)
        m = jnp.clip(m, 0, s.npair - 1)
        near = partner[m] - me * s.occ

        @pl.when(inside & (near >= 0) & (near < s.occ))
        def _():
            amp = wide[side * s.pairs + p]
            masked = kept(amp, lens[s.first_orbital(m)], lens[partner[m]])
            dens[near] += dot(masked, masked, TN)

    @pl.when(p == 0)
    def _():
        for fetch in fetches:
            fetch.wait()

    left, right = me * s.occ + lax.rem(p, s.occ), partner[me * s.pairs + p]
    l, kind = s.where_partner(me, right)

    @pl.when(kind == 2)
    def _():
        sums[...] = dot(aligned[0], near_blocks[lax.rem(right, s.occ)], NT)

    @pl.when(kind == 0)
    def _():
        compacted(s, counts[l], offsets[l], rows_of(lens[right]), aligned.at[0], halo, sums)

    @pl.when(kind != 1)
    def _():
        new_amps[0], energy[p] = update(
            s, lens[left], lens[right], sums[...], own[p], coupling[0], gaps[pl.ds(left, 1), :], gaps[pl.ds(right, 1), :]
        )

    @pl.when(kind == 1)
    def _():
        energy[p] = 0.0

    @pl.when(p == s.pairs - 1)
    def _():
        dens[...] = (dens[...] + dens_own[...]) * (1.0 / s.pao)


def update(s, lens_left, lens_right, exchange, amp, coupling, gap_left, gap_right):
    left = column(gap_left)
    parts = []
    energy = jnp.zeros((s.pao, LANES), jnp.float32)
    for at in range(0, s.pao, LANES):
        lanes = slice(at, min(at + LANES, s.pao))
        part = amp[:, lanes].astype(jnp.float32)
        shape = part.shape
        mask = live(lens_left, lens_right - at, shape)
        denom = left[:, : shape[1]] + gap_right[:, lanes]
        inverse = pl.reciprocal(denom, approx=True)
        inverse = inverse * (2.0 - denom * inverse)
        moved = (exchange[:, lanes] - coupling[:, lanes]) * inverse
        parts.append(jnp.where(mask, 0.5 * (part - moved), 0.0).astype(jnp.bfloat16))
        term = jnp.where(mask, exchange[:, lanes] * part, 0.0)
        if shape[1] < LANES:
            term = jnp.concatenate([term, jnp.zeros((s.pao, LANES - shape[1]), jnp.float32)], axis=1)
        energy += term
    return jnp.concatenate(parts, axis=1), jnp.sum(energy) / s.pao


def compacted(s, count, at, step, aligned, halo, sums):
    chunks = s.aux // LANES
    usual = chunks - 2

    def some(low, high):
        parts = []
        for c in range(low, high):
            spot = pl.multiple_of(jnp.minimum(at + c * step, halo.shape[0] - s.pao), 16)
            part = halo[pl.ds(spot, s.pao), :]
            parts.append(jnp.where(c * LANES < count, part, jnp.zeros_like(part)))
        both = jnp.concatenate(parts, axis=1)
        return dot(aligned[:, low * LANES : high * LANES], both, NT)

    sums[...] = some(0, usual)

    @pl.when(count > usual * LANES)
    def _():
        sums[...] += some(usual, chunks)


def last_kernel(s, beyond, here, partner, lens, counts, offsets, energy_in, gaps, aligned, coupling, amps, other, *refs):
    if beyond:
        more, _, new_amps, energy, halo, news, sums, far, sems = refs
        halo[: s.first] = other[...]
        rest = pltpu.make_async_copy(
            more, halo.at[pl.ds(s.first, s.rows - s.first)], sems.at[s.pairs]
        )
        rest.start()
        rest.wait()
    else:
        _, new_amps, energy, news, sums, far, sems = refs
        halo = other
    me = here[0]

    def result(p):
        return pltpu.make_async_copy(news.at[p], new_amps.at[p], sems.at[p])

    number = jnp.int32(0)
    for p in range(s.pairs):
        energy[p] = energy_in[p]
        far[number] = p
        kind = s.where_partner(me, partner[me * s.pairs + p])[1]
        number += (kind == 1).astype(jnp.int32)

    def each(act):
        def one(n, _):
            p = far[n]
            right = partner[me * s.pairs + p]
            act(p, right, s.occ + lax.rem(right, s.occ))
            return 0

        lax.fori_loop(0, number, one, 0)

    def finish(p, right, l):
        left = me * s.occ + lax.rem(p, s.occ)
        compacted(s, counts[l], offsets[l], rows_of(lens[right]), aligned.at[p], halo, sums)
        news[p], energy[p] = update(
            s, lens[left], lens[right], sums[...], amps[p], coupling[p], gaps[pl.ds(left, 1), :], gaps[pl.ds(right, 1), :]
        )
        result(p).start()

    each(finish)
    each(lambda p, right, l: result(p).wait())


def position():
    return lax.axis_index(AXES)


def swap(array, role):
    count = 1
    for axis in AXES:
        count *= lax.axis_size(axis)
    route = []
    for low in range(role, count - 1, 2):
        route += [(low, low + 1), (low + 1, low)]
    return lax.ppermute(array, AXES, route)


def local(
    blocks, aux_domain, pao_domain, pao_gap, amplitudes, pair_partner, coupling_list, coupling_coef
):
    s = Sizes(blocks, amplitudes, pair_partner)
    ncpl = coupling_list.shape[1]
    me = position()
    here = me.astype(jnp.int32).reshape(1)
    blocks_t = jnp.swapaxes(blocks, 1, 2)

    smem = pl.BlockSpec(memory_space=pltpu.SMEM)
    vmem = pl.BlockSpec(memory_space=pltpu.VMEM)
    pinned = pl.BlockSpec(memory_space=pltpu.HBM)
    anywhere = pl.BlockSpec(memory_space=pl.ANY)
    plain = pltpu.CompilerParams(vmem_limit_bytes=24 * MIB)
    stepped = pltpu.CompilerParams(
        dimension_semantics=("arbitrary",), vmem_limit_bytes=30 * MIB
    )
    alone = pltpu.CompilerParams(vmem_limit_bytes=24 * MIB)
    square = pl.BlockSpec((1, s.pao, s.pao), lambda p, *_: (p, 0, 0))
    all_dens = pl.BlockSpec((s.occ, s.pao, s.pao), lambda p, *_: (0, 0, 0))
    squares = jax.ShapeDtypeStruct((s.pairs, s.pao, s.pao), jnp.float32)
    dens_shape = jax.ShapeDtypeStruct((s.occ, s.pao, s.pao), jnp.float32)

    def cost(work, data):
        return pl.CostEstimate(flops=work, bytes_accessed=data, transcendentals=0)

    whole, tail, share = packing(s)
    slots = s.pairs + s.pairs // share
    slim = pl.pallas_call(
        functools.partial(slim_kernel, s),
        in_specs=[vmem],
        out_specs=vmem,
        out_shape=jax.ShapeDtypeStruct((slots, s.pao, whole), jnp.bfloat16),
        compiler_params=plain,
        cost_estimate=cost(10**6, 4 * 10**6),
        name="slim",
    )(amplitudes)
    amps_other = swap(slim, 1)
    amps_sibling = swap(slim, 0)

    lens = jnp.sum((pao_domain >= 0).astype(jnp.int32), axis=1)

    lists = 3 * s.occ
    to_sibling, to_other, to_other_more, tables, pao_rows, gap_rows, counts, offsets = pl.pallas_call(
        functools.partial(pack_kernel, s),
        in_specs=[smem] * 3 + [vmem] * 4 + [anywhere],
        out_specs=[pinned] * 3 + [vmem] * 3 + [smem] * 2,
        out_shape=[
            jax.ShapeDtypeStruct((s.rows, LANES), jnp.bfloat16),
            jax.ShapeDtypeStruct((s.first, LANES), jnp.bfloat16),
            jax.ShapeDtypeStruct((s.rows - s.first, LANES), jnp.bfloat16),
            jax.ShapeDtypeStruct((3, 2 * LOW, s.occ * HIGH), jnp.bfloat16),
            jax.ShapeDtypeStruct(pao_domain.shape, pao_domain.dtype),
            jax.ShapeDtypeStruct(pao_gap.shape, pao_gap.dtype),
            jax.ShapeDtypeStruct((lists,), jnp.int32),
            jax.ShapeDtypeStruct((lists,), jnp.int32),
        ],
        scratch_shapes=[
            pltpu.VMEM((3, 2 * LOW, s.occ * HIGH), jnp.float32),
            pltpu.VMEM((3 * s.occ, 2 * LOW, s.occ * HIGH), jnp.float32),
            pltpu.VMEM((2, 2 * LOW, s.occ * HIGH), jnp.bfloat16),
            pltpu.VMEM((2, s.rows + s.pao, LANES), jnp.bfloat16),
            pltpu.SemaphoreType.DMA((3,)),
        ],
        compiler_params=plain,
        cost_estimate=cost(10**11, 10**5),
        name="pack",
    )(here, pair_partner, lens, aux_domain, blocks_t, pao_domain.T, pao_gap.T, slim)

    repeats = s.pairs // s.occ
    both = pl.BlockSpec((repeats, 1, s.pao, s.aux), lambda g: (0, g, 0, 0))
    aligned, dens, to_other, to_sibling = pl.pallas_call(
        functools.partial(own_kernel, s),
        grid=(s.occ,),
        in_specs=[smem] * 4
        + [
            vmem,
            vmem,
            pl.BlockSpec((1, s.pao, s.aux), lambda g: (g, 0, 0)),
            pl.BlockSpec((repeats, 1, s.pao, s.pao), lambda g: (0, g, 0, 0)),
            anywhere,
            anywhere,
        ],
        out_specs=[both, pl.BlockSpec((1, s.pao, s.pao), lambda g: (g, 0, 0)), anywhere, anywhere],
        out_shape=[
            jax.ShapeDtypeStruct((repeats, s.occ, s.pao, s.aux), jnp.bfloat16),
            dens_shape,
            jax.ShapeDtypeStruct(to_other.shape, to_other.dtype),
            jax.ShapeDtypeStruct(to_sibling.shape, to_sibling.dtype),
        ],
        input_output_aliases={8: 2, 9: 3},
        compiler_params=stepped,
        cost_estimate=cost(10**11, 10**5),
        name="own",
    )(
        here, pair_partner, lens, counts, tables, aux_domain, blocks_t,
        amplitudes.reshape(repeats, s.occ, s.pao, s.pao), to_other, to_sibling,
    )
    from_sibling = swap(to_sibling, 0)
    over, to_other = pl.pallas_call(
        functools.partial(count_kernel, s),
        in_specs=[smem] * 2 + [vmem, anywhere],
        out_specs=[smem, anywhere],
        out_shape=[
            jax.ShapeDtypeStruct((1,), jnp.int32),
            jax.ShapeDtypeStruct(to_other.shape, to_other.dtype),
        ],
        input_output_aliases={3: 1},
        compiler_params=plain,
        cost_estimate=cost(10**11, 10**5),
        name="count",
    )(pair_partner, lens, aux_domain, to_other)
    from_other = swap(to_other, 1)
    aligned = aligned.reshape(s.pairs, s.pao, s.aux)

    coupling, densities, some_amps, some_energies = pl.pallas_call(
        functools.partial(main_kernel, s, ncpl),
        grid=(s.pairs,),
        in_specs=[smem] * 7
        + [vmem] * 5
        + [pl.BlockSpec((1, s.pao, s.aux), lambda p: (p, 0, 0))]
        + [anywhere, pinned, anywhere],
        out_specs=[square, all_dens, square, smem],
        out_shape=[
            squares,
            dens_shape,
            jax.ShapeDtypeStruct(amplitudes.shape, amplitudes.dtype),
            jax.ShapeDtypeStruct((s.pairs,), jnp.float32),
        ],
        scratch_shapes=[
            pltpu.VMEM((3 * s.pairs, s.pao, s.pao), jnp.bfloat16),
            pltpu.VMEM((ncpl * s.pao, s.pao), jnp.bfloat16),
            pltpu.VMEM((s.occ, s.pao, s.pao), jnp.float32),
            pltpu.VMEM((s.occ, s.pao, s.aux), jnp.bfloat16),
            pltpu.VMEM((s.rows + s.pao, LANES), jnp.bfloat16),
            pltpu.VMEM((s.pao, s.pao), jnp.float32),
            pltpu.SemaphoreType.DMA((3,)),
        ],
        compiler_params=stepped,
        cost_estimate=cost(10**11, 10**5),
        name="main",
    )(
        here, pair_partner, coupling_list.T, lens, coupling_coef.T, counts, offsets,
        pao_rows, gap_rows, amps_sibling, amplitudes, amps_other, aligned, dens, blocks_t, from_sibling,
    )

    def last(beyond, energy, arrays, more, some_amps):
        scratch = [
            pltpu.VMEM((s.pairs, s.pao, s.pao), jnp.bfloat16),
            pltpu.VMEM((s.pao, s.pao), jnp.float32),
            pltpu.SMEM((s.pairs,), jnp.int32),
            pltpu.SemaphoreType.DMA((s.pairs + 1,)),
        ]
        if beyond:
            scratch = [pltpu.VMEM((s.rows + s.pao, LANES), jnp.bfloat16)] + scratch
        return pl.pallas_call(
            functools.partial(last_kernel, s, beyond),
            in_specs=[smem] * 6 + [vmem] * 5 + [pinned] * (len(more) + 1),
            out_specs=[pinned, smem],
            out_shape=[
                jax.ShapeDtypeStruct(amplitudes.shape, amplitudes.dtype),
                jax.ShapeDtypeStruct((s.pairs,), jnp.float32),
            ],
            scratch_shapes=scratch,
            input_output_aliases={11 + len(more): 0},
            compiler_params=alone,
            cost_estimate=cost(2 * s.pairs * s.pao * s.pao * s.aux, 2 * 10**7),
            name="again" if beyond else "last",
        )(here, pair_partner, lens, counts, offsets, energy, *arrays, *more, some_amps)

    arrays = (gap_rows, aligned, coupling, amplitudes, from_other)
    new_amps, energies = last(False, some_energies, arrays, (), some_amps)

    def again(ops):
        new_amps, energies, to_other_more, arrays = ops
        return tuple(last(True, energies, arrays, (swap(to_other_more, 1),), new_amps))

    new_amps, energies = lax.cond(
        over[0] > 0, again, lambda ops: ops[:2], (new_amps, energies, to_other_more, arrays)
    )
    return (new_amps, energies, densities)


def solution(mesh):
    return jax.shard_map(
        local,
        mesh=mesh,
        in_specs=(
            P(AXES, None, None),
            P(),
            P(),
            P(),
            P(AXES, None, None),
            P(),
            P(AXES, None),
            P(AXES, None),
        ),
        out_specs=(P(AXES, None, None), P(AXES), P(AXES, None, None)),
        check_vma=False,
    )
```

```python
import functools

import jax
import jax.numpy as jnp
from jax import lax
from jax.experimental import pallas as pl
from jax.experimental.pallas import tpu as pltpu
from jax.sharding import PartitionSpec as P

AXES = ("orb", "pair")
MIB = 1024 * 1024
AUX_IDS = 2048
LOW = 64
HIGH = AUX_IDS // LOW
BASE = 32
LANES = 128
FIRST, WHOLE = 37, 64
NN = (((1,), (0,)), ((), ()))
NT = (((1,), (1,)), ((), ()))
TN = (((0,), (0,)), ((), ()))


def dot(a, b, dims=NN):
    return lax.dot_general(a, b, dims, preferred_element_type=jnp.float32)


def one_where(equal, value=1.0):
    return jnp.where(equal, value, 0.0).astype(jnp.bfloat16)


def iota(shape, dim):
    return lax.broadcasted_iota(jnp.int32, shape, dim)


def live(rows, cols, shape):
    return (iota(shape, 0) < rows) & (iota(shape, 1) < cols)


def kept(amp, rows, cols):
    return jnp.where(live(rows, cols, amp.shape), amp.astype(jnp.float32), 0.0).astype(amp.dtype)


def short_where(equal):
    one = jnp.ones(equal.shape, jnp.bfloat16)
    return jnp.where(equal, one, jnp.zeros_like(one))


def column(row):
    return jnp.broadcast_to(row, (LANES, row.shape[1])).T


def same(col, row):
    parts = []
    for at in range(0, row.shape[1], LANES):
        piece = row[:, at : at + LANES]
        wide = jnp.broadcast_to(piece, (col.shape[0], piece.shape[1]))
        parts.append(short_where(col[:, : piece.shape[1]] == wide))
    return jnp.concatenate(parts, axis=1)


def chunks_of(count):
    return (count + LANES - 1) // LANES


def rows_of(length):
    return (length + 15) // 16 * 16


def swapped(me):
    odd = lax.rem(me, 2)
    return me + 1 - 2 * odd, me - 1 + 2 * odd


class Sizes:
    def __init__(self, blocks, amplitudes, pair_partner):
        self.occ = blocks.shape[0]
        self.aux = blocks.shape[1]
        self.pao = blocks.shape[2]
        self.pairs = amplitudes.shape[0]
        self.npair = pair_partner.shape[0]
        self.nocc = self.npair // self.pairs * self.occ
        self.rows = self.occ * self.pao * (self.aux // LANES)
        self.first = self.rows * FIRST // WHOLE // 16 * 16
        self.room = self.first - self.pao // 2

    def first_orbital(self, pair):
        return pair // self.pairs * self.occ + lax.rem(pair, self.occ)

    def where_partner(self, me, right):
        device = right // self.occ
        sibling, _ = swapped(me)
        kind = jnp.where(device == me, 2, jnp.where(device == sibling, 0, 1))
        return kind * self.occ + lax.rem(right, self.occ), kind


def packing(s):
    whole = s.pao // LANES * LANES
    tail = s.pao - whole
    share = whole // tail
    return whole, tail, share


def slim_kernel(s, amps, out):
    whole, tail, share = packing(s)
    for k in range(s.pairs):
        out[k] = amps[k, :, :whole]
    for g in range(s.pairs // share):
        tails = [amps[g * share + t, :, whole:] for t in range(share)]
        out[s.pairs + g] = jnp.concatenate(tails, axis=1)


def unpack(s, packed, k, out):
    whole, tail, share = packing(s)
    out[:, :whole] = packed[k]
    spot = k % share * tail
    out[:, whole:] = packed[s.pairs + k // share, :, spot : spot + tail]


def bits(values, count, lanes):
    levels = iota((count, lanes), 0).astype(jnp.bfloat16)
    return short_where(levels == jnp.broadcast_to(values.astype(jnp.bfloat16), (count, lanes)))


def places(row, table, k):
    found = dot(table, bits(row // LOW + k * HIGH, table.shape[1], row.shape[1]))
    low = bits(lax.rem(row, LOW), LOW, row.shape[1]).astype(jnp.float32)
    return jnp.sum((found[:LOW] * BASE + found[LOW:]) * low, axis=0, keepdims=True)


def picker(place, chunk):
    wide = 2 * LANES
    middle = chunk * wide + LANES + 1
    spot = (place - jnp.asarray(middle).astype(jnp.float32)).astype(jnp.bfloat16)
    levels = (iota((wide, place.shape[1]), 0) - LANES).astype(jnp.bfloat16)
    return short_where(levels == jnp.broadcast_to(spot, levels.shape))


def chunkwise(s, count, act):
    for c in range(s.aux // (2 * LANES)):
        pl.when(count > c * 2 * LANES)(functools.partial(act, c))


def split_place(place, row):
    part = jnp.where(row < LOW, place // BASE, lax.rem(place, BASE))
    return part.astype(jnp.float32).astype(jnp.bfloat16)


def pack_kernel(
    s, here, partner, lens, aux_rows, blocks, pao_cols, gap_cols, _, to_sibling, to_other, to_other_more, tables, pao_rows, gap_rows, counts, offsets, maps, users, sends, bufs, sems
):
    me = here[0]
    peers = swapped(me)
    pao_rows[...] = pao_cols[...].T
    gap_rows[...] = gap_cols[...].T

    for g, device in enumerate((me,) + peers):
        for k in range(s.occ):
            orbital = jnp.clip(device * s.occ + k, 0, s.nocc - 1)
            row = aux_rows[pl.ds(orbital, 1), :]
            by_high = bits(row // LOW, HIGH, s.aux)
            by_low = bits(lax.rem(row, LOW), LOW, s.aux)
            here_map = dot(jnp.concatenate([by_low, by_low], axis=0), by_high, NT)
            maps[g, :, k * HIGH : (k + 1) * HIGH] = here_map
            users[g * s.occ + k] = jnp.concatenate([here_map] * s.occ, axis=1)
            if g == 0:
                spot = iota((LOW, s.aux), 1) + 1
                parts = jnp.concatenate(
                    [
                        (spot // BASE).astype(jnp.float32).astype(jnp.bfloat16) * by_low,
                        lax.rem(spot, BASE).astype(jnp.float32).astype(jnp.bfloat16) * by_low,
                    ],
                    axis=0,
                )
                tables[2, :, k * HIGH : (k + 1) * HIGH] = dot(parts, by_high, NT).astype(
                    jnp.bfloat16
                )

    wide = s.occ * HIGH
    sub, lane = iota((2 * LOW, 2 * LOW), 0), iota((2 * LOW, 2 * LOW), 1)
    ahead = one_where((lane < LOW) & (lane < lax.rem(sub, LOW)))
    first = one_where(lane < LOW)
    sub, lane = iota((wide, wide), 0), iota((wide, wide), 1)
    above = one_where((sub // HIGH == lane // HIGH) & (sub < lane))
    level = iota((2 * LOW, wide), 0)
    owner = iota((1, wide), 1) // HIGH

    def listing(target, target_device, user, user_device):
        union = jnp.zeros((2 * LOW, wide), jnp.float32)
        for q in range(s.occ):
            uses = jnp.zeros((1, wide), jnp.float32)
            for pair in range(q, s.pairs, s.occ):
                pair += user_device * s.pairs
                inside = (pair >= 0) & (pair < s.npair)
                k = partner[jnp.clip(pair, 0, s.npair - 1)] - target_device * s.occ
                uses += jnp.where((owner == k) & inside, 1.0, 0.0)
            union += uses * users[user * s.occ + q]
        taken = (union > 0.0) & (maps[target] > 0.0)
        flags = one_where(taken)
        total = dot(first, flags)
        place = dot(ahead, flags) + dot(total.astype(jnp.bfloat16), above) + 1.0
        place = jnp.where(taken, place, 0.0).astype(jnp.int32)
        found = [
            jnp.sum(jnp.where(owner == k, total[:1], 0.0)).astype(jnp.int32) for k in range(s.occ)
        ]
        return split_place(place, level), found

    copies = {
        0: [pltpu.make_async_copy(bufs.at[0, pl.ds(0, s.rows)], to_sibling, sems.at[0])],
        1: [
            pltpu.make_async_copy(bufs.at[1, pl.ds(0, s.first)], to_other, sems.at[1]),
            pltpu.make_async_copy(
                bufs.at[1, pl.ds(s.first, s.rows - s.first)], to_other_more, sems.at[2]
            ),
        ],
    }
    for r in (1, 0):
        sends[r], found = listing(0, me, 1 + r, peers[r])
        at = jnp.int32(0)
        for k, count in enumerate(found):
            step = rows_of(lens[me * s.occ + k])

            @pl.when(count > 0)
            def _(k=k, at=at, step=step, count=count):
                place = places(aux_rows[pl.ds(me * s.occ + k, 1), :], sends[r], k)

                def some(c):
                    got = dot(blocks[k], picker(place, c), NT).astype(jnp.bfloat16)
                    spot = pl.multiple_of(at + 2 * c * step, 16)
                    bufs[r, pl.ds(spot, s.pao), :] = got[:, :LANES]

                    @pl.when((2 * c + 1) * LANES < count)
                    def _():
                        bufs[r, pl.ds(pl.multiple_of(spot + step, 16), s.pao), :] = got[:, LANES:]

                chunkwise(s, count, some)

            at += chunks_of(count) * step

        for copy in copies[r]:
            copy.start()

    for r in range(2):
        tables[r], found = listing(1 + r, peers[r], 0, me)
        at = jnp.int32(0)
        for k, count in enumerate(found):
            orbital = jnp.clip(peers[r] * s.occ + k, 0, s.nocc - 1)
            counts[r * s.occ + k] = count
            offsets[r * s.occ + k] = at
            at += chunks_of(count) * rows_of(lens[orbital])
    for k in range(s.occ):
        counts[2 * s.occ + k] = jnp.int32(s.aux)
        offsets[2 * s.occ + k] = jnp.int32(0)

    for copy in copies[1] + copies[0]:
        copy.wait()


def count_kernel(s, partner, lens, aux_rows, _, over, __):
    devices = s.nocc // s.occ
    full = s.aux // LANES

    def ids(orbital):
        row = aux_rows[pl.ds(orbital, 1), :]
        return dot(bits(row // LOW, HIGH, s.aux), bits(lax.rem(row, LOW), LOW, s.aux), NT)

    over[0] = jnp.int32(0)

    def edge(e, _):
        source = e + 1
        user = source + 1 - 2 * lax.rem(e, 2)
        reads = [partner[user * s.pairs + q] - source * s.occ for q in range(s.pairs)]
        bound = jnp.int32(0)
        for k in range(s.occ):
            used = functools.reduce(jnp.logical_or, [read == k for read in reads])
            bound += jnp.where(used, full * rows_of(lens[source * s.occ + k]), 0)

        @pl.when(bound > s.room)
        def _():
            domains = [ids(user * s.occ + q) for q in range(s.occ)]
            need = jnp.int32(0)
            for k in range(s.occ):
                union = jnp.zeros((HIGH, LOW), jnp.float32)
                for q, domain in enumerate(domains):
                    used = functools.reduce(
                        jnp.logical_or, [read == k for read in reads[q :: s.occ]]
                    )
                    union += jnp.where(used, 1.0, 0.0) * domain
                taken = (union > 0.0) & (ids(source * s.occ + k) > 0.0)
                count = jnp.sum(jnp.where(taken, 1.0, 0.0)).astype(jnp.int32)
                need += chunks_of(count) * rows_of(lens[source * s.occ + k])
            over[0] = jnp.maximum(over[0], (need > s.room).astype(jnp.int32))

        return 0

    lax.fori_loop(0, devices - 2, edge, 0)


def own_kernel(
    s, here, partner, lens, counts, tables, aux_rows, blocks, amps, _, __, aligned, dens, ___, ____
):
    left = pl.program_id(0)
    me = here[0]
    wide = 2 * LANES
    chunks = s.aux // wide
    row = aux_rows[pl.ds(me * s.occ + left, 1), :]
    term = jnp.zeros((s.pao, s.pao), jnp.float32)
    rest = []

    for t in range(s.pairs // s.occ):
        right = partner[me * s.pairs + t * s.occ + left]
        l, kind = s.where_partner(me, right)
        place = places(row, tables[kind], lax.rem(right, s.occ))

        def some(c, t=t, place=place):
            aligned[t, 0, :, c * wide : (c + 1) * wide] = dot(
                blocks[0], picker(place, c), NT
            ).astype(jnp.bfloat16)

        for c in range(chunks - 1):
            some(c)
        rest.append((counts[l] > (chunks - 1) * wide, functools.partial(some, chunks - 1)))
        masked = kept(amps[t, 0], lens[me * s.occ + left], lens[right])
        term += dot(masked, masked, NT)

    dens[0] = term
    for needed, act in rest:
        pl.when(needed)(act)


def column_of(pao_rows, orbital):
    row = pao_rows[pl.ds(orbital, 1), :]
    return column(jnp.where(row < 0, -2, row)).astype(jnp.int16)


def row_of(pao_rows, orbital):
    return pao_rows[pl.ds(orbital, 1), :]


def near_kernel(
    s, ncpl, here, partner, listed, lens, coef, counts, offsets, pao_rows, sibling, own, aligned, dens_in, blocks, from_sibling, coupling, exchange, dens, wide, tall, dens_own, near_blocks, halo, sums, sems
):
    p = pl.program_id(0)
    me = here[0]
    buddy = swapped(me)[0]
    low = jnp.minimum(me, buddy)
    fetches = [
        pltpu.make_async_copy(from_sibling, halo.at[pl.ds(0, s.rows), :], sems.at[0]),
        pltpu.make_async_copy(blocks, near_blocks, sems.at[1]),
        pltpu.make_async_copy(dens_in, dens_own, sems.at[2]),
    ]

    @pl.when(p == 0)
    def _():
        for fetch in fetches:
            fetch.start()
        dens[...] = jnp.zeros_like(dens)
        for k in range(s.pairs):
            wide[(me - low) * s.pairs + k] = own[k]
            unpack(s, sibling, k, wide.at[(buddy - low) * s.pairs + k])

    right_col = column_of(pao_rows, partner[me * s.pairs + p])
    left_col = column_of(pao_rows, me * s.occ + lax.rem(p, s.occ))
    left_rows = []
    for c in range(ncpl):
        m = listed[c, p]
        spot = m - low * s.pairs
        inside = (spot >= 0) & (spot < 2 * s.pairs)
        weight = jnp.where(inside, coef[c, p], 0.0)
        left_rows.append(row_of(pao_rows, s.first_orbital(m)))
        right_row = row_of(pao_rows, partner[m]).astype(jnp.int16)
        moved = dot(wide[jnp.clip(spot, 0, 2 * s.pairs - 1)], same(right_col, right_row), NT)
        tall[c * s.pao : (c + 1) * s.pao] = (weight * moved).astype(jnp.bfloat16)
    left_row = jnp.concatenate(left_rows, axis=1).astype(jnp.int16)
    coupling[0] = dot(same(left_col, left_row), tall[...])

    for side in range(2):
        m = (low + side) * s.pairs + p
        near = partner[m] - me * s.occ

        @pl.when((near >= 0) & (near < s.occ))
        def _():
            masked = kept(wide[side * s.pairs + p], lens[s.first_orbital(m)], lens[partner[m]])
            dens[near] += dot(masked, masked, TN)

    @pl.when(p == 0)
    def _():
        for fetch in fetches:
            fetch.wait()

    right = partner[me * s.pairs + p]
    l, kind = s.where_partner(me, right)

    @pl.when(kind == 2)
    def _():
        exchange[0] = dot(aligned[0], near_blocks[lax.rem(right, s.occ)], NT)

    @pl.when(kind == 0)
    def _():
        compacted(s, counts[l], offsets[l], rows_of(lens[right]), aligned.at[0], halo, sums)
        exchange[0] = sums[...]

    @pl.when(p == s.pairs - 1)
    def _():
        dens[...] = (dens[...] + dens_own[...]) * (1.0 / s.pao)


def far_kernel(
    s, ncpl, here, partner, listed, lens, coef, pao_rows, gaps, other, own, near_coupling, exchange, near_dens, coupling, dens, new_amps, energy, wide, news, whose, which, sems
):
    me = here[0]
    device = swapped(me)[1]
    dens[...] = near_dens[...]
    coupling[...] = near_coupling[...]
    for k in range(s.pairs):
        unpack(s, other, k, wide.at[k])

    number = jnp.int32(0)
    for p in range(s.pairs):
        for c in range(ncpl):
            spot = listed[c, p] - device * s.pairs
            whose[number] = p
            which[number] = c
            number += ((spot >= 0) & (spot < s.pairs)).astype(jnp.int32)

    def term(n, _):
        p = whose[n]
        c = which[n]
        m = listed[c, p]
        right_col = column_of(pao_rows, partner[me * s.pairs + p])
        left_col = column_of(pao_rows, me * s.occ + lax.rem(p, s.occ))
        right_row = row_of(pao_rows, partner[m]).astype(jnp.int16)
        left_row = row_of(pao_rows, s.first_orbital(m)).astype(jnp.int16)
        moved = dot(wide[m - device * s.pairs], same(right_col, right_row), NT)
        moved = dot(same(left_col, left_row), moved.astype(jnp.bfloat16))
        coupling[p] += coef[c, p] * moved
        return 0

    lax.fori_loop(0, number, term, 0)

    for k in range(s.pairs):
        m = device * s.pairs + k
        inside = (m >= 0) & (m < s.npair)
        m = jnp.clip(m, 0, s.npair - 1)
        near = partner[m] - me * s.occ

        @pl.when(inside & (near >= 0) & (near < s.occ))
        def _():
            masked = kept(wide[k], lens[s.first_orbital(m)], lens[partner[m]])
            dens[near] += dot(masked, masked, TN) * (1.0 / s.pao)

    def result(p):
        return pltpu.make_async_copy(news.at[p], new_amps.at[p], sems.at[p])

    def finish(p, _):
        left, right = me * s.occ + lax.rem(p, s.occ), partner[me * s.pairs + p]
        kind = s.where_partner(me, right)[1]
        energy[p] = 0.0

        @pl.when(kind != 1)
        def _():
            news[p], energy[p] = update(
                s, lens[left], lens[right], exchange[p], own[p], coupling[p], gaps[pl.ds(left, 1), :], gaps[pl.ds(right, 1), :]
            )
            result(p).start()

        return 0

    def wait(p, _):
        kind = s.where_partner(me, partner[me * s.pairs + p])[1]
        pl.when(kind != 1)(result(p).wait)
        return 0

    lax.fori_loop(0, s.pairs, finish, 0)
    lax.fori_loop(0, s.pairs, wait, 0)


def update(s, lens_left, lens_right, exchange, amp, coupling, gap_left, gap_right):
    left = column(gap_left)
    parts = []
    energy = jnp.zeros((s.pao, LANES), jnp.float32)
    for at in range(0, s.pao, LANES):
        lanes = slice(at, min(at + LANES, s.pao))
        part = amp[:, lanes].astype(jnp.float32)
        shape = part.shape
        mask = live(lens_left, lens_right - at, shape)
        denom = left[:, : shape[1]] + gap_right[:, lanes]
        inverse = pl.reciprocal(denom, approx=True)
        inverse = inverse * (2.0 - denom * inverse)
        moved = (exchange[:, lanes] - coupling[:, lanes]) * inverse
        parts.append(jnp.where(mask, 0.5 * (part - moved), 0.0).astype(jnp.bfloat16))
        term = jnp.where(mask, exchange[:, lanes] * part, 0.0)
        if shape[1] < LANES:
            term = jnp.concatenate([term, jnp.zeros((s.pao, LANES - shape[1]), jnp.float32)], axis=1)
        energy += term
    return jnp.concatenate(parts, axis=1), jnp.sum(energy) / s.pao


def compacted(s, count, at, step, aligned, halo, sums):
    chunks = s.aux // LANES
    usual = chunks - 2

    def some(low, high):
        parts = []
        for c in range(low, high):
            spot = pl.multiple_of(jnp.minimum(at + c * step, halo.shape[0] - s.pao), 16)
            part = halo[pl.ds(spot, s.pao), :]
            parts.append(jnp.where(c * LANES < count, part, jnp.zeros_like(part)))
        both = jnp.concatenate(parts, axis=1)
        return dot(aligned[:, low * LANES : high * LANES], both, NT)

    sums[...] = some(0, usual)

    @pl.when(count > usual * LANES)
    def _():
        sums[...] += some(usual, chunks)


def last_kernel(s, beyond, here, partner, lens, counts, offsets, energy_in, gaps, aligned, coupling, amps, other, *refs):
    if beyond:
        more, _, new_amps, energy, halo, news, sums, far, sems = refs
        halo[: s.first] = other[...]
        rest = pltpu.make_async_copy(
            more, halo.at[pl.ds(s.first, s.rows - s.first)], sems.at[s.pairs]
        )
        rest.start()
        rest.wait()
    else:
        _, new_amps, energy, news, sums, far, sems = refs
        halo = other
    me = here[0]

    def result(p):
        return pltpu.make_async_copy(news.at[p], new_amps.at[p], sems.at[p])

    number = jnp.int32(0)
    for p in range(s.pairs):
        energy[p] = energy_in[p]
        far[number] = p
        kind = s.where_partner(me, partner[me * s.pairs + p])[1]
        number += (kind == 1).astype(jnp.int32)

    def each(act):
        def one(n, _):
            p = far[n]
            right = partner[me * s.pairs + p]
            act(p, right, s.occ + lax.rem(right, s.occ))
            return 0

        lax.fori_loop(0, number, one, 0)

    def finish(p, right, l):
        left = me * s.occ + lax.rem(p, s.occ)
        compacted(s, counts[l], offsets[l], rows_of(lens[right]), aligned.at[p], halo, sums)
        news[p], energy[p] = update(
            s, lens[left], lens[right], sums[...], amps[p], coupling[p], gaps[pl.ds(left, 1), :], gaps[pl.ds(right, 1), :]
        )
        result(p).start()

    each(finish)
    each(lambda p, right, l: result(p).wait())


def position():
    return lax.axis_index(AXES)


def swap(array, role):
    count = 1
    for axis in AXES:
        count *= lax.axis_size(axis)
    route = []
    for low in range(role, count - 1, 2):
        route += [(low, low + 1), (low + 1, low)]
    return lax.ppermute(array, AXES, route)


def local(
    blocks, aux_domain, pao_domain, pao_gap, amplitudes, pair_partner, coupling_list, coupling_coef
):
    s = Sizes(blocks, amplitudes, pair_partner)
    ncpl = coupling_list.shape[1]
    me = position()
    here = me.astype(jnp.int32).reshape(1)
    blocks_t = jnp.swapaxes(blocks, 1, 2)

    smem = pl.BlockSpec(memory_space=pltpu.SMEM)
    vmem = pl.BlockSpec(memory_space=pltpu.VMEM)
    pinned = pl.BlockSpec(memory_space=pltpu.HBM)
    anywhere = pl.BlockSpec(memory_space=pl.ANY)
    plain = pltpu.CompilerParams(vmem_limit_bytes=24 * MIB)
    stepped = pltpu.CompilerParams(
        dimension_semantics=("arbitrary",), vmem_limit_bytes=30 * MIB
    )
    alone = pltpu.CompilerParams(vmem_limit_bytes=24 * MIB)
    square = pl.BlockSpec((1, s.pao, s.pao), lambda p, *_: (p, 0, 0))
    all_dens = pl.BlockSpec((s.occ, s.pao, s.pao), lambda p, *_: (0, 0, 0))
    squares = jax.ShapeDtypeStruct((s.pairs, s.pao, s.pao), jnp.float32)
    dens_shape = jax.ShapeDtypeStruct((s.occ, s.pao, s.pao), jnp.float32)

    def cost(work, data):
        return pl.CostEstimate(flops=work, bytes_accessed=data, transcendentals=0)

    whole, tail, share = packing(s)
    slots = s.pairs + s.pairs // share
    slim = pl.pallas_call(
        functools.partial(slim_kernel, s),
        in_specs=[vmem],
        out_specs=vmem,
        out_shape=jax.ShapeDtypeStruct((slots, s.pao, whole), jnp.bfloat16),
        compiler_params=plain,
        cost_estimate=cost(10**6, 4 * 10**6),
        name="slim",
    )(amplitudes)
    amps_other = swap(slim, 1)
    amps_sibling = swap(slim, 0)

    lens = jnp.sum((pao_domain >= 0).astype(jnp.int32), axis=1)

    lists = 3 * s.occ
    to_sibling, to_other, to_other_more, tables, pao_rows, gap_rows, counts, offsets = pl.pallas_call(
        functools.partial(pack_kernel, s),
        in_specs=[smem] * 3 + [vmem] * 4 + [anywhere],
        out_specs=[pinned] * 3 + [vmem] * 3 + [smem] * 2,
        out_shape=[
            jax.ShapeDtypeStruct((s.rows, LANES), jnp.bfloat16),
            jax.ShapeDtypeStruct((s.first, LANES), jnp.bfloat16),
            jax.ShapeDtypeStruct((s.rows - s.first, LANES), jnp.bfloat16),
            jax.ShapeDtypeStruct((3, 2 * LOW, s.occ * HIGH), jnp.bfloat16),
            jax.ShapeDtypeStruct(pao_domain.shape, pao_domain.dtype),
            jax.ShapeDtypeStruct(pao_gap.shape, pao_gap.dtype),
            jax.ShapeDtypeStruct((lists,), jnp.int32),
            jax.ShapeDtypeStruct((lists,), jnp.int32),
        ],
        scratch_shapes=[
            pltpu.VMEM((3, 2 * LOW, s.occ * HIGH), jnp.float32),
            pltpu.VMEM((3 * s.occ, 2 * LOW, s.occ * HIGH), jnp.float32),
            pltpu.VMEM((2, 2 * LOW, s.occ * HIGH), jnp.bfloat16),
            pltpu.VMEM((2, s.rows + s.pao, LANES), jnp.bfloat16),
            pltpu.SemaphoreType.DMA((3,)),
        ],
        compiler_params=plain,
        cost_estimate=cost(10**11, 10**5),
        name="pack",
    )(here, pair_partner, lens, aux_domain, blocks_t, pao_domain.T, pao_gap.T, slim)

    repeats = s.pairs // s.occ
    both = pl.BlockSpec((repeats, 1, s.pao, s.aux), lambda g: (0, g, 0, 0))
    aligned, dens, to_other, to_sibling = pl.pallas_call(
        functools.partial(own_kernel, s),
        grid=(s.occ,),
        in_specs=[smem] * 4
        + [
            vmem,
            vmem,
            pl.BlockSpec((1, s.pao, s.aux), lambda g: (g, 0, 0)),
            pl.BlockSpec((repeats, 1, s.pao, s.pao), lambda g: (0, g, 0, 0)),
            anywhere,
            anywhere,
        ],
        out_specs=[both, pl.BlockSpec((1, s.pao, s.pao), lambda g: (g, 0, 0)), anywhere, anywhere],
        out_shape=[
            jax.ShapeDtypeStruct((repeats, s.occ, s.pao, s.aux), jnp.bfloat16),
            dens_shape,
            jax.ShapeDtypeStruct(to_other.shape, to_other.dtype),
            jax.ShapeDtypeStruct(to_sibling.shape, to_sibling.dtype),
        ],
        input_output_aliases={8: 2, 9: 3},
        compiler_params=stepped,
        cost_estimate=cost(10**11, 10**5),
        name="own",
    )(
        here, pair_partner, lens, counts, tables, aux_domain, blocks_t,
        amplitudes.reshape(repeats, s.occ, s.pao, s.pao), to_other, to_sibling,
    )
    from_sibling = swap(to_sibling, 0)
    over, to_other = pl.pallas_call(
        functools.partial(count_kernel, s),
        in_specs=[smem] * 2 + [vmem, anywhere],
        out_specs=[smem, anywhere],
        out_shape=[
            jax.ShapeDtypeStruct((1,), jnp.int32),
            jax.ShapeDtypeStruct(to_other.shape, to_other.dtype),
        ],
        input_output_aliases={3: 1},
        compiler_params=plain,
        cost_estimate=cost(10**11, 10**5),
        name="count",
    )(pair_partner, lens, aux_domain, to_other)
    from_other = swap(to_other, 1)
    aligned = aligned.reshape(s.pairs, s.pao, s.aux)

    coupling, exchange, dens = pl.pallas_call(
        functools.partial(near_kernel, s, ncpl),
        grid=(s.pairs,),
        in_specs=[smem] * 7
        + [vmem] * 3
        + [pl.BlockSpec((1, s.pao, s.aux), lambda p: (p, 0, 0))]
        + [anywhere, pinned, anywhere],
        out_specs=[square, square, all_dens],
        out_shape=[squares, squares, dens_shape],
        scratch_shapes=[
            pltpu.VMEM((2 * s.pairs, s.pao, s.pao), jnp.bfloat16),
            pltpu.VMEM((ncpl * s.pao, s.pao), jnp.bfloat16),
            pltpu.VMEM((s.occ, s.pao, s.pao), jnp.float32),
            pltpu.VMEM((s.occ, s.pao, s.aux), jnp.bfloat16),
            pltpu.VMEM((s.rows + s.pao, LANES), jnp.bfloat16),
            pltpu.VMEM((s.pao, s.pao), jnp.float32),
            pltpu.SemaphoreType.DMA((3,)),
        ],
        compiler_params=stepped,
        cost_estimate=cost(10**11, 10**5),
        name="near",
    )(
        here, pair_partner, coupling_list.T, lens, coupling_coef.T, counts, offsets,
        pao_rows, amps_sibling, amplitudes, aligned, dens, blocks_t, from_sibling,
    )

    coupling, densities, some_amps, some_energies = pl.pallas_call(
        functools.partial(far_kernel, s, ncpl),
        in_specs=[smem] * 5 + [vmem] * 7,
        out_specs=[vmem, vmem, pinned, smem],
        out_shape=[
            squares,
            dens_shape,
            jax.ShapeDtypeStruct(amplitudes.shape, amplitudes.dtype),
            jax.ShapeDtypeStruct((s.pairs,), jnp.float32),
        ],
        scratch_shapes=[
            pltpu.VMEM((s.pairs, s.pao, s.pao), jnp.bfloat16),
            pltpu.VMEM((s.pairs, s.pao, s.pao), jnp.bfloat16),
            pltpu.SMEM((s.pairs * ncpl,), jnp.int32),
            pltpu.SMEM((s.pairs * ncpl,), jnp.int32),
            pltpu.SemaphoreType.DMA((s.pairs,)),
        ],
        compiler_params=alone,
        cost_estimate=cost(10**10, 10**5),
        name="far",
    )(
        here, pair_partner, coupling_list.T, lens, coupling_coef.T,
        pao_rows, gap_rows, amps_other, amplitudes, coupling, exchange, dens,
    )

    def last(beyond, energy, arrays, more, some_amps):
        scratch = [
            pltpu.VMEM((s.pairs, s.pao, s.pao), jnp.bfloat16),
            pltpu.VMEM((s.pao, s.pao), jnp.float32),
            pltpu.SMEM((s.pairs,), jnp.int32),
            pltpu.SemaphoreType.DMA((s.pairs + 1,)),
        ]
        if beyond:
            scratch = [pltpu.VMEM((s.rows + s.pao, LANES), jnp.bfloat16)] + scratch
        return pl.pallas_call(
            functools.partial(last_kernel, s, beyond),
            in_specs=[smem] * 6 + [vmem] * 5 + [pinned] * (len(more) + 1),
            out_specs=[pinned, smem],
            out_shape=[
                jax.ShapeDtypeStruct(amplitudes.shape, amplitudes.dtype),
                jax.ShapeDtypeStruct((s.pairs,), jnp.float32),
            ],
            scratch_shapes=scratch,
            input_output_aliases={11 + len(more): 0},
            compiler_params=alone,
            cost_estimate=cost(2 * s.pairs * s.pao * s.pao * s.aux, 2 * 10**7),
            name="again" if beyond else "last",
        )(here, pair_partner, lens, counts, offsets, energy, *arrays, *more, some_amps)

    arrays = (gap_rows, aligned, coupling, amplitudes, from_other)
    new_amps, energies = last(False, some_energies, arrays, (), some_amps)

    def again(ops):
        new_amps, energies, to_other_more, arrays = ops
        return tuple(last(True, energies, arrays, (swap(to_other_more, 1),), new_amps))

    new_amps, energies = lax.cond(
        over[0] > 0, again, lambda ops: ops[:2], (new_amps, energies, to_other_more, arrays)
    )
    return (new_amps, energies, densities)


def solution(mesh):
    return jax.shard_map(
        local,
        mesh=mesh,
        in_specs=(
            P(AXES, None, None),
            P(),
            P(),
            P(),
            P(AXES, None, None),
            P(),
            P(AXES, None),
            P(AXES, None),
        ),
        out_specs=(P(AXES, None, None), P(AXES), P(AXES, None, None)),
        check_vma=False,
    )
```

```python
import functools

import jax
import jax.numpy as jnp
from jax import lax
from jax.experimental import pallas as pl
from jax.experimental.pallas import tpu as pltpu
from jax.sharding import PartitionSpec as P

AXES = ("orb", "pair")
MIB = 1024 * 1024
AUX_IDS = 2048
LOW = 64
HIGH = AUX_IDS // LOW
BASE = 32
LANES = 128
FIRST, WHOLE = 37, 64
NN = (((1,), (0,)), ((), ()))
NT = (((1,), (1,)), ((), ()))
TN = (((0,), (0,)), ((), ()))


def dot(a, b, dims=NN):
    return lax.dot_general(a, b, dims, preferred_element_type=jnp.float32)


def one_where(equal, value=1.0):
    return jnp.where(equal, value, 0.0).astype(jnp.bfloat16)


def iota(shape, dim):
    return lax.broadcasted_iota(jnp.int32, shape, dim)


def live(rows, cols, shape):
    return (iota(shape, 0) < rows) & (iota(shape, 1) < cols)


def kept(amp, rows, cols):
    return jnp.where(live(rows, cols, amp.shape), amp.astype(jnp.float32), 0.0).astype(amp.dtype)


def short_where(equal):
    one = jnp.ones(equal.shape, jnp.bfloat16)
    return jnp.where(equal, one, jnp.zeros_like(one))


def column(row):
    return jnp.broadcast_to(row, (LANES, row.shape[1])).T


def same(col, row):
    parts = []
    for at in range(0, row.shape[1], LANES):
        piece = row[:, at : at + LANES]
        wide = jnp.broadcast_to(piece, (col.shape[0], piece.shape[1]))
        parts.append(short_where(col[:, : piece.shape[1]] == wide))
    return jnp.concatenate(parts, axis=1)


def chunks_of(count):
    return (count + LANES - 1) // LANES


def rows_of(length):
    return (length + 15) // 16 * 16


def swapped(me):
    odd = lax.rem(me, 2)
    return me + 1 - 2 * odd, me - 1 + 2 * odd


class Sizes:
    def __init__(self, blocks, amplitudes, pair_partner):
        self.occ = blocks.shape[0]
        self.aux = blocks.shape[1]
        self.pao = blocks.shape[2]
        self.pairs = amplitudes.shape[0]
        self.npair = pair_partner.shape[0]
        self.nocc = self.npair // self.pairs * self.occ
        self.rows = self.occ * self.pao * (self.aux // LANES)
        self.first = self.rows * FIRST // WHOLE // 16 * 16
        self.room = self.first - self.pao // 2

    def first_orbital(self, pair):
        return pair // self.pairs * self.occ + lax.rem(pair, self.occ)

    def where_partner(self, me, right):
        device = right // self.occ
        sibling, _ = swapped(me)
        kind = jnp.where(device == me, 2, jnp.where(device == sibling, 0, 1))
        return kind * self.occ + lax.rem(right, self.occ), kind


def packing(s):
    whole = s.pao // LANES * LANES
    tail = s.pao - whole
    share = whole // tail
    return whole, tail, share


def slim_kernel(s, amps, out):
    whole, tail, share = packing(s)
    for k in range(s.pairs):
        out[k] = amps[k, :, :whole]
    for g in range(s.pairs // share):
        tails = [amps[g * share + t, :, whole:] for t in range(share)]
        out[s.pairs + g] = jnp.concatenate(tails, axis=1)


def unpack(s, packed, k, out):
    whole, tail, share = packing(s)
    out[:, :whole] = packed[k]
    spot = k % share * tail
    out[:, whole:] = packed[s.pairs + k // share, :, spot : spot + tail]


def bits(values, count, lanes):
    levels = iota((count, lanes), 0).astype(jnp.bfloat16)
    return short_where(levels == jnp.broadcast_to(values.astype(jnp.bfloat16), (count, lanes)))


def places(row, table, k):
    found = dot(table, bits(row // LOW + k * HIGH, table.shape[1], row.shape[1]))
    low = bits(lax.rem(row, LOW), LOW, row.shape[1]).astype(jnp.float32)
    return jnp.sum((found[:LOW] * BASE + found[LOW:]) * low, axis=0, keepdims=True)


def picker(place, chunk):
    wide = 2 * LANES
    middle = chunk * wide + LANES + 1
    spot = (place - jnp.asarray(middle).astype(jnp.float32)).astype(jnp.bfloat16)
    levels = (iota((wide, place.shape[1]), 0) - LANES).astype(jnp.bfloat16)
    return short_where(levels == jnp.broadcast_to(spot, levels.shape))


def chunkwise(s, count, act):
    for c in range(s.aux // (2 * LANES)):
        pl.when(count > c * 2 * LANES)(functools.partial(act, c))


def split_place(place, row):
    part = jnp.where(row < LOW, place // BASE, lax.rem(place, BASE))
    return part.astype(jnp.float32).astype(jnp.bfloat16)


def pack_kernel(
    s, here, partner, lens, aux_rows, blocks, pao_cols, gap_cols, _, to_sibling, to_other, to_other_more, tables, pao_rows, gap_rows, counts, offsets, maps, users, sends, bufs, sems
):
    me = here[0]
    peers = swapped(me)
    pao_rows[...] = pao_cols[...].T
    gap_rows[...] = gap_cols[...].T

    for g, device in enumerate((me,) + peers):
        for k in range(s.occ):
            orbital = jnp.clip(device * s.occ + k, 0, s.nocc - 1)
            row = aux_rows[pl.ds(orbital, 1), :]
            by_high = bits(row // LOW, HIGH, s.aux)
            by_low = bits(lax.rem(row, LOW), LOW, s.aux)
            here_map = dot(jnp.concatenate([by_low, by_low], axis=0), by_high, NT)
            maps[g, :, k * HIGH : (k + 1) * HIGH] = here_map
            users[g * s.occ + k] = jnp.concatenate([here_map] * s.occ, axis=1)
            if g == 0:
                spot = iota((LOW, s.aux), 1) + 1
                parts = jnp.concatenate(
                    [
                        (spot // BASE).astype(jnp.float32).astype(jnp.bfloat16) * by_low,
                        lax.rem(spot, BASE).astype(jnp.float32).astype(jnp.bfloat16) * by_low,
                    ],
                    axis=0,
                )
                tables[2, :, k * HIGH : (k + 1) * HIGH] = dot(parts, by_high, NT).astype(
                    jnp.bfloat16
                )

    wide = s.occ * HIGH
    sub, lane = iota((2 * LOW, 2 * LOW), 0), iota((2 * LOW, 2 * LOW), 1)
    ahead = one_where((lane < LOW) & (lane < lax.rem(sub, LOW)))
    first = one_where(lane < LOW)
    sub, lane = iota((wide, wide), 0), iota((wide, wide), 1)
    above = one_where((sub // HIGH == lane // HIGH) & (sub < lane))
    level = iota((2 * LOW, wide), 0)
    owner = iota((1, wide), 1) // HIGH

    def listing(target, target_device, user, user_device):
        union = jnp.zeros((2 * LOW, wide), jnp.float32)
        for q in range(s.occ):
            uses = jnp.zeros((1, wide), jnp.float32)
            for pair in range(q, s.pairs, s.occ):
                pair += user_device * s.pairs
                inside = (pair >= 0) & (pair < s.npair)
                k = partner[jnp.clip(pair, 0, s.npair - 1)] - target_device * s.occ
                uses += jnp.where((owner == k) & inside, 1.0, 0.0)
            union += uses * users[user * s.occ + q]
        taken = (union > 0.0) & (maps[target] > 0.0)
        flags = one_where(taken)
        total = dot(first, flags)
        place = dot(ahead, flags) + dot(total.astype(jnp.bfloat16), above) + 1.0
        place = jnp.where(taken, place, 0.0).astype(jnp.int32)
        found = [
            jnp.sum(jnp.where(owner == k, total[:1], 0.0)).astype(jnp.int32) for k in range(s.occ)
        ]
        return split_place(place, level), found

    copies = {
        0: [pltpu.make_async_copy(bufs.at[0, pl.ds(0, s.rows)], to_sibling, sems.at[0])],
        1: [
            pltpu.make_async_copy(bufs.at[1, pl.ds(0, s.first)], to_other, sems.at[1]),
            pltpu.make_async_copy(
                bufs.at[1, pl.ds(s.first, s.rows - s.first)], to_other_more, sems.at[2]
            ),
        ],
    }
    for r in (1, 0):
        sends[r], found = listing(0, me, 1 + r, peers[r])
        at = jnp.int32(0)
        for k, count in enumerate(found):
            step = rows_of(lens[me * s.occ + k])

            @pl.when(count > 0)
            def _(k=k, at=at, step=step, count=count):
                place = places(aux_rows[pl.ds(me * s.occ + k, 1), :], sends[r], k)

                def some(c):
                    got = dot(blocks[k], picker(place, c), NT).astype(jnp.bfloat16)
                    spot = pl.multiple_of(at + 2 * c * step, 16)
                    bufs[r, pl.ds(spot, s.pao), :] = got[:, :LANES]

                    @pl.when((2 * c + 1) * LANES < count)
                    def _():
                        bufs[r, pl.ds(pl.multiple_of(spot + step, 16), s.pao), :] = got[:, LANES:]

                chunkwise(s, count, some)

            at += chunks_of(count) * step

        for copy in copies[r]:
            copy.start()

    for r in range(2):
        tables[r], found = listing(1 + r, peers[r], 0, me)
        at = jnp.int32(0)
        for k, count in enumerate(found):
            orbital = jnp.clip(peers[r] * s.occ + k, 0, s.nocc - 1)
            counts[r * s.occ + k] = count
            offsets[r * s.occ + k] = at
            at += chunks_of(count) * rows_of(lens[orbital])
    for k in range(s.occ):
        counts[2 * s.occ + k] = jnp.int32(s.aux)
        offsets[2 * s.occ + k] = jnp.int32(0)

    for copy in copies[1] + copies[0]:
        copy.wait()


def count_kernel(s, partner, lens, aux_rows, _, over):
    devices = s.nocc // s.occ
    full = s.aux // LANES

    def ids(orbital):
        row = aux_rows[pl.ds(orbital, 1), :]
        return dot(bits(row // LOW, HIGH, s.aux), bits(lax.rem(row, LOW), LOW, s.aux), NT)

    over[0] = jnp.int32(0)

    def edge(e, _):
        source = e + 1
        user = source + 1 - 2 * lax.rem(e, 2)
        reads = [partner[user * s.pairs + q] - source * s.occ for q in range(s.pairs)]
        bound = jnp.int32(0)
        for k in range(s.occ):
            used = functools.reduce(jnp.logical_or, [read == k for read in reads])
            bound += jnp.where(used, full * rows_of(lens[source * s.occ + k]), 0)

        @pl.when(bound > s.room)
        def _():
            domains = [ids(user * s.occ + q) for q in range(s.occ)]
            need = jnp.int32(0)
            for k in range(s.occ):
                union = jnp.zeros((HIGH, LOW), jnp.float32)
                for q, domain in enumerate(domains):
                    used = functools.reduce(
                        jnp.logical_or, [read == k for read in reads[q :: s.occ]]
                    )
                    union += jnp.where(used, 1.0, 0.0) * domain
                taken = (union > 0.0) & (ids(source * s.occ + k) > 0.0)
                count = jnp.sum(jnp.where(taken, 1.0, 0.0)).astype(jnp.int32)
                need += chunks_of(count) * rows_of(lens[source * s.occ + k])
            over[0] = jnp.maximum(over[0], (need > s.room).astype(jnp.int32))

        return 0

    lax.fori_loop(0, devices - 2, edge, 0)


def own_kernel(
    s, here, partner, lens, counts, tables, aux_rows, blocks, amps, _, __, aligned, dens, ___, ____
):
    left = pl.program_id(0)
    me = here[0]
    wide = 2 * LANES
    chunks = s.aux // wide
    row = aux_rows[pl.ds(me * s.occ + left, 1), :]
    term = jnp.zeros((s.pao, s.pao), jnp.float32)
    rest = []

    for t in range(s.pairs // s.occ):
        right = partner[me * s.pairs + t * s.occ + left]
        l, kind = s.where_partner(me, right)
        place = places(row, tables[kind], lax.rem(right, s.occ))

        def some(c, t=t, place=place):
            aligned[t, 0, :, c * wide : (c + 1) * wide] = dot(
                blocks[0], picker(place, c), NT
            ).astype(jnp.bfloat16)

        for c in range(chunks - 1):
            some(c)
        rest.append((counts[l] > (chunks - 1) * wide, functools.partial(some, chunks - 1)))
        masked = kept(amps[t, 0], lens[me * s.occ + left], lens[right])
        term += dot(masked, masked, NT)

    dens[0] = term
    for needed, act in rest:
        pl.when(needed)(act)


def column_of(pao_rows, orbital):
    row = pao_rows[pl.ds(orbital, 1), :]
    return column(jnp.where(row < 0, -2, row)).astype(jnp.int16)


def row_of(pao_rows, orbital):
    return pao_rows[pl.ds(orbital, 1), :]


def near_kernel(
    s, ncpl, here, partner, listed, lens, coef, counts, offsets, _, pao_rows, sibling, own, aligned, dens_in, blocks, from_sibling, coupling, exchange, dens, wide, tall, dens_own, near_blocks, halo, sums, sems
):
    p = pl.program_id(0)
    me = here[0]
    buddy = swapped(me)[0]
    low = jnp.minimum(me, buddy)
    fetches = [
        pltpu.make_async_copy(from_sibling, halo.at[pl.ds(0, s.rows), :], sems.at[0]),
        pltpu.make_async_copy(blocks, near_blocks, sems.at[1]),
        pltpu.make_async_copy(dens_in, dens_own, sems.at[2]),
    ]

    @pl.when(p == 0)
    def _():
        for fetch in fetches:
            fetch.start()
        dens[...] = jnp.zeros_like(dens)
        for k in range(s.pairs):
            wide[(me - low) * s.pairs + k] = own[k]
            unpack(s, sibling, k, wide.at[(buddy - low) * s.pairs + k])

    right_col = column_of(pao_rows, partner[me * s.pairs + p])
    left_col = column_of(pao_rows, me * s.occ + lax.rem(p, s.occ))
    left_rows = []
    for c in range(ncpl):
        m = listed[c, p]
        spot = m - low * s.pairs
        inside = (spot >= 0) & (spot < 2 * s.pairs)
        weight = jnp.where(inside, coef[c, p], 0.0)
        left_rows.append(row_of(pao_rows, s.first_orbital(m)))
        right_row = row_of(pao_rows, partner[m]).astype(jnp.int16)
        moved = dot(wide[jnp.clip(spot, 0, 2 * s.pairs - 1)], same(right_col, right_row), NT)
        tall[c * s.pao : (c + 1) * s.pao] = (weight * moved).astype(jnp.bfloat16)
    left_row = jnp.concatenate(left_rows, axis=1).astype(jnp.int16)
    coupling[0] = dot(same(left_col, left_row), tall[...])

    for side in range(2):
        m = (low + side) * s.pairs + p
        near = partner[m] - me * s.occ

        @pl.when((near >= 0) & (near < s.occ))
        def _():
            masked = kept(wide[side * s.pairs + p], lens[s.first_orbital(m)], lens[partner[m]])
            dens[near] += dot(masked, masked, TN)

    @pl.when(p == 0)
    def _():
        for fetch in fetches:
            fetch.wait()

    right = partner[me * s.pairs + p]
    l, kind = s.where_partner(me, right)

    @pl.when(kind == 2)
    def _():
        exchange[0] = dot(aligned[0], near_blocks[lax.rem(right, s.occ)], NT)

    @pl.when(kind == 0)
    def _():
        compacted(s, counts[l], offsets[l], rows_of(lens[right]), aligned.at[0], halo, sums)
        exchange[0] = sums[...]

    @pl.when(p == s.pairs - 1)
    def _():
        dens[...] = (dens[...] + dens_own[...]) * (1.0 / s.pao)


def far_kernel(
    s, ncpl, here, partner, listed, lens, coef, pao_rows, gaps, other, own, near_coupling, exchange, near_dens, coupling, dens, new_amps, energy, wide, news, whose, which, sems
):
    me = here[0]
    device = swapped(me)[1]
    dens[...] = near_dens[...]
    coupling[...] = near_coupling[...]
    for k in range(s.pairs):
        unpack(s, other, k, wide.at[k])

    number = jnp.int32(0)
    for p in range(s.pairs):
        for c in range(ncpl):
            spot = listed[c, p] - device * s.pairs
            whose[number] = p
            which[number] = c
            number += ((spot >= 0) & (spot < s.pairs)).astype(jnp.int32)

    def term(n, _):
        p = whose[n]
        c = which[n]
        m = listed[c, p]
        right_col = column_of(pao_rows, partner[me * s.pairs + p])
        left_col = column_of(pao_rows, me * s.occ + lax.rem(p, s.occ))
        right_row = row_of(pao_rows, partner[m]).astype(jnp.int16)
        left_row = row_of(pao_rows, s.first_orbital(m)).astype(jnp.int16)
        moved = dot(wide[m - device * s.pairs], same(right_col, right_row), NT)
        moved = dot(same(left_col, left_row), moved.astype(jnp.bfloat16))
        coupling[p] += coef[c, p] * moved
        return 0

    lax.fori_loop(0, number, term, 0)

    for k in range(s.pairs):
        m = device * s.pairs + k
        inside = (m >= 0) & (m < s.npair)
        m = jnp.clip(m, 0, s.npair - 1)
        near = partner[m] - me * s.occ

        @pl.when(inside & (near >= 0) & (near < s.occ))
        def _():
            masked = kept(wide[k], lens[s.first_orbital(m)], lens[partner[m]])
            dens[near] += dot(masked, masked, TN) * (1.0 / s.pao)

    def result(p):
        return pltpu.make_async_copy(news.at[p], new_amps.at[p], sems.at[p])

    def finish(p, _):
        left, right = me * s.occ + lax.rem(p, s.occ), partner[me * s.pairs + p]
        kind = s.where_partner(me, right)[1]
        energy[p] = 0.0

        @pl.when(kind != 1)
        def _():
            news[p], energy[p] = update(
                s, lens[left], lens[right], exchange[p], own[p], coupling[p], gaps[pl.ds(left, 1), :], gaps[pl.ds(right, 1), :]
            )
            result(p).start()

        return 0

    def wait(p, _):
        kind = s.where_partner(me, partner[me * s.pairs + p])[1]
        pl.when(kind != 1)(result(p).wait)
        return 0

    lax.fori_loop(0, s.pairs, finish, 0)
    lax.fori_loop(0, s.pairs, wait, 0)


def update(s, lens_left, lens_right, exchange, amp, coupling, gap_left, gap_right):
    left = column(gap_left)
    parts = []
    energy = jnp.zeros((s.pao, LANES), jnp.float32)
    for at in range(0, s.pao, LANES):
        lanes = slice(at, min(at + LANES, s.pao))
        part = amp[:, lanes].astype(jnp.float32)
        shape = part.shape
        mask = live(lens_left, lens_right - at, shape)
        denom = left[:, : shape[1]] + gap_right[:, lanes]
        inverse = pl.reciprocal(denom, approx=True)
        inverse = inverse * (2.0 - denom * inverse)
        moved = (exchange[:, lanes] - coupling[:, lanes]) * inverse
        parts.append(jnp.where(mask, 0.5 * (part - moved), 0.0).astype(jnp.bfloat16))
        term = jnp.where(mask, exchange[:, lanes] * part, 0.0)
        if shape[1] < LANES:
            term = jnp.concatenate([term, jnp.zeros((s.pao, LANES - shape[1]), jnp.float32)], axis=1)
        energy += term
    return jnp.concatenate(parts, axis=1), jnp.sum(energy) / s.pao


def compacted(s, count, at, step, aligned, halo, sums):
    chunks = s.aux // LANES
    usual = chunks - 2

    def some(low, high):
        parts = []
        for c in range(low, high):
            spot = pl.multiple_of(jnp.minimum(at + c * step, halo.shape[0] - s.pao), 16)
            part = halo[pl.ds(spot, s.pao), :]
            parts.append(jnp.where(c * LANES < count, part, jnp.zeros_like(part)))
        both = jnp.concatenate(parts, axis=1)
        return dot(aligned[:, low * LANES : high * LANES], both, NT)

    sums[...] = some(0, usual)

    @pl.when(count > usual * LANES)
    def _():
        sums[...] += some(usual, chunks)


def last_kernel(s, beyond, here, partner, lens, counts, offsets, energy_in, gaps, aligned, coupling, amps, other, *refs):
    if beyond:
        more, _, new_amps, energy, halo, news, sums, far, sems = refs
        halo[: s.first] = other[...]
        rest = pltpu.make_async_copy(
            more, halo.at[pl.ds(s.first, s.rows - s.first)], sems.at[s.pairs]
        )
        rest.start()
        rest.wait()
    else:
        _, new_amps, energy, news, sums, far, sems = refs
        halo = other
    me = here[0]

    def result(p):
        return pltpu.make_async_copy(news.at[p], new_amps.at[p], sems.at[p])

    number = jnp.int32(0)
    for p in range(s.pairs):
        energy[p] = energy_in[p]
        far[number] = p
        kind = s.where_partner(me, partner[me * s.pairs + p])[1]
        number += (kind == 1).astype(jnp.int32)

    def each(act):
        def one(n, _):
            p = far[n]
            right = partner[me * s.pairs + p]
            act(p, right, s.occ + lax.rem(right, s.occ))
            return 0

        lax.fori_loop(0, number, one, 0)

    def finish(p, right, l):
        left = me * s.occ + lax.rem(p, s.occ)
        compacted(s, counts[l], offsets[l], rows_of(lens[right]), aligned.at[p], halo, sums)
        news[p], energy[p] = update(
            s, lens[left], lens[right], sums[...], amps[p], coupling[p], gaps[pl.ds(left, 1), :], gaps[pl.ds(right, 1), :]
        )
        result(p).start()

    each(finish)
    each(lambda p, right, l: result(p).wait())


def position():
    return lax.axis_index(AXES)


def swap(array, role):
    count = 1
    for axis in AXES:
        count *= lax.axis_size(axis)
    route = []
    for low in range(role, count - 1, 2):
        route += [(low, low + 1), (low + 1, low)]
    return lax.ppermute(array, AXES, route)


def run(
    beyond, blocks, aux_domain, pao_domain, pao_gap, amplitudes, pair_partner, coupling_list, coupling_coef
):
    s = Sizes(blocks, amplitudes, pair_partner)
    ncpl = coupling_list.shape[1]
    me = position()
    here = me.astype(jnp.int32).reshape(1)
    blocks_t = jnp.swapaxes(blocks, 1, 2)

    smem = pl.BlockSpec(memory_space=pltpu.SMEM)
    vmem = pl.BlockSpec(memory_space=pltpu.VMEM)
    pinned = pl.BlockSpec(memory_space=pltpu.HBM)
    anywhere = pl.BlockSpec(memory_space=pl.ANY)
    plain = pltpu.CompilerParams(vmem_limit_bytes=24 * MIB)
    stepped = pltpu.CompilerParams(
        dimension_semantics=("arbitrary",), vmem_limit_bytes=30 * MIB
    )
    alone = pltpu.CompilerParams(vmem_limit_bytes=24 * MIB)
    square = pl.BlockSpec((1, s.pao, s.pao), lambda p, *_: (p, 0, 0))
    all_dens = pl.BlockSpec((s.occ, s.pao, s.pao), lambda p, *_: (0, 0, 0))
    squares = jax.ShapeDtypeStruct((s.pairs, s.pao, s.pao), jnp.float32)
    dens_shape = jax.ShapeDtypeStruct((s.occ, s.pao, s.pao), jnp.float32)

    def cost(work, data):
        return pl.CostEstimate(flops=work, bytes_accessed=data, transcendentals=0)

    whole, tail, share = packing(s)
    slots = s.pairs + s.pairs // share
    slim = pl.pallas_call(
        functools.partial(slim_kernel, s),
        in_specs=[vmem],
        out_specs=vmem,
        out_shape=jax.ShapeDtypeStruct((slots, s.pao, whole), jnp.bfloat16),
        compiler_params=plain,
        cost_estimate=cost(10**6, 4 * 10**6),
        name="slim",
    )(amplitudes)
    amps_other = swap(slim, 1)
    amps_sibling = swap(slim, 0)

    lens = jnp.sum((pao_domain >= 0).astype(jnp.int32), axis=1)

    lists = 3 * s.occ
    to_sibling, to_other, to_other_more, tables, pao_rows, gap_rows, counts, offsets = pl.pallas_call(
        functools.partial(pack_kernel, s),
        in_specs=[smem] * 3 + [vmem] * 4 + [anywhere],
        out_specs=[pinned] * 3 + [vmem] * 3 + [smem] * 2,
        out_shape=[
            jax.ShapeDtypeStruct((s.rows, LANES), jnp.bfloat16),
            jax.ShapeDtypeStruct((s.first, LANES), jnp.bfloat16),
            jax.ShapeDtypeStruct((s.rows - s.first, LANES), jnp.bfloat16),
            jax.ShapeDtypeStruct((3, 2 * LOW, s.occ * HIGH), jnp.bfloat16),
            jax.ShapeDtypeStruct(pao_domain.shape, pao_domain.dtype),
            jax.ShapeDtypeStruct(pao_gap.shape, pao_gap.dtype),
            jax.ShapeDtypeStruct((lists,), jnp.int32),
            jax.ShapeDtypeStruct((lists,), jnp.int32),
        ],
        scratch_shapes=[
            pltpu.VMEM((3, 2 * LOW, s.occ * HIGH), jnp.float32),
            pltpu.VMEM((3 * s.occ, 2 * LOW, s.occ * HIGH), jnp.float32),
            pltpu.VMEM((2, 2 * LOW, s.occ * HIGH), jnp.bfloat16),
            pltpu.VMEM((2, s.rows + s.pao, LANES), jnp.bfloat16),
            pltpu.SemaphoreType.DMA((3,)),
        ],
        compiler_params=plain,
        cost_estimate=cost(10**11, 10**5),
        name="pack",
    )(here, pair_partner, lens, aux_domain, blocks_t, pao_domain.T, pao_gap.T, slim)

    repeats = s.pairs // s.occ
    both = pl.BlockSpec((repeats, 1, s.pao, s.aux), lambda g: (0, g, 0, 0))
    aligned, dens, to_other, to_sibling = pl.pallas_call(
        functools.partial(own_kernel, s),
        grid=(s.occ,),
        in_specs=[smem] * 4
        + [
            vmem,
            vmem,
            pl.BlockSpec((1, s.pao, s.aux), lambda g: (g, 0, 0)),
            pl.BlockSpec((repeats, 1, s.pao, s.pao), lambda g: (0, g, 0, 0)),
            anywhere,
            anywhere,
        ],
        out_specs=[both, pl.BlockSpec((1, s.pao, s.pao), lambda g: (g, 0, 0)), anywhere, anywhere],
        out_shape=[
            jax.ShapeDtypeStruct((repeats, s.occ, s.pao, s.aux), jnp.bfloat16),
            dens_shape,
            jax.ShapeDtypeStruct(to_other.shape, to_other.dtype),
            jax.ShapeDtypeStruct(to_sibling.shape, to_sibling.dtype),
        ],
        input_output_aliases={8: 2, 9: 3},
        compiler_params=stepped,
        cost_estimate=cost(10**11, 10**5),
        name="own",
    )(
        here, pair_partner, lens, counts, tables, aux_domain, blocks_t,
        amplitudes.reshape(repeats, s.occ, s.pao, s.pao), to_other, to_sibling,
    )
    from_other = swap(to_other, 1)
    from_sibling = swap(to_sibling, 0)
    aligned = aligned.reshape(s.pairs, s.pao, s.aux)

    (over,) = pl.pallas_call(
        functools.partial(count_kernel, s),
        in_specs=[smem] * 2 + [vmem, anywhere],
        out_specs=[smem],
        out_shape=[jax.ShapeDtypeStruct((1,), jnp.int32)],
        compiler_params=plain,
        cost_estimate=cost(10**11, 10**5),
        name="count",
    )(pair_partner, lens, aux_domain, dens)

    coupling, exchange, dens = pl.pallas_call(
        functools.partial(near_kernel, s, ncpl),
        grid=(s.pairs,),
        in_specs=[smem] * 8
        + [vmem] * 3
        + [pl.BlockSpec((1, s.pao, s.aux), lambda p: (p, 0, 0))]
        + [anywhere, pinned, anywhere],
        out_specs=[square, square, all_dens],
        out_shape=[squares, squares, dens_shape],
        scratch_shapes=[
            pltpu.VMEM((2 * s.pairs, s.pao, s.pao), jnp.bfloat16),
            pltpu.VMEM((ncpl * s.pao, s.pao), jnp.bfloat16),
            pltpu.VMEM((s.occ, s.pao, s.pao), jnp.float32),
            pltpu.VMEM((s.occ, s.pao, s.aux), jnp.bfloat16),
            pltpu.VMEM((s.rows + s.pao, LANES), jnp.bfloat16),
            pltpu.VMEM((s.pao, s.pao), jnp.float32),
            pltpu.SemaphoreType.DMA((3,)),
        ],
        compiler_params=stepped,
        cost_estimate=cost(10**11, 10**5),
        name="near",
    )(
        here, pair_partner, coupling_list.T, lens, coupling_coef.T, counts, offsets, over,
        pao_rows, amps_sibling, amplitudes, aligned, dens, blocks_t, from_sibling,
    )

    coupling, densities, some_amps, some_energies = pl.pallas_call(
        functools.partial(far_kernel, s, ncpl),
        in_specs=[smem] * 5 + [vmem] * 7,
        out_specs=[vmem, vmem, pinned, smem],
        out_shape=[
            squares,
            dens_shape,
            jax.ShapeDtypeStruct(amplitudes.shape, amplitudes.dtype),
            jax.ShapeDtypeStruct((s.pairs,), jnp.float32),
        ],
        scratch_shapes=[
            pltpu.VMEM((s.pairs, s.pao, s.pao), jnp.bfloat16),
            pltpu.VMEM((s.pairs, s.pao, s.pao), jnp.bfloat16),
            pltpu.SMEM((s.pairs * ncpl,), jnp.int32),
            pltpu.SMEM((s.pairs * ncpl,), jnp.int32),
            pltpu.SemaphoreType.DMA((s.pairs,)),
        ],
        compiler_params=alone,
        cost_estimate=cost(10**10, 10**5),
        name="far",
    )(
        here, pair_partner, coupling_list.T, lens, coupling_coef.T,
        pao_rows, gap_rows, amps_other, amplitudes, coupling, exchange, dens,
    )

    more = (swap(to_other_more, 1),) if beyond else ()
    scratch = [
        pltpu.VMEM((s.pairs, s.pao, s.pao), jnp.bfloat16),
        pltpu.VMEM((s.pao, s.pao), jnp.float32),
        pltpu.SMEM((s.pairs,), jnp.int32),
        pltpu.SemaphoreType.DMA((s.pairs + 1,)),
    ]
    if beyond:
        scratch = [pltpu.VMEM((s.rows + s.pao, LANES), jnp.bfloat16)] + scratch
    new_amps, energies = pl.pallas_call(
        functools.partial(last_kernel, s, beyond),
        in_specs=[smem] * 6 + [vmem] * 5 + [pinned] * (len(more) + 1),
        out_specs=[pinned, smem],
        out_shape=[
            jax.ShapeDtypeStruct(amplitudes.shape, amplitudes.dtype),
            jax.ShapeDtypeStruct((s.pairs,), jnp.float32),
        ],
        scratch_shapes=scratch,
        input_output_aliases={11 + len(more): 0},
        compiler_params=alone,
        cost_estimate=cost(2 * s.pairs * s.pao * s.pao * s.aux, 2 * 10**7),
        name="last",
    )(
        here, pair_partner, lens, counts, offsets, some_energies,
        gap_rows, aligned, coupling, amplitudes, from_other, *more, some_amps,
    )
    return new_amps, energies, densities, over


def local(*arrays):
    new_amps, energies, densities, over = run(False, *arrays)
    new_amps, energies = lax.cond(
        over[0] > 0, lambda ops: run(True, *ops[2:])[:2], lambda ops: ops[:2], (new_amps, energies) + arrays
    )
    return (new_amps, energies, densities)


def solution(mesh):
    return jax.shard_map(
        local,
        mesh=mesh,
        in_specs=(
            P(AXES, None, None),
            P(),
            P(),
            P(),
            P(AXES, None, None),
            P(),
            P(AXES, None),
            P(AXES, None),
        ),
        out_specs=(P(AXES, None, None), P(AXES), P(AXES, None, None)),
        check_vma=False,
    )
```

```python
import functools

import jax
import jax.numpy as jnp
from jax import lax
from jax.experimental import pallas as pl
from jax.experimental.pallas import tpu as pltpu
from jax.sharding import PartitionSpec as P

AXES = ("orb", "pair")
MIB = 1024 * 1024
AUX_IDS = 2048
LOW = 64
HIGH = AUX_IDS // LOW
BASE = 32
LANES = 128
FIRST, WHOLE = 40, 64
NN = (((1,), (0,)), ((), ()))
NT = (((1,), (1,)), ((), ()))
TN = (((0,), (0,)), ((), ()))


def dot(a, b, dims=NN):
    return lax.dot_general(a, b, dims, preferred_element_type=jnp.float32)


def one_where(equal, value=1.0):
    return jnp.where(equal, value, 0.0).astype(jnp.bfloat16)


def iota(shape, dim):
    return lax.broadcasted_iota(jnp.int32, shape, dim)


def live(rows, cols, shape):
    return (iota(shape, 0) < rows) & (iota(shape, 1) < cols)


def kept(amp, rows, cols):
    return jnp.where(live(rows, cols, amp.shape), amp.astype(jnp.float32), 0.0).astype(amp.dtype)


def short_where(equal):
    one = jnp.ones(equal.shape, jnp.bfloat16)
    return jnp.where(equal, one, jnp.zeros_like(one))


def column(row):
    return jnp.broadcast_to(row, (LANES, row.shape[1])).T


def same(col, row):
    parts = []
    for at in range(0, row.shape[1], LANES):
        piece = row[:, at : at + LANES]
        wide = jnp.broadcast_to(piece, (col.shape[0], piece.shape[1]))
        parts.append(short_where(col[:, : piece.shape[1]] == wide))
    return jnp.concatenate(parts, axis=1)


def chunks_of(count):
    return (count + LANES - 1) // LANES


def rows_of(length):
    return (length + 15) // 16 * 16


def swapped(me):
    odd = lax.rem(me, 2)
    return me + 1 - 2 * odd, me - 1 + 2 * odd


class Sizes:
    def __init__(self, blocks, amplitudes, pair_partner):
        self.occ = blocks.shape[0]
        self.aux = blocks.shape[1]
        self.pao = blocks.shape[2]
        self.pairs = amplitudes.shape[0]
        self.npair = pair_partner.shape[0]
        self.nocc = self.npair // self.pairs * self.occ
        self.rows = self.occ * self.pao * (self.aux // LANES)
        self.first = self.rows * FIRST // WHOLE // 16 * 16
        self.room = self.first - self.pao // 2

    def first_orbital(self, pair):
        return pair // self.pairs * self.occ + lax.rem(pair, self.occ)

    def where_partner(self, me, right):
        device = right // self.occ
        sibling, _ = swapped(me)
        kind = jnp.where(device == me, 2, jnp.where(device == sibling, 0, 1))
        return kind * self.occ + lax.rem(right, self.occ), kind


def packing(s):
    whole = s.pao // LANES * LANES
    tail = s.pao - whole
    share = whole // tail
    return whole, tail, share


def slim_kernel(s, amps, out):
    whole, tail, share = packing(s)
    for k in range(s.pairs):
        out[k] = amps[k, :, :whole]
    for g in range(s.pairs // share):
        tails = [amps[g * share + t, :, whole:] for t in range(share)]
        out[s.pairs + g] = jnp.concatenate(tails, axis=1)


def unpack(s, packed, k, out):
    whole, tail, share = packing(s)
    out[:, :whole] = packed[k]
    spot = k % share * tail
    out[:, whole:] = packed[s.pairs + k // share, :, spot : spot + tail]


def bits(values, count, lanes):
    levels = iota((count, lanes), 0).astype(jnp.bfloat16)
    return short_where(levels == jnp.broadcast_to(values.astype(jnp.bfloat16), (count, lanes)))


def places(row, table, k):
    found = dot(table, bits(row // LOW + k * HIGH, table.shape[1], row.shape[1]))
    low = bits(lax.rem(row, LOW), LOW, row.shape[1]).astype(jnp.float32)
    return jnp.sum((found[:LOW] * BASE + found[LOW:]) * low, axis=0, keepdims=True)


def picker(place, chunk):
    wide = 2 * LANES
    middle = chunk * wide + LANES + 1
    spot = (place - jnp.asarray(middle).astype(jnp.float32)).astype(jnp.bfloat16)
    levels = (iota((wide, place.shape[1]), 0) - LANES).astype(jnp.bfloat16)
    return short_where(levels == jnp.broadcast_to(spot, levels.shape))


def chunkwise(s, count, act):
    for c in range(s.aux // (2 * LANES)):
        pl.when(count > c * 2 * LANES)(functools.partial(act, c))


def split_place(place, row):
    part = jnp.where(row < LOW, place // BASE, lax.rem(place, BASE))
    return part.astype(jnp.float32).astype(jnp.bfloat16)


def pack_kernel(
    s, here, partner, lens, aux_rows, blocks, pao_cols, gap_cols, _, to_sibling, to_other, to_other_more, tables, pao_rows, gap_rows, counts, offsets, maps, users, sends, bufs, sems
):
    me = here[0]
    peers = swapped(me)
    pao_rows[...] = pao_cols[...].T
    gap_rows[...] = gap_cols[...].T

    for g, device in enumerate((me,) + peers):
        for k in range(s.occ):
            orbital = jnp.clip(device * s.occ + k, 0, s.nocc - 1)
            row = aux_rows[pl.ds(orbital, 1), :]
            by_high = bits(row // LOW, HIGH, s.aux)
            by_low = bits(lax.rem(row, LOW), LOW, s.aux)
            here_map = dot(jnp.concatenate([by_low, by_low], axis=0), by_high, NT)
            maps[g, :, k * HIGH : (k + 1) * HIGH] = here_map
            users[g * s.occ + k] = jnp.concatenate([here_map] * s.occ, axis=1)
            if g == 0:
                spot = iota((LOW, s.aux), 1) + 1
                parts = jnp.concatenate(
                    [
                        (spot // BASE).astype(jnp.float32).astype(jnp.bfloat16) * by_low,
                        lax.rem(spot, BASE).astype(jnp.float32).astype(jnp.bfloat16) * by_low,
                    ],
                    axis=0,
                )
                tables[2, :, k * HIGH : (k + 1) * HIGH] = dot(parts, by_high, NT).astype(
                    jnp.bfloat16
                )

    wide = s.occ * HIGH
    sub, lane = iota((2 * LOW, 2 * LOW), 0), iota((2 * LOW, 2 * LOW), 1)
    ahead = one_where((lane < LOW) & (lane < lax.rem(sub, LOW)))
    first = one_where(lane < LOW)
    sub, lane = iota((wide, wide), 0), iota((wide, wide), 1)
    above = one_where((sub // HIGH == lane // HIGH) & (sub < lane))
    level = iota((2 * LOW, wide), 0)
    owner = iota((1, wide), 1) // HIGH

    def listing(target, target_device, user, user_device):
        union = jnp.zeros((2 * LOW, wide), jnp.float32)
        for q in range(s.occ):
            uses = jnp.zeros((1, wide), jnp.float32)
            for pair in range(q, s.pairs, s.occ):
                pair += user_device * s.pairs
                inside = (pair >= 0) & (pair < s.npair)
                k = partner[jnp.clip(pair, 0, s.npair - 1)] - target_device * s.occ
                uses += jnp.where((owner == k) & inside, 1.0, 0.0)
            union += uses * users[user * s.occ + q]
        taken = (union > 0.0) & (maps[target] > 0.0)
        flags = one_where(taken)
        total = dot(first, flags)
        place = dot(ahead, flags) + dot(total.astype(jnp.bfloat16), above) + 1.0
        place = jnp.where(taken, place, 0.0).astype(jnp.int32)
        found = [
            jnp.sum(jnp.where(owner == k, total[:1], 0.0)).astype(jnp.int32) for k in range(s.occ)
        ]
        return split_place(place, level), found

    copies = {
        0: [pltpu.make_async_copy(bufs.at[0, pl.ds(0, s.rows)], to_sibling, sems.at[0])],
        1: [
            pltpu.make_async_copy(bufs.at[1, pl.ds(0, s.first)], to_other, sems.at[1]),
            pltpu.make_async_copy(
                bufs.at[1, pl.ds(s.first, s.rows - s.first)], to_other_more, sems.at[2]
            ),
        ],
    }
    for r in (1, 0):
        sends[r], found = listing(0, me, 1 + r, peers[r])
        at = jnp.int32(0)
        for k, count in enumerate(found):
            step = rows_of(lens[me * s.occ + k])

            @pl.when(count > 0)
            def _(k=k, at=at, step=step, count=count):
                place = places(aux_rows[pl.ds(me * s.occ + k, 1), :], sends[r], k)

                def some(c):
                    got = dot(blocks[k], picker(place, c), NT).astype(jnp.bfloat16)
                    spot = pl.multiple_of(at + 2 * c * step, 16)
                    bufs[r, pl.ds(spot, s.pao), :] = got[:, :LANES]

                    @pl.when((2 * c + 1) * LANES < count)
                    def _():
                        bufs[r, pl.ds(pl.multiple_of(spot + step, 16), s.pao), :] = got[:, LANES:]

                chunkwise(s, count, some)

            at += chunks_of(count) * step

        for copy in copies[r]:
            copy.start()

    for r in range(2):
        tables[r], found = listing(1 + r, peers[r], 0, me)
        at = jnp.int32(0)
        for k, count in enumerate(found):
            orbital = jnp.clip(peers[r] * s.occ + k, 0, s.nocc - 1)
            counts[r * s.occ + k] = count
            offsets[r * s.occ + k] = at
            at += chunks_of(count) * rows_of(lens[orbital])
    for k in range(s.occ):
        counts[2 * s.occ + k] = jnp.int32(s.aux)
        offsets[2 * s.occ + k] = jnp.int32(0)

    for copy in copies[1] + copies[0]:
        copy.wait()


def count_kernel(s, partner, lens, aux_rows, _, over):
    devices = s.nocc // s.occ
    full = s.aux // LANES

    def ids(orbital):
        row = aux_rows[pl.ds(orbital, 1), :]
        return dot(bits(row // LOW, HIGH, s.aux), bits(lax.rem(row, LOW), LOW, s.aux), NT)

    over[0] = jnp.int32(0)

    def edge(e, _):
        source = e + 1
        user = source + 1 - 2 * lax.rem(e, 2)
        reads = [partner[user * s.pairs + q] - source * s.occ for q in range(s.pairs)]
        bound = jnp.int32(0)
        for k in range(s.occ):
            used = functools.reduce(jnp.logical_or, [read == k for read in reads])
            bound += jnp.where(used, full * rows_of(lens[source * s.occ + k]), 0)

        @pl.when(bound > s.room)
        def _():
            domains = [ids(user * s.occ + q) for q in range(s.occ)]
            need = jnp.int32(0)
            for k in range(s.occ):
                union = jnp.zeros((HIGH, LOW), jnp.float32)
                for q, domain in enumerate(domains):
                    used = functools.reduce(
                        jnp.logical_or, [read == k for read in reads[q :: s.occ]]
                    )
                    union += jnp.where(used, 1.0, 0.0) * domain
                taken = (union > 0.0) & (ids(source * s.occ + k) > 0.0)
                count = jnp.sum(jnp.where(taken, 1.0, 0.0)).astype(jnp.int32)
                need += chunks_of(count) * rows_of(lens[source * s.occ + k])
            over[0] = jnp.maximum(over[0], (need > s.room).astype(jnp.int32))

        return 0

    lax.fori_loop(0, devices - 2, edge, 0)


def own_kernel(
    s, here, partner, lens, counts, tables, aux_rows, blocks, amps, _, __, aligned, dens, ___, ____
):
    left = pl.program_id(0)
    me = here[0]
    wide = 2 * LANES
    chunks = s.aux // wide
    row = aux_rows[pl.ds(me * s.occ + left, 1), :]
    term = jnp.zeros((s.pao, s.pao), jnp.float32)
    rest = []

    for t in range(s.pairs // s.occ):
        right = partner[me * s.pairs + t * s.occ + left]
        l, kind = s.where_partner(me, right)
        place = places(row, tables[kind], lax.rem(right, s.occ))

        def some(c, t=t, place=place):
            aligned[t, 0, :, c * wide : (c + 1) * wide] = dot(
                blocks[0], picker(place, c), NT
            ).astype(jnp.bfloat16)

        for c in range(chunks - 1):
            some(c)
        rest.append((counts[l] > (chunks - 1) * wide, functools.partial(some, chunks - 1)))
        masked = kept(amps[t, 0], lens[me * s.occ + left], lens[right])
        term += dot(masked, masked, NT)

    dens[0] = term
    for needed, act in rest:
        pl.when(needed)(act)


def column_of(pao_rows, orbital):
    row = pao_rows[pl.ds(orbital, 1), :]
    return column(jnp.where(row < 0, -2, row)).astype(jnp.int16)


def row_of(pao_rows, orbital):
    return pao_rows[pl.ds(orbital, 1), :]


def near_kernel(
    s, ncpl, here, partner, listed, lens, coef, counts, offsets, _, pao_rows, sibling, own, aligned, dens_in, blocks, from_sibling, coupling, exchange, dens, wide, tall, dens_own, near_blocks, halo, sems
):
    p = pl.program_id(0)
    me = here[0]
    buddy = swapped(me)[0]
    low = jnp.minimum(me, buddy)
    fetches = [
        pltpu.make_async_copy(from_sibling, halo.at[pl.ds(0, s.rows), :], sems.at[0]),
        pltpu.make_async_copy(blocks, near_blocks, sems.at[1]),
        pltpu.make_async_copy(dens_in, dens_own, sems.at[2]),
    ]

    @pl.when(p == 0)
    def _():
        for fetch in fetches:
            fetch.start()
        dens[...] = jnp.zeros_like(dens)
        for k in range(s.pairs):
            wide[(me - low) * s.pairs + k] = own[k]
            unpack(s, sibling, k, wide.at[(buddy - low) * s.pairs + k])

    right_col = column_of(pao_rows, partner[me * s.pairs + p])
    left_col = column_of(pao_rows, me * s.occ + lax.rem(p, s.occ))
    left_rows = []
    for c in range(ncpl):
        m = listed[c, p]
        spot = m - low * s.pairs
        inside = (spot >= 0) & (spot < 2 * s.pairs)
        weight = jnp.where(inside, coef[c, p], 0.0)
        left_rows.append(row_of(pao_rows, s.first_orbital(m)))
        right_row = row_of(pao_rows, partner[m]).astype(jnp.int16)
        moved = dot(wide[jnp.clip(spot, 0, 2 * s.pairs - 1)], same(right_col, right_row), NT)
        tall[c * s.pao : (c + 1) * s.pao] = (weight * moved).astype(jnp.bfloat16)
    left_row = jnp.concatenate(left_rows, axis=1).astype(jnp.int16)
    coupling[0] = dot(same(left_col, left_row), tall[...])

    for side in range(2):
        m = (low + side) * s.pairs + p
        near = partner[m] - me * s.occ

        @pl.when((near >= 0) & (near < s.occ))
        def _():
            masked = kept(wide[side * s.pairs + p], lens[s.first_orbital(m)], lens[partner[m]])
            dens[near] += dot(masked, masked, TN)

    @pl.when(p == 0)
    def _():
        for fetch in fetches:
            fetch.wait()

    right = partner[me * s.pairs + p]
    l, kind = s.where_partner(me, right)

    @pl.when(kind == 2)
    def _():
        exchange[0] = dot(aligned[0], near_blocks[lax.rem(right, s.occ)], NT)

    @pl.when(kind == 0)
    def _():
        usual = s.aux - 2 * LANES
        use = functools.partial(
            compacted, s, counts[l], offsets[l], rows_of(lens[right]), aligned.at[0], halo
        )
        exchange[0] = use(0, usual)

        @pl.when(counts[l] > usual)
        def _():
            exchange[0] += use(usual, s.aux)

    @pl.when(p == s.pairs - 1)
    def _():
        dens[...] = (dens[...] + dens_own[...]) * (1.0 / s.pao)


def far_kernel(
    s, ncpl, here, partner, listed, lens, coef, pao_rows, gaps, other, own, near_coupling, exchange, near_dens, coupling, dens, new_amps, energy, wide, news, whose, which, sems
):
    me = here[0]
    device = swapped(me)[1]
    dens[...] = near_dens[...]
    coupling[...] = near_coupling[...]
    for k in range(s.pairs):
        unpack(s, other, k, wide.at[k])

    number = jnp.int32(0)
    for p in range(s.pairs):
        for c in range(ncpl):
            spot = listed[c, p] - device * s.pairs
            whose[number] = p
            which[number] = c
            number += ((spot >= 0) & (spot < s.pairs)).astype(jnp.int32)

    def term(n):
        weight = jnp.where(n < number, 1.0, 0.0)
        n = jnp.minimum(n, number - 1)
        p, c = whose[n], which[n]
        m = listed[c, p]
        right_col = column_of(pao_rows, partner[me * s.pairs + p])
        left_col = column_of(pao_rows, me * s.occ + lax.rem(p, s.occ))
        right_row = row_of(pao_rows, partner[m]).astype(jnp.int16)
        left_row = row_of(pao_rows, s.first_orbital(m)).astype(jnp.int16)
        moved = dot(wide[m - device * s.pairs], same(right_col, right_row), NT)
        return p, weight * coef[c, p] * dot(same(left_col, left_row), moved.astype(jnp.bfloat16))

    def some(n, _):
        terms = [term(2 * n), term(2 * n + 1)]
        for p, value in terms:
            coupling[p] += value
        return 0

    lax.fori_loop(0, (number + 1) // 2, some, 0)

    for k in range(s.pairs):
        m = device * s.pairs + k
        inside = (m >= 0) & (m < s.npair)
        m = jnp.clip(m, 0, s.npair - 1)
        near = partner[m] - me * s.occ

        @pl.when(inside & (near >= 0) & (near < s.occ))
        def _():
            masked = kept(wide[k], lens[s.first_orbital(m)], lens[partner[m]])
            dens[near] += dot(masked, masked, TN) * (1.0 / s.pao)

    def result(p):
        return pltpu.make_async_copy(news.at[p], new_amps.at[p], sems.at[p])

    def finish(p, _):
        left, right = me * s.occ + lax.rem(p, s.occ), partner[me * s.pairs + p]
        kind = s.where_partner(me, right)[1]
        energy[p] = 0.0

        @pl.when(kind != 1)
        def _():
            news[p], energy[p] = update(
                s, lens[left], lens[right], exchange[p], own[p], coupling[p], gaps[pl.ds(left, 1), :], gaps[pl.ds(right, 1), :]
            )
            result(p).start()

        return 0

    def wait(p, _):
        kind = s.where_partner(me, partner[me * s.pairs + p])[1]
        pl.when(kind != 1)(result(p).wait)
        return 0

    lax.fori_loop(0, s.pairs, finish, 0)
    lax.fori_loop(0, s.pairs, wait, 0)


def update(s, lens_left, lens_right, exchange, amp, coupling, gap_left, gap_right):
    left = column(gap_left)
    parts = []
    energy = jnp.zeros((s.pao, LANES), jnp.float32)
    for at in range(0, s.pao, LANES):
        lanes = slice(at, min(at + LANES, s.pao))
        part = amp[:, lanes].astype(jnp.float32)
        shape = part.shape
        mask = live(lens_left, lens_right - at, shape)
        denom = left[:, : shape[1]] + gap_right[:, lanes]
        inverse = pl.reciprocal(denom, approx=True)
        inverse = inverse * (2.0 - denom * inverse)
        moved = (exchange[:, lanes] - coupling[:, lanes]) * inverse
        parts.append(jnp.where(mask, 0.5 * (part - moved), 0.0).astype(jnp.bfloat16))
        term = jnp.where(mask, exchange[:, lanes] * part, 0.0)
        if shape[1] < LANES:
            term = jnp.concatenate([term, jnp.zeros((s.pao, LANES - shape[1]), jnp.float32)], axis=1)
        energy += term
    return jnp.concatenate(parts, axis=1), jnp.sum(energy) / s.pao


def compacted(s, count, at, step, aligned, halo, low, high):
    parts = []
    for c in range(low // LANES, high // LANES):
        spot = pl.multiple_of(jnp.minimum(at + c * step, halo.shape[0] - s.pao), 16)
        part = halo[pl.ds(spot, s.pao), :]
        parts.append(jnp.where(c * LANES < count, part, jnp.zeros_like(part)))
    return dot(aligned[:, low:high], jnp.concatenate(parts, axis=1), NT)


def last_kernel(s, beyond, here, partner, lens, counts, offsets, energy_in, gaps, aligned, coupling, amps, other, *refs):
    if beyond:
        more, _, new_amps, energy, halo, news, sums, far, sems = refs
        halo[: s.first] = other[...]
        rest = pltpu.make_async_copy(
            more, halo.at[pl.ds(s.first, s.rows - s.first)], sems.at[s.pairs]
        )
        rest.start()
        rest.wait()
    else:
        _, new_amps, energy, news, sums, far, sems = refs
        halo = other
    me = here[0]

    def result(n):
        return pltpu.make_async_copy(news.at[n], new_amps.at[far[n]], sems.at[n])

    number = jnp.int32(0)
    for p in range(s.pairs):
        energy[p] = energy_in[p]
        far[number] = p
        kind = s.where_partner(me, partner[me * s.pairs + p])[1]
        number += (kind == 1).astype(jnp.int32)

    usual = s.aux - 2 * LANES

    def pair_of(n):
        p = far[jnp.minimum(n, number - 1)]
        right = partner[me * s.pairs + p]
        return p, right, s.occ + lax.rem(right, s.occ)

    def some(n, _):
        pairs = [pair_of(2 * n + t) for t in range(2)]
        for t, (p, right, l) in enumerate(pairs):
            sums[t] = compacted(s, counts[l], offsets[l], rows_of(lens[right]), aligned.at[p], halo, 0, usual)
        for t, (p, right, l) in enumerate(pairs):

            @pl.when(counts[l] > usual)
            def _():
                sums[t] += compacted(
                    s, counts[l], offsets[l], rows_of(lens[right]), aligned.at[p], halo, usual, s.aux
                )

        for t, (p, right, l) in enumerate(pairs):
            left = me * s.occ + lax.rem(p, s.occ)
            news[2 * n + t], energy[p] = update(
                s, lens[left], lens[right], sums[t], amps[p], coupling[p], gaps[pl.ds(left, 1), :], gaps[pl.ds(right, 1), :]
            )
        for t in range(2):
            pl.when(2 * n + t < number)(result(2 * n + t).start)
        return 0

    def wait(n, _):
        result(n).wait()
        return 0

    lax.fori_loop(0, (number + 1) // 2, some, 0)
    lax.fori_loop(0, number, wait, 0)


def position():
    return lax.axis_index(AXES)


def swap(array, role):
    count = 1
    for axis in AXES:
        count *= lax.axis_size(axis)
    route = []
    for low in range(role, count - 1, 2):
        route += [(low, low + 1), (low + 1, low)]
    return lax.ppermute(array, AXES, route)


def run(
    beyond, blocks, aux_domain, pao_domain, pao_gap, amplitudes, pair_partner, coupling_list, coupling_coef
):
    s = Sizes(blocks, amplitudes, pair_partner)
    ncpl = coupling_list.shape[1]
    me = position()
    here = me.astype(jnp.int32).reshape(1)
    blocks_t = jnp.swapaxes(blocks, 1, 2)

    smem = pl.BlockSpec(memory_space=pltpu.SMEM)
    vmem = pl.BlockSpec(memory_space=pltpu.VMEM)
    pinned = pl.BlockSpec(memory_space=pltpu.HBM)
    anywhere = pl.BlockSpec(memory_space=pl.ANY)
    plain = pltpu.CompilerParams(vmem_limit_bytes=24 * MIB)
    stepped = pltpu.CompilerParams(
        dimension_semantics=("arbitrary",), vmem_limit_bytes=30 * MIB
    )
    alone = pltpu.CompilerParams(vmem_limit_bytes=24 * MIB)
    square = pl.BlockSpec((1, s.pao, s.pao), lambda p, *_: (p, 0, 0))
    all_dens = pl.BlockSpec((s.occ, s.pao, s.pao), lambda p, *_: (0, 0, 0))
    squares = jax.ShapeDtypeStruct((s.pairs, s.pao, s.pao), jnp.float32)
    dens_shape = jax.ShapeDtypeStruct((s.occ, s.pao, s.pao), jnp.float32)

    def cost(work, data):
        return pl.CostEstimate(flops=work, bytes_accessed=data, transcendentals=0)

    whole, tail, share = packing(s)
    slots = s.pairs + s.pairs // share
    slim = pl.pallas_call(
        functools.partial(slim_kernel, s),
        in_specs=[vmem],
        out_specs=vmem,
        out_shape=jax.ShapeDtypeStruct((slots, s.pao, whole), jnp.bfloat16),
        compiler_params=plain,
        cost_estimate=cost(10**6, 4 * 10**6),
        name="slim",
    )(amplitudes)
    amps_other = swap(slim, 1)
    amps_sibling = swap(slim, 0)

    lens = jnp.sum((pao_domain >= 0).astype(jnp.int32), axis=1)

    lists = 3 * s.occ
    to_sibling, to_other, to_other_more, tables, pao_rows, gap_rows, counts, offsets = pl.pallas_call(
        functools.partial(pack_kernel, s),
        in_specs=[smem] * 3 + [vmem] * 4 + [anywhere],
        out_specs=[pinned] * 3 + [vmem] * 3 + [smem] * 2,
        out_shape=[
            jax.ShapeDtypeStruct((s.rows, LANES), jnp.bfloat16),
            jax.ShapeDtypeStruct((s.first, LANES), jnp.bfloat16),
            jax.ShapeDtypeStruct((s.rows - s.first, LANES), jnp.bfloat16),
            jax.ShapeDtypeStruct((3, 2 * LOW, s.occ * HIGH), jnp.bfloat16),
            jax.ShapeDtypeStruct(pao_domain.shape, pao_domain.dtype),
            jax.ShapeDtypeStruct(pao_gap.shape, pao_gap.dtype),
            jax.ShapeDtypeStruct((lists,), jnp.int32),
            jax.ShapeDtypeStruct((lists,), jnp.int32),
        ],
        scratch_shapes=[
            pltpu.VMEM((3, 2 * LOW, s.occ * HIGH), jnp.float32),
            pltpu.VMEM((3 * s.occ, 2 * LOW, s.occ * HIGH), jnp.float32),
            pltpu.VMEM((2, 2 * LOW, s.occ * HIGH), jnp.bfloat16),
            pltpu.VMEM((2, s.rows + s.pao, LANES), jnp.bfloat16),
            pltpu.SemaphoreType.DMA((3,)),
        ],
        compiler_params=plain,
        cost_estimate=cost(10**11, 10**5),
        name="pack",
    )(here, pair_partner, lens, aux_domain, blocks_t, pao_domain.T, pao_gap.T, slim)

    repeats = s.pairs // s.occ
    both = pl.BlockSpec((repeats, 1, s.pao, s.aux), lambda g: (0, g, 0, 0))
    aligned, dens, to_other, to_sibling = pl.pallas_call(
        functools.partial(own_kernel, s),
        grid=(s.occ,),
        in_specs=[smem] * 4
        + [
            vmem,
            vmem,
            pl.BlockSpec((1, s.pao, s.aux), lambda g: (g, 0, 0)),
            pl.BlockSpec((repeats, 1, s.pao, s.pao), lambda g: (0, g, 0, 0)),
            anywhere,
            anywhere,
        ],
        out_specs=[both, pl.BlockSpec((1, s.pao, s.pao), lambda g: (g, 0, 0)), anywhere, anywhere],
        out_shape=[
            jax.ShapeDtypeStruct((repeats, s.occ, s.pao, s.aux), jnp.bfloat16),
            dens_shape,
            jax.ShapeDtypeStruct(to_other.shape, to_other.dtype),
            jax.ShapeDtypeStruct(to_sibling.shape, to_sibling.dtype),
        ],
        input_output_aliases={8: 2, 9: 3},
        compiler_params=stepped,
        cost_estimate=cost(10**11, 10**5),
        name="own",
    )(
        here, pair_partner, lens, counts, tables, aux_domain, blocks_t,
        amplitudes.reshape(repeats, s.occ, s.pao, s.pao), to_other, to_sibling,
    )
    from_other = swap(to_other, 1)
    from_sibling = swap(to_sibling, 0)
    aligned = aligned.reshape(s.pairs, s.pao, s.aux)

    (over,) = pl.pallas_call(
        functools.partial(count_kernel, s),
        in_specs=[smem] * 2 + [vmem, anywhere],
        out_specs=[smem],
        out_shape=[jax.ShapeDtypeStruct((1,), jnp.int32)],
        compiler_params=plain,
        cost_estimate=cost(10**11, 10**5),
        name="count",
    )(pair_partner, lens, aux_domain, dens)

    coupling, exchange, dens = pl.pallas_call(
        functools.partial(near_kernel, s, ncpl),
        grid=(s.pairs,),
        in_specs=[smem] * 8
        + [vmem] * 3
        + [pl.BlockSpec((1, s.pao, s.aux), lambda p: (p, 0, 0))]
        + [anywhere, pinned, anywhere],
        out_specs=[square, square, all_dens],
        out_shape=[squares, squares, dens_shape],
        scratch_shapes=[
            pltpu.VMEM((2 * s.pairs, s.pao, s.pao), jnp.bfloat16),
            pltpu.VMEM((ncpl * s.pao, s.pao), jnp.bfloat16),
            pltpu.VMEM((s.occ, s.pao, s.pao), jnp.float32),
            pltpu.VMEM((s.occ, s.pao, s.aux), jnp.bfloat16),
            pltpu.VMEM((s.rows + s.pao, LANES), jnp.bfloat16),
            pltpu.SemaphoreType.DMA((3,)),
        ],
        compiler_params=stepped,
        cost_estimate=cost(10**11, 10**5),
        name="near",
    )(
        here, pair_partner, coupling_list.T, lens, coupling_coef.T, counts, offsets, over,
        pao_rows, amps_sibling, amplitudes, aligned, dens, blocks_t, from_sibling,
    )

    coupling, densities, some_amps, some_energies = pl.pallas_call(
        functools.partial(far_kernel, s, ncpl),
        in_specs=[smem] * 5 + [vmem] * 7,
        out_specs=[vmem, vmem, pinned, smem],
        out_shape=[
            squares,
            dens_shape,
            jax.ShapeDtypeStruct(amplitudes.shape, amplitudes.dtype),
            jax.ShapeDtypeStruct((s.pairs,), jnp.float32),
        ],
        scratch_shapes=[
            pltpu.VMEM((s.pairs, s.pao, s.pao), jnp.bfloat16),
            pltpu.VMEM((s.pairs, s.pao, s.pao), jnp.bfloat16),
            pltpu.SMEM((s.pairs * ncpl,), jnp.int32),
            pltpu.SMEM((s.pairs * ncpl,), jnp.int32),
            pltpu.SemaphoreType.DMA((s.pairs,)),
        ],
        compiler_params=alone,
        cost_estimate=cost(10**10, 10**5),
        name="far",
    )(
        here, pair_partner, coupling_list.T, lens, coupling_coef.T,
        pao_rows, gap_rows, amps_other, amplitudes, coupling, exchange, dens,
    )

    more = (swap(to_other_more, 1),) if beyond else ()
    scratch = [
        pltpu.VMEM((s.pairs, s.pao, s.pao), jnp.bfloat16),
        pltpu.VMEM((2, s.pao, s.pao), jnp.float32),
        pltpu.SMEM((s.pairs,), jnp.int32),
        pltpu.SemaphoreType.DMA((s.pairs + 1,)),
    ]
    if beyond:
        scratch = [pltpu.VMEM((s.rows + s.pao, LANES), jnp.bfloat16)] + scratch
    new_amps, energies = pl.pallas_call(
        functools.partial(last_kernel, s, beyond),
        in_specs=[smem] * 6 + [vmem] * 5 + [pinned] * (len(more) + 1),
        out_specs=[pinned, smem],
        out_shape=[
            jax.ShapeDtypeStruct(amplitudes.shape, amplitudes.dtype),
            jax.ShapeDtypeStruct((s.pairs,), jnp.float32),
        ],
        scratch_shapes=scratch,
        input_output_aliases={11 + len(more): 0},
        compiler_params=alone,
        cost_estimate=cost(2 * s.pairs * s.pao * s.pao * s.aux, 2 * 10**7),
        name="last",
    )(
        here, pair_partner, lens, counts, offsets, some_energies,
        gap_rows, aligned, coupling, amplitudes, from_other, *more, some_amps,
    )
    return new_amps, energies, densities, over


def local(*arrays):
    new_amps, energies, densities, over = run(False, *arrays)
    new_amps, energies = lax.cond(
        over[0] > 0, lambda ops: run(True, *ops[2:])[:2], lambda ops: ops[:2], (new_amps, energies) + arrays
    )
    return (new_amps, energies, densities)


def solution(mesh):
    return jax.shard_map(
        local,
        mesh=mesh,
        in_specs=(
            P(AXES, None, None),
            P(),
            P(),
            P(),
            P(AXES, None, None),
            P(),
            P(AXES, None),
            P(AXES, None),
        ),
        out_specs=(P(AXES, None, None), P(AXES), P(AXES, None, None)),
        check_vma=False,
    )
```

```python
import functools

import jax
import jax.numpy as jnp
from jax import lax
from jax.experimental import pallas as pl
from jax.experimental.pallas import tpu as pltpu
from jax.sharding import PartitionSpec as P

AXES = ("orb", "pair")
MIB = 1024 * 1024
AUX_IDS = 2048
LOW = 64
HIGH = AUX_IDS // LOW
BASE = 32
LANES = 128
FIRST, WHOLE = 40, 64
NN = (((1,), (0,)), ((), ()))
NT = (((1,), (1,)), ((), ()))
TN = (((0,), (0,)), ((), ()))


def dot(a, b, dims=NN):
    return lax.dot_general(a, b, dims, preferred_element_type=jnp.float32)


def one_where(equal, value=1.0):
    return jnp.where(equal, value, 0.0).astype(jnp.bfloat16)


def iota(shape, dim):
    return lax.broadcasted_iota(jnp.int32, shape, dim)


def live(rows, cols, shape):
    return (iota(shape, 0) < rows) & (iota(shape, 1) < cols)


def kept(amp, rows, cols):
    return jnp.where(live(rows, cols, amp.shape), amp.astype(jnp.float32), 0.0).astype(amp.dtype)


def short_where(equal):
    one = jnp.ones(equal.shape, jnp.bfloat16)
    return jnp.where(equal, one, jnp.zeros_like(one))


def column(row):
    return jnp.broadcast_to(row, (LANES, row.shape[1])).T


def same(col, row):
    parts = []
    for at in range(0, row.shape[1], LANES):
        piece = row[:, at : at + LANES]
        wide = jnp.broadcast_to(piece, (col.shape[0], piece.shape[1]))
        parts.append(short_where(col[:, : piece.shape[1]] == wide))
    return jnp.concatenate(parts, axis=1)


def chunks_of(count):
    return (count + LANES - 1) // LANES


def rows_of(length):
    return (length + 15) // 16 * 16


def swapped(me):
    odd = lax.rem(me, 2)
    return me + 1 - 2 * odd, me - 1 + 2 * odd


class Sizes:
    def __init__(self, blocks, amplitudes, pair_partner):
        self.occ = blocks.shape[0]
        self.aux = blocks.shape[1]
        self.pao = blocks.shape[2]
        self.pairs = amplitudes.shape[0]
        self.npair = pair_partner.shape[0]
        self.nocc = self.npair // self.pairs * self.occ
        self.rows = self.occ * self.pao * (self.aux // LANES)
        self.first = self.rows * FIRST // WHOLE // 16 * 16
        self.room = self.first - self.pao // 2

    def first_orbital(self, pair):
        return pair // self.pairs * self.occ + lax.rem(pair, self.occ)

    def where_partner(self, me, right):
        device = right // self.occ
        sibling, _ = swapped(me)
        kind = jnp.where(device == me, 2, jnp.where(device == sibling, 0, 1))
        return kind * self.occ + lax.rem(right, self.occ), kind


def packing(s):
    whole = s.pao // LANES * LANES
    tail = s.pao - whole
    share = whole // tail
    return whole, tail, share


def slim_kernel(s, amps, out):
    whole, tail, share = packing(s)
    for k in range(s.pairs):
        out[k] = amps[k, :, :whole]
    for g in range(s.pairs // share):
        tails = [amps[g * share + t, :, whole:] for t in range(share)]
        out[s.pairs + g] = jnp.concatenate(tails, axis=1)


def unpack(s, packed, k, out):
    whole, tail, share = packing(s)
    out[:, :whole] = packed[k]
    spot = k % share * tail
    out[:, whole:] = packed[s.pairs + k // share, :, spot : spot + tail]


def bits(values, count, lanes):
    levels = iota((count, lanes), 0).astype(jnp.bfloat16)
    return short_where(levels == jnp.broadcast_to(values.astype(jnp.bfloat16), (count, lanes)))


def places(row, table, k):
    found = dot(table, bits(row // LOW + k * HIGH, table.shape[1], row.shape[1]))
    low = bits(lax.rem(row, LOW), LOW, row.shape[1]).astype(jnp.float32)
    return jnp.sum((found[:LOW] * BASE + found[LOW:]) * low, axis=0, keepdims=True)


def picker(place, chunk):
    wide = 2 * LANES
    middle = chunk * wide + LANES + 1
    spot = (place - jnp.asarray(middle).astype(jnp.float32)).astype(jnp.bfloat16)
    levels = (iota((wide, place.shape[1]), 0) - LANES).astype(jnp.bfloat16)
    return short_where(levels == jnp.broadcast_to(spot, levels.shape))


def chunkwise(s, count, act):
    for c in range(s.aux // (2 * LANES)):
        pl.when(count > c * 2 * LANES)(functools.partial(act, c))


def split_place(place, row):
    part = jnp.where(row < LOW, place // BASE, lax.rem(place, BASE))
    return part.astype(jnp.float32).astype(jnp.bfloat16)


def pack_kernel(
    s, here, partner, lens, aux_rows, blocks, pao_cols, gap_cols, _, to_sibling, to_other, to_other_more, tables, pao_rows, gap_rows, counts, offsets, maps, users, sends, needed, bufs, sems
):
    me = here[0]
    peers = swapped(me)
    pao_rows[...] = pao_cols[...].T
    gap_rows[...] = gap_cols[...].T

    for g, device in enumerate((me,) + peers):
        for k in range(s.occ):
            orbital = jnp.clip(device * s.occ + k, 0, s.nocc - 1)
            row = aux_rows[pl.ds(orbital, 1), :]
            by_high = bits(row // LOW, HIGH, s.aux)
            by_low = bits(lax.rem(row, LOW), LOW, s.aux)
            here_map = dot(jnp.concatenate([by_low, by_low], axis=0), by_high, NT)
            maps[g, :, k * HIGH : (k + 1) * HIGH] = here_map
            users[g * s.occ + k] = jnp.concatenate([here_map] * s.occ, axis=1)
            if g == 0:
                spot = iota((LOW, s.aux), 1) + 1
                parts = jnp.concatenate(
                    [
                        (spot // BASE).astype(jnp.float32).astype(jnp.bfloat16) * by_low,
                        lax.rem(spot, BASE).astype(jnp.float32).astype(jnp.bfloat16) * by_low,
                    ],
                    axis=0,
                )
                tables[2, :, k * HIGH : (k + 1) * HIGH] = dot(parts, by_high, NT).astype(
                    jnp.bfloat16
                )

    wide = s.occ * HIGH
    sub, lane = iota((2 * LOW, 2 * LOW), 0), iota((2 * LOW, 2 * LOW), 1)
    ahead = one_where((lane < LOW) & (lane < lax.rem(sub, LOW)))
    first = one_where(lane < LOW)
    sub, lane = iota((wide, wide), 0), iota((wide, wide), 1)
    above = one_where((sub // HIGH == lane // HIGH) & (sub < lane))
    level = iota((2 * LOW, wide), 0)
    owner = iota((1, wide), 1) // HIGH

    def listing(target, target_device, user, user_device):
        union = jnp.zeros((2 * LOW, wide), jnp.float32)
        for q in range(s.occ):
            uses = jnp.zeros((1, wide), jnp.float32)
            for pair in range(q, s.pairs, s.occ):
                pair += user_device * s.pairs
                inside = (pair >= 0) & (pair < s.npair)
                k = partner[jnp.clip(pair, 0, s.npair - 1)] - target_device * s.occ
                uses += jnp.where((owner == k) & inside, 1.0, 0.0)
            union += uses * users[user * s.occ + q]
        taken = (union > 0.0) & (maps[target] > 0.0)
        flags = one_where(taken)
        total = dot(first, flags)
        place = dot(ahead, flags) + dot(total.astype(jnp.bfloat16), above) + 1.0
        place = jnp.where(taken, place, 0.0).astype(jnp.int32)
        found = [
            jnp.sum(jnp.where(owner == k, total[:1], 0.0)).astype(jnp.int32) for k in range(s.occ)
        ]
        return split_place(place, level), found

    copies = {
        0: [pltpu.make_async_copy(bufs.at[0, pl.ds(0, s.rows)], to_sibling, sems.at[0])],
        1: [
            pltpu.make_async_copy(bufs.at[1, pl.ds(0, s.first)], to_other, sems.at[1]),
            pltpu.make_async_copy(
                bufs.at[1, pl.ds(s.first, s.rows - s.first)], to_other_more, sems.at[2]
            ),
        ],
    }
    for r in (1, 0):
        sends[r], found = listing(0, me, 1 + r, peers[r])
        for k, count in enumerate(found):
            needed[k] = count

        def send(k, at, r=r):
            count = needed[k]
            step = rows_of(lens[me * s.occ + k])

            @pl.when(count > 0)
            def _():
                place = places(aux_rows[pl.ds(me * s.occ + k, 1), :], sends[r], k)

                def some(c):
                    got = dot(blocks[k], picker(place, c), NT).astype(jnp.bfloat16)
                    spot = pl.multiple_of(at + 2 * c * step, 16)
                    bufs[r, pl.ds(spot, s.pao), :] = got[:, :LANES]

                    @pl.when((2 * c + 1) * LANES < count)
                    def _():
                        bufs[r, pl.ds(pl.multiple_of(spot + step, 16), s.pao), :] = got[:, LANES:]

                chunkwise(s, count, some)

            return at + chunks_of(count) * step

        lax.fori_loop(0, s.occ, send, jnp.int32(0))
        for copy in copies[r]:
            copy.start()

    for r in range(2):
        tables[r], found = listing(1 + r, peers[r], 0, me)
        at = jnp.int32(0)
        for k, count in enumerate(found):
            orbital = jnp.clip(peers[r] * s.occ + k, 0, s.nocc - 1)
            counts[r * s.occ + k] = count
            offsets[r * s.occ + k] = at
            at += chunks_of(count) * rows_of(lens[orbital])
    for k in range(s.occ):
        counts[2 * s.occ + k] = jnp.int32(s.aux)
        offsets[2 * s.occ + k] = jnp.int32(0)

    for copy in copies[1] + copies[0]:
        copy.wait()


def count_kernel(s, partner, lens, aux_rows, _, over):
    devices = s.nocc // s.occ
    full = s.aux // LANES

    def ids(orbital):
        row = aux_rows[pl.ds(orbital, 1), :]
        return dot(bits(row // LOW, HIGH, s.aux), bits(lax.rem(row, LOW), LOW, s.aux), NT)

    over[0] = jnp.int32(0)

    def edge(e, _):
        source = e + 1
        user = source + 1 - 2 * lax.rem(e, 2)
        reads = [partner[user * s.pairs + q] - source * s.occ for q in range(s.pairs)]
        bound = jnp.int32(0)
        for k in range(s.occ):
            used = functools.reduce(jnp.logical_or, [read == k for read in reads])
            bound += jnp.where(used, full * rows_of(lens[source * s.occ + k]), 0)

        @pl.when(bound > s.room)
        def _():
            domains = [ids(user * s.occ + q) for q in range(s.occ)]
            need = jnp.int32(0)
            for k in range(s.occ):
                union = jnp.zeros((HIGH, LOW), jnp.float32)
                for q, domain in enumerate(domains):
                    used = functools.reduce(
                        jnp.logical_or, [read == k for read in reads[q :: s.occ]]
                    )
                    union += jnp.where(used, 1.0, 0.0) * domain
                taken = (union > 0.0) & (ids(source * s.occ + k) > 0.0)
                count = jnp.sum(jnp.where(taken, 1.0, 0.0)).astype(jnp.int32)
                need += chunks_of(count) * rows_of(lens[source * s.occ + k])
            over[0] = jnp.maximum(over[0], (need > s.room).astype(jnp.int32))

        return 0

    lax.fori_loop(0, devices - 2, edge, 0)


def own_kernel(
    s, here, partner, lens, counts, tables, aux_rows, blocks, amps, _, __, aligned, dens, ___, ____
):
    left = pl.program_id(0)
    me = here[0]
    wide = 2 * LANES
    chunks = s.aux // wide
    row = aux_rows[pl.ds(me * s.occ + left, 1), :]
    term = jnp.zeros((s.pao, s.pao), jnp.float32)
    rest = []

    for t in range(s.pairs // s.occ):
        right = partner[me * s.pairs + t * s.occ + left]
        l, kind = s.where_partner(me, right)
        place = places(row, tables[kind], lax.rem(right, s.occ))

        def some(c, t=t, place=place):
            aligned[t, 0, :, c * wide : (c + 1) * wide] = dot(
                blocks[0], picker(place, c), NT
            ).astype(jnp.bfloat16)

        for c in range(chunks - 1):
            some(c)
        rest.append((counts[l] > (chunks - 1) * wide, functools.partial(some, chunks - 1)))
        masked = kept(amps[t, 0], lens[me * s.occ + left], lens[right])
        term += dot(masked, masked, NT)

    dens[0] = term
    for needed, act in rest:
        pl.when(needed)(act)


def column_of(pao_rows, orbital):
    row = pao_rows[pl.ds(orbital, 1), :]
    return column(jnp.where(row < 0, -2, row)).astype(jnp.int16)


def row_of(pao_rows, orbital):
    return pao_rows[pl.ds(orbital, 1), :]


def near_kernel(
    s, ncpl, here, partner, listed, lens, coef, counts, offsets, _, pao_rows, sibling, own, aligned, dens_in, blocks, from_sibling, coupling, exchange, dens, wide, tall, dens_own, near_blocks, halo, sems
):
    p = pl.program_id(0)
    me = here[0]
    buddy = swapped(me)[0]
    low = jnp.minimum(me, buddy)
    fetches = [
        pltpu.make_async_copy(from_sibling, halo.at[pl.ds(0, s.rows), :], sems.at[0]),
        pltpu.make_async_copy(blocks, near_blocks, sems.at[1]),
        pltpu.make_async_copy(dens_in, dens_own, sems.at[2]),
    ]

    @pl.when(p == 0)
    def _():
        for fetch in fetches:
            fetch.start()
        dens[...] = jnp.zeros_like(dens)
        for k in range(s.pairs):
            wide[(me - low) * s.pairs + k] = own[k]
            unpack(s, sibling, k, wide.at[(buddy - low) * s.pairs + k])

    right_col = column_of(pao_rows, partner[me * s.pairs + p])
    left_col = column_of(pao_rows, me * s.occ + lax.rem(p, s.occ))
    left_rows = []
    for c in range(ncpl):
        m = listed[c, p]
        spot = m - low * s.pairs
        inside = (spot >= 0) & (spot < 2 * s.pairs)
        weight = jnp.where(inside, coef[c, p], 0.0)
        left_rows.append(row_of(pao_rows, s.first_orbital(m)))
        right_row = row_of(pao_rows, partner[m]).astype(jnp.int16)
        moved = dot(wide[jnp.clip(spot, 0, 2 * s.pairs - 1)], same(right_col, right_row), NT)
        tall[c * s.pao : (c + 1) * s.pao] = (weight * moved).astype(jnp.bfloat16)
    left_row = jnp.concatenate(left_rows, axis=1).astype(jnp.int16)
    coupling[0] = dot(same(left_col, left_row), tall[...])

    for side in range(2):
        m = (low + side) * s.pairs + p
        near = partner[m] - me * s.occ

        @pl.when((near >= 0) & (near < s.occ))
        def _():
            masked = kept(wide[side * s.pairs + p], lens[s.first_orbital(m)], lens[partner[m]])
            dens[near] += dot(masked, masked, TN)

    @pl.when(p == 0)
    def _():
        for fetch in fetches:
            fetch.wait()

    right = partner[me * s.pairs + p]
    l, kind = s.where_partner(me, right)

    @pl.when(kind == 2)
    def _():
        exchange[0] = dot(aligned[0], near_blocks[lax.rem(right, s.occ)], NT)

    @pl.when(kind == 0)
    def _():
        usual = s.aux - 2 * LANES
        use = functools.partial(
            compacted, s, counts[l], offsets[l], rows_of(lens[right]), aligned.at[0], halo
        )
        exchange[0] = use(0, usual)

        @pl.when(counts[l] > usual)
        def _():
            exchange[0] += use(usual, s.aux)

    @pl.when(p == s.pairs - 1)
    def _():
        dens[...] = (dens[...] + dens_own[...]) * (1.0 / s.pao)


def far_kernel(
    s, ncpl, here, partner, listed, lens, coef, pao_rows, gaps, other, own, near_coupling, exchange, near_dens, coupling, dens, new_amps, energy, wide, news, whose, which, sems
):
    me = here[0]
    device = swapped(me)[1]
    dens[...] = near_dens[...]
    coupling[...] = near_coupling[...]
    for k in range(s.pairs):
        unpack(s, other, k, wide.at[k])

    number = jnp.int32(0)
    for p in range(s.pairs):
        for c in range(ncpl):
            spot = listed[c, p] - device * s.pairs
            whose[number] = p
            which[number] = c
            number += ((spot >= 0) & (spot < s.pairs)).astype(jnp.int32)

    def term(n):
        weight = jnp.where(n < number, 1.0, 0.0)
        n = jnp.minimum(n, number - 1)
        p, c = whose[n], which[n]
        m = listed[c, p]
        right_col = column_of(pao_rows, partner[me * s.pairs + p])
        left_col = column_of(pao_rows, me * s.occ + lax.rem(p, s.occ))
        right_row = row_of(pao_rows, partner[m]).astype(jnp.int16)
        left_row = row_of(pao_rows, s.first_orbital(m)).astype(jnp.int16)
        moved = dot(wide[m - device * s.pairs], same(right_col, right_row), NT)
        return p, weight * coef[c, p] * dot(same(left_col, left_row), moved.astype(jnp.bfloat16))

    def some(n, _):
        terms = [term(2 * n), term(2 * n + 1)]
        for p, value in terms:
            coupling[p] += value
        return 0

    lax.fori_loop(0, (number + 1) // 2, some, 0)

    for k in range(s.pairs):
        m = device * s.pairs + k
        inside = (m >= 0) & (m < s.npair)
        m = jnp.clip(m, 0, s.npair - 1)
        near = partner[m] - me * s.occ

        @pl.when(inside & (near >= 0) & (near < s.occ))
        def _():
            masked = kept(wide[k], lens[s.first_orbital(m)], lens[partner[m]])
            dens[near] += dot(masked, masked, TN) * (1.0 / s.pao)

    def result(p):
        return pltpu.make_async_copy(news.at[p], new_amps.at[p], sems.at[p])

    def finish(p, _):
        left, right = me * s.occ + lax.rem(p, s.occ), partner[me * s.pairs + p]
        kind = s.where_partner(me, right)[1]
        energy[p] = 0.0

        @pl.when(kind != 1)
        def _():
            news[p], energy[p] = update(
                s, lens[left], lens[right], exchange[p], own[p], coupling[p], gaps[pl.ds(left, 1), :], gaps[pl.ds(right, 1), :]
            )
            result(p).start()

        return 0

    def wait(p, _):
        kind = s.where_partner(me, partner[me * s.pairs + p])[1]
        pl.when(kind != 1)(result(p).wait)
        return 0

    lax.fori_loop(0, s.pairs, finish, 0)
    lax.fori_loop(0, s.pairs, wait, 0)


def update(s, lens_left, lens_right, exchange, amp, coupling, gap_left, gap_right):
    left = column(gap_left)
    parts = []
    energy = jnp.zeros((s.pao, LANES), jnp.float32)
    for at in range(0, s.pao, LANES):
        lanes = slice(at, min(at + LANES, s.pao))
        part = amp[:, lanes].astype(jnp.float32)
        shape = part.shape
        mask = live(lens_left, lens_right - at, shape)
        denom = left[:, : shape[1]] + gap_right[:, lanes]
        inverse = pl.reciprocal(denom, approx=True)
        inverse = inverse * (2.0 - denom * inverse)
        moved = (exchange[:, lanes] - coupling[:, lanes]) * inverse
        parts.append(jnp.where(mask, 0.5 * (part - moved), 0.0).astype(jnp.bfloat16))
        term = jnp.where(mask, exchange[:, lanes] * part, 0.0)
        if shape[1] < LANES:
            term = jnp.concatenate([term, jnp.zeros((s.pao, LANES - shape[1]), jnp.float32)], axis=1)
        energy += term
    return jnp.concatenate(parts, axis=1), jnp.sum(energy) / s.pao


def compacted(s, count, at, step, aligned, halo, low, high):
    parts = []
    for c in range(low // LANES, high // LANES):
        spot = pl.multiple_of(jnp.minimum(at + c * step, halo.shape[0] - s.pao), 16)
        part = halo[pl.ds(spot, s.pao), :]
        parts.append(jnp.where(c * LANES < count, part, jnp.zeros_like(part)))
    return dot(aligned[:, low:high], jnp.concatenate(parts, axis=1), NT)


def last_kernel(s, beyond, here, partner, lens, counts, offsets, energy_in, gaps, aligned, coupling, amps, other, *refs):
    if beyond:
        more, _, new_amps, energy, halo, news, sums, far, sems = refs
        halo[: s.first] = other[...]
        rest = pltpu.make_async_copy(
            more, halo.at[pl.ds(s.first, s.rows - s.first)], sems.at[s.pairs]
        )
        rest.start()
        rest.wait()
    else:
        _, new_amps, energy, news, sums, far, sems = refs
        halo = other
    me = here[0]

    def result(n):
        return pltpu.make_async_copy(news.at[n], new_amps.at[far[n]], sems.at[n])

    number = jnp.int32(0)
    for p in range(s.pairs):
        energy[p] = energy_in[p]
        far[number] = p
        kind = s.where_partner(me, partner[me * s.pairs + p])[1]
        number += (kind == 1).astype(jnp.int32)

    usual = s.aux - 2 * LANES

    def pair_of(n):
        p = far[jnp.minimum(n, number - 1)]
        right = partner[me * s.pairs + p]
        return p, right, s.occ + lax.rem(right, s.occ)

    def some(n, _):
        pairs = [pair_of(2 * n + t) for t in range(2)]
        for t, (p, right, l) in enumerate(pairs):
            sums[t] = compacted(s, counts[l], offsets[l], rows_of(lens[right]), aligned.at[p], halo, 0, usual)
        for t, (p, right, l) in enumerate(pairs):

            @pl.when(counts[l] > usual)
            def _():
                sums[t] += compacted(
                    s, counts[l], offsets[l], rows_of(lens[right]), aligned.at[p], halo, usual, s.aux
                )

        for t, (p, right, l) in enumerate(pairs):
            left = me * s.occ + lax.rem(p, s.occ)
            news[2 * n + t], energy[p] = update(
                s, lens[left], lens[right], sums[t], amps[p], coupling[p], gaps[pl.ds(left, 1), :], gaps[pl.ds(right, 1), :]
            )
        for t in range(2):
            pl.when(2 * n + t < number)(result(2 * n + t).start)
        return 0

    def wait(n, _):
        result(n).wait()
        return 0

    lax.fori_loop(0, (number + 1) // 2, some, 0)
    lax.fori_loop(0, number, wait, 0)


def position():
    return lax.axis_index(AXES)


def swap(array, role):
    count = 1
    for axis in AXES:
        count *= lax.axis_size(axis)
    route = []
    for low in range(role, count - 1, 2):
        route += [(low, low + 1), (low + 1, low)]
    return lax.ppermute(array, AXES, route)


def run(
    beyond, blocks, aux_domain, pao_domain, pao_gap, amplitudes, pair_partner, coupling_list, coupling_coef
):
    s = Sizes(blocks, amplitudes, pair_partner)
    ncpl = coupling_list.shape[1]
    me = position()
    here = me.astype(jnp.int32).reshape(1)
    blocks_t = jnp.swapaxes(blocks, 1, 2)

    smem = pl.BlockSpec(memory_space=pltpu.SMEM)
    vmem = pl.BlockSpec(memory_space=pltpu.VMEM)
    pinned = pl.BlockSpec(memory_space=pltpu.HBM)
    anywhere = pl.BlockSpec(memory_space=pl.ANY)
    plain = pltpu.CompilerParams(vmem_limit_bytes=24 * MIB)
    stepped = pltpu.CompilerParams(
        dimension_semantics=("arbitrary",), vmem_limit_bytes=30 * MIB
    )
    alone = pltpu.CompilerParams(vmem_limit_bytes=24 * MIB)
    square = pl.BlockSpec((1, s.pao, s.pao), lambda p, *_: (p, 0, 0))
    all_dens = pl.BlockSpec((s.occ, s.pao, s.pao), lambda p, *_: (0, 0, 0))
    squares = jax.ShapeDtypeStruct((s.pairs, s.pao, s.pao), jnp.float32)
    dens_shape = jax.ShapeDtypeStruct((s.occ, s.pao, s.pao), jnp.float32)

    def cost(work, data):
        return pl.CostEstimate(flops=work, bytes_accessed=data, transcendentals=0)

    whole, tail, share = packing(s)
    slots = s.pairs + s.pairs // share
    slim = pl.pallas_call(
        functools.partial(slim_kernel, s),
        in_specs=[vmem],
        out_specs=vmem,
        out_shape=jax.ShapeDtypeStruct((slots, s.pao, whole), jnp.bfloat16),
        compiler_params=plain,
        cost_estimate=cost(10**6, 4 * 10**6),
        name="slim",
    )(amplitudes)
    amps_other = swap(slim, 1)
    amps_sibling = swap(slim, 0)

    lens = jnp.sum((pao_domain >= 0).astype(jnp.int32), axis=1)

    lists = 3 * s.occ
    to_sibling, to_other, to_other_more, tables, pao_rows, gap_rows, counts, offsets = pl.pallas_call(
        functools.partial(pack_kernel, s),
        in_specs=[smem] * 3 + [vmem] * 4 + [anywhere],
        out_specs=[pinned] * 3 + [vmem] * 3 + [smem] * 2,
        out_shape=[
            jax.ShapeDtypeStruct((s.rows, LANES), jnp.bfloat16),
            jax.ShapeDtypeStruct((s.first, LANES), jnp.bfloat16),
            jax.ShapeDtypeStruct((s.rows - s.first, LANES), jnp.bfloat16),
            jax.ShapeDtypeStruct((3, 2 * LOW, s.occ * HIGH), jnp.bfloat16),
            jax.ShapeDtypeStruct(pao_domain.shape, pao_domain.dtype),
            jax.ShapeDtypeStruct(pao_gap.shape, pao_gap.dtype),
            jax.ShapeDtypeStruct((lists,), jnp.int32),
            jax.ShapeDtypeStruct((lists,), jnp.int32),
        ],
        scratch_shapes=[
            pltpu.VMEM((3, 2 * LOW, s.occ * HIGH), jnp.float32),
            pltpu.VMEM((3 * s.occ, 2 * LOW, s.occ * HIGH), jnp.float32),
            pltpu.VMEM((2, 2 * LOW, s.occ * HIGH), jnp.bfloat16),
            pltpu.SMEM((s.occ,), jnp.int32),
            pltpu.VMEM((2, s.rows + s.pao, LANES), jnp.bfloat16),
            pltpu.SemaphoreType.DMA((3,)),
        ],
        compiler_params=plain,
        cost_estimate=cost(10**11, 10**5),
        name="pack",
    )(here, pair_partner, lens, aux_domain, blocks_t, pao_domain.T, pao_gap.T, slim)

    repeats = s.pairs // s.occ
    both = pl.BlockSpec((repeats, 1, s.pao, s.aux), lambda g: (0, g, 0, 0))
    aligned, dens, to_other, to_sibling = pl.pallas_call(
        functools.partial(own_kernel, s),
        grid=(s.occ,),
        in_specs=[smem] * 4
        + [
            vmem,
            vmem,
            pl.BlockSpec((1, s.pao, s.aux), lambda g: (g, 0, 0)),
            pl.BlockSpec((repeats, 1, s.pao, s.pao), lambda g: (0, g, 0, 0)),
            anywhere,
            anywhere,
        ],
        out_specs=[both, pl.BlockSpec((1, s.pao, s.pao), lambda g: (g, 0, 0)), anywhere, anywhere],
        out_shape=[
            jax.ShapeDtypeStruct((repeats, s.occ, s.pao, s.aux), jnp.bfloat16),
            dens_shape,
            jax.ShapeDtypeStruct(to_other.shape, to_other.dtype),
            jax.ShapeDtypeStruct(to_sibling.shape, to_sibling.dtype),
        ],
        input_output_aliases={8: 2, 9: 3},
        compiler_params=stepped,
        cost_estimate=cost(10**11, 10**5),
        name="own",
    )(
        here, pair_partner, lens, counts, tables, aux_domain, blocks_t,
        amplitudes.reshape(repeats, s.occ, s.pao, s.pao), to_other, to_sibling,
    )
    from_other = swap(to_other, 1)
    from_sibling = swap(to_sibling, 0)
    aligned = aligned.reshape(s.pairs, s.pao, s.aux)

    (over,) = pl.pallas_call(
        functools.partial(count_kernel, s),
        in_specs=[smem] * 2 + [vmem, anywhere],
        out_specs=[smem],
        out_shape=[jax.ShapeDtypeStruct((1,), jnp.int32)],
        compiler_params=plain,
        cost_estimate=cost(10**11, 10**5),
        name="count",
    )(pair_partner, lens, aux_domain, dens)

    coupling, exchange, dens = pl.pallas_call(
        functools.partial(near_kernel, s, ncpl),
        grid=(s.pairs,),
        in_specs=[smem] * 8
        + [vmem] * 3
        + [pl.BlockSpec((1, s.pao, s.aux), lambda p: (p, 0, 0))]
        + [anywhere, pinned, anywhere],
        out_specs=[square, square, all_dens],
        out_shape=[squares, squares, dens_shape],
        scratch_shapes=[
            pltpu.VMEM((2 * s.pairs, s.pao, s.pao), jnp.bfloat16),
            pltpu.VMEM((ncpl * s.pao, s.pao), jnp.bfloat16),
            pltpu.VMEM((s.occ, s.pao, s.pao), jnp.float32),
            pltpu.VMEM((s.occ, s.pao, s.aux), jnp.bfloat16),
            pltpu.VMEM((s.rows + s.pao, LANES), jnp.bfloat16),
            pltpu.SemaphoreType.DMA((3,)),
        ],
        compiler_params=stepped,
        cost_estimate=cost(10**11, 10**5),
        name="near",
    )(
        here, pair_partner, coupling_list.T, lens, coupling_coef.T, counts, offsets, over,
        pao_rows, amps_sibling, amplitudes, aligned, dens, blocks_t, from_sibling,
    )

    coupling, densities, some_amps, some_energies = pl.pallas_call(
        functools.partial(far_kernel, s, ncpl),
        in_specs=[smem] * 5 + [vmem] * 7,
        out_specs=[vmem, vmem, pinned, smem],
        out_shape=[
            squares,
            dens_shape,
            jax.ShapeDtypeStruct(amplitudes.shape, amplitudes.dtype),
            jax.ShapeDtypeStruct((s.pairs,), jnp.float32),
        ],
        scratch_shapes=[
            pltpu.VMEM((s.pairs, s.pao, s.pao), jnp.bfloat16),
            pltpu.VMEM((s.pairs, s.pao, s.pao), jnp.bfloat16),
            pltpu.SMEM((s.pairs * ncpl,), jnp.int32),
            pltpu.SMEM((s.pairs * ncpl,), jnp.int32),
            pltpu.SemaphoreType.DMA((s.pairs,)),
        ],
        compiler_params=alone,
        cost_estimate=cost(10**10, 10**5),
        name="far",
    )(
        here, pair_partner, coupling_list.T, lens, coupling_coef.T,
        pao_rows, gap_rows, amps_other, amplitudes, coupling, exchange, dens,
    )

    more = (swap(to_other_more, 1),) if beyond else ()
    scratch = [
        pltpu.VMEM((s.pairs, s.pao, s.pao), jnp.bfloat16),
        pltpu.VMEM((2, s.pao, s.pao), jnp.float32),
        pltpu.SMEM((s.pairs,), jnp.int32),
        pltpu.SemaphoreType.DMA((s.pairs + 1,)),
    ]
    if beyond:
        scratch = [pltpu.VMEM((s.rows + s.pao, LANES), jnp.bfloat16)] + scratch
    new_amps, energies = pl.pallas_call(
        functools.partial(last_kernel, s, beyond),
        in_specs=[smem] * 6 + [vmem] * 5 + [pinned] * (len(more) + 1),
        out_specs=[pinned, smem],
        out_shape=[
            jax.ShapeDtypeStruct(amplitudes.shape, amplitudes.dtype),
            jax.ShapeDtypeStruct((s.pairs,), jnp.float32),
        ],
        scratch_shapes=scratch,
        input_output_aliases={11 + len(more): 0},
        compiler_params=alone,
        cost_estimate=cost(2 * s.pairs * s.pao * s.pao * s.aux, 2 * 10**7),
        name="last",
    )(
        here, pair_partner, lens, counts, offsets, some_energies,
        gap_rows, aligned, coupling, amplitudes, from_other, *more, some_amps,
    )
    return new_amps, energies, densities, over


def local(*arrays):
    new_amps, energies, densities, over = run(False, *arrays)
    new_amps, energies = lax.cond(
        over[0] > 0, lambda ops: run(True, *ops[2:])[:2], lambda ops: ops[:2], (new_amps, energies) + arrays
    )
    return (new_amps, energies, densities)


def solution(mesh):
    return jax.shard_map(
        local,
        mesh=mesh,
        in_specs=(
            P(AXES, None, None),
            P(),
            P(),
            P(),
            P(AXES, None, None),
            P(),
            P(AXES, None),
            P(AXES, None),
        ),
        out_specs=(P(AXES, None, None), P(AXES), P(AXES, None, None)),
        check_vma=False,
    )
```

```python
import functools

import jax
import jax.numpy as jnp
from jax import lax
from jax.experimental import pallas as pl
from jax.experimental.pallas import tpu as pltpu
from jax.sharding import PartitionSpec as P

AXES = ("orb", "pair")
MIB = 1024 * 1024
AUX_IDS = 2048
LOW = 64
HIGH = AUX_IDS // LOW
BASE = 32
LANES = 128
FIRST, WHOLE = 16, 64
NN = (((1,), (0,)), ((), ()))
NT = (((1,), (1,)), ((), ()))
TN = (((0,), (0,)), ((), ()))


def dot(a, b, dims=NN):
    return lax.dot_general(a, b, dims, preferred_element_type=jnp.float32)


def one_where(equal, value=1.0):
    return jnp.where(equal, value, 0.0).astype(jnp.bfloat16)


def iota(shape, dim):
    return lax.broadcasted_iota(jnp.int32, shape, dim)


def live(rows, cols, shape):
    return (iota(shape, 0) < rows) & (iota(shape, 1) < cols)


def kept(amp, rows, cols):
    return jnp.where(live(rows, cols, amp.shape), amp.astype(jnp.float32), 0.0).astype(amp.dtype)


def short_where(equal):
    one = jnp.ones(equal.shape, jnp.bfloat16)
    return jnp.where(equal, one, jnp.zeros_like(one))


def column(row):
    return jnp.broadcast_to(row, (LANES, row.shape[1])).T


def same(col, row):
    parts = []
    for at in range(0, row.shape[1], LANES):
        piece = row[:, at : at + LANES]
        wide = jnp.broadcast_to(piece, (col.shape[0], piece.shape[1]))
        parts.append(short_where(col[:, : piece.shape[1]] == wide))
    return jnp.concatenate(parts, axis=1)


def chunks_of(count):
    return (count + LANES - 1) // LANES


def rows_of(length):
    return (length + 15) // 16 * 16


def swapped(me):
    odd = lax.rem(me, 2)
    return me + 1 - 2 * odd, me - 1 + 2 * odd


class Sizes:
    def __init__(self, blocks, amplitudes, pair_partner):
        self.occ = blocks.shape[0]
        self.aux = blocks.shape[1]
        self.pao = blocks.shape[2]
        self.pairs = amplitudes.shape[0]
        self.npair = pair_partner.shape[0]
        self.nocc = self.npair // self.pairs * self.occ
        self.rows = self.occ * self.pao * (self.aux // LANES)
        self.first = self.rows * FIRST // WHOLE // 16 * 16
        self.room = self.first - self.pao // 2

    def first_orbital(self, pair):
        return pair // self.pairs * self.occ + lax.rem(pair, self.occ)

    def where_partner(self, me, right):
        device = right // self.occ
        sibling, _ = swapped(me)
        kind = jnp.where(device == me, 2, jnp.where(device == sibling, 0, 1))
        return kind * self.occ + lax.rem(right, self.occ), kind


def packing(s):
    whole = s.pao // LANES * LANES
    tail = s.pao - whole
    share = whole // tail
    return whole, tail, share


def slim_kernel(s, amps, out):
    whole, tail, share = packing(s)
    for k in range(s.pairs):
        out[k] = amps[k, :, :whole]
    for g in range(s.pairs // share):
        tails = [amps[g * share + t, :, whole:] for t in range(share)]
        out[s.pairs + g] = jnp.concatenate(tails, axis=1)


def unpack(s, packed, k, out):
    whole, tail, share = packing(s)
    out[:, :whole] = packed[k]
    spot = k % share * tail
    out[:, whole:] = packed[s.pairs + k // share, :, spot : spot + tail]


def bits(values, count, lanes):
    levels = iota((count, lanes), 0).astype(jnp.bfloat16)
    return short_where(levels == jnp.broadcast_to(values.astype(jnp.bfloat16), (count, lanes)))


def places(row, table, k):
    found = dot(table, bits(row // LOW + k * HIGH, table.shape[1], row.shape[1]))
    low = bits(lax.rem(row, LOW), LOW, row.shape[1]).astype(jnp.float32)
    return jnp.sum((found[:LOW] * BASE + found[LOW:]) * low, axis=0, keepdims=True)


def picker(place, chunk):
    wide = 2 * LANES
    middle = chunk * wide + LANES + 1
    spot = (place - jnp.asarray(middle).astype(jnp.float32)).astype(jnp.bfloat16)
    levels = (iota((wide, place.shape[1]), 0) - LANES).astype(jnp.bfloat16)
    return short_where(levels == jnp.broadcast_to(spot, levels.shape))


def chunkwise(s, count, act):
    for c in range(s.aux // (2 * LANES)):
        pl.when(count > c * 2 * LANES)(functools.partial(act, c))


def split_place(place, row):
    part = jnp.where(row < LOW, place // BASE, lax.rem(place, BASE))
    return part.astype(jnp.float32).astype(jnp.bfloat16)


def pack_kernel(
    s, here, partner, lens, aux_rows, blocks, pao_cols, gap_cols, _, to_sibling, to_other, to_other_more, tables, pao_rows, gap_rows, counts, offsets, maps, users, sends, needed, bufs, sems
):
    me = here[0]
    peers = swapped(me)
    pao_rows[...] = pao_cols[...].T
    gap_rows[...] = gap_cols[...].T

    for g, device in enumerate((me,) + peers):
        for k in range(s.occ):
            orbital = jnp.clip(device * s.occ + k, 0, s.nocc - 1)
            row = aux_rows[pl.ds(orbital, 1), :]
            by_high = bits(row // LOW, HIGH, s.aux)
            by_low = bits(lax.rem(row, LOW), LOW, s.aux)
            here_map = dot(jnp.concatenate([by_low, by_low], axis=0), by_high, NT)
            maps[g, :, k * HIGH : (k + 1) * HIGH] = here_map
            users[g * s.occ + k] = jnp.concatenate([here_map] * s.occ, axis=1)
            if g == 0:
                spot = iota((LOW, s.aux), 1) + 1
                parts = jnp.concatenate(
                    [
                        (spot // BASE).astype(jnp.float32).astype(jnp.bfloat16) * by_low,
                        lax.rem(spot, BASE).astype(jnp.float32).astype(jnp.bfloat16) * by_low,
                    ],
                    axis=0,
                )
                tables[2, :, k * HIGH : (k + 1) * HIGH] = dot(parts, by_high, NT).astype(
                    jnp.bfloat16
                )

    wide = s.occ * HIGH
    sub, lane = iota((2 * LOW, 2 * LOW), 0), iota((2 * LOW, 2 * LOW), 1)
    ahead = one_where((lane < LOW) & (lane < lax.rem(sub, LOW)))
    first = one_where(lane < LOW)
    sub, lane = iota((wide, wide), 0), iota((wide, wide), 1)
    above = one_where((sub // HIGH == lane // HIGH) & (sub < lane))
    level = iota((2 * LOW, wide), 0)
    owner = iota((1, wide), 1) // HIGH

    def listing(target, target_device, user, user_device):
        union = jnp.zeros((2 * LOW, wide), jnp.float32)
        for q in range(s.occ):
            uses = jnp.zeros((1, wide), jnp.float32)
            for pair in range(q, s.pairs, s.occ):
                pair += user_device * s.pairs
                inside = (pair >= 0) & (pair < s.npair)
                k = partner[jnp.clip(pair, 0, s.npair - 1)] - target_device * s.occ
                uses += jnp.where((owner == k) & inside, 1.0, 0.0)
            union += uses * users[user * s.occ + q]
        taken = (union > 0.0) & (maps[target] > 0.0)
        flags = one_where(taken)
        total = dot(first, flags)
        place = dot(ahead, flags) + dot(total.astype(jnp.bfloat16), above) + 1.0
        place = jnp.where(taken, place, 0.0).astype(jnp.int32)
        found = [
            jnp.sum(jnp.where(owner == k, total[:1], 0.0)).astype(jnp.int32) for k in range(s.occ)
        ]
        return split_place(place, level), found

    copies = {
        0: [pltpu.make_async_copy(bufs.at[0, pl.ds(0, s.rows)], to_sibling, sems.at[0])],
        1: [
            pltpu.make_async_copy(bufs.at[1, pl.ds(0, s.first)], to_other, sems.at[1]),
            pltpu.make_async_copy(
                bufs.at[1, pl.ds(s.first, s.rows - s.first)], to_other_more, sems.at[2]
            ),
        ],
    }
    for r in (1, 0):
        sends[r], found = listing(0, me, 1 + r, peers[r])
        for k, count in enumerate(found):
            needed[k] = count

        def send(k, at, r=r):
            count = needed[k]
            step = rows_of(lens[me * s.occ + k])

            @pl.when(count > 0)
            def _():
                place = places(aux_rows[pl.ds(me * s.occ + k, 1), :], sends[r], k)

                def some(c):
                    got = dot(blocks[k], picker(place, c), NT).astype(jnp.bfloat16)
                    spot = pl.multiple_of(at + 2 * c * step, 16)
                    bufs[r, pl.ds(spot, s.pao), :] = got[:, :LANES]

                    @pl.when((2 * c + 1) * LANES < count)
                    def _():
                        bufs[r, pl.ds(pl.multiple_of(spot + step, 16), s.pao), :] = got[:, LANES:]

                chunkwise(s, count, some)

            return at + chunks_of(count) * step

        lax.fori_loop(0, s.occ, send, jnp.int32(0))
        for copy in copies[r]:
            copy.start()

    for r in range(2):
        tables[r], found = listing(1 + r, peers[r], 0, me)
        at = jnp.int32(0)
        for k, count in enumerate(found):
            orbital = jnp.clip(peers[r] * s.occ + k, 0, s.nocc - 1)
            counts[r * s.occ + k] = count
            offsets[r * s.occ + k] = at
            at += chunks_of(count) * rows_of(lens[orbital])
    for k in range(s.occ):
        counts[2 * s.occ + k] = jnp.int32(s.aux)
        offsets[2 * s.occ + k] = jnp.int32(0)

    for copy in copies[1] + copies[0]:
        copy.wait()


def count_kernel(s, partner, lens, aux_rows, _, over):
    devices = s.nocc // s.occ
    full = s.aux // LANES

    def ids(orbital):
        row = aux_rows[pl.ds(orbital, 1), :]
        return dot(bits(row // LOW, HIGH, s.aux), bits(lax.rem(row, LOW), LOW, s.aux), NT)

    over[0] = jnp.int32(0)

    def edge(e, _):
        source = e + 1
        user = source + 1 - 2 * lax.rem(e, 2)
        reads = [partner[user * s.pairs + q] - source * s.occ for q in range(s.pairs)]
        bound = jnp.int32(0)
        for k in range(s.occ):
            used = functools.reduce(jnp.logical_or, [read == k for read in reads])
            bound += jnp.where(used, full * rows_of(lens[source * s.occ + k]), 0)

        @pl.when(bound > s.room)
        def _():
            domains = [ids(user * s.occ + q) for q in range(s.occ)]
            need = jnp.int32(0)
            for k in range(s.occ):
                union = jnp.zeros((HIGH, LOW), jnp.float32)
                for q, domain in enumerate(domains):
                    used = functools.reduce(
                        jnp.logical_or, [read == k for read in reads[q :: s.occ]]
                    )
                    union += jnp.where(used, 1.0, 0.0) * domain
                taken = (union > 0.0) & (ids(source * s.occ + k) > 0.0)
                count = jnp.sum(jnp.where(taken, 1.0, 0.0)).astype(jnp.int32)
                need += chunks_of(count) * rows_of(lens[source * s.occ + k])
            over[0] = jnp.maximum(over[0], (need > s.room).astype(jnp.int32))

        return 0

    lax.fori_loop(0, devices - 2, edge, 0)


def own_kernel(
    s, here, partner, lens, counts, tables, aux_rows, blocks, amps, _, __, aligned, dens, ___, ____
):
    left = pl.program_id(0)
    me = here[0]
    wide = 2 * LANES
    chunks = s.aux // wide
    row = aux_rows[pl.ds(me * s.occ + left, 1), :]
    term = jnp.zeros((s.pao, s.pao), jnp.float32)
    rest = []

    for t in range(s.pairs // s.occ):
        right = partner[me * s.pairs + t * s.occ + left]
        l, kind = s.where_partner(me, right)
        place = places(row, tables[kind], lax.rem(right, s.occ))

        def some(c, t=t, place=place):
            aligned[t, 0, :, c * wide : (c + 1) * wide] = dot(
                blocks[0], picker(place, c), NT
            ).astype(jnp.bfloat16)

        for c in range(chunks - 1):
            some(c)
        rest.append((counts[l] > (chunks - 1) * wide, functools.partial(some, chunks - 1)))
        masked = kept(amps[t, 0], lens[me * s.occ + left], lens[right])
        term += dot(masked, masked, NT)

    dens[0] = term
    for needed, act in rest:
        pl.when(needed)(act)


def column_of(pao_rows, orbital):
    row = pao_rows[pl.ds(orbital, 1), :]
    return column(jnp.where(row < 0, -2, row)).astype(jnp.int16)


def row_of(pao_rows, orbital):
    return pao_rows[pl.ds(orbital, 1), :]


def near_kernel(
    s, ncpl, here, partner, listed, lens, coef, counts, offsets, _, pao_rows, sibling, own, aligned, dens_in, blocks, from_sibling, coupling, exchange, dens, wide, tall, dens_own, near_blocks, halo, sems
):
    p = pl.program_id(0)
    me = here[0]
    buddy = swapped(me)[0]
    low = jnp.minimum(me, buddy)
    fetches = [
        pltpu.make_async_copy(from_sibling, halo.at[pl.ds(0, s.rows), :], sems.at[0]),
        pltpu.make_async_copy(blocks, near_blocks, sems.at[1]),
        pltpu.make_async_copy(dens_in, dens_own, sems.at[2]),
    ]

    @pl.when(p == 0)
    def _():
        for fetch in fetches:
            fetch.start()
        dens[...] = jnp.zeros_like(dens)
        for k in range(s.pairs):
            wide[(me - low) * s.pairs + k] = own[k]
            unpack(s, sibling, k, wide.at[(buddy - low) * s.pairs + k])

    right_col = column_of(pao_rows, partner[me * s.pairs + p])
    left_col = column_of(pao_rows, me * s.occ + lax.rem(p, s.occ))
    left_rows = []
    for c in range(ncpl):
        m = listed[c, p]
        spot = m - low * s.pairs
        inside = (spot >= 0) & (spot < 2 * s.pairs)
        weight = jnp.where(inside, coef[c, p], 0.0)
        left_rows.append(row_of(pao_rows, s.first_orbital(m)))
        right_row = row_of(pao_rows, partner[m]).astype(jnp.int16)
        moved = dot(wide[jnp.clip(spot, 0, 2 * s.pairs - 1)], same(right_col, right_row), NT)
        tall[c * s.pao : (c + 1) * s.pao] = (weight * moved).astype(jnp.bfloat16)
    left_row = jnp.concatenate(left_rows, axis=1).astype(jnp.int16)
    coupling[0] = dot(same(left_col, left_row), tall[...])

    for side in range(2):
        m = (low + side) * s.pairs + p
        near = partner[m] - me * s.occ

        @pl.when((near >= 0) & (near < s.occ))
        def _():
            masked = kept(wide[side * s.pairs + p], lens[s.first_orbital(m)], lens[partner[m]])
            dens[near] += dot(masked, masked, TN)

    @pl.when(p == 0)
    def _():
        for fetch in fetches:
            fetch.wait()

    right = partner[me * s.pairs + p]
    l, kind = s.where_partner(me, right)

    @pl.when(kind == 2)
    def _():
        exchange[0] = dot(aligned[0], near_blocks[lax.rem(right, s.occ)], NT)

    @pl.when(kind == 0)
    def _():
        usual = s.aux - 2 * LANES
        use = functools.partial(
            compacted, s, counts[l], offsets[l], rows_of(lens[right]), aligned.at[0], halo
        )
        exchange[0] = use(0, usual)

        @pl.when(counts[l] > usual)
        def _():
            exchange[0] += use(usual, s.aux)

    @pl.when(p == s.pairs - 1)
    def _():
        dens[...] = (dens[...] + dens_own[...]) * (1.0 / s.pao)


def far_kernel(
    s, ncpl, here, partner, listed, lens, coef, pao_rows, gaps, other, own, near_coupling, exchange, near_dens, coupling, dens, new_amps, energy, wide, news, whose, which, sems
):
    me = here[0]
    device = swapped(me)[1]
    dens[...] = near_dens[...]
    coupling[...] = near_coupling[...]
    for k in range(s.pairs):
        unpack(s, other, k, wide.at[k])

    number = jnp.int32(0)
    for p in range(s.pairs):
        for c in range(ncpl):
            spot = listed[c, p] - device * s.pairs
            whose[number] = p
            which[number] = c
            number += ((spot >= 0) & (spot < s.pairs)).astype(jnp.int32)

    def term(n):
        weight = jnp.where(n < number, 1.0, 0.0)
        n = jnp.minimum(n, number - 1)
        p, c = whose[n], which[n]
        m = listed[c, p]
        right_col = column_of(pao_rows, partner[me * s.pairs + p])
        left_col = column_of(pao_rows, me * s.occ + lax.rem(p, s.occ))
        right_row = row_of(pao_rows, partner[m]).astype(jnp.int16)
        left_row = row_of(pao_rows, s.first_orbital(m)).astype(jnp.int16)
        moved = dot(wide[m - device * s.pairs], same(right_col, right_row), NT)
        return p, weight * coef[c, p] * dot(same(left_col, left_row), moved.astype(jnp.bfloat16))

    def some(n, _):
        terms = [term(2 * n), term(2 * n + 1)]
        for p, value in terms:
            coupling[p] += value
        return 0

    lax.fori_loop(0, (number + 1) // 2, some, 0)

    for k in range(s.pairs):
        m = device * s.pairs + k
        inside = (m >= 0) & (m < s.npair)
        m = jnp.clip(m, 0, s.npair - 1)
        near = partner[m] - me * s.occ

        @pl.when(inside & (near >= 0) & (near < s.occ))
        def _():
            masked = kept(wide[k], lens[s.first_orbital(m)], lens[partner[m]])
            dens[near] += dot(masked, masked, TN) * (1.0 / s.pao)

    def result(p):
        return pltpu.make_async_copy(news.at[p], new_amps.at[p], sems.at[p])

    def finish(p, _):
        left, right = me * s.occ + lax.rem(p, s.occ), partner[me * s.pairs + p]
        kind = s.where_partner(me, right)[1]
        energy[p] = 0.0

        @pl.when(kind != 1)
        def _():
            news[p], energy[p] = update(
                s, lens[left], lens[right], exchange[p], own[p], coupling[p], gaps[pl.ds(left, 1), :], gaps[pl.ds(right, 1), :]
            )
            result(p).start()

        return 0

    def wait(p, _):
        kind = s.where_partner(me, partner[me * s.pairs + p])[1]
        pl.when(kind != 1)(result(p).wait)
        return 0

    lax.fori_loop(0, s.pairs, finish, 0)
    lax.fori_loop(0, s.pairs, wait, 0)


def update(s, lens_left, lens_right, exchange, amp, coupling, gap_left, gap_right):
    left = column(gap_left)
    parts = []
    energy = jnp.zeros((s.pao, LANES), jnp.float32)
    for at in range(0, s.pao, LANES):
        lanes = slice(at, min(at + LANES, s.pao))
        part = amp[:, lanes].astype(jnp.float32)
        shape = part.shape
        mask = live(lens_left, lens_right - at, shape)
        denom = left[:, : shape[1]] + gap_right[:, lanes]
        inverse = pl.reciprocal(denom, approx=True)
        inverse = inverse * (2.0 - denom * inverse)
        moved = (exchange[:, lanes] - coupling[:, lanes]) * inverse
        parts.append(jnp.where(mask, 0.5 * (part - moved), 0.0).astype(jnp.bfloat16))
        term = jnp.where(mask, exchange[:, lanes] * part, 0.0)
        if shape[1] < LANES:
            term = jnp.concatenate([term, jnp.zeros((s.pao, LANES - shape[1]), jnp.float32)], axis=1)
        energy += term
    return jnp.concatenate(parts, axis=1), jnp.sum(energy) / s.pao


def compacted(s, count, at, step, aligned, halo, low, high):
    parts = []
    for c in range(low // LANES, high // LANES):
        spot = pl.multiple_of(jnp.minimum(at + c * step, halo.shape[0] - s.pao), 16)
        part = halo[pl.ds(spot, s.pao), :]
        parts.append(jnp.where(c * LANES < count, part, jnp.zeros_like(part)))
    return dot(aligned[:, low:high], jnp.concatenate(parts, axis=1), NT)


def last_kernel(s, beyond, here, partner, lens, counts, offsets, energy_in, gaps, aligned, coupling, amps, other, *refs):
    if beyond:
        more, _, new_amps, energy, halo, news, sums, far, sems = refs
        halo[: s.first] = other[...]
        rest = pltpu.make_async_copy(
            more, halo.at[pl.ds(s.first, s.rows - s.first)], sems.at[s.pairs]
        )
        rest.start()
        rest.wait()
    else:
        _, new_amps, energy, news, sums, far, sems = refs
        halo = other
    me = here[0]

    def result(n):
        return pltpu.make_async_copy(news.at[n], new_amps.at[far[n]], sems.at[n])

    number = jnp.int32(0)
    for p in range(s.pairs):
        energy[p] = energy_in[p]
        far[number] = p
        kind = s.where_partner(me, partner[me * s.pairs + p])[1]
        number += (kind == 1).astype(jnp.int32)

    usual = s.aux - 2 * LANES

    def pair_of(n):
        p = far[jnp.minimum(n, number - 1)]
        right = partner[me * s.pairs + p]
        return p, right, s.occ + lax.rem(right, s.occ)

    def some(n, _):
        pairs = [pair_of(2 * n + t) for t in range(2)]
        for t, (p, right, l) in enumerate(pairs):
            sums[t] = compacted(s, counts[l], offsets[l], rows_of(lens[right]), aligned.at[p], halo, 0, usual)
        for t, (p, right, l) in enumerate(pairs):

            @pl.when(counts[l] > usual)
            def _():
                sums[t] += compacted(
                    s, counts[l], offsets[l], rows_of(lens[right]), aligned.at[p], halo, usual, s.aux
                )

        for t, (p, right, l) in enumerate(pairs):
            left = me * s.occ + lax.rem(p, s.occ)
            news[2 * n + t], energy[p] = update(
                s, lens[left], lens[right], sums[t], amps[p], coupling[p], gaps[pl.ds(left, 1), :], gaps[pl.ds(right, 1), :]
            )
        for t in range(2):
            pl.when(2 * n + t < number)(result(2 * n + t).start)
        return 0

    def wait(n, _):
        result(n).wait()
        return 0

    lax.fori_loop(0, (number + 1) // 2, some, 0)
    lax.fori_loop(0, number, wait, 0)


def position():
    return lax.axis_index(AXES)


def swap(array, role):
    count = 1
    for axis in AXES:
        count *= lax.axis_size(axis)
    route = []
    for low in range(role, count - 1, 2):
        route += [(low, low + 1), (low + 1, low)]
    return lax.ppermute(array, AXES, route)


def run(
    beyond, blocks, aux_domain, pao_domain, pao_gap, amplitudes, pair_partner, coupling_list, coupling_coef
):
    s = Sizes(blocks, amplitudes, pair_partner)
    ncpl = coupling_list.shape[1]
    me = position()
    here = me.astype(jnp.int32).reshape(1)
    blocks_t = jnp.swapaxes(blocks, 1, 2)

    smem = pl.BlockSpec(memory_space=pltpu.SMEM)
    vmem = pl.BlockSpec(memory_space=pltpu.VMEM)
    pinned = pl.BlockSpec(memory_space=pltpu.HBM)
    anywhere = pl.BlockSpec(memory_space=pl.ANY)
    plain = pltpu.CompilerParams(vmem_limit_bytes=24 * MIB)
    stepped = pltpu.CompilerParams(
        dimension_semantics=("arbitrary",), vmem_limit_bytes=30 * MIB
    )
    alone = pltpu.CompilerParams(vmem_limit_bytes=24 * MIB)
    square = pl.BlockSpec((1, s.pao, s.pao), lambda p, *_: (p, 0, 0))
    all_dens = pl.BlockSpec((s.occ, s.pao, s.pao), lambda p, *_: (0, 0, 0))
    squares = jax.ShapeDtypeStruct((s.pairs, s.pao, s.pao), jnp.float32)
    dens_shape = jax.ShapeDtypeStruct((s.occ, s.pao, s.pao), jnp.float32)

    def cost(work, data):
        return pl.CostEstimate(flops=work, bytes_accessed=data, transcendentals=0)

    whole, tail, share = packing(s)
    slots = s.pairs + s.pairs // share
    slim = pl.pallas_call(
        functools.partial(slim_kernel, s),
        in_specs=[vmem],
        out_specs=vmem,
        out_shape=jax.ShapeDtypeStruct((slots, s.pao, whole), jnp.bfloat16),
        compiler_params=plain,
        cost_estimate=cost(10**6, 4 * 10**6),
        name="slim",
    )(amplitudes)
    amps_other = swap(slim, 1)
    amps_sibling = swap(slim, 0)

    lens = jnp.sum((pao_domain >= 0).astype(jnp.int32), axis=1)

    lists = 3 * s.occ
    to_sibling, to_other, to_other_more, tables, pao_rows, gap_rows, counts, offsets = pl.pallas_call(
        functools.partial(pack_kernel, s),
        in_specs=[smem] * 3 + [vmem] * 4 + [anywhere],
        out_specs=[pinned] * 3 + [vmem] * 3 + [smem] * 2,
        out_shape=[
            jax.ShapeDtypeStruct((s.rows, LANES), jnp.bfloat16),
            jax.ShapeDtypeStruct((s.first, LANES), jnp.bfloat16),
            jax.ShapeDtypeStruct((s.rows - s.first, LANES), jnp.bfloat16),
            jax.ShapeDtypeStruct((3, 2 * LOW, s.occ * HIGH), jnp.bfloat16),
            jax.ShapeDtypeStruct(pao_domain.shape, pao_domain.dtype),
            jax.ShapeDtypeStruct(pao_gap.shape, pao_gap.dtype),
            jax.ShapeDtypeStruct((lists,), jnp.int32),
            jax.ShapeDtypeStruct((lists,), jnp.int32),
        ],
        scratch_shapes=[
            pltpu.VMEM((3, 2 * LOW, s.occ * HIGH), jnp.float32),
            pltpu.VMEM((3 * s.occ, 2 * LOW, s.occ * HIGH), jnp.float32),
            pltpu.VMEM((2, 2 * LOW, s.occ * HIGH), jnp.bfloat16),
            pltpu.SMEM((s.occ,), jnp.int32),
            pltpu.VMEM((2, s.rows + s.pao, LANES), jnp.bfloat16),
            pltpu.SemaphoreType.DMA((3,)),
        ],
        compiler_params=plain,
        cost_estimate=cost(10**11, 10**5),
        name="pack",
    )(here, pair_partner, lens, aux_domain, blocks_t, pao_domain.T, pao_gap.T, slim)

    repeats = s.pairs // s.occ
    both = pl.BlockSpec((repeats, 1, s.pao, s.aux), lambda g: (0, g, 0, 0))
    aligned, dens, to_other, to_sibling = pl.pallas_call(
        functools.partial(own_kernel, s),
        grid=(s.occ,),
        in_specs=[smem] * 4
        + [
            vmem,
            vmem,
            pl.BlockSpec((1, s.pao, s.aux), lambda g: (g, 0, 0)),
            pl.BlockSpec((repeats, 1, s.pao, s.pao), lambda g: (0, g, 0, 0)),
            anywhere,
            anywhere,
        ],
        out_specs=[both, pl.BlockSpec((1, s.pao, s.pao), lambda g: (g, 0, 0)), anywhere, anywhere],
        out_shape=[
            jax.ShapeDtypeStruct((repeats, s.occ, s.pao, s.aux), jnp.bfloat16),
            dens_shape,
            jax.ShapeDtypeStruct(to_other.shape, to_other.dtype),
            jax.ShapeDtypeStruct(to_sibling.shape, to_sibling.dtype),
        ],
        input_output_aliases={8: 2, 9: 3},
        compiler_params=stepped,
        cost_estimate=cost(10**11, 10**5),
        name="own",
    )(
        here, pair_partner, lens, counts, tables, aux_domain, blocks_t,
        amplitudes.reshape(repeats, s.occ, s.pao, s.pao), to_other, to_sibling,
    )
    from_other = swap(to_other, 1)
    from_sibling = swap(to_sibling, 0)
    aligned = aligned.reshape(s.pairs, s.pao, s.aux)

    (over,) = pl.pallas_call(
        functools.partial(count_kernel, s),
        in_specs=[smem] * 2 + [vmem, anywhere],
        out_specs=[smem],
        out_shape=[jax.ShapeDtypeStruct((1,), jnp.int32)],
        compiler_params=plain,
        cost_estimate=cost(10**11, 10**5),
        name="count",
    )(pair_partner, lens, aux_domain, dens)

    coupling, exchange, dens = pl.pallas_call(
        functools.partial(near_kernel, s, ncpl),
        grid=(s.pairs,),
        in_specs=[smem] * 8
        + [vmem] * 3
        + [pl.BlockSpec((1, s.pao, s.aux), lambda p: (p, 0, 0))]
        + [anywhere, pinned, anywhere],
        out_specs=[square, square, all_dens],
        out_shape=[squares, squares, dens_shape],
        scratch_shapes=[
            pltpu.VMEM((2 * s.pairs, s.pao, s.pao), jnp.bfloat16),
            pltpu.VMEM((ncpl * s.pao, s.pao), jnp.bfloat16),
            pltpu.VMEM((s.occ, s.pao, s.pao), jnp.float32),
            pltpu.VMEM((s.occ, s.pao, s.aux), jnp.bfloat16),
            pltpu.VMEM((s.rows + s.pao, LANES), jnp.bfloat16),
            pltpu.SemaphoreType.DMA((3,)),
        ],
        compiler_params=stepped,
        cost_estimate=cost(10**11, 10**5),
        name="near",
    )(
        here, pair_partner, coupling_list.T, lens, coupling_coef.T, counts, offsets, over,
        pao_rows, amps_sibling, amplitudes, aligned, dens, blocks_t, from_sibling,
    )

    coupling, densities, some_amps, some_energies = pl.pallas_call(
        functools.partial(far_kernel, s, ncpl),
        in_specs=[smem] * 5 + [vmem] * 7,
        out_specs=[vmem, vmem, pinned, smem],
        out_shape=[
            squares,
            dens_shape,
            jax.ShapeDtypeStruct(amplitudes.shape, amplitudes.dtype),
            jax.ShapeDtypeStruct((s.pairs,), jnp.float32),
        ],
        scratch_shapes=[
            pltpu.VMEM((s.pairs, s.pao, s.pao), jnp.bfloat16),
            pltpu.VMEM((s.pairs, s.pao, s.pao), jnp.bfloat16),
            pltpu.SMEM((s.pairs * ncpl,), jnp.int32),
            pltpu.SMEM((s.pairs * ncpl,), jnp.int32),
            pltpu.SemaphoreType.DMA((s.pairs,)),
        ],
        compiler_params=alone,
        cost_estimate=cost(10**10, 10**5),
        name="far",
    )(
        here, pair_partner, coupling_list.T, lens, coupling_coef.T,
        pao_rows, gap_rows, amps_other, amplitudes, coupling, exchange, dens,
    )

    more = (swap(to_other_more, 1),) if beyond else ()
    scratch = [
        pltpu.VMEM((s.pairs, s.pao, s.pao), jnp.bfloat16),
        pltpu.VMEM((2, s.pao, s.pao), jnp.float32),
        pltpu.SMEM((s.pairs,), jnp.int32),
        pltpu.SemaphoreType.DMA((s.pairs + 1,)),
    ]
    if beyond:
        scratch = [pltpu.VMEM((s.rows + s.pao, LANES), jnp.bfloat16)] + scratch
    new_amps, energies = pl.pallas_call(
        functools.partial(last_kernel, s, beyond),
        in_specs=[smem] * 6 + [vmem] * 5 + [pinned] * (len(more) + 1),
        out_specs=[pinned, smem],
        out_shape=[
            jax.ShapeDtypeStruct(amplitudes.shape, amplitudes.dtype),
            jax.ShapeDtypeStruct((s.pairs,), jnp.float32),
        ],
        scratch_shapes=scratch,
        input_output_aliases={11 + len(more): 0},
        compiler_params=alone,
        cost_estimate=cost(2 * s.pairs * s.pao * s.pao * s.aux, 2 * 10**7),
        name="last",
    )(
        here, pair_partner, lens, counts, offsets, some_energies,
        gap_rows, aligned, coupling, amplitudes, from_other, *more, some_amps,
    )
    return new_amps, energies, densities, over


def local(*arrays):
    new_amps, energies, densities, over = run(False, *arrays)
    new_amps, energies = lax.cond(
        over[0] > 0, lambda ops: run(True, *ops[2:])[:2], lambda ops: ops[:2], (new_amps, energies) + arrays
    )
    return (new_amps, energies, densities)


def solution(mesh):
    return jax.shard_map(
        local,
        mesh=mesh,
        in_specs=(
            P(AXES, None, None),
            P(),
            P(),
            P(),
            P(AXES, None, None),
            P(),
            P(AXES, None),
            P(AXES, None),
        ),
        out_specs=(P(AXES, None, None), P(AXES), P(AXES, None, None)),
        check_vma=False,
    )
```

```python
import functools

import jax
import jax.numpy as jnp
from jax import lax
from jax.experimental import pallas as pl
from jax.experimental.pallas import tpu as pltpu
from jax.sharding import PartitionSpec as P

AXES = ("orb", "pair")
MIB = 1024 * 1024
AUX_IDS = 2048
LOW = 64
HIGH = AUX_IDS // LOW
BASE = 32
LANES = 128
FIRST, WHOLE = 40, 64
NN = (((1,), (0,)), ((), ()))
NT = (((1,), (1,)), ((), ()))
TN = (((0,), (0,)), ((), ()))


def dot(a, b, dims=NN):
    return lax.dot_general(a, b, dims, preferred_element_type=jnp.float32)


def one_where(equal, value=1.0):
    return jnp.where(equal, value, 0.0).astype(jnp.bfloat16)


def iota(shape, dim):
    return lax.broadcasted_iota(jnp.int32, shape, dim)


def live(rows, cols, shape):
    return (iota(shape, 0) < rows) & (iota(shape, 1) < cols)


def kept(amp, rows, cols):
    return jnp.where(live(rows, cols, amp.shape), amp.astype(jnp.float32), 0.0).astype(amp.dtype)


def short_where(equal):
    one = jnp.ones(equal.shape, jnp.bfloat16)
    return jnp.where(equal, one, jnp.zeros_like(one))


def column(row):
    return jnp.broadcast_to(row, (LANES, row.shape[1])).T


def same(col, row):
    parts = []
    for at in range(0, row.shape[1], LANES):
        piece = row[:, at : at + LANES]
        wide = jnp.broadcast_to(piece, (col.shape[0], piece.shape[1]))
        parts.append(short_where(col[:, : piece.shape[1]] == wide))
    return jnp.concatenate(parts, axis=1)


def chunks_of(count):
    return (count + LANES - 1) // LANES


def rows_of(length):
    return (length + 15) // 16 * 16


def swapped(me):
    odd = lax.rem(me, 2)
    return me + 1 - 2 * odd, me - 1 + 2 * odd


class Sizes:
    def __init__(self, blocks, amplitudes, pair_partner):
        self.occ = blocks.shape[0]
        self.aux = blocks.shape[1]
        self.pao = blocks.shape[2]
        self.pairs = amplitudes.shape[0]
        self.npair = pair_partner.shape[0]
        self.nocc = self.npair // self.pairs * self.occ
        self.rows = self.occ * self.pao * (self.aux // LANES)
        self.first = self.rows * FIRST // WHOLE // 16 * 16
        self.room = self.first - self.pao // 2

    def first_orbital(self, pair):
        return pair // self.pairs * self.occ + lax.rem(pair, self.occ)

    def where_partner(self, me, right):
        device = right // self.occ
        sibling, _ = swapped(me)
        kind = jnp.where(device == me, 2, jnp.where(device == sibling, 0, 1))
        return kind * self.occ + lax.rem(right, self.occ), kind


def packing(s):
    whole = s.pao // LANES * LANES
    tail = s.pao - whole
    share = whole // tail
    return whole, tail, share


def slim_kernel(s, amps, out):
    whole, tail, share = packing(s)
    for k in range(s.pairs):
        out[k] = amps[k, :, :whole]
    for g in range(s.pairs // share):
        tails = [amps[g * share + t, :, whole:] for t in range(share)]
        out[s.pairs + g] = jnp.concatenate(tails, axis=1)


def unpack(s, packed, k, out):
    whole, tail, share = packing(s)
    out[:, :whole] = packed[k]
    spot = k % share * tail
    out[:, whole:] = packed[s.pairs + k // share, :, spot : spot + tail]


def bits(values, count, lanes):
    levels = iota((count, lanes), 0).astype(jnp.bfloat16)
    return short_where(levels == jnp.broadcast_to(values.astype(jnp.bfloat16), (count, lanes)))


def places(row, table, k):
    found = dot(table, bits(row // LOW + k * HIGH, table.shape[1], row.shape[1]))
    low = bits(lax.rem(row, LOW), LOW, row.shape[1]).astype(jnp.float32)
    return jnp.sum((found[:LOW] * BASE + found[LOW:]) * low, axis=0, keepdims=True)


def picker(place, chunk):
    wide = 2 * LANES
    middle = chunk * wide + LANES + 1
    spot = (place - jnp.asarray(middle).astype(jnp.float32)).astype(jnp.bfloat16)
    levels = (iota((wide, place.shape[1]), 0) - LANES).astype(jnp.bfloat16)
    return short_where(levels == jnp.broadcast_to(spot, levels.shape))


def chunkwise(s, count, act):
    for c in range(s.aux // (2 * LANES)):
        pl.when(count > c * 2 * LANES)(functools.partial(act, c))


def split_place(place, row):
    part = jnp.where(row < LOW, place // BASE, lax.rem(place, BASE))
    return part.astype(jnp.float32).astype(jnp.bfloat16)


def pack_kernel(
    s, here, partner, lens, aux_rows, blocks, pao_cols, gap_cols, _, to_sibling, to_other, to_other_more, tables, pao_rows, gap_rows, counts, offsets, maps, users, sends, needed, bufs, sems
):
    me = here[0]
    peers = swapped(me)
    pao_rows[...] = pao_cols[...].T
    gap_rows[...] = gap_cols[...].T

    for g, device in enumerate((me,) + peers):
        for k in range(s.occ):
            orbital = jnp.clip(device * s.occ + k, 0, s.nocc - 1)
            row = aux_rows[pl.ds(orbital, 1), :]
            by_high = bits(row // LOW, HIGH, s.aux)
            by_low = bits(lax.rem(row, LOW), LOW, s.aux)
            here_map = dot(jnp.concatenate([by_low, by_low], axis=0), by_high, NT)
            maps[g, :, k * HIGH : (k + 1) * HIGH] = here_map
            users[g * s.occ + k] = jnp.concatenate([here_map] * s.occ, axis=1)
            if g == 0:
                spot = iota((LOW, s.aux), 1) + 1
                parts = jnp.concatenate(
                    [
                        (spot // BASE).astype(jnp.float32).astype(jnp.bfloat16) * by_low,
                        lax.rem(spot, BASE).astype(jnp.float32).astype(jnp.bfloat16) * by_low,
                    ],
                    axis=0,
                )
                tables[2, :, k * HIGH : (k + 1) * HIGH] = dot(parts, by_high, NT).astype(
                    jnp.bfloat16
                )

    wide = s.occ * HIGH
    sub, lane = iota((2 * LOW, 2 * LOW), 0), iota((2 * LOW, 2 * LOW), 1)
    ahead = one_where((lane < LOW) & (lane < lax.rem(sub, LOW)))
    first = one_where(lane < LOW)
    sub, lane = iota((wide, wide), 0), iota((wide, wide), 1)
    above = one_where((sub // HIGH == lane // HIGH) & (sub < lane))
    level = iota((2 * LOW, wide), 0)
    owner = iota((1, wide), 1) // HIGH

    def listing(target, target_device, user, user_device):
        union = jnp.zeros((2 * LOW, wide), jnp.float32)
        for q in range(s.occ):
            uses = jnp.zeros((1, wide), jnp.float32)
            for pair in range(q, s.pairs, s.occ):
                pair += user_device * s.pairs
                inside = (pair >= 0) & (pair < s.npair)
                k = partner[jnp.clip(pair, 0, s.npair - 1)] - target_device * s.occ
                uses += jnp.where((owner == k) & inside, 1.0, 0.0)
            union += uses * users[user * s.occ + q]
        taken = (union > 0.0) & (maps[target] > 0.0)
        flags = one_where(taken)
        total = dot(first, flags)
        place = dot(ahead, flags) + dot(total.astype(jnp.bfloat16), above) + 1.0
        place = jnp.where(taken, place, 0.0).astype(jnp.int32)
        found = [
            jnp.sum(jnp.where(owner == k, total[:1], 0.0)).astype(jnp.int32) for k in range(s.occ)
        ]
        return split_place(place, level), found

    copies = {
        0: [pltpu.make_async_copy(bufs.at[0, pl.ds(0, s.rows)], to_sibling, sems.at[0])],
        1: [
            pltpu.make_async_copy(bufs.at[1, pl.ds(0, s.first)], to_other, sems.at[1]),
            pltpu.make_async_copy(
                bufs.at[1, pl.ds(s.first, s.rows - s.first)], to_other_more, sems.at[2]
            ),
        ],
    }
    for r in (1, 0):
        sends[r], found = listing(0, me, 1 + r, peers[r])
        for k, count in enumerate(found):
            needed[k] = count

        def send(k, at, r=r):
            count = needed[k]
            step = rows_of(lens[me * s.occ + k])

            @pl.when(count > 0)
            def _():
                place = places(aux_rows[pl.ds(me * s.occ + k, 1), :], sends[r], k)

                def some(c):
                    got = dot(blocks[k], picker(place, c), NT).astype(jnp.bfloat16)
                    spot = pl.multiple_of(at + 2 * c * step, 16)
                    bufs[r, pl.ds(spot, s.pao), :] = got[:, :LANES]

                    @pl.when((2 * c + 1) * LANES < count)
                    def _():
                        bufs[r, pl.ds(pl.multiple_of(spot + step, 16), s.pao), :] = got[:, LANES:]

                chunkwise(s, count, some)

            return at + chunks_of(count) * step

        lax.fori_loop(0, s.occ, send, jnp.int32(0))
        for copy in copies[r]:
            copy.start()

    for r in range(2):
        tables[r], found = listing(1 + r, peers[r], 0, me)
        at = jnp.int32(0)
        for k, count in enumerate(found):
            orbital = jnp.clip(peers[r] * s.occ + k, 0, s.nocc - 1)
            counts[r * s.occ + k] = count
            offsets[r * s.occ + k] = at
            at += chunks_of(count) * rows_of(lens[orbital])
    for k in range(s.occ):
        counts[2 * s.occ + k] = jnp.int32(s.aux)
        offsets[2 * s.occ + k] = jnp.int32(0)

    for copy in copies[1] + copies[0]:
        copy.wait()


def count_kernel(s, partner, lens, aux_rows, _, over):
    devices = s.nocc // s.occ
    full = s.aux // LANES

    def ids(orbital):
        row = aux_rows[pl.ds(orbital, 1), :]
        return dot(bits(row // LOW, HIGH, s.aux), bits(lax.rem(row, LOW), LOW, s.aux), NT)

    over[0] = jnp.int32(0)

    def edge(e, _):
        source = e + 1
        user = source + 1 - 2 * lax.rem(e, 2)
        reads = [partner[user * s.pairs + q] - source * s.occ for q in range(s.pairs)]
        bound = jnp.int32(0)
        for k in range(s.occ):
            used = functools.reduce(jnp.logical_or, [read == k for read in reads])
            bound += jnp.where(used, full * rows_of(lens[source * s.occ + k]), 0)

        @pl.when(bound > s.room)
        def _():
            domains = [ids(user * s.occ + q) for q in range(s.occ)]
            need = jnp.int32(0)
            for k in range(s.occ):
                union = jnp.zeros((HIGH, LOW), jnp.float32)
                for q, domain in enumerate(domains):
                    used = functools.reduce(
                        jnp.logical_or, [read == k for read in reads[q :: s.occ]]
                    )
                    union += jnp.where(used, 1.0, 0.0) * domain
                taken = (union > 0.0) & (ids(source * s.occ + k) > 0.0)
                count = jnp.sum(jnp.where(taken, 1.0, 0.0)).astype(jnp.int32)
                need += chunks_of(count) * rows_of(lens[source * s.occ + k])
            over[0] = jnp.maximum(over[0], (need > s.room).astype(jnp.int32))

        return 0

    lax.fori_loop(0, devices - 2, edge, 0)


def own_kernel(
    s, here, partner, lens, counts, tables, aux_rows, blocks, amps, _, __, aligned, dens, ___, ____
):
    left = pl.program_id(0)
    me = here[0]
    wide = 2 * LANES
    chunks = s.aux // wide
    row = aux_rows[pl.ds(me * s.occ + left, 1), :]
    term = jnp.zeros((s.pao, s.pao), jnp.float32)
    rest = []

    for t in range(s.pairs // s.occ):
        right = partner[me * s.pairs + t * s.occ + left]
        l, kind = s.where_partner(me, right)
        place = places(row, tables[kind], lax.rem(right, s.occ))

        def some(c, t=t, place=place):
            aligned[t, 0, :, c * wide : (c + 1) * wide] = dot(
                blocks[0], picker(place, c), NT
            ).astype(jnp.bfloat16)

        for c in range(chunks - 1):
            some(c)
        rest.append((counts[l] > (chunks - 1) * wide, functools.partial(some, chunks - 1)))
        masked = kept(amps[t, 0], lens[me * s.occ + left], lens[right])
        term += dot(masked, masked, NT)

    dens[0] = term
    for needed, act in rest:
        pl.when(needed)(act)


def column_of(pao_rows, orbital):
    row = pao_rows[pl.ds(orbital, 1), :]
    return column(jnp.where(row < 0, -2, row)).astype(jnp.int16)


def row_of(pao_rows, orbital):
    return pao_rows[pl.ds(orbital, 1), :]


def near_kernel(
    s, ncpl, here, partner, listed, lens, coef, counts, offsets, _, pao_rows, sibling, own, aligned, dens_in, blocks, from_sibling, coupling, exchange, dens, wide, tall, dens_own, near_blocks, halo, sems
):
    p = pl.program_id(0)
    me = here[0]
    buddy = swapped(me)[0]
    low = jnp.minimum(me, buddy)
    fetches = [
        pltpu.make_async_copy(from_sibling, halo.at[pl.ds(0, s.rows), :], sems.at[0]),
        pltpu.make_async_copy(blocks, near_blocks, sems.at[1]),
        pltpu.make_async_copy(dens_in, dens_own, sems.at[2]),
    ]

    @pl.when(p == 0)
    def _():
        for fetch in fetches:
            fetch.start()
        dens[...] = jnp.zeros_like(dens)
        for k in range(s.pairs):
            wide[(me - low) * s.pairs + k] = own[k]
            unpack(s, sibling, k, wide.at[(buddy - low) * s.pairs + k])

    right_col = column_of(pao_rows, partner[me * s.pairs + p])
    left_col = column_of(pao_rows, me * s.occ + lax.rem(p, s.occ))
    left_rows = []
    for c in range(ncpl):
        m = listed[c, p]
        spot = m - low * s.pairs
        inside = (spot >= 0) & (spot < 2 * s.pairs)
        weight = jnp.where(inside, coef[c, p], 0.0)
        left_rows.append(row_of(pao_rows, s.first_orbital(m)))
        right_row = row_of(pao_rows, partner[m]).astype(jnp.int16)
        moved = dot(wide[jnp.clip(spot, 0, 2 * s.pairs - 1)], same(right_col, right_row), NT)
        tall[c * s.pao : (c + 1) * s.pao] = (weight * moved).astype(jnp.bfloat16)
    left_row = jnp.concatenate(left_rows, axis=1).astype(jnp.int16)
    coupling[0] = dot(same(left_col, left_row), tall[...])

    for side in range(2):
        m = (low + side) * s.pairs + p
        near = partner[m] - me * s.occ

        @pl.when((near >= 0) & (near < s.occ))
        def _():
            masked = kept(wide[side * s.pairs + p], lens[s.first_orbital(m)], lens[partner[m]])
            dens[near] += dot(masked, masked, TN)

    @pl.when(p == 0)
    def _():
        for fetch in fetches:
            fetch.wait()

    right = partner[me * s.pairs + p]
    l, kind = s.where_partner(me, right)

    @pl.when(kind == 2)
    def _():
        exchange[0] = dot(aligned[0], near_blocks[lax.rem(right, s.occ)], NT)

    @pl.when(kind == 0)
    def _():
        usual = s.aux - 2 * LANES
        use = functools.partial(
            compacted, s, counts[l], offsets[l], rows_of(lens[right]), aligned.at[0], halo
        )
        exchange[0] = use(0, usual)

        @pl.when(counts[l] > usual)
        def _():
            exchange[0] += use(usual, s.aux)

    @pl.when(p == s.pairs - 1)
    def _():
        dens[...] = (dens[...] + dens_own[...]) * (1.0 / s.pao)


def far_kernel(
    s, ncpl, here, partner, listed, lens, coef, pao_rows, gaps, other, own, near_coupling, exchange, near_dens, coupling, halves, dens, new_amps, energy, wide, news, whose, which, sems
):
    me = here[0]
    device = swapped(me)[1]
    dens[...] = near_dens[...]
    coupling[...] = near_coupling[...]
    for k in range(s.pairs):
        unpack(s, other, k, wide.at[k])

    number = jnp.int32(0)
    for p in range(s.pairs):
        for c in range(ncpl):
            spot = listed[c, p] - device * s.pairs
            whose[number] = p
            which[number] = c
            number += ((spot >= 0) & (spot < s.pairs)).astype(jnp.int32)

    def term(n):
        weight = jnp.where(n < number, 1.0, 0.0)
        n = jnp.minimum(n, number - 1)
        p, c = whose[n], which[n]
        m = listed[c, p]
        right_col = column_of(pao_rows, partner[me * s.pairs + p])
        left_col = column_of(pao_rows, me * s.occ + lax.rem(p, s.occ))
        right_row = row_of(pao_rows, partner[m]).astype(jnp.int16)
        left_row = row_of(pao_rows, s.first_orbital(m)).astype(jnp.int16)
        moved = dot(wide[m - device * s.pairs], same(right_col, right_row), NT)
        return p, weight * coef[c, p] * dot(same(left_col, left_row), moved.astype(jnp.bfloat16))

    def some(n, _):
        terms = [term(2 * n), term(2 * n + 1)]
        for p, value in terms:
            coupling[p] += value
        return 0

    lax.fori_loop(0, (number + 1) // 2, some, 0)

    for k in range(s.pairs):
        m = device * s.pairs + k
        inside = (m >= 0) & (m < s.npair)
        m = jnp.clip(m, 0, s.npair - 1)
        near = partner[m] - me * s.occ

        @pl.when(inside & (near >= 0) & (near < s.occ))
        def _():
            masked = kept(wide[k], lens[s.first_orbital(m)], lens[partner[m]])
            dens[near] += dot(masked, masked, TN) * (1.0 / s.pao)

    def result(p):
        return pltpu.make_async_copy(news.at[p], new_amps.at[p], sems.at[p])

    def finish(p, _):
        left, right = me * s.occ + lax.rem(p, s.occ), partner[me * s.pairs + p]
        kind = s.where_partner(me, right)[1]
        energy[p] = 0.0

        @pl.when(kind != 1)
        def _():
            news[p], energy[p] = update(
                s, lens[left], lens[right], exchange[p], own[p], coupling[p], gaps[pl.ds(left, 1), :], gaps[pl.ds(right, 1), :]
            )
            result(p).start()

        @pl.when(kind == 1)
        def _():
            coupling[p], halves[p] = ready(
                s, lens[left], lens[right], own[p], coupling[p], gaps[pl.ds(left, 1), :], gaps[pl.ds(right, 1), :]
            )

        return 0

    def wait(p, _):
        kind = s.where_partner(me, partner[me * s.pairs + p])[1]
        pl.when(kind != 1)(result(p).wait)
        return 0

    lax.fori_loop(0, s.pairs, finish, 0)
    lax.fori_loop(0, s.pairs, wait, 0)


def update(s, lens_left, lens_right, exchange, amp, coupling, gap_left, gap_right):
    left = column(gap_left)
    parts = []
    energy = jnp.zeros((s.pao, LANES), jnp.float32)
    for at in range(0, s.pao, LANES):
        lanes = slice(at, min(at + LANES, s.pao))
        part = amp[:, lanes].astype(jnp.float32)
        shape = part.shape
        mask = live(lens_left, lens_right - at, shape)
        denom = left[:, : shape[1]] + gap_right[:, lanes]
        inverse = pl.reciprocal(denom, approx=True)
        inverse = inverse * (2.0 - denom * inverse)
        moved = (exchange[:, lanes] - coupling[:, lanes]) * inverse
        parts.append(jnp.where(mask, 0.5 * (part - moved), 0.0).astype(jnp.bfloat16))
        term = jnp.where(mask, exchange[:, lanes] * part, 0.0)
        if shape[1] < LANES:
            term = jnp.concatenate([term, jnp.zeros((s.pao, LANES - shape[1]), jnp.float32)], axis=1)
        energy += term
    return jnp.concatenate(parts, axis=1), jnp.sum(energy) / s.pao


def ready(s, lens_left, lens_right, amp, coupling, gap_left, gap_right):
    left = column(gap_left)
    bases, halves = [], []
    for at in range(0, s.pao, LANES):
        lanes = slice(at, min(at + LANES, s.pao))
        part = amp[:, lanes].astype(jnp.float32)
        mask = live(lens_left, lens_right - at, part.shape)
        denom = left[:, : part.shape[1]] + gap_right[:, lanes]
        inverse = pl.reciprocal(denom, approx=True)
        inverse = inverse * (2.0 - denom * inverse)
        halves.append(jnp.where(mask, 0.5 * inverse, 0.0))
        bases.append(jnp.where(mask, 0.5 * (part + coupling[:, lanes] * inverse), 0.0))
    return jnp.concatenate(bases, axis=1), jnp.concatenate(halves, axis=1)


def compacted(s, count, at, step, aligned, halo, low, high):
    parts = []
    for c in range(low // LANES, high // LANES):
        spot = pl.multiple_of(jnp.minimum(at + c * step, halo.shape[0] - s.pao), 16)
        part = halo[pl.ds(spot, s.pao), :]
        parts.append(jnp.where(c * LANES < count, part, jnp.zeros_like(part)))
    return dot(aligned[:, low:high], jnp.concatenate(parts, axis=1), NT)


def last_kernel(s, beyond, here, partner, lens, counts, offsets, energy_in, halves, aligned, bases, amps, other, *refs):
    if beyond:
        more, _, new_amps, energy, halo, news, sums, far, sems = refs
        halo[: s.first] = other[...]
        rest = pltpu.make_async_copy(
            more, halo.at[pl.ds(s.first, s.rows - s.first)], sems.at[s.pairs]
        )
        rest.start()
        rest.wait()
    else:
        _, new_amps, energy, news, sums, far, sems = refs
        halo = other
    me = here[0]

    def result(n):
        return pltpu.make_async_copy(news.at[n], new_amps.at[far[n]], sems.at[n])

    number = jnp.int32(0)
    for p in range(s.pairs):
        energy[p] = energy_in[p]
        far[number] = p
        kind = s.where_partner(me, partner[me * s.pairs + p])[1]
        number += (kind == 1).astype(jnp.int32)

    usual = s.aux - 2 * LANES

    def pair_of(n):
        p = far[jnp.minimum(n, number - 1)]
        right = partner[me * s.pairs + p]
        return p, right, s.occ + lax.rem(right, s.occ)

    def some(n, _):
        pairs = [pair_of(2 * n + t) for t in range(2)]
        for t, (p, right, l) in enumerate(pairs):
            sums[t] = compacted(s, counts[l], offsets[l], rows_of(lens[right]), aligned.at[p], halo, 0, usual)
        for t, (p, right, l) in enumerate(pairs):

            @pl.when(counts[l] > usual)
            def _():
                sums[t] += compacted(
                    s, counts[l], offsets[l], rows_of(lens[right]), aligned.at[p], halo, usual, s.aux
                )

        for t, (p, right, l) in enumerate(pairs):
            exchange, half = sums[t], halves[p]
            news[2 * n + t] = (bases[p] - exchange * half).astype(jnp.bfloat16)
            product = jnp.where(half > 0.0, exchange * amps[p].astype(jnp.float32), 0.0)
            energy[p] = jnp.sum(product) / s.pao
        for t in range(2):
            pl.when(2 * n + t < number)(result(2 * n + t).start)
        return 0

    def wait(n, _):
        result(n).wait()
        return 0

    lax.fori_loop(0, (number + 1) // 2, some, 0)
    lax.fori_loop(0, number, wait, 0)


def position():
    return lax.axis_index(AXES)


def swap(array, role):
    count = 1
    for axis in AXES:
        count *= lax.axis_size(axis)
    route = []
    for low in range(role, count - 1, 2):
        route += [(low, low + 1), (low + 1, low)]
    return lax.ppermute(array, AXES, route)


def run(
    beyond, blocks, aux_domain, pao_domain, pao_gap, amplitudes, pair_partner, coupling_list, coupling_coef
):
    s = Sizes(blocks, amplitudes, pair_partner)
    ncpl = coupling_list.shape[1]
    me = position()
    here = me.astype(jnp.int32).reshape(1)
    blocks_t = jnp.swapaxes(blocks, 1, 2)

    smem = pl.BlockSpec(memory_space=pltpu.SMEM)
    vmem = pl.BlockSpec(memory_space=pltpu.VMEM)
    pinned = pl.BlockSpec(memory_space=pltpu.HBM)
    anywhere = pl.BlockSpec(memory_space=pl.ANY)
    plain = pltpu.CompilerParams(vmem_limit_bytes=24 * MIB)
    stepped = pltpu.CompilerParams(
        dimension_semantics=("arbitrary",), vmem_limit_bytes=30 * MIB
    )
    alone = pltpu.CompilerParams(vmem_limit_bytes=34 * MIB)
    square = pl.BlockSpec((1, s.pao, s.pao), lambda p, *_: (p, 0, 0))
    all_dens = pl.BlockSpec((s.occ, s.pao, s.pao), lambda p, *_: (0, 0, 0))
    squares = jax.ShapeDtypeStruct((s.pairs, s.pao, s.pao), jnp.float32)
    dens_shape = jax.ShapeDtypeStruct((s.occ, s.pao, s.pao), jnp.float32)

    def cost(work, data):
        return pl.CostEstimate(flops=work, bytes_accessed=data, transcendentals=0)

    whole, tail, share = packing(s)
    slots = s.pairs + s.pairs // share
    slim = pl.pallas_call(
        functools.partial(slim_kernel, s),
        in_specs=[vmem],
        out_specs=vmem,
        out_shape=jax.ShapeDtypeStruct((slots, s.pao, whole), jnp.bfloat16),
        compiler_params=plain,
        cost_estimate=cost(10**6, 4 * 10**6),
        name="slim",
    )(amplitudes)
    amps_other = swap(slim, 1)
    amps_sibling = swap(slim, 0)

    lens = jnp.sum((pao_domain >= 0).astype(jnp.int32), axis=1)

    lists = 3 * s.occ
    to_sibling, to_other, to_other_more, tables, pao_rows, gap_rows, counts, offsets = pl.pallas_call(
        functools.partial(pack_kernel, s),
        in_specs=[smem] * 3 + [vmem] * 4 + [anywhere],
        out_specs=[pinned] * 3 + [vmem] * 3 + [smem] * 2,
        out_shape=[
            jax.ShapeDtypeStruct((s.rows, LANES), jnp.bfloat16),
            jax.ShapeDtypeStruct((s.first, LANES), jnp.bfloat16),
            jax.ShapeDtypeStruct((s.rows - s.first, LANES), jnp.bfloat16),
            jax.ShapeDtypeStruct((3, 2 * LOW, s.occ * HIGH), jnp.bfloat16),
            jax.ShapeDtypeStruct(pao_domain.shape, pao_domain.dtype),
            jax.ShapeDtypeStruct(pao_gap.shape, pao_gap.dtype),
            jax.ShapeDtypeStruct((lists,), jnp.int32),
            jax.ShapeDtypeStruct((lists,), jnp.int32),
        ],
        scratch_shapes=[
            pltpu.VMEM((3, 2 * LOW, s.occ * HIGH), jnp.float32),
            pltpu.VMEM((3 * s.occ, 2 * LOW, s.occ * HIGH), jnp.float32),
            pltpu.VMEM((2, 2 * LOW, s.occ * HIGH), jnp.bfloat16),
            pltpu.SMEM((s.occ,), jnp.int32),
            pltpu.VMEM((2, s.rows + s.pao, LANES), jnp.bfloat16),
            pltpu.SemaphoreType.DMA((3,)),
        ],
        compiler_params=plain,
        cost_estimate=cost(10**11, 10**5),
        name="pack",
    )(here, pair_partner, lens, aux_domain, blocks_t, pao_domain.T, pao_gap.T, slim)

    repeats = s.pairs // s.occ
    both = pl.BlockSpec((repeats, 1, s.pao, s.aux), lambda g: (0, g, 0, 0))
    aligned, dens, to_other, to_sibling = pl.pallas_call(
        functools.partial(own_kernel, s),
        grid=(s.occ,),
        in_specs=[smem] * 4
        + [
            vmem,
            vmem,
            pl.BlockSpec((1, s.pao, s.aux), lambda g: (g, 0, 0)),
            pl.BlockSpec((repeats, 1, s.pao, s.pao), lambda g: (0, g, 0, 0)),
            anywhere,
            anywhere,
        ],
        out_specs=[both, pl.BlockSpec((1, s.pao, s.pao), lambda g: (g, 0, 0)), anywhere, anywhere],
        out_shape=[
            jax.ShapeDtypeStruct((repeats, s.occ, s.pao, s.aux), jnp.bfloat16),
            dens_shape,
            jax.ShapeDtypeStruct(to_other.shape, to_other.dtype),
            jax.ShapeDtypeStruct(to_sibling.shape, to_sibling.dtype),
        ],
        input_output_aliases={8: 2, 9: 3},
        compiler_params=stepped,
        cost_estimate=cost(10**11, 10**5),
        name="own",
    )(
        here, pair_partner, lens, counts, tables, aux_domain, blocks_t,
        amplitudes.reshape(repeats, s.occ, s.pao, s.pao), to_other, to_sibling,
    )
    from_other = swap(to_other, 1)
    from_sibling = swap(to_sibling, 0)
    aligned = aligned.reshape(s.pairs, s.pao, s.aux)

    (over,) = pl.pallas_call(
        functools.partial(count_kernel, s),
        in_specs=[smem] * 2 + [vmem, anywhere],
        out_specs=[smem],
        out_shape=[jax.ShapeDtypeStruct((1,), jnp.int32)],
        compiler_params=plain,
        cost_estimate=cost(10**11, 10**5),
        name="count",
    )(pair_partner, lens, aux_domain, dens)

    coupling, exchange, dens = pl.pallas_call(
        functools.partial(near_kernel, s, ncpl),
        grid=(s.pairs,),
        in_specs=[smem] * 8
        + [vmem] * 3
        + [pl.BlockSpec((1, s.pao, s.aux), lambda p: (p, 0, 0))]
        + [anywhere, pinned, anywhere],
        out_specs=[square, square, all_dens],
        out_shape=[squares, squares, dens_shape],
        scratch_shapes=[
            pltpu.VMEM((2 * s.pairs, s.pao, s.pao), jnp.bfloat16),
            pltpu.VMEM((ncpl * s.pao, s.pao), jnp.bfloat16),
            pltpu.VMEM((s.occ, s.pao, s.pao), jnp.float32),
            pltpu.VMEM((s.occ, s.pao, s.aux), jnp.bfloat16),
            pltpu.VMEM((s.rows + s.pao, LANES), jnp.bfloat16),
            pltpu.SemaphoreType.DMA((3,)),
        ],
        compiler_params=stepped,
        cost_estimate=cost(10**11, 10**5),
        name="near",
    )(
        here, pair_partner, coupling_list.T, lens, coupling_coef.T, counts, offsets, over,
        pao_rows, amps_sibling, amplitudes, aligned, dens, blocks_t, from_sibling,
    )

    bases, halves, densities, some_amps, some_energies = pl.pallas_call(
        functools.partial(far_kernel, s, ncpl),
        in_specs=[smem] * 5 + [vmem] * 7,
        out_specs=[vmem, vmem, vmem, pinned, smem],
        out_shape=[
            squares,
            squares,
            dens_shape,
            jax.ShapeDtypeStruct(amplitudes.shape, amplitudes.dtype),
            jax.ShapeDtypeStruct((s.pairs,), jnp.float32),
        ],
        scratch_shapes=[
            pltpu.VMEM((s.pairs, s.pao, s.pao), jnp.bfloat16),
            pltpu.VMEM((s.pairs, s.pao, s.pao), jnp.bfloat16),
            pltpu.SMEM((s.pairs * ncpl,), jnp.int32),
            pltpu.SMEM((s.pairs * ncpl,), jnp.int32),
            pltpu.SemaphoreType.DMA((s.pairs,)),
        ],
        compiler_params=alone,
        cost_estimate=cost(10**10, 10**5),
        name="far",
    )(
        here, pair_partner, coupling_list.T, lens, coupling_coef.T,
        pao_rows, gap_rows, amps_other, amplitudes, coupling, exchange, dens,
    )

    more = (swap(to_other_more, 1),) if beyond else ()
    scratch = [
        pltpu.VMEM((s.pairs, s.pao, s.pao), jnp.bfloat16),
        pltpu.VMEM((2, s.pao, s.pao), jnp.float32),
        pltpu.SMEM((s.pairs,), jnp.int32),
        pltpu.SemaphoreType.DMA((s.pairs + 1,)),
    ]
    if beyond:
        scratch = [pltpu.VMEM((s.rows + s.pao, LANES), jnp.bfloat16)] + scratch
    new_amps, energies = pl.pallas_call(
        functools.partial(last_kernel, s, beyond),
        in_specs=[smem] * 6 + [vmem] * 5 + [pinned] * (len(more) + 1),
        out_specs=[pinned, smem],
        out_shape=[
            jax.ShapeDtypeStruct(amplitudes.shape, amplitudes.dtype),
            jax.ShapeDtypeStruct((s.pairs,), jnp.float32),
        ],
        scratch_shapes=scratch,
        input_output_aliases={11 + len(more): 0},
        compiler_params=alone,
        cost_estimate=cost(2 * s.pairs * s.pao * s.pao * s.aux, 2 * 10**7),
        name="last",
    )(
        here, pair_partner, lens, counts, offsets, some_energies,
        halves, aligned, bases, amplitudes, from_other, *more, some_amps,
    )
    return new_amps, energies, densities, over


def local(*arrays):
    new_amps, energies, densities, over = run(False, *arrays)
    new_amps, energies = lax.cond(
        over[0] > 0, lambda ops: run(True, *ops[2:])[:2], lambda ops: ops[:2], (new_amps, energies) + arrays
    )
    return (new_amps, energies, densities)


def solution(mesh):
    return jax.shard_map(
        local,
        mesh=mesh,
        in_specs=(
            P(AXES, None, None),
            P(),
            P(),
            P(),
            P(AXES, None, None),
            P(),
            P(AXES, None),
            P(AXES, None),
        ),
        out_specs=(P(AXES, None, None), P(AXES), P(AXES, None, None)),
        check_vma=False,
    )
```

```python
import functools

import jax
import jax.numpy as jnp
from jax import lax
from jax.experimental import pallas as pl
from jax.experimental.pallas import tpu as pltpu
from jax.sharding import PartitionSpec as P

AXES = ("orb", "pair")
MIB = 1024 * 1024
AUX_IDS = 2048
LOW = 64
HIGH = AUX_IDS // LOW
BASE = 32
LANES = 128
FIRST, WHOLE = 40, 64
NN = (((1,), (0,)), ((), ()))
NT = (((1,), (1,)), ((), ()))
TN = (((0,), (0,)), ((), ()))


def dot(a, b, dims=NN):
    return lax.dot_general(a, b, dims, preferred_element_type=jnp.float32)


def one_where(equal, value=1.0):
    return jnp.where(equal, value, 0.0).astype(jnp.bfloat16)


def iota(shape, dim):
    return lax.broadcasted_iota(jnp.int32, shape, dim)


def live(rows, cols, shape):
    return (iota(shape, 0) < rows) & (iota(shape, 1) < cols)


def kept(amp, rows, cols):
    return jnp.where(live(rows, cols, amp.shape), amp.astype(jnp.float32), 0.0).astype(amp.dtype)


def short_where(equal):
    one = jnp.ones(equal.shape, jnp.bfloat16)
    return jnp.where(equal, one, jnp.zeros_like(one))


def column(row):
    return jnp.broadcast_to(row, (LANES, row.shape[1])).T


def same(col, row):
    parts = []
    for at in range(0, row.shape[1], LANES):
        piece = row[:, at : at + LANES]
        wide = jnp.broadcast_to(piece, (col.shape[0], piece.shape[1]))
        parts.append(short_where(col[:, : piece.shape[1]] == wide))
    return jnp.concatenate(parts, axis=1)


def chunks_of(count):
    return (count + LANES - 1) // LANES


def rows_of(length):
    return (length + 15) // 16 * 16


def swapped(me):
    odd = lax.rem(me, 2)
    return me + 1 - 2 * odd, me - 1 + 2 * odd


class Sizes:
    def __init__(self, blocks, amplitudes, pair_partner):
        self.occ = blocks.shape[0]
        self.aux = blocks.shape[1]
        self.pao = blocks.shape[2]
        self.pairs = amplitudes.shape[0]
        self.npair = pair_partner.shape[0]
        self.nocc = self.npair // self.pairs * self.occ
        self.rows = self.occ * self.pao * (self.aux // LANES)
        self.first = self.rows * FIRST // WHOLE // 16 * 16
        self.room = self.first - self.pao // 2

    def first_orbital(self, pair):
        return pair // self.pairs * self.occ + lax.rem(pair, self.occ)

    def where_partner(self, me, right):
        device = right // self.occ
        sibling, _ = swapped(me)
        kind = jnp.where(device == me, 2, jnp.where(device == sibling, 0, 1))
        return kind * self.occ + lax.rem(right, self.occ), kind


def packing(s):
    whole = s.pao // LANES * LANES
    tail = s.pao - whole
    share = whole // tail
    return whole, tail, share


def slim_kernel(s, amps, out):
    whole, tail, share = packing(s)
    for k in range(s.pairs):
        out[k] = amps[k, :, :whole]
    for g in range(s.pairs // share):
        tails = [amps[g * share + t, :, whole:] for t in range(share)]
        out[s.pairs + g] = jnp.concatenate(tails, axis=1)


def unpack(s, packed, k, out):
    whole, tail, share = packing(s)
    out[:, :whole] = packed[k]
    spot = k % share * tail
    out[:, whole:] = packed[s.pairs + k // share, :, spot : spot + tail]


def bits(values, count, lanes):
    levels = iota((count, lanes), 0).astype(jnp.bfloat16)
    return short_where(levels == jnp.broadcast_to(values.astype(jnp.bfloat16), (count, lanes)))


def places(row, table, k):
    found = dot(table, bits(row // LOW + k * HIGH, table.shape[1], row.shape[1]))
    low = bits(lax.rem(row, LOW), LOW, row.shape[1]).astype(jnp.float32)
    return jnp.sum((found[:LOW] * BASE + found[LOW:]) * low, axis=0, keepdims=True)


def picker(place, chunk):
    wide = 2 * LANES
    middle = chunk * wide + LANES + 1
    spot = (place - jnp.asarray(middle).astype(jnp.float32)).astype(jnp.bfloat16)
    levels = (iota((wide, place.shape[1]), 0) - LANES).astype(jnp.bfloat16)
    return short_where(levels == jnp.broadcast_to(spot, levels.shape))


def chunkwise(s, count, act):
    for c in range(s.aux // (2 * LANES)):
        pl.when(count > c * 2 * LANES)(functools.partial(act, c))


def split_place(place, row):
    part = jnp.where(row < LOW, place // BASE, lax.rem(place, BASE))
    return part.astype(jnp.float32).astype(jnp.bfloat16)


def pack_kernel(
    s, here, partner, lens, aux_rows, blocks, pao_cols, gap_cols, _, to_sibling, to_other, to_other_more, tables, pao_rows, gap_rows, counts, offsets, maps, users, sends, needed, bufs, sems
):
    me = here[0]
    peers = swapped(me)
    pao_rows[...] = pao_cols[...].T
    gap_rows[...] = gap_cols[...].T

    for g, device in enumerate((me,) + peers):
        for k in range(s.occ):
            orbital = jnp.clip(device * s.occ + k, 0, s.nocc - 1)
            row = aux_rows[pl.ds(orbital, 1), :]
            by_high = bits(row // LOW, HIGH, s.aux)
            by_low = bits(lax.rem(row, LOW), LOW, s.aux)
            here_map = dot(jnp.concatenate([by_low, by_low], axis=0), by_high, NT)
            maps[g, :, k * HIGH : (k + 1) * HIGH] = here_map
            users[g * s.occ + k] = jnp.concatenate([here_map] * s.occ, axis=1)
            if g == 0:
                spot = iota((LOW, s.aux), 1) + 1
                parts = jnp.concatenate(
                    [
                        (spot // BASE).astype(jnp.float32).astype(jnp.bfloat16) * by_low,
                        lax.rem(spot, BASE).astype(jnp.float32).astype(jnp.bfloat16) * by_low,
                    ],
                    axis=0,
                )
                tables[2, :, k * HIGH : (k + 1) * HIGH] = dot(parts, by_high, NT).astype(
                    jnp.bfloat16
                )

    wide = s.occ * HIGH
    sub, lane = iota((2 * LOW, 2 * LOW), 0), iota((2 * LOW, 2 * LOW), 1)
    ahead = one_where((lane < LOW) & (lane < lax.rem(sub, LOW)))
    first = one_where(lane < LOW)
    sub, lane = iota((wide, wide), 0), iota((wide, wide), 1)
    above = one_where((sub // HIGH == lane // HIGH) & (sub < lane))
    level = iota((2 * LOW, wide), 0)
    owner = iota((1, wide), 1) // HIGH

    def listing(target, target_device, user, user_device):
        union = jnp.zeros((2 * LOW, wide), jnp.float32)
        for q in range(s.occ):
            uses = jnp.zeros((1, wide), jnp.float32)
            for pair in range(q, s.pairs, s.occ):
                pair += user_device * s.pairs
                inside = (pair >= 0) & (pair < s.npair)
                k = partner[jnp.clip(pair, 0, s.npair - 1)] - target_device * s.occ
                uses += jnp.where((owner == k) & inside, 1.0, 0.0)
            union += uses * users[user * s.occ + q]
        taken = (union > 0.0) & (maps[target] > 0.0)
        flags = one_where(taken)
        total = dot(first, flags)
        place = dot(ahead, flags) + dot(total.astype(jnp.bfloat16), above) + 1.0
        place = jnp.where(taken, place, 0.0).astype(jnp.int32)
        found = [
            jnp.sum(jnp.where(owner == k, total[:1], 0.0)).astype(jnp.int32) for k in range(s.occ)
        ]
        return split_place(place, level), found

    copies = {
        0: [pltpu.make_async_copy(bufs.at[0, pl.ds(0, s.rows)], to_sibling, sems.at[0])],
        1: [
            pltpu.make_async_copy(bufs.at[1, pl.ds(0, s.first)], to_other, sems.at[1]),
            pltpu.make_async_copy(
                bufs.at[1, pl.ds(s.first, s.rows - s.first)], to_other_more, sems.at[2]
            ),
        ],
    }
    for r in (1, 0):
        sends[r], found = listing(0, me, 1 + r, peers[r])
        for k, count in enumerate(found):
            needed[k] = count

        def send(k, at, r=r):
            count = needed[k]
            step = rows_of(lens[me * s.occ + k])

            @pl.when(count > 0)
            def _():
                place = places(aux_rows[pl.ds(me * s.occ + k, 1), :], sends[r], k)

                def some(c):
                    got = dot(blocks[k], picker(place, c), NT).astype(jnp.bfloat16)
                    spot = pl.multiple_of(at + 2 * c * step, 16)
                    bufs[r, pl.ds(spot, s.pao), :] = got[:, :LANES]

                    @pl.when((2 * c + 1) * LANES < count)
                    def _():
                        bufs[r, pl.ds(pl.multiple_of(spot + step, 16), s.pao), :] = got[:, LANES:]

                chunkwise(s, count, some)

            return at + chunks_of(count) * step

        lax.fori_loop(0, s.occ, send, jnp.int32(0))
        for copy in copies[r]:
            copy.start()

    for r in range(2):
        tables[r], found = listing(1 + r, peers[r], 0, me)
        at = jnp.int32(0)
        for k, count in enumerate(found):
            orbital = jnp.clip(peers[r] * s.occ + k, 0, s.nocc - 1)
            counts[r * s.occ + k] = count
            offsets[r * s.occ + k] = at
            at += chunks_of(count) * rows_of(lens[orbital])
    for k in range(s.occ):
        counts[2 * s.occ + k] = jnp.int32(s.aux)
        offsets[2 * s.occ + k] = jnp.int32(0)

    for copy in copies[1] + copies[0]:
        copy.wait()


def count_kernel(s, partner, lens, aux_rows, _, over):
    devices = s.nocc // s.occ
    full = s.aux // LANES

    def ids(orbital):
        row = aux_rows[pl.ds(orbital, 1), :]
        return dot(bits(row // LOW, HIGH, s.aux), bits(lax.rem(row, LOW), LOW, s.aux), NT)

    over[0] = jnp.int32(0)

    def edge(e, _):
        source = e + 1
        user = source + 1 - 2 * lax.rem(e, 2)
        reads = [partner[user * s.pairs + q] - source * s.occ for q in range(s.pairs)]
        bound = jnp.int32(0)
        for k in range(s.occ):
            used = functools.reduce(jnp.logical_or, [read == k for read in reads])
            bound += jnp.where(used, full * rows_of(lens[source * s.occ + k]), 0)

        @pl.when(bound > s.room)
        def _():
            domains = [ids(user * s.occ + q) for q in range(s.occ)]
            need = jnp.int32(0)
            for k in range(s.occ):
                union = jnp.zeros((HIGH, LOW), jnp.float32)
                for q, domain in enumerate(domains):
                    used = functools.reduce(
                        jnp.logical_or, [read == k for read in reads[q :: s.occ]]
                    )
                    union += jnp.where(used, 1.0, 0.0) * domain
                taken = (union > 0.0) & (ids(source * s.occ + k) > 0.0)
                count = jnp.sum(jnp.where(taken, 1.0, 0.0)).astype(jnp.int32)
                need += chunks_of(count) * rows_of(lens[source * s.occ + k])
            over[0] = jnp.maximum(over[0], (need > s.room).astype(jnp.int32))

        return 0

    lax.fori_loop(0, devices - 2, edge, 0)


def own_kernel(
    s, here, partner, lens, counts, tables, aux_rows, blocks, amps, _, __, aligned, dens, ___, ____
):
    left = pl.program_id(0)
    me = here[0]
    wide = 2 * LANES
    chunks = s.aux // wide
    row = aux_rows[pl.ds(me * s.occ + left, 1), :]
    term = jnp.zeros((s.pao, s.pao), jnp.float32)
    rest = []

    for t in range(s.pairs // s.occ):
        right = partner[me * s.pairs + t * s.occ + left]
        l, kind = s.where_partner(me, right)
        place = places(row, tables[kind], lax.rem(right, s.occ))

        def some(c, t=t, place=place):
            aligned[t, 0, :, c * wide : (c + 1) * wide] = dot(
                blocks[0], picker(place, c), NT
            ).astype(jnp.bfloat16)

        for c in range(chunks - 1):
            some(c)
        rest.append((counts[l] > (chunks - 1) * wide, functools.partial(some, chunks - 1)))
        masked = kept(amps[t, 0], lens[me * s.occ + left], lens[right])
        term += dot(masked, masked, NT)

    dens[0] = term
    for needed, act in rest:
        pl.when(needed)(act)


def column_of(pao_rows, orbital):
    row = pao_rows[pl.ds(orbital, 1), :]
    return column(jnp.where(row < 0, -2, row)).astype(jnp.int16)


def row_of(pao_rows, orbital):
    return pao_rows[pl.ds(orbital, 1), :]


def near_kernel(
    s, ncpl, here, partner, listed, lens, coef, counts, offsets, _, pao_rows, sibling, own, aligned, dens_in, blocks, from_sibling, coupling, exchange, dens, wide, tall, dens_own, near_blocks, halo, sems
):
    p = pl.program_id(0)
    me = here[0]
    buddy = swapped(me)[0]
    low = jnp.minimum(me, buddy)
    fetches = [
        pltpu.make_async_copy(from_sibling, halo.at[pl.ds(0, s.rows), :], sems.at[0]),
        pltpu.make_async_copy(blocks, near_blocks, sems.at[1]),
        pltpu.make_async_copy(dens_in, dens_own, sems.at[2]),
    ]

    @pl.when(p == 0)
    def _():
        for fetch in fetches:
            fetch.start()
        dens[...] = jnp.zeros_like(dens)
        for k in range(s.pairs):
            wide[(me - low) * s.pairs + k] = own[k]
            unpack(s, sibling, k, wide.at[(buddy - low) * s.pairs + k])

    right_col = column_of(pao_rows, partner[me * s.pairs + p])
    left_col = column_of(pao_rows, me * s.occ + lax.rem(p, s.occ))
    left_rows = []
    for c in range(ncpl):
        m = listed[c, p]
        spot = m - low * s.pairs
        inside = (spot >= 0) & (spot < 2 * s.pairs)
        weight = jnp.where(inside, coef[c, p], 0.0)
        left_rows.append(row_of(pao_rows, s.first_orbital(m)))
        right_row = row_of(pao_rows, partner[m]).astype(jnp.int16)
        moved = dot(wide[jnp.clip(spot, 0, 2 * s.pairs - 1)], same(right_col, right_row), NT)
        tall[c * s.pao : (c + 1) * s.pao] = (weight * moved).astype(jnp.bfloat16)
    left_row = jnp.concatenate(left_rows, axis=1).astype(jnp.int16)
    coupling[0] = dot(same(left_col, left_row), tall[...])

    for side in range(2):
        m = (low + side) * s.pairs + p
        near = partner[m] - me * s.occ

        @pl.when((near >= 0) & (near < s.occ))
        def _():
            masked = kept(wide[side * s.pairs + p], lens[s.first_orbital(m)], lens[partner[m]])
            dens[near] += dot(masked, masked, TN)

    @pl.when(p == 0)
    def _():
        for fetch in fetches:
            fetch.wait()

    right = partner[me * s.pairs + p]
    l, kind = s.where_partner(me, right)

    @pl.when(kind == 2)
    def _():
        exchange[0] = dot(aligned[0], near_blocks[lax.rem(right, s.occ)], NT)

    @pl.when(kind == 0)
    def _():
        usual = s.aux - 2 * LANES
        use = functools.partial(
            compacted, s, counts[l], offsets[l], rows_of(lens[right]), aligned.at[0], halo
        )
        exchange[0] = use(0, usual)

        @pl.when(counts[l] > usual)
        def _():
            exchange[0] += use(usual, s.aux)

    @pl.when(p == s.pairs - 1)
    def _():
        dens[...] = (dens[...] + dens_own[...]) * (1.0 / s.pao)


def far_kernel(
    s, ncpl, here, partner, listed, lens, coef, pao_rows, gaps, other, own, near_coupling, exchange, near_dens, coupling, halves, dens, new_amps, energy, wide, news, whose, which, sems
):
    me = here[0]
    device = swapped(me)[1]
    dens[...] = near_dens[...]
    coupling[...] = near_coupling[...]
    for k in range(s.pairs):
        unpack(s, other, k, wide.at[k])

    number = jnp.int32(0)
    for p in range(s.pairs):
        for c in range(ncpl):
            spot = listed[c, p] - device * s.pairs
            whose[number] = p
            which[number] = c
            number += ((spot >= 0) & (spot < s.pairs)).astype(jnp.int32)

    def term(n):
        weight = jnp.where(n < number, 1.0, 0.0)
        n = jnp.minimum(n, number - 1)
        p, c = whose[n], which[n]
        m = listed[c, p]
        right_col = column_of(pao_rows, partner[me * s.pairs + p])
        left_col = column_of(pao_rows, me * s.occ + lax.rem(p, s.occ))
        right_row = row_of(pao_rows, partner[m]).astype(jnp.int16)
        left_row = row_of(pao_rows, s.first_orbital(m)).astype(jnp.int16)
        moved = dot(wide[m - device * s.pairs], same(right_col, right_row), NT)
        return p, weight * coef[c, p] * dot(same(left_col, left_row), moved.astype(jnp.bfloat16))

    def some(n, _):
        terms = [term(2 * n), term(2 * n + 1)]
        for p, value in terms:
            coupling[p] += value
        return 0

    lax.fori_loop(0, (number + 1) // 2, some, 0)

    for k in range(s.pairs):
        m = device * s.pairs + k
        inside = (m >= 0) & (m < s.npair)
        m = jnp.clip(m, 0, s.npair - 1)
        near = partner[m] - me * s.occ

        @pl.when(inside & (near >= 0) & (near < s.occ))
        def _():
            masked = kept(wide[k], lens[s.first_orbital(m)], lens[partner[m]])
            dens[near] += dot(masked, masked, TN) * (1.0 / s.pao)

    def result(p):
        return pltpu.make_async_copy(news.at[p], new_amps.at[p], sems.at[p])

    def finish(p, _):
        left, right = me * s.occ + lax.rem(p, s.occ), partner[me * s.pairs + p]
        kind = s.where_partner(me, right)[1]
        energy[p] = 0.0

        @pl.when(kind != 1)
        def _():
            news[p], energy[p] = update(
                s, lens[left], lens[right], exchange[p], own[p], coupling[p], gaps[pl.ds(left, 1), :], gaps[pl.ds(right, 1), :]
            )
            result(p).start()

        @pl.when(kind == 1)
        def _():
            coupling[p], halves[p] = ready(
                s, lens[left], lens[right], own[p], coupling[p], gaps[pl.ds(left, 1), :], gaps[pl.ds(right, 1), :]
            )

        return 0

    def wait(p, _):
        kind = s.where_partner(me, partner[me * s.pairs + p])[1]
        pl.when(kind != 1)(result(p).wait)
        return 0

    lax.fori_loop(0, s.pairs, finish, 0)
    lax.fori_loop(0, s.pairs, wait, 0)


def update(s, lens_left, lens_right, exchange, amp, coupling, gap_left, gap_right):
    left = column(gap_left)
    parts = []
    energy = jnp.zeros((s.pao, LANES), jnp.float32)
    for at in range(0, s.pao, LANES):
        lanes = slice(at, min(at + LANES, s.pao))
        part = amp[:, lanes].astype(jnp.float32)
        shape = part.shape
        mask = live(lens_left, lens_right - at, shape)
        denom = left[:, : shape[1]] + gap_right[:, lanes]
        inverse = pl.reciprocal(denom, approx=True)
        inverse = inverse * (2.0 - denom * inverse)
        moved = (exchange[:, lanes] - coupling[:, lanes]) * inverse
        parts.append(jnp.where(mask, 0.5 * (part - moved), 0.0).astype(jnp.bfloat16))
        term = jnp.where(mask, exchange[:, lanes] * part, 0.0)
        if shape[1] < LANES:
            term = jnp.concatenate([term, jnp.zeros((s.pao, LANES - shape[1]), jnp.float32)], axis=1)
        energy += term
    return jnp.concatenate(parts, axis=1), jnp.sum(energy) / s.pao


def ready(s, lens_left, lens_right, amp, coupling, gap_left, gap_right):
    left = column(gap_left)
    bases, halves = [], []
    for at in range(0, s.pao, LANES):
        lanes = slice(at, min(at + LANES, s.pao))
        part = amp[:, lanes].astype(jnp.float32)
        mask = live(lens_left, lens_right - at, part.shape)
        denom = left[:, : part.shape[1]] + gap_right[:, lanes]
        inverse = pl.reciprocal(denom, approx=True)
        inverse = inverse * (2.0 - denom * inverse)
        halves.append(jnp.where(mask, 0.5 * inverse, 0.0))
        bases.append(jnp.where(mask, 0.5 * (part + coupling[:, lanes] * inverse), 0.0))
    return jnp.concatenate(bases, axis=1), jnp.concatenate(halves, axis=1)


def compacted(s, count, at, step, aligned, halo, low, high):
    parts = []
    for c in range(low // LANES, high // LANES):
        spot = pl.multiple_of(jnp.minimum(at + c * step, halo.shape[0] - s.pao), 16)
        part = halo[pl.ds(spot, s.pao), :]
        parts.append(jnp.where(c * LANES < count, part, jnp.zeros_like(part)))
    return dot(aligned[:, low:high], jnp.concatenate(parts, axis=1), NT)


def last_kernel(s, beyond, here, partner, lens, counts, offsets, energy_in, halves, aligned, bases, amps, other, *refs):
    if beyond:
        more, _, new_amps, energy, halo, news, sums, far, sems = refs
        halo[: s.first] = other[...]
        rest = pltpu.make_async_copy(
            more, halo.at[pl.ds(s.first, s.rows - s.first)], sems.at[s.pairs]
        )
        rest.start()
        rest.wait()
    else:
        _, new_amps, energy, news, sums, far, sems = refs
        halo = other
    me = here[0]

    def result(n):
        return pltpu.make_async_copy(news.at[n], new_amps.at[far[n]], sems.at[n])

    number = jnp.int32(0)
    for p in range(s.pairs):
        energy[p] = energy_in[p]
        far[number] = p
        kind = s.where_partner(me, partner[me * s.pairs + p])[1]
        number += (kind == 1).astype(jnp.int32)

    usual = s.aux - 2 * LANES

    def pair_of(n):
        p = far[jnp.minimum(n, number - 1)]
        right = partner[me * s.pairs + p]
        return p, right, s.occ + lax.rem(right, s.occ)

    def some(n, _):
        pairs = [pair_of(2 * n + t) for t in range(2)]
        for t, (p, right, l) in enumerate(pairs):
            sums[t] = compacted(s, counts[l], offsets[l], rows_of(lens[right]), aligned.at[p], halo, 0, usual)
        for t, (p, right, l) in enumerate(pairs):

            @pl.when(counts[l] > usual)
            def _():
                sums[t] += compacted(
                    s, counts[l], offsets[l], rows_of(lens[right]), aligned.at[p], halo, usual, s.aux
                )

        for t, (p, right, l) in enumerate(pairs):
            exchange, half = sums[t], halves[p]
            news[2 * n + t] = (bases[p] - exchange * half).astype(jnp.bfloat16)
            product = jnp.where(half > 0.0, exchange * amps[p].astype(jnp.float32), 0.0)
            energy[p] = jnp.sum(product) / s.pao
        for t in range(2):
            pl.when(2 * n + t < number)(result(2 * n + t).start)
        return 0

    def wait(n, _):
        result(n).wait()
        return 0

    lax.fori_loop(0, (number + 1) // 2, some, 0)
    lax.fori_loop(0, number, wait, 0)


def position():
    return lax.axis_index(AXES)


def swap(array, role):
    count = 1
    for axis in AXES:
        count *= lax.axis_size(axis)
    route = []
    for low in range(role, count - 1, 2):
        route += [(low, low + 1), (low + 1, low)]
    return lax.ppermute(array, AXES, route)


def run(
    beyond, blocks, aux_domain, pao_domain, pao_gap, amplitudes, pair_partner, coupling_list, coupling_coef
):
    s = Sizes(blocks, amplitudes, pair_partner)
    ncpl = coupling_list.shape[1]
    me = position()
    here = me.astype(jnp.int32).reshape(1)
    blocks_t = jnp.swapaxes(blocks, 1, 2)

    smem = pl.BlockSpec(memory_space=pltpu.SMEM)
    vmem = pl.BlockSpec(memory_space=pltpu.VMEM)
    pinned = pl.BlockSpec(memory_space=pltpu.HBM)
    anywhere = pl.BlockSpec(memory_space=pl.ANY)
    plain = pltpu.CompilerParams(vmem_limit_bytes=24 * MIB)
    stepped = pltpu.CompilerParams(
        dimension_semantics=("arbitrary",), vmem_limit_bytes=30 * MIB
    )
    alone = pltpu.CompilerParams(vmem_limit_bytes=28 * MIB)
    square = pl.BlockSpec((1, s.pao, s.pao), lambda p, *_: (p, 0, 0))
    all_dens = pl.BlockSpec((s.occ, s.pao, s.pao), lambda p, *_: (0, 0, 0))
    squares = jax.ShapeDtypeStruct((s.pairs, s.pao, s.pao), jnp.float32)
    dens_shape = jax.ShapeDtypeStruct((s.occ, s.pao, s.pao), jnp.float32)

    def cost(work, data):
        return pl.CostEstimate(flops=work, bytes_accessed=data, transcendentals=0)

    whole, tail, share = packing(s)
    slots = s.pairs + s.pairs // share
    slim = pl.pallas_call(
        functools.partial(slim_kernel, s),
        in_specs=[vmem],
        out_specs=vmem,
        out_shape=jax.ShapeDtypeStruct((slots, s.pao, whole), jnp.bfloat16),
        compiler_params=plain,
        cost_estimate=cost(10**6, 4 * 10**6),
        name="slim",
    )(amplitudes)
    amps_other = swap(slim, 1)
    amps_sibling = swap(slim, 0)

    lens = jnp.sum((pao_domain >= 0).astype(jnp.int32), axis=1)

    lists = 3 * s.occ
    to_sibling, to_other, to_other_more, tables, pao_rows, gap_rows, counts, offsets = pl.pallas_call(
        functools.partial(pack_kernel, s),
        in_specs=[smem] * 3 + [vmem] * 4 + [anywhere],
        out_specs=[pinned] * 3 + [vmem] * 3 + [smem] * 2,
        out_shape=[
            jax.ShapeDtypeStruct((s.rows, LANES), jnp.bfloat16),
            jax.ShapeDtypeStruct((s.first, LANES), jnp.bfloat16),
            jax.ShapeDtypeStruct((s.rows - s.first, LANES), jnp.bfloat16),
            jax.ShapeDtypeStruct((3, 2 * LOW, s.occ * HIGH), jnp.bfloat16),
            jax.ShapeDtypeStruct(pao_domain.shape, pao_domain.dtype),
            jax.ShapeDtypeStruct(pao_gap.shape, pao_gap.dtype),
            jax.ShapeDtypeStruct((lists,), jnp.int32),
            jax.ShapeDtypeStruct((lists,), jnp.int32),
        ],
        scratch_shapes=[
            pltpu.VMEM((3, 2 * LOW, s.occ * HIGH), jnp.float32),
            pltpu.VMEM((3 * s.occ, 2 * LOW, s.occ * HIGH), jnp.float32),
            pltpu.VMEM((2, 2 * LOW, s.occ * HIGH), jnp.bfloat16),
            pltpu.SMEM((s.occ,), jnp.int32),
            pltpu.VMEM((2, s.rows + s.pao, LANES), jnp.bfloat16),
            pltpu.SemaphoreType.DMA((3,)),
        ],
        compiler_params=plain,
        cost_estimate=cost(10**11, 10**5),
        name="pack",
    )(here, pair_partner, lens, aux_domain, blocks_t, pao_domain.T, pao_gap.T, slim)

    repeats = s.pairs // s.occ
    both = pl.BlockSpec((repeats, 1, s.pao, s.aux), lambda g: (0, g, 0, 0))
    aligned, dens, to_other, to_sibling = pl.pallas_call(
        functools.partial(own_kernel, s),
        grid=(s.occ,),
        in_specs=[smem] * 4
        + [
            vmem,
            vmem,
            pl.BlockSpec((1, s.pao, s.aux), lambda g: (g, 0, 0)),
            pl.BlockSpec((repeats, 1, s.pao, s.pao), lambda g: (0, g, 0, 0)),
            anywhere,
            anywhere,
        ],
        out_specs=[both, pl.BlockSpec((1, s.pao, s.pao), lambda g: (g, 0, 0)), anywhere, anywhere],
        out_shape=[
            jax.ShapeDtypeStruct((repeats, s.occ, s.pao, s.aux), jnp.bfloat16),
            dens_shape,
            jax.ShapeDtypeStruct(to_other.shape, to_other.dtype),
            jax.ShapeDtypeStruct(to_sibling.shape, to_sibling.dtype),
        ],
        input_output_aliases={8: 2, 9: 3},
        compiler_params=stepped,
        cost_estimate=cost(10**11, 10**5),
        name="own",
    )(
        here, pair_partner, lens, counts, tables, aux_domain, blocks_t,
        amplitudes.reshape(repeats, s.occ, s.pao, s.pao), to_other, to_sibling,
    )
    from_other = swap(to_other, 1)
    from_sibling = swap(to_sibling, 0)
    aligned = aligned.reshape(s.pairs, s.pao, s.aux)

    (over,) = pl.pallas_call(
        functools.partial(count_kernel, s),
        in_specs=[smem] * 2 + [vmem, anywhere],
        out_specs=[smem],
        out_shape=[jax.ShapeDtypeStruct((1,), jnp.int32)],
        compiler_params=plain,
        cost_estimate=cost(10**11, 10**5),
        name="count",
    )(pair_partner, lens, aux_domain, dens)

    coupling, exchange, dens = pl.pallas_call(
        functools.partial(near_kernel, s, ncpl),
        grid=(s.pairs,),
        in_specs=[smem] * 8
        + [vmem] * 3
        + [pl.BlockSpec((1, s.pao, s.aux), lambda p: (p, 0, 0))]
        + [anywhere, pinned, anywhere],
        out_specs=[square, square, all_dens],
        out_shape=[squares, squares, dens_shape],
        scratch_shapes=[
            pltpu.VMEM((2 * s.pairs, s.pao, s.pao), jnp.bfloat16),
            pltpu.VMEM((ncpl * s.pao, s.pao), jnp.bfloat16),
            pltpu.VMEM((s.occ, s.pao, s.pao), jnp.float32),
            pltpu.VMEM((s.occ, s.pao, s.aux), jnp.bfloat16),
            pltpu.VMEM((s.rows + s.pao, LANES), jnp.bfloat16),
            pltpu.SemaphoreType.DMA((3,)),
        ],
        compiler_params=stepped,
        cost_estimate=cost(10**11, 10**5),
        name="near",
    )(
        here, pair_partner, coupling_list.T, lens, coupling_coef.T, counts, offsets, over,
        pao_rows, amps_sibling, amplitudes, aligned, dens, blocks_t, from_sibling,
    )

    bases, halves, densities, some_amps, some_energies = pl.pallas_call(
        functools.partial(far_kernel, s, ncpl),
        in_specs=[smem] * 5 + [vmem] * 7,
        out_specs=[vmem, vmem, vmem, pinned, smem],
        out_shape=[
            squares,
            squares,
            dens_shape,
            jax.ShapeDtypeStruct(amplitudes.shape, amplitudes.dtype),
            jax.ShapeDtypeStruct((s.pairs,), jnp.float32),
        ],
        scratch_shapes=[
            pltpu.VMEM((s.pairs, s.pao, s.pao), jnp.bfloat16),
            pltpu.VMEM((s.pairs, s.pao, s.pao), jnp.bfloat16),
            pltpu.SMEM((s.pairs * ncpl,), jnp.int32),
            pltpu.SMEM((s.pairs * ncpl,), jnp.int32),
            pltpu.SemaphoreType.DMA((s.pairs,)),
        ],
        input_output_aliases={9: 0},
        compiler_params=alone,
        cost_estimate=cost(10**10, 10**5),
        name="far",
    )(
        here, pair_partner, coupling_list.T, lens, coupling_coef.T,
        pao_rows, gap_rows, amps_other, amplitudes, coupling, exchange, dens,
    )

    more = (swap(to_other_more, 1),) if beyond else ()
    scratch = [
        pltpu.VMEM((s.pairs, s.pao, s.pao), jnp.bfloat16),
        pltpu.VMEM((2, s.pao, s.pao), jnp.float32),
        pltpu.SMEM((s.pairs,), jnp.int32),
        pltpu.SemaphoreType.DMA((s.pairs + 1,)),
    ]
    if beyond:
        scratch = [pltpu.VMEM((s.rows + s.pao, LANES), jnp.bfloat16)] + scratch
    new_amps, energies = pl.pallas_call(
        functools.partial(last_kernel, s, beyond),
        in_specs=[smem] * 6 + [vmem] * 5 + [pinned] * (len(more) + 1),
        out_specs=[pinned, smem],
        out_shape=[
            jax.ShapeDtypeStruct(amplitudes.shape, amplitudes.dtype),
            jax.ShapeDtypeStruct((s.pairs,), jnp.float32),
        ],
        scratch_shapes=scratch,
        input_output_aliases={11 + len(more): 0},
        compiler_params=alone,
        cost_estimate=cost(2 * s.pairs * s.pao * s.pao * s.aux, 2 * 10**7),
        name="last",
    )(
        here, pair_partner, lens, counts, offsets, some_energies,
        halves, aligned, bases, amplitudes, from_other, *more, some_amps,
    )
    return new_amps, energies, densities, over


def local(*arrays):
    new_amps, energies, densities, over = run(False, *arrays)
    new_amps, energies = lax.cond(
        over[0] > 0, lambda ops: run(True, *ops[2:])[:2], lambda ops: ops[:2], (new_amps, energies) + arrays
    )
    return (new_amps, energies, densities)


def solution(mesh):
    return jax.shard_map(
        local,
        mesh=mesh,
        in_specs=(
            P(AXES, None, None),
            P(),
            P(),
            P(),
            P(AXES, None, None),
            P(),
            P(AXES, None),
            P(AXES, None),
        ),
        out_specs=(P(AXES, None, None), P(AXES), P(AXES, None, None)),
        check_vma=False,
    )
```
